128 devices in a mesh: ex: 32 (over z, x, core), mp: 4 (over y).
Axes of the slice: x: 4, y: 4, z: 4, core: 2. Of those that a mesh axis runs over, the one named last changes fastest.
Arguments:
- tokens: bfloat16 [8192, 1024], P('ex'), may hold values from -6 to 6
- hash_ids: int32 [8192, 1], P('ex'), may hold values from 0 to 63; in each aligned block of 256 rows (0 to 255, 256 to 511, ...) at most 8 rows name the same one
- lengths: int32 [9], replicated, may hold values from 1 to 8064, 8192 in all
- norm1_gain: float32 [1024], replicated, may hold values from 0.5 to 1.5
- qkv_weight: bfloat16 [1024, 3, 1024], P(None, None, 'mp'), may hold values from -0.1875 to 0.1875
- out_weight: bfloat16 [1024, 1024], P('mp'), may hold values from -6 to 6
- norm2_gain: float32 [1024], replicated, may hold values from 0.5 to 1.5
- expert_in: bfloat16 [64, 1024, 4096], P('ex', None, 'mp'), may hold values from -0.1875 to 0.1875
- expert_out: bfloat16 [64, 4096, 1024], P('ex', 'mp'), may hold values from -0.09375 to 0.09375
- cotangent: bfloat16 [8192, 1024], P('ex'), may hold values from -6 to 6
Outputs:
- out: bfloat16 [8192, 1024], P('ex', 'mp')
- input_grad: bfloat16 [8192, 1024], P('ex')
- norm1_gain_grad: float32 [1024], replicated
- qkv_grad: float32 [1024, 3, 1024], P(None, None, 'mp')
- out_weight_grad: float32 [1024, 1024], P('mp')
- norm2_gain_grad: float32 [1024], replicated
- expert_in_grad: float32 [64, 1024, 4096], P('ex', None, 'mp')
- expert_out_grad: float32 [64, 4096, 1024], P('ex', 'mp')
The draws below stay inside these ranges and needn't reach their ends.
Inputs may be any that keep to these rules, and one draw needn't show every extreme that they name: `hash_ids`: among the 256 rows of one device no expert is named more than 8 times, a bound that some block reaches. The documents lie end to end in the order given, so the lengths sum to 8192; the longest has exactly 8064 tokens.
All inputs are finite; a program needn't handle non-finite values.
Results may differ from the reference program's by a relative error of at most 0.03.
Values may be sent and summed in bfloat16 or wider, within the bound.
A program may use at most 128 MiB of HBM per device.

```python
import functools
import math
import jax
import jax.numpy as jnp
import numpy as np
from jax import lax

D = 1024
HEADS = 16
HEAD_DIM = 64
FF = 4096
TOK_DEV = 256
NDOCS = 9
EXPERTS = 64
TOKENS = 8192
CAP = 8
LONGEST = 8064


def block_scale(stream_key, shape, cuts, smallest, largest):
    loudness = 1.0
    for position, parts in cuts:
        steps = jax.random.uniform(jax.random.fold_in(jax.random.fold_in(stream_key, 6), position), (parts,), jnp.float32, smallest / len(cuts), largest / len(cuts))
        loudness = loudness * jnp.repeat(jnp.exp(steps), shape[position] // parts).reshape((-1,) + (1,) * (len(shape) - 1 - position))
    return loudness


def split_up(number_of, total, most, lean):
    portions = [(1 << 20) // math.isqrt(standing ** lean) + 1 for standing in range(2, number_of + 1)]
    surplus, counts = total - most - (number_of - 1), [1] * (number_of - 1)
    while surplus > 0:
        free = [i for i in range(number_of - 1) if counts[i] < most]
        pool, left = sum([portions[i] for i in free]), surplus
        for i in free:
            addition = min(most - counts[i], max(1, left * portions[i] // pool), surplus)
            counts[i] = counts[i] + addition
            surplus = surplus - addition
    return np.array([most] + counts)


def uneven_parts(rng, amount, total, reach, lean):
    if amount == 2:
        one = jax.random.randint(rng, (), max(1, total - reach), min(reach, total - 1) + 1)
        return jnp.stack([one, total - one])
    sizes = jnp.asarray(split_up(amount, total, reach, lean), jnp.int32)
    couples = (amount - 1) // 2
    donor, sink = sizes[1:1 + 2 * couples:2], sizes[2:2 + 2 * couples:2]
    slack = jnp.minimum(donor - 1, reach - sink)
    moved = jax.random.randint(jax.random.fold_in(rng, 1), (couples,), 0, 1 << 20) % (slack + 1)
    sizes = sizes.at[1:1 + 2 * couples:2].set(donor - moved).at[2:2 + 2 * couples:2].set(sink + moved)
    return sizes[jax.random.permutation(jax.random.fold_in(rng, 2), amount)]


def deal_out(key, own, number, rows, number_of, top, most, skew):
    ranking = jax.random.permutation(key, number_of)
    crowded, usual = load_shares(number_of, rows * top, most, skew, True), load_shares(number_of, rows * top, most, skew, False)
    places = jnp.arange(number_of)

    def named(tallies, turn):
        used = int((tallies > 0).sum())
        fixed = max(1, used // 4)
        passed = fixed + (places - fixed + turn * (used - fixed)) % max(1, number_of - fixed)
        return jnp.zeros((number_of,), jnp.int32).at[ranking[jnp.where(places < fixed, places, passed)]].set(jnp.asarray(tallies, jnp.int32))

    tallies = jnp.where(number % 4 == 0, named(crowded, number // 4), named(usual, number - number // 4 - 1))
    mixed = jax.random.permutation(jax.random.fold_in(own, 3), number_of)
    giver, sink = mixed[0:number_of // 2 * 2:2], mixed[1:number_of // 2 * 2:2]
    room = jnp.minimum(tallies[giver] - 1, most - tallies[sink]) // 2
    room = jnp.where((giver == ranking[0]) | (sink == ranking[0]) | (tallies[sink] == 0), 0, jnp.maximum(room, 0))
    passed = jax.random.randint(jax.random.fold_in(own, 4), (number_of // 2,), 0, 1 << 20) % (room + 1)
    tallies = tallies.at[giver].add(-passed).at[sink].add(passed)
    labels = jnp.searchsorted(jnp.cumsum(tallies), jnp.arange(rows * top), side="right").astype(jnp.int32)
    table = labels.reshape(top, rows).T
    table = table[jax.random.permutation(jax.random.fold_in(own, 1), rows)]
    turn = jax.random.randint(jax.random.fold_in(own, 2), (rows, 1), 0, top)
    return jnp.take_along_axis(table, (jnp.arange(top)[None, :] + turn) % top, axis=1)


def load_shares(amount, total, bound, slope, full):
    loads = [(1 << 20) // math.isqrt(rank ** slope) + 1 for rank in range(1, amount + 1)]
    largest = bound if full else min(bound, max(-(-total // amount), total * loads[0] // sum(loads)))
    least = 1 if total - largest >= amount - 1 else 0
    counts, rest = [largest] + [least] * (amount - 1), total - largest - least * (amount - 1)
    while rest > 0:
        movable = [i for i in range(1, amount) if counts[i] < largest] or [i for i in range(1, amount) if counts[i] < bound]
        pool, left = sum([loads[i] for i in movable]), rest
        for i in movable:
            extra = min(bound - counts[i], max(1, left * loads[i] // pool), rest)
            counts[i] = counts[i] + extra
            rest = rest - extra
    return np.array(counts)


def gaussian(rng, shape, width, limit, split=(), kind=jnp.bfloat16):
    factor_of = block_scale(rng, shape, split, -0.22, 0.18) if split else 1.0
    values = jax.random.normal(rng, shape, jnp.float32) * width * factor_of
    return jnp.minimum(jnp.maximum(values, -limit), limit).astype(kind)


def setup_inputs(seed: int = 0) -> dict:
    key_list = jax.random.split(jax.random.key(seed), 11)
    tokens = gaussian(key_list[0], (TOKENS, D), 1.0, 6.0, ((0, 32),))
    hash_ids_keys = jax.random.split(jax.random.fold_in(key_list[1], 1), TOKENS // TOK_DEV)
    hash_ids_turns = jax.random.permutation(jax.random.fold_in(key_list[1], 3), TOKENS // TOK_DEV)
    hash_ids = jax.vmap(lambda own, number: deal_out(jax.random.fold_in(key_list[1], 2), own, number, TOK_DEV, EXPERTS, 1, CAP, 1))(hash_ids_keys, hash_ids_turns).reshape((TOKENS, 1))
    lengths = uneven_parts(key_list[2], NDOCS, TOKENS, LONGEST, 2).astype(jnp.int32)
    norm1_gain = jnp.clip(jax.random.uniform(key_list[3], (D,), jnp.float32, 0.5, 1.5), 0.5, 1.5)
    qkv_weight = gaussian(key_list[4], (D, 3, D), D ** -0.5, 0.1875, ((2, 4),))
    out_weight = gaussian(key_list[5], (D, D), 1.0, 6.0, ((0, 4),))
    norm2_gain = jnp.clip(jax.random.uniform(key_list[6], (D,), jnp.float32, 0.5, 1.5), 0.5, 1.5)
    expert_in = gaussian(key_list[7], (EXPERTS, D, FF), D ** -0.5, 0.1875, ((0, 32), (2, 4)))
    expert_out = gaussian(key_list[8], (EXPERTS, FF, D), FF ** -0.5, 0.09375, ((0, 32), (1, 4)))
    cotangent = gaussian(key_list[9], (TOKENS, D), 1.0, 6.0, ((0, 32),))
    return dict(tokens=tokens, hash_ids=hash_ids, lengths=lengths, norm1_gain=norm1_gain, qkv_weight=qkv_weight, out_weight=out_weight, norm2_gain=norm2_gain, expert_in=expert_in, expert_out=expert_out, cotangent=cotangent)


epsilon = 1e-05
negative_fill = -1e+30
highest = lax.Precision.HIGHEST

@jax.custom_vjp
def low(v):
    return lax.optimization_barrier(v.astype(jnp.bfloat16)).astype(jnp.float32)

@jax.custom_vjp
def low_back(v):
    return v

def low_keep(v):
    return (low(v), None)

def low_pass(kept, grad):
    return (grad,)

def back_keep(v):
    return (v, None)

def back_low(kept, grad):
    return (low(grad),)
low.defvjp(low_keep, low_pass)
low_back.defvjp(back_keep, back_low)

def doc_numbers(lengths, first, count):
    doc_ends = jnp.cumsum(lengths.astype(jnp.int32))
    positions = first + jnp.arange(count, dtype=jnp.int32)
    return lax.optimization_barrier(jnp.sum((positions[:, None] >= doc_ends[None, :]).astype(jnp.int32), axis=1))

def slot_numbers(hash_ids):
    chosen = hash_ids[:, 0].astype(jnp.int32)
    one_hot = (chosen[:, None] == jnp.arange(EXPERTS, dtype=jnp.int32)[None, :]).astype(jnp.int32)
    blocked = one_hot.reshape(TOKENS // TOK_DEV, TOK_DEV, EXPERTS)
    earlier = jnp.cumsum(blocked, axis=1) - blocked
    slot_rank = lax.optimization_barrier(jnp.sum(earlier * blocked, axis=2)).reshape(TOKENS)
    block_ids = jnp.arange(TOKENS, dtype=jnp.int32) // TOK_DEV
    return (chosen * (TOKENS // TOK_DEV) + block_ids) * CAP + slot_rank

def layer_norm(inputs, gain_row):
    row_mean = lax.optimization_barrier(jnp.mean(inputs, axis=-1, keepdims=True))
    centred = inputs - row_mean
    variance = lax.optimization_barrier(jnp.mean(centred * centred, axis=-1, keepdims=True))
    return centred * lax.rsqrt(variance + epsilon) * gain_row

def attend_block(block_start, query_rows, key_rows, value_rows, query_docs, key_docs):
    scores = jnp.einsum('qhd,khd->hqk', query_rows, key_rows, precision=highest) * HEAD_DIM ** (-0.5)
    scores = low_back(scores)
    query_pos = block_start + jnp.arange(query_rows.shape[0], dtype=jnp.int32)
    key_pos = jnp.arange(key_rows.shape[0], dtype=jnp.int32)
    allowed = (key_pos[None, :] <= query_pos[:, None]) & (key_docs[None, :] == query_docs[:, None])
    masked = jnp.where(allowed[None], scores, negative_fill)
    row_peak = lax.optimization_barrier(jnp.max(masked, axis=2, keepdims=True))
    weights = jnp.where(allowed[None], jnp.exp(masked - row_peak), 0.0)
    weights = low(weights / lax.optimization_barrier(jnp.sum(weights, axis=2, keepdims=True)))
    return jnp.einsum('hqk,khd->qhd', weights, value_rows, precision=highest)

def expert_item(expert_trio):
    hidden_pre = low_back(jnp.dot(expert_trio[0], expert_trio[1], precision=highest))
    hidden = low(jax.nn.gelu(hidden_pre))
    return jnp.dot(hidden, expert_trio[2], precision=highest)

def forward(inputs, gain_one, weight_qkv, weight_out, gain_two, weight_in, weight_back, doc_ids, slot_ids):
    normed = low(layer_norm(inputs, gain_one))
    projected = low_back(low(jnp.dot(normed, weight_qkv.reshape(D, 3 * D), precision=highest)))
    query_all = projected[:, :D].reshape(TOKENS, HEADS, HEAD_DIM)
    key_all = projected[:, D:2 * D].reshape(TOKENS, HEADS, HEAD_DIM)
    value_all = projected[:, 2 * D:].reshape(TOKENS, HEADS, HEAD_DIM)
    block_len = min(512, TOKENS)
    pieces = []
    for block_start in range(0, TOKENS, block_len):
        block_end = min(block_start + block_len, TOKENS)
        block_fn = jax.checkpoint(functools.partial(attend_block, block_start))
        pieces.append(block_fn(query_all[block_start:block_end], key_all[:block_end], value_all[:block_end], doc_ids[block_start:block_end], doc_ids[:block_end]))
    attended = low_back(low(jnp.concatenate(pieces, axis=0).reshape(TOKENS, D)))
    residual = inputs + low_back(jnp.dot(attended, weight_out, precision=highest))
    mixed = low_back(low(layer_norm(residual, gain_two)))
    slotted = jnp.zeros((EXPERTS * (TOKENS // TOK_DEV) * CAP, D), jnp.float32).at[slot_ids].set(mixed)
    slotted = slotted.reshape(EXPERTS, TOKENS // TOK_DEV * CAP, D)
    expert_outs = lax.map(jax.checkpoint(expert_item), (slotted, weight_in, weight_back))
    branch = low_back(low(expert_outs.reshape(EXPERTS * (TOKENS // TOK_DEV) * CAP, D)))[slot_ids]
    return residual + branch

def reference(tokens, hash_ids, lengths, norm1_gain, qkv_weight, out_weight, norm2_gain, expert_in, expert_out, cotangent):
    doc_ids = doc_numbers(lengths, 0, TOKENS)
    slot_ids = slot_numbers(hash_ids)
    layer_fn = functools.partial(forward, doc_ids=doc_ids, slot_ids=slot_ids)
    outputs, pullback = jax.vjp(layer_fn, tokens.astype(jnp.float32), norm1_gain.astype(jnp.float32), qkv_weight.astype(jnp.float32), out_weight.astype(jnp.float32), norm2_gain.astype(jnp.float32), expert_in.astype(jnp.float32), expert_out.astype(jnp.float32))
    gradients = pullback(cotangent.astype(jnp.float32))
    return (outputs.astype(jnp.bfloat16), gradients[0].astype(jnp.bfloat16), gradients[1], gradients[2], gradients[3], gradients[4], gradients[5], gradients[6])
```

```python
import functools

import jax
import jax.numpy as jnp
from jax import lax
from jax.experimental import pallas as pl
from jax.experimental.pallas import tpu as pltpu
from jax.sharding import PartitionSpec as P

HEAD_DIM = 64
epsilon = 1e-05
negative_fill = -1e30
MESH = pl.DeviceIdType.MESH
bf16, f32 = jnp.bfloat16, jnp.float32
EX, MP = 32, 4


def dot(a, b, ca=1, cb=0):
    return lax.dot_general(a, b, (((ca,), (cb,)), ((), ())), preferred_element_type=f32)


def place():
    ex, mp = lax.axis_index("ex"), lax.axis_index("mp")
    z, x, c = ex // 8, (ex // 2) % 4, ex % 2
    return ex, mp, z, x, c


def send(src, dst, ssem, rsem, device):
    copy = pltpu.make_async_remote_copy(
        src_ref=src, dst_ref=dst, send_sem=ssem, recv_sem=rsem, device_id=device, device_id_type=MESH
    )
    copy.start()
    return copy


def greet(ex, mp):
    bar = pltpu.get_barrier_semaphore()

    def one(d, carry):
        pl.semaphore_signal(bar, inc=1, device_id=(lax.rem(ex + d, EX), mp), device_id_type=MESH)
        return carry

    lax.fori_loop(1, EX, one, 0)
    for d in range(1, MP):
        pl.semaphore_signal(bar, inc=1, device_id=(ex, lax.rem(mp + d, MP)), device_id_type=MESH)
    return bar


def greeted(bar):
    pl.semaphore_wait(bar, EX - 1 + MP - 1)


def slot_matrix(chosen_row):
    tok = chosen_row.shape[1]
    experts = lax.broadcasted_iota(jnp.int32, (64, tok), 0)
    hot = (experts == chosen_row).astype(f32)
    rows = lax.broadcasted_iota(jnp.int32, (tok, tok), 0)
    cols = lax.broadcasted_iota(jnp.int32, (tok, tok), 1)
    before = (rows < cols).astype(bf16)
    earlier = dot(hot.astype(bf16), before)
    rank = jnp.sum(earlier * hot, axis=0, keepdims=True)
    target = chosen_row * 8 + rank.astype(jnp.int32)
    slots = lax.broadcasted_iota(jnp.int32, (512, tok), 0)
    return (slots == target).astype(f32).astype(bf16)


def doc_row(ends, first, count):
    pos = first + lax.broadcasted_iota(jnp.int32, (1, count), 1)
    row = jnp.zeros((1, count), jnp.int32)
    for end in ends:
        row = row + (pos >= end).astype(jnp.int32)
    return row


def doc_ends(lengths_ref):
    ends, total = [], 0
    for i in range(9):
        total = total + lengths_ref[i]
        ends.append(total)
    return ends


def norm_parts(v):
    mean = jnp.mean(v, axis=-1, keepdims=True)
    centred = v - mean
    inverse = lax.rsqrt(jnp.mean(centred * centred, axis=-1, keepdims=True) + epsilon)
    return centred * inverse, inverse


def transposed(v):
    return v.T


def front_kernel(
    lengths, tokens, gain, chosen, wqkv_hbm, wout, cot,
    normed_out, kvt, q_out, ot_out, lse_out, att, cot_rows, wfull,
    wqkv, q_s, kv_s, qaug, kaug, vt1, acc, peak, o_s, outgoing,
    wsem, az_s, az_r, ag_s, ag_r, cot_s, cot_r, oz_s, oz_r, oy_s, oy_r, wf_s, wf_r,
):
    ex, mp, z, x, c = place()
    d = 1 - 2 * c
    j = x * 2 + c
    bar = greet(ex, mp)
    wcopy = pltpu.make_async_copy(wqkv_hbm, wqkv, wsem)
    wcopy.start()
    unit, _ = norm_parts(tokens[...].astype(f32))
    normed = (unit * gain[...]).astype(bf16)
    normed_out[...] = normed
    wcopy.wait()
    qt = transposed((dot(normed, wqkv[0]).astype(bf16) * HEAD_DIM ** (-0.5)).astype(bf16))
    kt = transposed(dot(normed, wqkv[1]).astype(bf16))
    vt = transposed(dot(normed, wqkv[2]).astype(bf16))
    for h in range(4):
        q_s[h] = qt[64 * h:64 * h + 64]
        kv_s[h, 0:64] = kt[64 * h:64 * h + 64]
        kv_s[h, 64:128] = vt[64 * h:64 * h + 64]
    greeted(bar)
    zsends = []
    for i in range(1, 4):
        zp = lax.rem(z + i, 4)
        to = (zp * 8 + j, mp)
        zsends.append(send(kv_s.at[zp], kvt.at[0, z], az_s.at[i - 1], az_r.at[i - 1], to))
        zsends.append(send(q_s.at[zp], q_out.at[z], az_s.at[i + 2], az_r.at[i + 2], to))
    wsends = []
    for i in range(1, 4):
        wsends.append(
            send(wout, wfull.at[mp], wf_s.at[i - 1], wf_r.at[i - 1], (ex, lax.rem(mp + i, MP)))
        )
    kvt[0, z] = kv_s[z]
    q_out[z] = q_s[z]
    wfull[mp] = wout[...]
    vt1[64:80, :] = jnp.ones((16, 1024), bf16)
    ends = doc_ends(lengths)
    experts_rows = dot(slot_matrix(chosen[...]), cot[...]).astype(bf16)
    outgoing[...] = experts_rows.reshape(EX, 16, 1024)
    cot_rows[ex] = outgoing[ex]
    feature = lax.broadcasted_iota(jnp.int32, (64, 256), 0)
    for i in range(1, 4):
        zp = lax.rem(z + 4 - i, 4)
        pltpu.make_async_remote_copy(
            src_ref=kv_s.at[zp], dst_ref=kvt.at[0, zp], send_sem=az_s.at[i - 1], recv_sem=az_r.at[i - 1],
            device_id=(zp * 8 + j, mp), device_id_type=MESH).wait_recv()
    sib = (ex + d, mp)
    ahead = (z * 8 + lax.rem(x + d + 4, 4) * 2 + c, mp)
    behind = (z * 8 + lax.rem(x - d + 4, 4) * 2 + c, mp)
    asends = [
        send(kvt.at[0], kvt.at[2], ag_s.at[1], ag_r.at[2], ahead),
        send(kvt.at[0], kvt.at[6], ag_s.at[2], ag_r.at[6], behind),
        send(kvt.at[0], kvt.at[1], ag_s.at[0], ag_r.at[1], sib),
    ]

    def came(slot):
        pltpu.make_async_remote_copy(
            src_ref=kvt.at[0], dst_ref=kvt.at[slot], send_sem=ag_s.at[0], recv_sem=ag_r.at[slot],
            device_id=sib, device_id_type=MESH).wait_recv()

    for i in range(1, 4):
        zp = lax.rem(z + 4 - i, 4)
        pltpu.make_async_remote_copy(
            src_ref=q_s.at[zp], dst_ref=q_out.at[zp], send_sem=az_s.at[i + 2], recv_sem=az_r.at[i + 2],
            device_id=(zp * 8 + j, mp), device_id_type=MESH).wait_recv()
    for b in range(4):
        docs = doc_row(ends, (b * 8 + j) * 256, 256)
        qaug[b, 0:64] = q_out[b]
        qaug[b, 64:128] = jnp.where(feature == docs, 0.0, negative_fill).astype(bf16)
        peak[b] = jnp.full((1, 256), negative_fill, f32)
        acc[b] = jnp.zeros((80, 256), f32)

    def load_chunk(slot, jp):
        for b in range(4):
            docs = doc_row(ends, (b * 8 + jp) * 256, 256)
            hot = (feature == docs).astype(f32).astype(bf16)
            block = kvt[slot, b]
            kaug[256 * b:256 * b + 256, :] = transposed(jnp.concatenate([block[0:64], hot], axis=0))
            vt1[0:64, 256 * b:256 * b + 256] = block[64:128]

    def update(b, n, causal):
        s = dot(kaug[0:n, :], qaug[b])
        if causal:
            rows = lax.broadcasted_iota(jnp.int32, (n, 256), 0)
            cols = lax.broadcasted_iota(jnp.int32, (n, 256), 1)
            s = jnp.where(rows - 256 * b <= cols, s, negative_fill)
        old = peak[b]
        new = jnp.maximum(old, jnp.max(s, axis=0, keepdims=True))
        p = jnp.exp(s - new).astype(bf16)
        acc[b] = acc[b] * jnp.exp(old - new) + dot(vt1[:, 0:n], p)
        peak[b] = new

    load_chunk(0, j)
    for b in range(4):
        update(b, 256 * b + 256, True)

    def chunk(i, carry):
        t = i + (i // 4) * (2 - 4 * ((i // 2) % 2))
        jp = ((x - d * (t // 2) + 8) % 4) * 2 + (c + t) % 2

        @pl.when(i == 1)
        def _():
            came(1)

        @pl.when(i == 2)
        def _():
            came(2)
            send(kvt.at[2], kvt.at[4], ag_s.at[3], ag_r.at[4], ahead)
            send(kvt.at[2], kvt.at[7], ag_s.at[4], ag_r.at[7], sib)
            came(6)
            send(kvt.at[6], kvt.at[3], ag_s.at[5], ag_r.at[3], sib)

        @pl.when(i == 3)
        def _():
            came(3)

        @pl.when(i == 4)
        def _():
            came(4)
            send(kvt.at[4], kvt.at[5], ag_s.at[6], ag_r.at[5], sib)

            def cot_send(k, carry):
                to = lax.rem(ex + k, EX)
                send(outgoing.at[to], cot_rows.at[ex], cot_s.at[k - 1], cot_r.at[k - 1], (to, mp))
                return carry

            lax.fori_loop(1, EX, cot_send, 0)

        @pl.when(i == 5)
        def _():
            came(7)

        @pl.when(i == 7)
        def _():
            came(5)

        load_chunk(t, jp)

        @pl.when(jp < j)
        def _():
            for b in range(4):
                update(b, 256 * b + 256, False)

        @pl.when(jp > j)
        def _():
            for b in range(1, 4):
                update(b, 256 * b, False)

        return carry

    lax.fori_loop(1, 8, chunk, 0)
    for b in range(4):
        total = acc[b, 64:65]
        ot = acc[b, 0:64] / total
        ot_out[b] = ot
        lse_out[b] = peak[b] + jnp.log(total)
        o_s[b] = ot.astype(bf16)
    osends = []
    for i in range(1, 4):
        zp = lax.rem(z + i, 4)
        osends.append(send(o_s.at[zp], att.at[mp, z], oz_s.at[i - 1], oz_r.at[i - 1], (zp * 8 + j, mp)))
    att[mp, z] = o_s[z]
    for i in range(1, 4):
        zp = lax.rem(z + 4 - i, 4)
        pltpu.make_async_remote_copy(
            src_ref=o_s.at[zp], dst_ref=att.at[mp, zp], send_sem=oz_s.at[i - 1], recv_sem=oz_r.at[i - 1],
            device_id=(zp * 8 + j, mp), device_id_type=MESH).wait_recv()
    ysends = []
    for i in range(1, 4):
        ysends.append(send(att.at[mp], att.at[mp], oy_s.at[i - 1], oy_r.at[i - 1], (ex, lax.rem(mp + i, MP))))
    for i in range(1, 4):
        ym = lax.rem(mp + 4 - i, MP)
        pltpu.make_async_remote_copy(
            src_ref=att.at[mp], dst_ref=att.at[ym], send_sem=oy_s.at[i - 1], recv_sem=oy_r.at[i - 1],
            device_id=(ex, ym), device_id_type=MESH).wait_recv()
        pltpu.make_async_remote_copy(
            src_ref=wout, dst_ref=wfull.at[ym], send_sem=wf_s.at[i - 1], recv_sem=wf_r.at[i - 1],
            device_id=(ex, ym), device_id_type=MESH).wait_recv()

    def cot_wait(k, carry):
        to, back = lax.rem(ex + k, EX), lax.rem(ex + EX - k, EX)
        copy = pltpu.make_async_remote_copy(
            src_ref=outgoing.at[to], dst_ref=cot_rows.at[back], send_sem=cot_s.at[k - 1],
            recv_sem=cot_r.at[k - 1], device_id=(to, mp), device_id_type=MESH)
        copy.wait_send()
        copy.wait_recv()
        return carry

    lax.fori_loop(1, EX, cot_wait, 0)
    for copy in zsends + wsends + asends + osends + ysends:
        copy.wait_send()
    for i in range(3, 7):
        pltpu.make_async_remote_copy(
            src_ref=kvt.at[0], dst_ref=kvt.at[1], send_sem=ag_s.at[i], recv_sem=ag_r.at[1],
            device_id=sib, device_id_type=MESH).wait_send()


VM = pl.BlockSpec(memory_space=pltpu.VMEM)
SM = pl.BlockSpec(memory_space=pltpu.SMEM)
ANY = pl.BlockSpec(memory_space=pl.ANY)
DMA = pltpu.SemaphoreType.DMA


def front(lengths, tokens, gain, chosen, wqkv, wout, cot):
    outs = [
        ((256, 1024), bf16), ((8, 4, 128, 256), bf16), ((4, 64, 256), bf16), ((4, 64, 256), f32),
        ((4, 1, 256), f32), ((4, 4, 64, 256), bf16), ((32, 16, 1024), bf16), ((4, 256, 1024), bf16),
    ]
    return pl.pallas_call(
        front_kernel,
        out_shape=[jax.ShapeDtypeStruct(s, t) for s, t in outs],
        in_specs=[SM, VM, VM, VM, ANY, VM, VM],
        out_specs=[VM] * 8,
        scratch_shapes=[
            pltpu.VMEM((3, 1024, 256), bf16), pltpu.VMEM((4, 64, 256), bf16), pltpu.VMEM((4, 128, 256), bf16),
            pltpu.VMEM((4, 128, 256), bf16), pltpu.VMEM((1024, 128), bf16), pltpu.VMEM((80, 1024), bf16),
            pltpu.VMEM((4, 80, 256), f32), pltpu.VMEM((4, 1, 256), f32), pltpu.VMEM((4, 64, 256), bf16),
            pltpu.VMEM((32, 16, 1024), bf16),
            DMA, DMA((6,)), DMA((6,)), DMA((7,)), DMA((8,)), DMA((31,)), DMA((31,)),
            DMA((3,)), DMA((3,)), DMA((3,)), DMA((3,)), DMA((3,)), DMA((3,)),
        ],
        name="front",
        compiler_params=pltpu.CompilerParams(
            collective_id=0, has_side_effects=True, vmem_limit_bytes=56 << 20),
    )(lengths, tokens, gain, chosen, wqkv, wout, cot)
def norm_back(grad_out, gain_row, unit, inverse):
    scaled = grad_out * gain_row
    centred = scaled - jnp.mean(scaled, axis=-1, keepdims=True)
    grad_in = inverse * (centred - unit * jnp.mean(scaled * unit, axis=-1, keepdims=True))
    return grad_in, jnp.sum(grad_out * unit, axis=0, keepdims=True)


def gelu_parts(pre):
    k = 0.7978845608028654
    square = pre * pre
    t = jnp.tanh(k * pre * (1.0 + 0.044715 * square))
    half = 0.5 * (1.0 + t)
    slope = half + 0.5 * pre * (1.0 - t * t) * (k * (1.0 + 3 * 0.044715 * square))
    return pre * half, slope


def one_expert(rows, le):
    wide = rows.astype(f32)
    return wide[:, 8 * le:8 * le + 8].reshape(256, rows.shape[2]).astype(bf16)


def both_experts(first, second):
    width = first.shape[1]
    return jnp.concatenate([first.reshape(32, 8, width), second.reshape(32, 8, width)], axis=1).astype(bf16)


def middle_kernel(
    att, wfull, tokens, cot, gain, chosen, cot_hbm, win_hbm, wex_hbm,
    x_out, c_out, hid_out, gpre_out, branch_out, rescol_out, gres_out, dot_out, wgrad_out, ggrad_out,
    win, wex, cot_rows, outgoing, arrived, gh, part, rs, back_s, back, gn, resid,
    csem, wsem, di_s, di_r, rs_s, rs_r, ba_s, ba_r, gy_s, gy_r,
):
    ex, mp, z, x, c = place()
    bar = greet(ex, mp)
    copies = [
        pltpu.make_async_copy(cot_hbm, cot_rows, csem),
        pltpu.make_async_copy(wex_hbm, wex, wsem.at[0]),
        pltpu.make_async_copy(win_hbm, win, wsem.at[1]),
    ]
    for copy in copies:
        copy.start()
    placer = slot_matrix(chosen[...])
    branch = dot(att[...].reshape(1024, 256), wfull[...].reshape(1024, 1024), 0, 0)
    value = tokens[...].astype(f32) + branch
    resid[...] = value
    for q in range(4):
        @pl.when(mp == q)
        def _():
            rescol_out[...] = value[:, 256 * q:256 * q + 256]
    unit, inverse = norm_parts(value)
    outgoing[...] = dot(placer, (unit * gain[...]).astype(bf16)).astype(bf16).reshape(EX, 16, 1024)
    greeted(bar)

    def dispatch(k, carry):
        to = lax.rem(ex + k, EX)
        send(outgoing.at[to], arrived.at[ex], di_s.at[k - 1], di_r.at[k - 1], (to, mp))
        return carry

    lax.fori_loop(1, EX, dispatch, 0)
    arrived[ex] = outgoing[ex]
    copies[0].wait()
    copies[1].wait()
    for le in range(2):
        rows = one_expert(cot_rows[...], le)
        c_out[le] = rows
        gh[le] = dot(rows, wex[le], 1, 1)
    copies[2].wait()

    def dispatched(k, carry):
        to, source = lax.rem(ex + k, EX), lax.rem(ex + EX - k, EX)
        copy = pltpu.make_async_remote_copy(
            src_ref=outgoing.at[to], dst_ref=arrived.at[source], send_sem=di_s.at[k - 1],
            recv_sem=di_r.at[k - 1], device_id=(to, mp), device_id_type=MESH)
        copy.wait_send()
        copy.wait_recv()
        return carry

    lax.fori_loop(1, EX, dispatched, 0)
    sends = []
    for le in range(2):
        rows = one_expert(arrived[...], le)
        x_out[le] = rows
        hidden, slope = gelu_parts(dot(rows, win[le]))
        hid_out[le] = hidden.astype(bf16)
        gpre = (gh[le] * slope).astype(bf16)
        gpre_out[le] = gpre
        for q in range(4):
            part[le, q] = dot(gpre, win[le, 256 * q:256 * q + 256, :], 1, 1).astype(bf16)
        for i in range(1, 4):
            ym = lax.rem(mp + i, MP)
            sends.append(
                send(part.at[le, ym], rs.at[le, i - 1], rs_s.at[3 * le + i - 1], rs_r.at[3 * le + i - 1], (ex, ym)))
    firsts = dot(hid_out[0], wex[0])
    branch_out[...] = both_experts(firsts, dot(hid_out[1], wex[1]))
    sums = []
    for le in range(2):
        total = part[le, mp].astype(f32)
        for i in range(1, 4):
            sends[3 * le + i - 1].wait_recv()
            total = total + rs[le, i - 1].astype(f32)
        sums.append(total)
    back_s[...] = both_experts(sums[0], sums[1])

    def give(k, carry):
        to = lax.rem(ex + k, EX)
        send(back_s.at[to], back.at[ex], ba_s.at[k - 1], ba_r.at[k - 1], (to, mp))
        return carry

    lax.fori_loop(1, EX, give, 0)
    back[ex] = back_s[ex]

    def given(k, carry):
        to, source = lax.rem(ex + k, EX), lax.rem(ex + EX - k, EX)
        copy = pltpu.make_async_remote_copy(
            src_ref=back_s.at[to], dst_ref=back.at[source], send_sem=ba_s.at[k - 1],
            recv_sem=ba_r.at[k - 1], device_id=(to, mp), device_id_type=MESH)
        copy.wait_send()
        copy.wait_recv()
        return carry

    lax.fori_loop(1, EX, given, 0)
    gn[mp] = dot(slot_matrix(chosen[...]), back[...].reshape(512, 256), 0, 0).astype(bf16)
    ysends = []
    for i in range(1, 4):
        ysends.append(send(gn.at[mp], gn.at[mp], gy_s.at[i - 1], gy_r.at[i - 1], (ex, lax.rem(mp + i, MP))))
    unit, inverse = norm_parts(resid[...])
    for i in range(1, 4):
        ym = lax.rem(mp + 4 - i, MP)
        pltpu.make_async_remote_copy(
            src_ref=gn.at[mp], dst_ref=gn.at[ym], send_sem=gy_s.at[i - 1], recv_sem=gy_r.at[i - 1],
            device_id=(ex, ym), device_id_type=MESH).wait_recv()
    grad = jnp.concatenate([gn[q] for q in range(4)], axis=1).astype(f32)
    grad_in, ggrad = norm_back(grad, gain[...], unit, inverse)
    ggrad_out[...] = ggrad
    gres = cot[...].astype(f32) + grad_in
    gres_out[...] = gres
    low = gres.astype(bf16)
    dot_out[...] = dot(wfull[mp], low, 1, 1).astype(bf16).reshape(4, 64, 256)
    wgrad_out[...] = dot(att[mp].reshape(256, 256), low).astype(bf16)
    for copy in sends + ysends:
        copy.wait_send()


def middle(att, wfull, tokens, cot, gain, chosen, cot_rows, win, wex):
    rows = ((2, 256, 1024), bf16)
    outs = [
        rows, rows, rows, rows, ((32, 16, 1024), bf16), ((256, 256), f32), ((256, 1024), f32),
        ((4, 64, 256), bf16), ((256, 1024), bf16), ((1, 1024), f32),
    ]
    slots = pltpu.VMEM((32, 16, 1024), bf16)
    return pl.pallas_call(
        middle_kernel,
        out_shape=[jax.ShapeDtypeStruct(s, t) for s, t in outs],
        in_specs=[VM, VM, VM, VM, VM, VM, ANY, ANY, ANY],
        out_specs=[VM] * 10,
        scratch_shapes=[
            pltpu.VMEM((2, 1024, 1024), bf16), pltpu.VMEM((2, 1024, 1024), bf16), slots, slots, slots,
            pltpu.VMEM((2, 256, 1024), f32), pltpu.VMEM((2, 4, 256, 256), bf16),
            pltpu.VMEM((2, 3, 256, 256), bf16), pltpu.VMEM((32, 16, 256), bf16), pltpu.VMEM((32, 16, 256), bf16),
            pltpu.VMEM((4, 256, 256), bf16), pltpu.VMEM((256, 1024), f32),
            DMA, DMA((2,)), DMA((31,)), DMA((31,)), DMA((6,)), DMA((6,)), DMA((31,)), DMA((31,)), DMA((3,)), DMA((3,)),
        ],
        name="middle",
        compiler_params=pltpu.CompilerParams(
            collective_id=1, has_side_effects=True, vmem_limit_bytes=56 << 20),
    )(att, wfull, tokens, cot, gain, chosen, cot_rows, win, wex)
def last_kernel(
    lengths, dot_in, kvt, q_in, ot, lse, normed, wqkv_hbm, tokens, gain, gres, branch, rescol, chosen, ggrad,
    out, igrad, gains_out, wgrad_out,
    wqkv, dob, nall, brs, bs, bret, qaug, dopad, qd, delta, kaug, kvn, kt, dkv, dq,
    sb, sr, xs, xr, zs, zr, wp, wr, pieces, gnp, ry, small, smally, smalle,
    wsem, dz_s, dz_r, na_s, na_r, br_s, br_r, sb_s, sb_r, xs_s, xs_r, ba_s, ba_r, zq_s, zq_r,
    wp_s, wp_r, ag_s, ag_r, fw_s, fw_r, ry_s, ry_r, ay_s, ay_r, gy_s, gy_r, ge_s, ge_r,
):
    ex, mp, z, x, c = place()
    d = 1 - 2 * c
    j = x * 2 + c
    sib = (ex + d, mp)
    bar = greet(ex, mp)
    wcopy = pltpu.make_async_copy(wqkv_hbm, wqkv, wsem)
    wcopy.start()

    def zpeer(i):
        zp = lax.rem(z + i, 4)
        return zp, (zp * 8 + j, mp)

    def ypeer(i):
        ym = lax.rem(mp + i, MP)
        return ym, (ex, ym)

    greeted(bar)
    waits = []
    for i in range(1, 4):
        zp, to = zpeer(i)
        waits.append(send(dot_in.at[zp], dob.at[z], dz_s.at[i - 1], dz_r.at[i - 1], to))
    late = []
    for i in range(1, 4):
        ym, to = ypeer(i)
        late.append(send(
            branch.at[:, :, pl.ds(pl.multiple_of(256 * ym, 256), 256)], brs.at[i - 1],
            br_s.at[i - 1], br_r.at[i - 1], to))
    nsends = []
    for i in range(1, 4):
        zp, to = zpeer(i)
        nsends.append(send(normed, nall.at[z], na_s.at[i - 1], na_r.at[i - 1], to))
    dob[z] = dot_in[z]
    nall[z] = normed[...]
    ends = doc_ends(lengths)
    feature = lax.broadcasted_iota(jnp.int32, (64, 256), 0)
    zero = jnp.zeros((64, 256), bf16)

    def zcame(copy, dst, ssem, rsem, i):
        zp, to = zpeer(4 - i)
        pltpu.make_async_remote_copy(
            src_ref=copy, dst_ref=dst.at[zp], send_sem=ssem.at[i - 1], recv_sem=rsem.at[i - 1],
            device_id=to, device_id_type=MESH).wait_recv()

    for i in range(1, 4):
        zcame(dot_in.at[0], dob, dz_s, dz_r, i)
    for b in range(4):
        docs = doc_row(ends, (b * 8 + j) * 256, 256)
        mask = jnp.where(feature == docs, 0.0, negative_fill).astype(bf16)
        qaug[b, 0:64] = q_in[b]
        qaug[b, 64:128] = mask
        dopad[b, 0:64] = zero
        dopad[b, 64:128] = dob[b]
        qd[b, 0:256] = transposed(jnp.concatenate([q_in[b], zero], axis=0))
        qd[b, 256:512] = transposed(jnp.concatenate([zero, dob[b]], axis=0))
        delta[b] = jnp.sum(dob[b].astype(f32) * ot[b], axis=0, keepdims=True)
        dq[b] = jnp.zeros((64, 256), f32)

    def load_chunk(slot, jp):
        for b in range(4):
            docs = doc_row(ends, (b * 8 + jp) * 256, 256)
            hot = (feature == docs).astype(f32).astype(bf16)
            block = kvt[slot, b]
            kaug[256 * b:256 * b + 256, :] = transposed(jnp.concatenate([block[0:64], hot], axis=0))
            kvn[256 * b:256 * b + 256, :] = transposed(block)
            kt[:, 256 * b:256 * b + 256] = block[0:64]

    def update(b, n, causal):
        s = dot(kaug[0:n, :], qaug[b])
        if causal:
            rows = lax.broadcasted_iota(jnp.int32, (n, 256), 0)
            cols = lax.broadcasted_iota(jnp.int32, (n, 256), 1)
            s = jnp.where(rows - 256 * b <= cols, s, negative_fill)
        p = jnp.exp(s - lse[b])
        dp = dot(kvn[0:n, :], dopad[b])
        ds = (p * (dp - delta[b])).astype(bf16)
        added = dot(ds, qd[b, 0:256]) + dot(p.astype(bf16), qd[b, 256:512])
        if b == 3:
            dkv[0:n] = added
        else:
            dkv[0:n] = dkv[0:n] + added
        dq[b] = dq[b] + dot(kt[:, 0:n], ds)

    def sib_came(p):
        pltpu.make_async_remote_copy(
            src_ref=sb.at[p], dst_ref=sr.at[p], send_sem=sb_s.at[p], recv_sem=sb_r.at[p],
            device_id=sib, device_id_type=MESH).wait_recv()

    def chunk(i, carry):
        p = i // 2
        w = p + (p // 2) * (1 - 2 * (p % 2))
        g = (2 + d * w + 4) % 4
        t = 2 * g + 1 - i % 2
        xp = (x - d * g + 8) % 4
        jp = xp * 2 + (c + t) % 2
        load_chunk(t, jp)

        @pl.when(jp < j)
        def _():
            for b in range(3, -1, -1):
                update(b, 256 * b + 256, False)

        @pl.when(jp > j)
        def _():
            dkv[768:1024] = jnp.zeros((256, 128), f32)
            for b in range(3, 0, -1):
                update(b, 256 * b, False)

        @pl.when(i % 2 == 0)
        def _():
            sb[p] = dkv[...].astype(bf16)
            send(sb.at[p], sr.at[p], sb_s.at[p], sb_r.at[p], sib)

        @pl.when(i % 2 == 1)
        def _():
            sib_came(p)
            xs[p] = (dkv[...] + sr[p].astype(f32)).astype(bf16)
            send(xs.at[p], xr.at[p], xs_s.at[p], xs_r.at[p], (z * 8 + xp * 2 + c, mp))

        @pl.when(i == 4)
        def _():
            total = branch[:, :, pl.ds(pl.multiple_of(256 * mp, 256), 256)].astype(f32)
            for k in range(3):
                late[k].wait_recv()
                total = total + brs[k].astype(f32)
            bs[...] = total.astype(bf16)

            def give(k, carry):
                to = lax.rem(ex + k, EX)
                send(bs.at[to], bret.at[ex], ba_s.at[k - 1], ba_r.at[k - 1], (to, mp))
                return carry

            lax.fori_loop(1, EX, give, 0)
            bret[ex] = bs[ex]

        return carry

    lax.fori_loop(0, 7, chunk, 0)
    load_chunk(0, j)
    for b in range(3, -1, -1):
        update(b, 256 * b + 256, True)
    sib_came(3)
    total = dkv[...] + sr[3].astype(f32)
    for p in range(3):
        pltpu.make_async_remote_copy(
            src_ref=xs.at[p], dst_ref=xr.at[p], send_sem=xs_s.at[p], recv_sem=xs_r.at[p],
            device_id=sib, device_id_type=MESH).wait_recv()
        total = total + xr[p].astype(f32)
    low = total.astype(bf16)
    for b in range(4):
        zs[b, 0:64] = (dq[b] * HEAD_DIM ** (-0.5)).astype(bf16)
        zs[b, 64:192] = transposed(low[256 * b:256 * b + 256])
    for i in range(1, 4):
        zp, to = zpeer(i)
        waits.append(send(zs.at[zp], zr.at[z], zq_s.at[i - 1], zq_r.at[i - 1], to))
    zr[z] = zs[z]
    for i in range(1, 4):
        zcame(normed, nall, na_s, na_r, i)
    wt = dot(zs[0], nall[0])
    for b in range(1, 4):
        wt = wt + dot(zs[b], nall[b])
    wt = wt.astype(bf16)
    for k in range(8):
        wp[k] = wt[:, 128 * k:128 * k + 128]
    for i in range(1, 8):
        jt = lax.rem(j + i, 8)
        waits.append(send(wp.at[jt], wr.at[i - 1], wp_s.at[i - 1], wp_r.at[i - 1], (z * 8 + jt, mp)))
    for i in range(1, 4):
        zcame(zs.at[0], zr, zq_s, zq_r, i)
    wcopy.wait()
    part = None
    for k in range(3):
        heads = transposed(jnp.concatenate([zr[h, 64 * k:64 * k + 64] for h in range(4)], axis=0))
        term = dot(heads, wqkv[k], 1, 1)
        part = term if part is None else part + term
    gnp[...] = part.astype(bf16).reshape(4, 64, 1024)
    rsends = []
    for i in range(1, 4):
        ym, to = ypeer(i)
        rsends.append(send(gnp.at[ym], ry.at[i - 1], ry_s.at[i - 1], ry_r.at[i - 1], to))
    summed = wp[j].astype(f32)
    for i in range(7):
        waits[6 + i].wait_recv()
        summed = summed + wr[i].astype(f32)
    pieces[ex] = summed.astype(bf16)
    chip = ex // 2

    def spread(k, carry):
        to = lax.rem(chip + k, 16) * 2 + c
        send(pieces.at[ex], pieces.at[ex], ag_s.at[k - 1], ag_r.at[k - 1], (to, mp))
        return carry

    lax.fori_loop(1, 16, spread, 0)
    send(pieces.at[ex], pieces.at[ex], fw_s.at[0], fw_r.at[0], sib)
    grad = gnp[mp].astype(f32)
    for i in range(3):
        rsends[i].wait_recv()
        grad = grad + ry[i].astype(f32)
    mine = pl.ds(pl.multiple_of(64 * mp, 64), 64)
    unit, inverse = norm_parts(tokens[mine, :].astype(f32))
    grad_in, one_gain = norm_back(grad, gain[...], unit, inverse)
    igrad[mine, :] = (gres[mine, :] + grad_in).astype(bf16)
    small[...] = one_gain
    asends = []
    for i in range(1, 4):
        ym, to = ypeer(i)
        asends.append(send(small, smally.at[i - 1], gy_s.at[i - 1], gy_r.at[i - 1], to))
        asends.append(send(igrad.at[mine, :], igrad.at[mine, :], ay_s.at[i - 1], ay_r.at[i - 1], to))
    one_gain = small[...]
    for i in range(3):
        asends[2 * i].wait_recv()
        one_gain = one_gain + smally[i]
    smalle[ex, 0:1] = one_gain
    smalle[ex, 1:2] = ggrad[...]

    def gain_send(k, carry):
        to = lax.rem(ex + k, EX)
        send(smalle.at[ex], smalle.at[ex], ge_s.at[k - 1], ge_r.at[k - 1], (to, mp))
        return carry

    lax.fori_loop(1, EX, gain_send, 0)

    def given(k, carry):
        to, source = lax.rem(ex + k, EX), lax.rem(ex + EX - k, EX)
        copy = pltpu.make_async_remote_copy(
            src_ref=bs.at[to], dst_ref=bret.at[source], send_sem=ba_s.at[k - 1], recv_sem=ba_r.at[k - 1],
            device_id=(to, mp), device_id_type=MESH)
        copy.wait_send()
        copy.wait_recv()
        return carry

    lax.fori_loop(1, EX, given, 0)
    rows = dot(slot_matrix(chosen[...]), bret[...].reshape(512, 256), 0, 0)
    out[...] = (rescol[...] + rows).astype(bf16)

    def pass_on(k, carry):
        to = lax.rem(chip + k, 16) * 2 + c
        source = lax.rem(chip + 16 - k, 16) * 2 + c
        copy = pltpu.make_async_remote_copy(
            src_ref=pieces.at[ex], dst_ref=pieces.at[source], send_sem=ag_s.at[k - 1], recv_sem=ag_r.at[k - 1],
            device_id=(to, mp), device_id_type=MESH)
        copy.wait_send()
        copy.wait_recv()
        send(pieces.at[source], pieces.at[source], fw_s.at[k], fw_r.at[k], sib)
        return carry

    lax.fori_loop(1, 16, pass_on, 0)

    def passed(k, carry):
        source = lax.rem(chip + 16 - k, 16) * 2 + 1 - c
        copy = pltpu.make_async_remote_copy(
            src_ref=pieces.at[ex], dst_ref=pieces.at[source], send_sem=fw_s.at[k], recv_sem=fw_r.at[k],
            device_id=sib, device_id_type=MESH)
        copy.wait_send()
        copy.wait_recv()
        return carry

    lax.fori_loop(0, 16, passed, 0)
    for k in range(3):
        for r in range(8):
            block = jnp.concatenate([pieces[8 * h + r, 64 * k:64 * k + 64] for h in range(4)], axis=0)
            wgrad_out[k, 128 * r:128 * r + 128] = transposed(block)

    def gain_wait(k, carry):
        to, source = lax.rem(ex + k, EX), lax.rem(ex + EX - k, EX)
        copy = pltpu.make_async_remote_copy(
            src_ref=smalle.at[ex], dst_ref=smalle.at[source], send_sem=ge_s.at[k - 1], recv_sem=ge_r.at[k - 1],
            device_id=(to, mp), device_id_type=MESH)
        copy.wait_send()
        copy.wait_recv()
        return carry

    lax.fori_loop(1, EX, gain_wait, 0)
    gains_out[...] = jnp.sum(smalle[...], axis=0)
    for i in range(1, 4):
        ym, to = ypeer(4 - i)
        other = pl.ds(pl.multiple_of(64 * ym, 64), 64)
        pltpu.make_async_remote_copy(
            src_ref=igrad.at[mine, :], dst_ref=igrad.at[other, :], send_sem=ay_s.at[i - 1], recv_sem=ay_r.at[i - 1],
            device_id=to, device_id_type=MESH).wait_recv()
    for copy in waits + late + nsends + rsends + asends:
        copy.wait_send()
    for p in range(4):
        pltpu.make_async_remote_copy(
            src_ref=sb.at[p], dst_ref=sr.at[p], send_sem=sb_s.at[p], recv_sem=sb_r.at[p],
            device_id=sib, device_id_type=MESH).wait_send()
    for p in range(3):
        pltpu.make_async_remote_copy(
            src_ref=xs.at[p], dst_ref=xr.at[p], send_sem=xs_s.at[p], recv_sem=xs_r.at[p],
            device_id=sib, device_id_type=MESH).wait_send()


def last(lengths, dot_in, kvt, q_in, ot, lse, normed, wqkv, tokens, gain, gres, branch, rescol, chosen, ggrad):
    outs = [((256, 256), bf16), ((256, 1024), bf16), ((2, 1024), f32), ((3, 1024, 256), bf16)]

    def vmem(kind, *shape):
        return pltpu.VMEM(shape, kind)

    scratch = [
        vmem(bf16, 3, 1024, 256), vmem(bf16, 4, 64, 256), vmem(bf16, 4, 256, 1024), vmem(bf16, 3, 32, 16, 256),
        vmem(bf16, 32, 16, 256), vmem(bf16, 32, 16, 256), vmem(bf16, 4, 128, 256), vmem(bf16, 4, 128, 256),
        vmem(bf16, 4, 512, 128), vmem(f32, 4, 1, 256), vmem(bf16, 1024, 128), vmem(bf16, 1024, 128),
        vmem(bf16, 64, 1024), vmem(f32, 1024, 128), vmem(f32, 4, 64, 256),
        vmem(bf16, 4, 1024, 128), vmem(bf16, 4, 1024, 128), vmem(bf16, 3, 1024, 128), vmem(bf16, 3, 1024, 128),
        vmem(bf16, 4, 192, 256), vmem(bf16, 4, 192, 256), vmem(bf16, 8, 192, 128), vmem(bf16, 7, 192, 128),
        vmem(bf16, 32, 192, 128), vmem(bf16, 4, 64, 1024), vmem(bf16, 3, 64, 1024),
        vmem(f32, 1, 1024), vmem(f32, 3, 1, 1024), vmem(f32, 32, 2, 1024), DMA,
    ]
    for n in (3, 3, 3, 4, 3, 31, 3, 7, 15, 16, 3, 3, 3, 31):
        scratch += [DMA((n,)), DMA((n,))]
    return pl.pallas_call(
        last_kernel,
        out_shape=[jax.ShapeDtypeStruct(s, t) for s, t in outs],
        in_specs=[SM, VM, VM, VM, VM, VM, VM, ANY] + [VM] * 7,
        out_specs=[VM] * 4,
        scratch_shapes=scratch,
        name="last",
        compiler_params=pltpu.CompilerParams(
            collective_id=2, has_side_effects=True, vmem_limit_bytes=56 << 20),
    )(lengths, dot_in, kvt, q_in, ot, lse, normed, wqkv, tokens, gain, gres, branch, rescol, chosen, ggrad)
def expert_grads_kernel(x, gpre, hidden, cots, in_grad, out_grad):
    in_grad[0] = dot(x[0], gpre[0], 0, 0)
    out_grad[0] = dot(hidden[0], cots[0], 0, 0)


def expert_grads(x, gpre, hidden, cots):
    shape = jax.ShapeDtypeStruct((2, 1024, 1024), f32)
    width = 256
    tall = pl.BlockSpec((1, 256, width), lambda e, i: (e, 0, i))
    whole = pl.BlockSpec((1, 256, 1024), lambda e, i: (e, 0, 0))
    made = pl.BlockSpec((1, width, 1024), lambda e, i: (e, i, 0))
    return pl.pallas_call(
        expert_grads_kernel,
        grid=(2, 1024 // width),
        out_shape=[shape, shape],
        in_specs=[tall, whole, tall, whole],
        out_specs=[made, made],
        name="expert_grads",
        compiler_params=pltpu.CompilerParams(vmem_limit_bytes=48 << 20),
        cost_estimate=pl.CostEstimate(flops=2 * 2 * 2 * 256 * 1024 * 1024, bytes_accessed=20 << 20, transcendentals=0),
    )(x, gpre, hidden, cots)


def on_device(
    tokens, hash_ids, lengths, norm1_gain, qkv_weight, out_weight, norm2_gain, expert_in, expert_out, cotangent,
):
    chosen = hash_ids.reshape(1, 256)
    gain1, gain2 = norm1_gain.reshape(1, 1024), norm2_gain.reshape(1, 1024)
    wqkv = jnp.transpose(qkv_weight, (1, 0, 2))
    normed, kvt, q, ot, lse, att, cot_rows, wfull = front(
        lengths, tokens, gain1, chosen, wqkv, out_weight, cotangent)
    x, cots, hidden, gpre, branch, rescol, gres, dheads, wout_part, ggrad = middle(
        att, wfull, tokens, cotangent, gain2, chosen, cot_rows, expert_in, expert_out)
    wout_grad = lax.psum(wout_part, "ex").astype(f32)
    in_grad, out_grad = expert_grads(x, gpre, hidden, cots)
    out, igrad, gains, wgrad = last(
        lengths, dheads, kvt, q, ot, lse, normed, wqkv, tokens, gain1, gres, branch, rescol, chosen, ggrad)
    qkv_grad = jnp.transpose(wgrad.astype(f32), (1, 0, 2))
    return out, igrad, gains[0], qkv_grad, wout_grad, gains[1], in_grad, out_grad


def solution(mesh):
    placed = (
        P("ex", None), P("ex", None), P(), P(), P(None, None, "mp"), P("mp", None), P(),
        P("ex", None, "mp"), P("ex", "mp", None), P("ex", None),
    )
    return jax.shard_map(
        on_device,
        mesh=mesh,
        in_specs=placed,
        out_specs=(
            P("ex", "mp"), P("ex", None), P(), P(None, None, "mp"), P("mp", None), P(),
            P("ex", None, "mp"), P("ex", "mp", None),
        ),
        check_vma=False,
    )
```

```python
import functools

import jax
import jax.numpy as jnp
from jax import lax
from jax.experimental import pallas as pl
from jax.experimental.pallas import tpu as pltpu
from jax.sharding import PartitionSpec as P

HEAD_DIM = 64
epsilon = 1e-05
negative_fill = -1e30
MESH = pl.DeviceIdType.MESH
bf16, f32 = jnp.bfloat16, jnp.float32
EX, MP = 32, 4
VMEM_BYTES = 60 << 20


def dot(a, b, ca=1, cb=0):
    return lax.dot_general(a, b, (((ca,), (cb,)), ((), ())), preferred_element_type=f32)


def place():
    ex, mp = lax.axis_index("ex"), lax.axis_index("mp")
    z, x, c = ex // 8, (ex // 2) % 4, ex % 2
    return ex, mp, z, x, c


def send(src, dst, ssem, rsem, device):
    copy = pltpu.make_async_remote_copy(
        src_ref=src, dst_ref=dst, send_sem=ssem, recv_sem=rsem, device_id=device, device_id_type=MESH
    )
    copy.start()
    return copy


def greet(ex, mp):
    bar = pltpu.get_barrier_semaphore()

    def one(d, carry):
        pl.semaphore_signal(bar, inc=1, device_id=(lax.rem(ex + d, EX), mp), device_id_type=MESH)
        return carry

    lax.fori_loop(1, EX, one, 0)
    for d in range(1, MP):
        pl.semaphore_signal(bar, inc=1, device_id=(ex, lax.rem(mp + d, MP)), device_id_type=MESH)
    return bar


def greeted(bar):
    pl.semaphore_wait(bar, EX - 1 + MP - 1)


def slot_matrix(chosen_row):
    tok = chosen_row.shape[1]
    experts = lax.broadcasted_iota(jnp.int32, (64, tok), 0)
    hot = (experts == chosen_row).astype(f32)
    rows = lax.broadcasted_iota(jnp.int32, (tok, tok), 0)
    cols = lax.broadcasted_iota(jnp.int32, (tok, tok), 1)
    before = (rows < cols).astype(bf16)
    earlier = dot(hot.astype(bf16), before)
    rank = jnp.sum(earlier * hot, axis=0, keepdims=True)
    target = chosen_row * 8 + rank.astype(jnp.int32)
    slots = lax.broadcasted_iota(jnp.int32, (512, tok), 0)
    return (slots == target).astype(f32).astype(bf16)


def doc_row(ends, first, count):
    pos = first + lax.broadcasted_iota(jnp.int32, (1, count), 1)
    row = jnp.zeros((1, count), jnp.int32)
    for end in ends:
        row = row + (pos >= end).astype(jnp.int32)
    return row


def doc_ends(lengths_ref):
    ends, total = [], 0
    for i in range(9):
        total = total + lengths_ref[i]
        ends.append(total)
    return ends


def norm_parts(v):
    mean = jnp.mean(v, axis=-1, keepdims=True)
    centred = v - mean
    inverse = lax.rsqrt(jnp.mean(centred * centred, axis=-1, keepdims=True) + epsilon)
    return centred * inverse, inverse


def transposed(v):
    return v.T


def norm_back(grad_out, gain_row, unit, inverse):
    scaled = grad_out * gain_row
    centred = scaled - jnp.mean(scaled, axis=-1, keepdims=True)
    grad_in = inverse * (centred - unit * jnp.mean(scaled * unit, axis=-1, keepdims=True))
    return grad_in, jnp.sum(grad_out * unit, axis=0, keepdims=True)


def gelu_parts(pre):
    k = 0.7978845608028654
    square = pre * pre
    t = jnp.tanh(k * pre * (1.0 + 0.044715 * square))
    half = 0.5 * (1.0 + t)
    slope = half + 0.5 * pre * (1.0 - t * t) * (k * (1.0 + 3 * 0.044715 * square))
    return pre * half, slope


def one_expert(rows, le):
    wide = rows.astype(f32)
    return wide[:, 8 * le:8 * le + 8].reshape(256, rows.shape[2]).astype(bf16)


def both_experts(first, second):
    width = first.shape[1]
    return jnp.concatenate([first.reshape(32, 8, width), second.reshape(32, 8, width)], axis=1).astype(bf16)


VM = pl.BlockSpec(memory_space=pltpu.VMEM)
SM = pl.BlockSpec(memory_space=pltpu.SMEM)
ANY = pl.BlockSpec(memory_space=pl.ANY)
DMA = pltpu.SemaphoreType.DMA
ROWS = (2, 256, 1024)

ARGS = ["lengths", "tokens", "gain1", "gain2", "chosen", "wqkv_hbm", "wout_hbm", "cot_hbm", "win_hbm", "wex_hbm"]
OUTS = {
    "x_hbm": (ROWS, bf16), "c_hbm": (ROWS, bf16), "hid_hbm": (ROWS, bf16), "gpre_hbm": (ROWS, bf16),
    "out": ((256, 256), bf16), "igrad": ((256, 1024), bf16), "gains": ((2, 1024), f32),
    "qkv_out": ((3, 1024, 256), bf16), "wout_out": ((256, 1024), bf16),
}
BUFFERS = {
    "wqkv": ((3, 1024, 256), bf16), "wout": ((256, 1024), bf16), "cot": ((256, 1024), bf16),
    "win": ((2, 1024, 1024), bf16), "wex": ((2, 1024, 1024), bf16), "normed": ((256, 1024), bf16),
    "nall": ((4, 256, 1024), bf16), "wfull": ((4, 256, 1024), bf16),
    "q_s": ((4, 64, 256), bf16), "kv_s": ((4, 128, 256), bf16), "q": ((4, 64, 256), bf16),
    "kvt": ((8, 4, 128, 256), bf16), "qaug": ((4, 128, 256), bf16), "kaug": ((1024, 128), bf16),
    "vt1": ((80, 1024), bf16), "acc": ((4, 80, 256), f32), "peak": ((4, 1, 256), f32),
    "ot": ((4, 64, 256), f32), "lse": ((4, 1, 256), f32), "o_s": ((4, 64, 256), bf16),
    "att": ((4, 4, 64, 256), bf16), "cotq_s": ((32, 16, 256), bf16), "cotq": ((4, 32, 16, 256), bf16),
    "outgoing": ((32, 16, 1024), bf16), "arrived": ((32, 16, 1024), bf16),
    "xrows": (ROWS, bf16), "crows": (ROWS, bf16), "hid": (ROWS, bf16), "gpre": (ROWS, bf16), "gh": (ROWS, f32),
    "part": ((2, 4, 256, 256), bf16), "rs": ((2, 3, 256, 256), bf16), "back_s": ((32, 16, 256), bf16),
    "back": ((32, 16, 256), bf16), "gn": ((4, 256, 256), bf16), "resid": ((256, 1024), f32),
    "rescol": ((256, 256), f32), "gres": ((256, 1024), f32), "branch": ((32, 16, 1024), bf16),
    "wgp": ((2, 16, 16, 512), bf16), "wgs": ((16, 16, 512), bf16), "wgq": ((16, 16, 512), bf16),
    "wgr": ((15, 16, 512), bf16), "wgf": ((32, 16, 512), bf16),
    "dheads": ((4, 64, 256), bf16), "dob": ((4, 64, 256), bf16), "brs": ((3, 32, 16, 256), bf16),
    "bs": ((32, 16, 256), bf16), "bret": ((32, 16, 256), bf16), "dopad": ((4, 128, 256), bf16),
    "qd": ((4, 512, 128), bf16), "delta": ((4, 1, 256), f32), "kvn": ((1024, 128), bf16),
    "kt": ((64, 1024), bf16), "dkv": ((1024, 128), f32), "dq": ((4, 64, 256), f32),
    "sb": ((4, 1024, 128), bf16), "sr": ((4, 1024, 128), bf16), "xs": ((3, 1024, 128), bf16),
    "xr": ((3, 1024, 128), bf16), "zs": ((4, 192, 256), bf16), "zr": ((4, 192, 256), bf16),
    "wp": ((8, 192, 128), bf16), "wr": ((7, 192, 128), bf16), "pieces": ((32, 192, 128), bf16),
    "gnp": ((4, 64, 1024), bf16), "ry": ((3, 64, 1024), bf16), "small": ((1, 1024), f32),
    "smally": ((3, 1, 1024), f32), "smalle": ((32, 2, 1024), f32), "ggrad": ((1, 1024), f32),
}
LOCAL = {"load": (5,), "store": (4,)}
SENT = {
    "az": (6,), "ag": (28,), "wf": (3,), "wd": (3,), "co": (31,), "cy": (3,), "na": (3,), "oz": (3,), "oy": (3,),
    "di": (31,), "rs": (6,), "ba": (31,), "gy": (3,), "dz": (3,), "br": (3,), "bb": (31,), "sb": (4,), "xs": (3,),
    "wg": (1,), "wq": (15,), "wa": (15,), "wb": (16,), "zq": (3,), "wp": (7,), "pa": (15,), "pb": (16,),
    "ry": (3,), "ay": (3,), "sy": (3,), "se": (31,),
}
TAKEN = dict(SENT, ag=(32,))


class Refs:
    pass


def layer_kernel(*refs):
    r, ls, ss, rr = Refs(), Refs(), Refs(), Refs()
    names = [(r, k) for k in ARGS + list(OUTS) + list(BUFFERS)] + [(ls, k) for k in LOCAL]
    names += [(ss, k) for k in SENT] + [(rr, k) for k in TAKEN]
    for (group, name), ref in zip(names, refs, strict=True):
        setattr(group, name, ref)
    ex, mp, z, x, c = place()
    d = 1 - 2 * c
    j = x * 2 + c
    chip = ex // 2
    sib = (ex + d, mp)
    ahead = (z * 8 + lax.rem(x + d + 4, 4) * 2 + c, mp)
    behind = (z * 8 + lax.rem(x - d + 4, 4) * 2 + c, mp)
    pending = []

    def zpeer(i):
        zp = lax.rem(z + i, 4)
        return zp, (zp * 8 + j, mp)

    def ypeer(i):
        ym = lax.rem(mp + i, MP)
        return ym, (ex, ym)

    def remote(src, dst, ssem, rsem, device):
        return pltpu.make_async_remote_copy(
            src_ref=src, dst_ref=dst, send_sem=ssem, recv_sem=rsem, device_id=device, device_id_type=MESH)

    def push(src, dst, ssem, rsem, device):
        remote(src, dst, ssem, rsem, device).start()
        pending.append((src, ssem))

    def arrive(dst, rsem):
        remote(dst, dst, rsem, rsem, sib).wait_recv()

    def left(src, ssem):
        remote(src, src, ssem, ssem, sib).wait_send()

    def to_all(src_of, dst, name):
        def one(k, carry):
            to = lax.rem(ex + k, EX)
            remote(src_of(to), dst, getattr(ss, name).at[k - 1], getattr(rr, name).at[k - 1], (to, mp)).start()
            return carry

        lax.fori_loop(1, EX, one, 0)

    def from_all(src, dst_of, name):
        def one(k, carry):
            left(src, getattr(ss, name).at[k - 1])
            arrive(dst_of(lax.rem(ex + EX - k, EX)), getattr(rr, name).at[k - 1])
            return carry

        lax.fori_loop(1, EX, one, 0)

    def spread(buf, far, near):
        def one(k, carry):
            to = lax.rem(chip + k, 16) * 2 + c
            remote(buf.at[ex], buf.at[ex], getattr(ss, far).at[k - 1], getattr(rr, far).at[k - 1], (to, mp)).start()
            return carry

        lax.fori_loop(1, 16, one, 0)
        remote(buf.at[ex], buf.at[ex], getattr(ss, near).at[0], getattr(rr, near).at[0], sib).start()

    def pass_on(buf, far, near):
        def one(k, carry):
            source = lax.rem(chip + 16 - k, 16) * 2 + c
            left(buf.at[ex], getattr(ss, far).at[k - 1])
            arrive(buf.at[source], getattr(rr, far).at[k - 1])
            remote(buf.at[source], buf.at[source], getattr(ss, near).at[k], getattr(rr, near).at[k], sib).start()
            return carry

        lax.fori_loop(1, 16, one, 0)

    def passed(buf, near):
        def one(k, carry):
            source = lax.rem(chip + 16 - k, 16) * 2 + 1 - c
            left(buf.at[ex], getattr(ss, near).at[k])
            arrive(buf.at[source], getattr(rr, near).at[k])
            return carry

        lax.fori_loop(0, 16, one, 0)

    bar = greet(ex, mp)
    loads = [
        pltpu.make_async_copy(src, dst, ls.load.at[i])
        for i, (src, dst) in enumerate([
            (r.wqkv_hbm, r.wqkv), (r.wout_hbm, r.wout), (r.cot_hbm, r.cot), (r.wex_hbm, r.wex), (r.win_hbm, r.win)])
    ]
    for copy in loads:
        copy.start()
    unit, _ = norm_parts(r.tokens[...].astype(f32))
    normed = (unit * r.gain1[...]).astype(bf16)
    r.normed[...] = normed
    loads[0].wait()
    kt = transposed(dot(normed, r.wqkv[1]).astype(bf16))
    vt = transposed(dot(normed, r.wqkv[2]).astype(bf16))
    qt = transposed((dot(normed, r.wqkv[0]).astype(bf16) * HEAD_DIM ** (-0.5)).astype(bf16))
    for h in range(4):
        r.q_s[h] = qt[64 * h:64 * h + 64]
        r.kv_s[h, 0:64] = kt[64 * h:64 * h + 64]
        r.kv_s[h, 64:128] = vt[64 * h:64 * h + 64]
    greeted(bar)
    for i in (1, 3, 2):
        zp, to = zpeer(i)
        push(r.kv_s.at[zp], r.kvt.at[0, z], ss.az.at[i - 1], rr.az.at[i - 1], to)
    r.kvt[0, z] = r.kv_s[z]

    def own_piece(k):
        zq = lax.rem(z + 4 - k, 4)
        remote(r.kvt.at[0, zq], r.kvt.at[2, zq], ss.ag.at[4 * 1 + k], rr.ag.at[4 * 2 + k], ahead).start()
        remote(r.kvt.at[0, zq], r.kvt.at[3, zq], ss.ag.at[4 * 2 + k], rr.ag.at[4 * 3 + k], behind).start()
        remote(r.kvt.at[0, zq], r.kvt.at[1, zq], ss.ag.at[k], rr.ag.at[4 * 1 + k], sib).start()

    def came(slot, k):
        arrive(r.kvt.at[slot, lax.rem(z + 4 - k, 4)], rr.ag.at[4 * slot + k])

    def from_sides(k):
        zq = lax.rem(z + 4 - k, 4)
        came(2, k)
        remote(r.kvt.at[2, zq], r.kvt.at[6, zq], ss.ag.at[4 * 3 + k], rr.ag.at[4 * 6 + k], ahead).start()
        remote(r.kvt.at[2, zq], r.kvt.at[5, zq], ss.ag.at[4 * 4 + k], rr.ag.at[4 * 5 + k], sib).start()
        came(3, k)
        remote(r.kvt.at[3, zq], r.kvt.at[4, zq], ss.ag.at[4 * 5 + k], rr.ag.at[4 * 4 + k], sib).start()

    def from_far(k):
        zq = lax.rem(z + 4 - k, 4)
        came(6, k)
        remote(r.kvt.at[6, zq], r.kvt.at[7, zq], ss.ag.at[4 * 6 + k], rr.ag.at[4 * 7 + k], sib).start()

    own_piece(0)
    for i in (1, 3, 2):
        zp, to = zpeer(i)
        push(r.q_s.at[zp], r.q.at[z], ss.az.at[i + 2], rr.az.at[i + 2], to)
    r.q[z] = r.q_s[z]
    loads[1].wait()
    half = pl.ds(pl.multiple_of(128 * c, 128), 128)
    for i in range(1, 4):
        ym, to = ypeer(i)
        push(r.wout.at[half, :], r.wfull.at[mp, half, :], ss.wf.at[i - 1], rr.wf.at[i - 1], to)
    r.wfull[mp] = r.wout[...]
    r.vt1[64:80, :] = jnp.ones((16, 1024), bf16)
    ends = doc_ends(r.lengths)
    feature = lax.broadcasted_iota(jnp.int32, (64, 256), 0)
    loads[2].wait()
    mine = pl.ds(pl.multiple_of(256 * mp, 256), 256)
    r.cotq_s[...] = dot(slot_matrix(r.chosen[...]), r.cot[:, mine]).astype(bf16).reshape(EX, 16, 256)
    r.cotq[mp, ex] = r.cotq_s[ex]
    arrive(r.kvt.at[0, lax.rem(z + 3, 4)], rr.az.at[0])
    own_piece(1)
    arrive(r.kvt.at[0, lax.rem(z + 1, 4)], rr.az.at[2])
    own_piece(3)
    from_sides(0)
    arrive(r.kvt.at[0, lax.rem(z + 2, 4)], rr.az.at[1])
    own_piece(2)
    zp, to = zpeer(2)
    push(r.normed, r.nall.at[z], ss.na.at[1], rr.na.at[1], to)
    r.nall[z] = r.normed[...]
    for i in range(1, 4):
        arrive(r.q.at[lax.rem(z + 4 - i, 4)], rr.az.at[i + 2])
    for b in range(4):
        docs = doc_row(ends, (b * 8 + j) * 256, 256)
        r.qaug[b, 0:64] = r.q[b]
        r.qaug[b, 64:128] = jnp.where(feature == docs, 0.0, negative_fill).astype(bf16)
        r.peak[b] = jnp.full((1, 256), negative_fill, f32)
        r.acc[b] = jnp.zeros((80, 256), f32)

    def load_keys(slot, jp):
        for b in range(4):
            docs = doc_row(ends, (b * 8 + jp) * 256, 256)
            hot = (feature == docs).astype(f32).astype(bf16)
            r.kaug[256 * b:256 * b + 256, :] = transposed(
                jnp.concatenate([r.kvt[slot, b, 0:64], hot], axis=0))

    def scores(b, n, causal):
        s = dot(r.kaug[0:n, :], r.qaug[b])
        if causal:
            rows = lax.broadcasted_iota(jnp.int32, (n, 256), 0)
            cols = lax.broadcasted_iota(jnp.int32, (n, 256), 1)
            s = jnp.where(rows - 256 * b <= cols, s, negative_fill)
        return s

    def load_chunk(slot, jp):
        load_keys(slot, jp)
        for b in range(4):
            r.vt1[0:64, 256 * b:256 * b + 256] = r.kvt[slot, b, 64:128]

    def update(b, n, causal):
        s = scores(b, n, causal)
        old = r.peak[b]
        new = jnp.maximum(old, jnp.max(s, axis=0, keepdims=True))
        p = jnp.exp(s - new).astype(bf16)
        r.acc[b] = r.acc[b] * jnp.exp(old - new) + dot(r.vt1[:, 0:n], p)
        r.peak[b] = new

    load_chunk(0, j)
    for b in range(4):
        update(b, 256 * b + 256, True)

    def chunk(i, carry):
        u = i // 2
        side = ((u + 1) // 2) % 2
        xp = (x + d * (2 * (i % 2) - 1) * side + 2 * (u // 3) + 8) % 4
        jp = xp * 2 + (c + (1 - side) * (i % 2) + side * (u // 2)) % 2

        @pl.when(i == 1)
        def _():
            from_sides(1)
            from_far(0)
            for k in range(4):
                came(1, k)

        @pl.when(i == 2)
        def _():
            from_sides(3)
            from_far(1)
            from_sides(2)

        @pl.when(i == 3)
        def _():
            from_far(3)

        @pl.when(i == 4)
        def _():
            from_far(2)
            for k in range(4):
                came(4, k)
            to_all(lambda to: r.cotq_s.at[to], r.cotq.at[mp, ex], "co")

        @pl.when(i == 5)
        def _():
            for k in range(4):
                came(5, k)
            for i in range(1, 4):
                ym, to = ypeer(4 - i)
                arrive(r.wfull.at[ym, half, :], rr.wf.at[i - 1])
                remote(
                    r.wfull.at[ym, half, :], r.wfull.at[ym, half, :], ss.wd.at[i - 1], rr.wd.at[i - 1], sib).start()

        @pl.when(i == 7)
        def _():
            for k in range(4):
                came(7, k)

        load_chunk(i, jp)

        @pl.when(jp < j)
        def _():
            for b in range(4):
                update(b, 256 * b + 256, False)

        @pl.when(jp > j)
        def _():
            for b in range(1, 4):
                update(b, 256 * b, False)

        return carry

    lax.fori_loop(1, 8, chunk, 0)
    for b in range(4):
        total = r.acc[b, 64:65]
        ot = r.acc[b, 0:64] / total
        r.ot[b] = ot
        r.lse[b] = r.peak[b] + jnp.log(total)
        r.o_s[b] = ot.astype(bf16)
    for i in (1, 3, 2):
        zp, to = zpeer(i)
        push(r.o_s.at[zp], r.att.at[mp, z], ss.oz.at[i - 1], rr.oz.at[i - 1], to)
    r.att[mp, z] = r.o_s[z]
    for i in range(1, 4):
        zp, _ = zpeer(4 - i)
        arrive(r.att.at[mp, zp], rr.oz.at[i - 1])
    for i in (1, 3, 2):
        ym, to = ypeer(i)
        push(r.att.at[mp], r.att.at[mp], ss.oy.at[i - 1], rr.oy.at[i - 1], to)
    from_all(r.cotq_s.at[ex], lambda source: r.cotq.at[mp, source], "co")
    other = pl.ds(pl.multiple_of(128 - 128 * c, 128), 128)
    for i in range(1, 4):
        ym, _ = ypeer(4 - i)
        arrive(r.wfull.at[ym, other, :], rr.wd.at[i - 1])
    for i in range(1, 4):
        ym, _ = ypeer(4 - i)
        arrive(r.att.at[ym], rr.oy.at[i - 1])
    for i in (1, 3, 2):
        ym, to = ypeer(i)
        push(r.cotq.at[mp], r.cotq.at[mp], ss.cy.at[i - 1], rr.cy.at[i - 1], to)
    value = r.tokens[...].astype(f32) + dot(r.att[...].reshape(1024, 256), r.wfull[...].reshape(1024, 1024), 0, 0)
    r.resid[...] = value
    for k in range(4):
        @pl.when(mp == k)
        def _():
            r.rescol[...] = value[:, 256 * k:256 * k + 256]
    unit, _ = norm_parts(value)
    r.outgoing[...] = dot(slot_matrix(r.chosen[...]), (unit * r.gain2[...]).astype(bf16)).astype(bf16).reshape(
        EX, 16, 1024)
    to_all(lambda to: r.outgoing.at[to], r.arrived.at[ex], "di")
    r.arrived[ex] = r.outgoing[ex]
    loads[3].wait()
    for i in range(1, 4):
        ym, _ = ypeer(4 - i)
        arrive(r.cotq.at[ym], rr.cy.at[i - 1])
    for le in range(2):
        rows = jnp.concatenate([one_expert(r.cotq[k], le) for k in range(4)], axis=1)
        r.crows[le] = rows
        r.gh[le] = dot(rows, r.wex[le], 1, 1)
    loads[4].wait()
    from_all(r.outgoing.at[ex], lambda source: r.arrived.at[source], "di")
    for le in range(2):
        rows = one_expert(r.arrived[...], le)
        r.xrows[le] = rows
        hidden, slope = gelu_parts(dot(rows, r.win[le]))
        r.hid[le] = hidden.astype(bf16)
        gpre = (r.gh[le] * slope).astype(bf16)
        r.gpre[le] = gpre
        for k in range(4):
            r.part[le, k] = dot(gpre, r.win[le, 256 * k:256 * k + 256, :], 1, 1).astype(bf16)
        for i in (1, 3, 2):
            ym, to = ypeer(i)
            push(r.part.at[le, ym], r.rs.at[le, i - 1], ss.rs.at[3 * le + i - 1], rr.rs.at[3 * le + i - 1], to)
    stores = [
        pltpu.make_async_copy(src, dst, ls.store.at[i])
        for i, (src, dst) in enumerate([
            (r.xrows, r.x_hbm), (r.crows, r.c_hbm), (r.hid, r.hid_hbm), (r.gpre, r.gpre_hbm)])
    ]
    for copy in stores:
        copy.start()
    first = dot(r.hid[0], r.wex[0])
    r.branch[...] = both_experts(first, dot(r.hid[1], r.wex[1]))
    sums = []
    for le in range(2):
        total = r.part[le, mp].astype(f32)
        for i in range(3):
            arrive(r.rs.at[le, i], rr.rs.at[3 * le + i])
            total = total + r.rs[le, i].astype(f32)
        sums.append(total)
    r.back_s[...] = both_experts(sums[0], sums[1])
    to_all(lambda to: r.back_s.at[to], r.back.at[ex], "ba")
    r.back[ex] = r.back_s[ex]
    from_all(r.back_s.at[ex], lambda source: r.back.at[source], "ba")
    r.gn[mp] = dot(slot_matrix(r.chosen[...]), r.back[...].reshape(512, 256), 0, 0).astype(bf16)
    for i in (1, 3, 2):
        ym, to = ypeer(i)
        push(r.gn.at[mp], r.gn.at[mp], ss.gy.at[i - 1], rr.gy.at[i - 1], to)
    unit, inverse = norm_parts(r.resid[...])
    for i in range(1, 4):
        ym, _ = ypeer(4 - i)
        arrive(r.gn.at[ym], rr.gy.at[i - 1])
    grad = jnp.concatenate([r.gn[k] for k in range(4)], axis=1).astype(f32)
    grad_in, ggrad = norm_back(grad, r.gain2[...], unit, inverse)
    r.ggrad[...] = ggrad
    gres = r.cot[...].astype(f32) + grad_in
    r.gres[...] = gres
    low = gres.astype(bf16)
    r.dheads[...] = dot(r.wfull[mp], low, 1, 1).astype(bf16).reshape(4, 64, 256)
    for i in (1, 3, 2):
        zp, to = zpeer(i)
        push(r.dheads.at[zp], r.dob.at[z], ss.dz.at[i - 1], rr.dz.at[i - 1], to)
    r.dob[z] = r.dheads[z]
    wgrad = dot(r.att[mp].reshape(256, 256), low).astype(bf16)
    r.wgp[0] = wgrad[:, 0:512].reshape(16, 16, 512)
    r.wgp[1] = wgrad[:, 512:1024].reshape(16, 16, 512)
    push(r.wgp.at[1 - c], r.wgs, ss.wg.at[0], rr.wg.at[0], sib)
    for i in range(1, 4):
        ym, to = ypeer(i)
        push(
            r.branch.at[:, :, pl.ds(pl.multiple_of(256 * ym, 256), 256)], r.brs.at[i - 1],
            ss.br.at[i - 1], rr.br.at[i - 1], to)
    zero = jnp.zeros((64, 256), bf16)
    for i in range(1, 4):
        zp, _ = zpeer(4 - i)
        arrive(r.dob.at[zp], rr.dz.at[i - 1])
    for i in (1, 3):
        zp, to = zpeer(i)
        push(r.normed, r.nall.at[z], ss.na.at[i - 1], rr.na.at[i - 1], to)
    for b in range(4):
        r.dopad[b, 0:64] = zero
        r.dopad[b, 64:128] = r.dob[b]
        r.qd[b, 0:256] = transposed(jnp.concatenate([r.q[b], zero], axis=0))
        r.qd[b, 256:512] = transposed(jnp.concatenate([zero, r.dob[b]], axis=0))
        r.delta[b] = jnp.sum(r.dob[b].astype(f32) * r.ot[b], axis=0, keepdims=True)
        r.dq[b] = jnp.zeros((64, 256), f32)

    def load_back(slot, jp):
        load_keys(slot, jp)
        for b in range(4):
            r.kvn[256 * b:256 * b + 256, :] = transposed(r.kvt[slot, b])
            r.kt[:, 256 * b:256 * b + 256] = r.kvt[slot, b, 0:64]

    def back_update(b, n, causal):
        p = jnp.exp(scores(b, n, causal) - r.lse[b])
        dp = dot(r.kvn[0:n, :], r.dopad[b])
        ds = (p * (dp - r.delta[b])).astype(bf16)
        added = dot(ds, r.qd[b, 0:256]) + dot(p.astype(bf16), r.qd[b, 256:512])
        if b == 3:
            r.dkv[0:n] = added
        else:
            r.dkv[0:n] = r.dkv[0:n] + added
        r.dq[b] = r.dq[b] + dot(r.kt[:, 0:n], ds)

    def back_chunk(i, carry):
        p = i // 2
        w = p + (p // 2) * (1 - 2 * (p % 2))
        g = (2 + d * w + 4) % 4
        flip = 1 - i % 2
        odd = g % 2
        slot = odd * (2 + g // 2 + 2 * flip) + (1 - odd) * (3 * g + flip)
        xp = (x - d * g + 8) % 4
        jp = xp * 2 + (c + flip) % 2
        load_back(slot, jp)

        @pl.when(jp < j)
        def _():
            for b in range(3, -1, -1):
                back_update(b, 256 * b + 256, False)

        @pl.when(jp > j)
        def _():
            r.dkv[768:1024] = jnp.zeros((256, 128), f32)
            for b in range(3, 0, -1):
                back_update(b, 256 * b, False)

        @pl.when(i % 2 == 0)
        def _():
            r.sb[p] = r.dkv[...].astype(bf16)
            remote(r.sb.at[p], r.sr.at[p], ss.sb.at[p], rr.sb.at[p], sib).start()

        @pl.when(i % 2 == 1)
        def _():
            arrive(r.sr.at[p], rr.sb.at[p])
            r.xs[p] = (r.dkv[...] + r.sr[p].astype(f32)).astype(bf16)
            remote(r.xs.at[p], r.xr.at[p], ss.xs.at[p], rr.xs.at[p], (z * 8 + xp * 2 + c, mp)).start()

        @pl.when(i == 1)
        def _():
            arrive(r.wgs, rr.wg.at[0])
            r.wgq[...] = (r.wgp[c].astype(f32) + r.wgs[...].astype(f32)).astype(bf16)

            def one(k, carry):
                to = lax.rem(chip + k, 16)
                remote(r.wgq.at[to], r.wgr.at[k - 1], ss.wq.at[k - 1], rr.wq.at[k - 1], (to * 2 + c, mp)).start()
                return carry

            lax.fori_loop(1, 16, one, 0)

        @pl.when(i == 4)
        def _():
            total = r.branch[:, :, mine].astype(f32)
            for k in range(3):
                arrive(r.brs.at[k], rr.br.at[k])
                total = total + r.brs[k].astype(f32)
            r.bs[...] = total.astype(bf16)
            to_all(lambda to: r.bs.at[to], r.bret.at[ex], "bb")
            r.bret[ex] = r.bs[ex]

        @pl.when(i == 5)
        def _():
            total = r.wgq[chip].astype(f32)
            for k in range(15):
                arrive(r.wgr.at[k], rr.wq.at[k])
                total = total + r.wgr[k].astype(f32)
            r.wgf[ex] = total.astype(bf16)
            spread(r.wgf, "wa", "wb")

        return carry

    lax.fori_loop(0, 7, back_chunk, 0)
    load_back(0, j)
    for b in range(3, -1, -1):
        back_update(b, 256 * b + 256, True)
    arrive(r.sr.at[3], rr.sb.at[3])
    total = r.dkv[...] + r.sr[3].astype(f32)
    pass_on(r.wgf, "wa", "wb")
    for p in range(3):
        arrive(r.xr.at[p], rr.xs.at[p])
        total = total + r.xr[p].astype(f32)
    low = total.astype(bf16)
    for b in range(4):
        r.zs[b, 0:64] = (r.dq[b] * HEAD_DIM ** (-0.5)).astype(bf16)
        r.zs[b, 64:192] = transposed(low[256 * b:256 * b + 256])
    for i in (1, 3, 2):
        zp, to = zpeer(i)
        push(r.zs.at[zp], r.zr.at[z], ss.zq.at[i - 1], rr.zq.at[i - 1], to)
    r.zr[z] = r.zs[z]
    for i in range(1, 4):
        zp, _ = zpeer(4 - i)
        arrive(r.nall.at[zp], rr.na.at[i - 1])
    wt = dot(r.zs[0], r.nall[0])
    for b in range(1, 4):
        wt = wt + dot(r.zs[b], r.nall[b])
    wt = wt.astype(bf16)
    for k in range(8):
        r.wp[k] = wt[:, 128 * k:128 * k + 128]
    for i in range(1, 8):
        jt = lax.rem(j + i, 8)
        push(r.wp.at[jt], r.wr.at[i - 1], ss.wp.at[i - 1], rr.wp.at[i - 1], (z * 8 + jt, mp))
    for i in range(1, 4):
        zp, _ = zpeer(4 - i)
        arrive(r.zr.at[zp], rr.zq.at[i - 1])
    part = None
    for k in range(3):
        heads = transposed(jnp.concatenate([r.zr[h, 64 * k:64 * k + 64] for h in range(4)], axis=0))
        term = dot(heads, r.wqkv[k], 1, 1)
        part = term if part is None else part + term
    r.gnp[...] = part.astype(bf16).reshape(4, 64, 1024)
    for i in (1, 3, 2):
        ym, to = ypeer(i)
        push(r.gnp.at[ym], r.ry.at[i - 1], ss.ry.at[i - 1], rr.ry.at[i - 1], to)
    summed = r.wp[j].astype(f32)
    for i in range(7):
        arrive(r.wr.at[i], rr.wp.at[i])
        summed = summed + r.wr[i].astype(f32)
    r.pieces[ex] = summed.astype(bf16)
    spread(r.pieces, "pa", "pb")
    from_all(r.bs.at[ex], lambda source: r.bret.at[source], "bb")
    rows = dot(slot_matrix(r.chosen[...]), r.bret[...].reshape(512, 256), 0, 0)
    r.out[...] = (r.rescol[...] + rows).astype(bf16)
    passed(r.wgf, "wb")
    for k in range(32):
        r.wout_out[16 * (k // 2):16 * (k // 2) + 16, 512 * (k % 2):512 * (k % 2) + 512] = r.wgf[k]
    grad = r.gnp[mp].astype(f32)
    for i in range(3):
        arrive(r.ry.at[i], rr.ry.at[i])
        grad = grad + r.ry[i].astype(f32)
    here = pl.ds(pl.multiple_of(64 * mp, 64), 64)
    unit, inverse = norm_parts(r.tokens[here, :].astype(f32))
    grad_in, one_gain = norm_back(grad, r.gain1[...], unit, inverse)
    r.small[...] = one_gain
    for i in (1, 3, 2):
        ym, to = ypeer(i)
        push(r.small, r.smally.at[i - 1], ss.sy.at[i - 1], rr.sy.at[i - 1], to)
    r.igrad[here, :] = (r.gres[here, :] + grad_in).astype(bf16)
    for i in (1, 3, 2):
        ym, to = ypeer(i)
        push(r.igrad.at[here, :], r.igrad.at[here, :], ss.ay.at[i - 1], rr.ay.at[i - 1], to)
    for i in range(3):
        arrive(r.smally.at[i], rr.sy.at[i])
        one_gain = one_gain + r.smally[i]
    r.smalle[ex, 0:1] = one_gain
    r.smalle[ex, 1:2] = r.ggrad[...]
    to_all(lambda to: r.smalle.at[ex], r.smalle.at[ex], "se")
    pass_on(r.pieces, "pa", "pb")
    passed(r.pieces, "pb")
    for k in range(3):
        for row in range(8):
            block = jnp.concatenate([r.pieces[8 * h + row, 64 * k:64 * k + 64] for h in range(4)], axis=0)
            r.qkv_out[k, 128 * row:128 * row + 128] = transposed(block)
    from_all(r.smalle.at[ex], lambda source: r.smalle.at[source], "se")
    r.gains[...] = jnp.sum(r.smalle[...], axis=0)
    for i in range(1, 4):
        ym, _ = ypeer(4 - i)
        there = pl.ds(pl.multiple_of(64 * ym, 64), 64)
        arrive(r.igrad.at[there, :], rr.ay.at[i - 1])
    for src, ssem in pending:
        left(src, ssem)
    for k in range(28):
        left(r.kvt.at[0, 0], ss.ag.at[k])
    for k in range(3):
        left(r.wfull.at[0, half, :], ss.wd.at[k])
    for p in range(4):
        left(r.sb.at[p], ss.sb.at[p])
    for p in range(3):
        left(r.xs.at[p], ss.xs.at[p])
    for k in range(15):
        left(r.wgq.at[0], ss.wq.at[k])
    for copy in stores:
        copy.wait()


def layer(*args):
    spaces = {"x_hbm": ANY, "c_hbm": ANY, "hid_hbm": ANY, "gpre_hbm": ANY}
    return pl.pallas_call(
        layer_kernel,
        out_shape=[jax.ShapeDtypeStruct(s, t) for s, t in OUTS.values()],
        in_specs=[SM, VM, VM, VM, VM, ANY, ANY, ANY, ANY, ANY],
        out_specs=[spaces.get(name, VM) for name in OUTS],
        scratch_shapes=[pltpu.VMEM(s, t) for s, t in BUFFERS.values()]
        + [DMA(s) for group in (LOCAL, SENT, TAKEN) for s in group.values()],
        name="layer",
        compiler_params=pltpu.CompilerParams(
            collective_id=0, has_side_effects=True, vmem_limit_bytes=VMEM_BYTES),
    )(*args)


def finish_kernel(x, gpre, hid, cots, qkv, wout, out, igrad, in_grad, out_grad, qkv_o, wout_o, out_o, igrad_o):
    in_grad[0] = dot(x[0], gpre[0], 0, 0)
    out_grad[0] = dot(hid[0], cots[0], 0, 0)
    qkv_o[...] = qkv[...].astype(f32)
    wout_o[...] = wout[...].astype(f32)
    out_o[...] = out[...]
    igrad_o[...] = igrad[...]


def finish(x, gpre, hid, cots, qkv, wout, out, igrad):
    width, steps = 256, 4
    n = 2 * steps
    tall = pl.BlockSpec((1, 256, width), lambda e, i: (e, 0, i))
    whole = pl.BlockSpec((1, 256, 1024), lambda e, i: (e, 0, 0))
    made = pl.BlockSpec((1, width, 1024), lambda e, i: (e, i, 0))

    def rows(shape):
        if len(shape) == 3:
            return pl.BlockSpec((shape[0], shape[1] // n, shape[2]), lambda e, i: (0, e * steps + i, 0))
        return pl.BlockSpec((shape[0] // n, shape[1]), lambda e, i: (e * steps + i, 0))

    plain = [rows(v.shape) for v in (qkv, wout, out, igrad)]
    big = jax.ShapeDtypeStruct((2, 1024, 1024), f32)
    return pl.pallas_call(
        finish_kernel,
        grid=(2, steps),
        out_shape=[
            big, big, jax.ShapeDtypeStruct(qkv.shape, f32), jax.ShapeDtypeStruct(wout.shape, f32),
            jax.ShapeDtypeStruct(out.shape, bf16), jax.ShapeDtypeStruct(igrad.shape, bf16)],
        in_specs=[tall, whole, tall, whole] + plain,
        out_specs=[made, made] + plain,
        name="finish",
        compiler_params=pltpu.CompilerParams(vmem_limit_bytes=48 << 20),
        cost_estimate=pl.CostEstimate(flops=2 * 2 * 2 * 256 * 1024 * 1024, bytes_accessed=28 << 20, transcendentals=0),
    )(x, gpre, hid, cots, qkv, wout, out, igrad)


def on_device(
    tokens, hash_ids, lengths, norm1_gain, qkv_weight, out_weight, norm2_gain, expert_in, expert_out, cotangent,
):
    x, cots, hid, gpre, out, igrad, gains, qkv, wout = layer(
        lengths, tokens, norm1_gain.reshape(1, 1024), norm2_gain.reshape(1, 1024), hash_ids.reshape(1, 256),
        jnp.transpose(qkv_weight, (1, 0, 2)), out_weight, cotangent, expert_in, expert_out)
    in_grad, out_grad, qkv, wout, out, igrad = finish(x, gpre, hid, cots, qkv, wout, out, igrad)
    return out, igrad, gains[0], jnp.transpose(qkv, (1, 0, 2)), wout, gains[1], in_grad, out_grad


def solution(mesh):
    placed = (
        P("ex", None), P("ex", None), P(), P(), P(None, None, "mp"), P("mp", None), P(),
        P("ex", None, "mp"), P("ex", "mp", None), P("ex", None),
    )
    return jax.shard_map(
        on_device,
        mesh=mesh,
        in_specs=placed,
        out_specs=(
            P("ex", "mp"), P("ex", None), P(), P(None, None, "mp"), P("mp", None), P(),
            P("ex", None, "mp"), P("ex", "mp", None),
        ),
        check_vma=False,
    )
```

```python
import functools

import jax
import jax.numpy as jnp
from jax import lax
from jax.experimental import pallas as pl
from jax.experimental.pallas import tpu as pltpu
from jax.sharding import PartitionSpec as P

HEAD_DIM = 64
epsilon = 1e-05
negative_fill = -1e30
MESH = pl.DeviceIdType.MESH
bf16, f32 = jnp.bfloat16, jnp.float32
EX, MP = 32, 4
VMEM_BYTES = 60 << 20


def dot(a, b, ca=1, cb=0):
    return lax.dot_general(a, b, (((ca,), (cb,)), ((), ())), preferred_element_type=f32)


def place():
    ex, mp = lax.axis_index("ex"), lax.axis_index("mp")
    z, x, c = ex // 8, (ex // 2) % 4, ex % 2
    return ex, mp, z, x, c


def send(src, dst, ssem, rsem, device):
    copy = pltpu.make_async_remote_copy(
        src_ref=src, dst_ref=dst, send_sem=ssem, recv_sem=rsem, device_id=device, device_id_type=MESH
    )
    copy.start()
    return copy


def greet(ex, mp):
    bar = pltpu.get_barrier_semaphore()

    def one(d, carry):
        pl.semaphore_signal(bar, inc=1, device_id=(lax.rem(ex + d, EX), mp), device_id_type=MESH)
        return carry

    lax.fori_loop(1, EX, one, 0)
    for d in range(1, MP):
        pl.semaphore_signal(bar, inc=1, device_id=(ex, lax.rem(mp + d, MP)), device_id_type=MESH)
    return bar


def greeted(bar):
    pl.semaphore_wait(bar, EX - 1 + MP - 1)


def slot_matrix(chosen_row):
    tok = chosen_row.shape[1]
    experts = lax.broadcasted_iota(jnp.int32, (64, tok), 0)
    hot = (experts == chosen_row).astype(f32)
    rows = lax.broadcasted_iota(jnp.int32, (tok, tok), 0)
    cols = lax.broadcasted_iota(jnp.int32, (tok, tok), 1)
    before = (rows < cols).astype(bf16)
    earlier = dot(hot.astype(bf16), before)
    rank = jnp.sum(earlier * hot, axis=0, keepdims=True)
    target = chosen_row * 8 + rank.astype(jnp.int32)
    slots = lax.broadcasted_iota(jnp.int32, (512, tok), 0)
    return (slots == target).astype(f32).astype(bf16)


def doc_row(ends, first, count):
    pos = first + lax.broadcasted_iota(jnp.int32, (1, count), 1)
    row = jnp.zeros((1, count), jnp.int32)
    for end in ends:
        row = row + (pos >= end).astype(jnp.int32)
    return row


def doc_ends(lengths_ref):
    ends, total = [], 0
    for i in range(9):
        total = total + lengths_ref[i]
        ends.append(total)
    return ends


def norm_parts(v):
    mean = jnp.mean(v, axis=-1, keepdims=True)
    centred = v - mean
    inverse = lax.rsqrt(jnp.mean(centred * centred, axis=-1, keepdims=True) + epsilon)
    return centred * inverse, inverse


def transposed(v):
    return v.T


def norm_back(grad_out, gain_row, unit, inverse):
    scaled = grad_out * gain_row
    centred = scaled - jnp.mean(scaled, axis=-1, keepdims=True)
    grad_in = inverse * (centred - unit * jnp.mean(scaled * unit, axis=-1, keepdims=True))
    return grad_in, jnp.sum(grad_out * unit, axis=0, keepdims=True)


def gelu_parts(pre):
    k = 0.7978845608028654
    square = pre * pre
    t = jnp.tanh(k * pre * (1.0 + 0.044715 * square))
    half = 0.5 * (1.0 + t)
    slope = half + 0.5 * pre * (1.0 - t * t) * (k * (1.0 + 3 * 0.044715 * square))
    return pre * half, slope


def one_expert(rows, le):
    wide = rows.astype(f32)
    return wide[:, 8 * le:8 * le + 8].reshape(256, rows.shape[2]).astype(bf16)


def both_experts(first, second):
    width = first.shape[1]
    return jnp.concatenate([first.reshape(32, 8, width), second.reshape(32, 8, width)], axis=1).astype(bf16)


VM = pl.BlockSpec(memory_space=pltpu.VMEM)
SM = pl.BlockSpec(memory_space=pltpu.SMEM)
ANY = pl.BlockSpec(memory_space=pl.ANY)
DMA = pltpu.SemaphoreType.DMA
ROWS = (2, 256, 1024)

ARGS = ["lengths", "tokens", "gain1", "gain2", "chosen", "wqkv_hbm", "wout_hbm", "cot_hbm", "win_hbm", "wex_hbm"]
OUTS = {
    "x_hbm": (ROWS, bf16), "c_hbm": (ROWS, bf16), "hid_hbm": (ROWS, bf16), "gpre_hbm": (ROWS, bf16),
    "out": ((256, 256), bf16), "igrad": ((256, 1024), bf16), "gain1_out": ((1, 1024), f32), "gain2_out": ((1, 1024), f32),
    "qkv_out": ((3, 1024, 256), bf16), "wout_out": ((256, 1024), bf16),
}
BUFFERS = {
    "wqkv": ((3, 1024, 256), bf16), "wout": ((256, 1024), bf16), "cot": ((256, 1024), bf16),
    "win": ((2, 1024, 1024), bf16), "wex": ((2, 1024, 1024), bf16), "normed": ((256, 1024), bf16),
    "nall": ((4, 256, 1024), bf16), "wfull": ((4, 256, 1024), bf16),
    "q_s": ((4, 64, 256), bf16), "kv_s": ((4, 128, 256), bf16), "q": ((4, 64, 256), bf16),
    "kvt": ((8, 4, 128, 256), bf16), "qaug": ((4, 128, 256), bf16), "kaug": ((1024, 128), bf16),
    "vt1": ((80, 1024), bf16), "acc": ((4, 80, 256), f32), "peak": ((4, 1, 256), f32),
    "ot": ((4, 64, 256), f32), "lse": ((4, 1, 256), f32), "o_s": ((4, 64, 256), bf16),
    "att": ((4, 4, 64, 256), bf16), "cotq_s": ((32, 16, 256), bf16), "cotq": ((4, 32, 16, 256), bf16),
    "outgoing": ((32, 16, 1024), bf16), "arrived": ((32, 16, 1024), bf16),
    "xrows": (ROWS, bf16), "crows": (ROWS, bf16), "hid": (ROWS, bf16), "gpre": (ROWS, bf16), "gh": (ROWS, f32),
    "part": ((2, 4, 256, 256), bf16), "rs": ((2, 3, 256, 256), bf16), "back_s": ((32, 16, 256), bf16),
    "back": ((32, 16, 256), bf16), "gn": ((4, 256, 256), bf16), "resid": ((256, 1024), f32),
    "rescol": ((256, 256), f32), "gres": ((256, 1024), f32), "branch": ((32, 16, 1024), bf16),
    "wgp": ((2, 4, 4, 16, 512), bf16), "wgs": ((4, 4, 16, 512), bf16), "wgq": ((4, 4, 16, 512), bf16),
    "wgz": ((3, 4, 16, 512), bf16), "wgx": ((4, 16, 512), bf16), "wgr": ((3, 16, 512), bf16),
    "wgf": ((2, 4, 4, 16, 512), bf16),
    "dheads": ((4, 64, 256), bf16), "dob": ((4, 64, 256), bf16), "brs": ((3, 32, 16, 256), bf16),
    "bs": ((32, 16, 256), bf16), "bret": ((32, 16, 256), bf16), "dopad": ((4, 128, 256), bf16),
    "qd": ((4, 512, 128), bf16), "delta": ((4, 1, 256), f32), "kvn": ((1024, 128), bf16),
    "kt": ((64, 1024), bf16), "dkv": ((1024, 128), f32), "dq": ((4, 64, 256), f32),
    "sb": ((4, 1024, 128), bf16), "sr": ((4, 1024, 128), bf16), "xs": ((4, 1024, 128), bf16),
    "xr": ((3, 1024, 128), bf16), "zs": ((4, 192, 256), bf16), "zr": ((4, 192, 256), bf16),
    "wp": ((8, 192, 128), bf16), "wr": ((7, 192, 128), bf16), "pieces": ((32, 192, 128), bf16),
    "gnp": ((4, 64, 1024), bf16), "ry": ((3, 64, 1024), bf16), "small": ((1, 1024), f32),
    "smally": ((3, 1, 1024), f32), "smalle": ((32, 2, 1024), f32), "ggrad": ((1, 1024), f32),
}
LOCAL = {"load": (5,), "store": (4,)}
SENT = {
    "az": (6,), "ag": (28,), "wf": (3,), "wd": (3,), "co": (31,), "cy": (3,), "na": (3,), "oz": (3,), "oy": (3,),
    "di": (31,), "rs": (6,), "ba": (31,), "gy": (3,), "dz": (3,), "br": (3,), "bb": (31,), "sb": (4,), "xs": (3,),
    "wg": (1,), "wz": (3,), "wx": (3,), "wa": (3,), "wb": (3,), "wc": (1,), "zq": (6,), "wp": (7,), "pa": (15,), "pb": (16,),
    "ry": (3,), "ay": (3,), "sy": (3,), "se": (31,),
}
TAKEN = dict(SENT, ag=(32,))


class Refs:
    pass


def layer_kernel(*refs):
    r, ls, ss, rr = Refs(), Refs(), Refs(), Refs()
    names = [(r, k) for k in ARGS + list(OUTS) + list(BUFFERS)] + [(ls, k) for k in LOCAL]
    names += [(ss, k) for k in SENT] + [(rr, k) for k in TAKEN]
    for (group, name), ref in zip(names, refs, strict=True):
        setattr(group, name, ref)
    ex, mp, z, x, c = place()
    d = 1 - 2 * c
    j = x * 2 + c
    chip = ex // 2
    sib = (ex + d, mp)
    ahead = (z * 8 + lax.rem(x + d + 4, 4) * 2 + c, mp)
    behind = (z * 8 + lax.rem(x - d + 4, 4) * 2 + c, mp)
    pending = []

    def zpeer(i):
        zp = lax.rem(z + i, 4)
        return zp, (zp * 8 + j, mp)

    def ypeer(i):
        ym = lax.rem(mp + i, MP)
        return ym, (ex, ym)

    def xpeer(i):
        xq = lax.rem(x + i, 4)
        return xq, (z * 8 + xq * 2 + c, mp)

    def remote(src, dst, ssem, rsem, device):
        return pltpu.make_async_remote_copy(
            src_ref=src, dst_ref=dst, send_sem=ssem, recv_sem=rsem, device_id=device, device_id_type=MESH)

    def push(src, dst, ssem, rsem, device):
        remote(src, dst, ssem, rsem, device).start()
        pending.append((src, ssem))

    def arrive(dst, rsem):
        remote(dst, dst, rsem, rsem, sib).wait_recv()

    def left(src, ssem):
        remote(src, src, ssem, ssem, sib).wait_send()

    def to_all(src_of, dst, name):
        def one(k, carry):
            to = lax.rem(ex + k, EX)
            remote(src_of(to), dst, getattr(ss, name).at[k - 1], getattr(rr, name).at[k - 1], (to, mp)).start()
            return carry

        lax.fori_loop(1, EX, one, 0)

    def from_all(src, dst_of, name):
        def one(k, carry):
            left(src, getattr(ss, name).at[k - 1])
            arrive(dst_of(lax.rem(ex + EX - k, EX)), getattr(rr, name).at[k - 1])
            return carry

        lax.fori_loop(1, EX, one, 0)

    def spread(buf, far, near):
        def one(k, carry):
            to = lax.rem(chip + k, 16) * 2 + c
            remote(buf.at[ex], buf.at[ex], getattr(ss, far).at[k - 1], getattr(rr, far).at[k - 1], (to, mp)).start()
            return carry

        lax.fori_loop(1, 16, one, 0)
        remote(buf.at[ex], buf.at[ex], getattr(ss, near).at[0], getattr(rr, near).at[0], sib).start()

    def pass_on(buf, far, near):
        def one(k, carry):
            source = lax.rem(chip + 16 - k, 16) * 2 + c
            left(buf.at[ex], getattr(ss, far).at[k - 1])
            arrive(buf.at[source], getattr(rr, far).at[k - 1])
            remote(buf.at[source], buf.at[source], getattr(ss, near).at[k], getattr(rr, near).at[k], sib).start()
            return carry

        lax.fori_loop(1, 16, one, 0)

    def passed(buf, near):
        def one(k, carry):
            source = lax.rem(chip + 16 - k, 16) * 2 + 1 - c
            left(buf.at[ex], getattr(ss, near).at[k])
            arrive(buf.at[source], getattr(rr, near).at[k])
            return carry

        lax.fori_loop(0, 16, one, 0)

    bar = greet(ex, mp)
    loads = [
        pltpu.make_async_copy(src, dst, ls.load.at[i])
        for i, (src, dst) in enumerate([
            (r.wqkv_hbm, r.wqkv), (r.wout_hbm, r.wout), (r.cot_hbm, r.cot), (r.wex_hbm, r.wex), (r.win_hbm, r.win)])
    ]
    for copy in loads:
        copy.start()
    unit, _ = norm_parts(r.tokens[...].astype(f32))
    normed = (unit * r.gain1[...]).astype(bf16)
    r.normed[...] = normed
    loads[0].wait()
    kt = transposed(dot(normed, r.wqkv[1]).astype(bf16))
    vt = transposed(dot(normed, r.wqkv[2]).astype(bf16))
    qt = transposed((dot(normed, r.wqkv[0]).astype(bf16) * HEAD_DIM ** (-0.5)).astype(bf16))
    for h in range(4):
        r.q_s[h] = qt[64 * h:64 * h + 64]
        r.kv_s[h, 0:64] = kt[64 * h:64 * h + 64]
        r.kv_s[h, 64:128] = vt[64 * h:64 * h + 64]
    greeted(bar)
    for i in (1, 3, 2):
        zp, to = zpeer(i)
        push(r.kv_s.at[zp], r.kvt.at[0, z], ss.az.at[i - 1], rr.az.at[i - 1], to)
    r.kvt[0, z] = r.kv_s[z]

    def own_piece(k):
        zq = lax.rem(z + 4 - k, 4)
        remote(r.kvt.at[0, zq], r.kvt.at[2, zq], ss.ag.at[4 * 1 + k], rr.ag.at[4 * 2 + k], ahead).start()
        remote(r.kvt.at[0, zq], r.kvt.at[3, zq], ss.ag.at[4 * 2 + k], rr.ag.at[4 * 3 + k], behind).start()
        remote(r.kvt.at[0, zq], r.kvt.at[1, zq], ss.ag.at[k], rr.ag.at[4 * 1 + k], sib).start()

    def came(slot, k):
        arrive(r.kvt.at[slot, lax.rem(z + 4 - k, 4)], rr.ag.at[4 * slot + k])

    def from_sides(k):
        zq = lax.rem(z + 4 - k, 4)
        came(2, k)
        remote(r.kvt.at[2, zq], r.kvt.at[6, zq], ss.ag.at[4 * 3 + k], rr.ag.at[4 * 6 + k], ahead).start()
        remote(r.kvt.at[2, zq], r.kvt.at[5, zq], ss.ag.at[4 * 4 + k], rr.ag.at[4 * 5 + k], sib).start()
        came(3, k)
        remote(r.kvt.at[3, zq], r.kvt.at[4, zq], ss.ag.at[4 * 5 + k], rr.ag.at[4 * 4 + k], sib).start()

    def from_far(k):
        zq = lax.rem(z + 4 - k, 4)
        came(6, k)
        remote(r.kvt.at[6, zq], r.kvt.at[7, zq], ss.ag.at[4 * 6 + k], rr.ag.at[4 * 7 + k], sib).start()

    own_piece(0)
    for i in (1, 3, 2):
        zp, to = zpeer(i)
        push(r.q_s.at[zp], r.q.at[z], ss.az.at[i + 2], rr.az.at[i + 2], to)
    r.q[z] = r.q_s[z]
    loads[1].wait()
    half = pl.ds(pl.multiple_of(128 * c, 128), 128)
    for i in range(1, 4):
        ym, to = ypeer(i)
        push(r.wout.at[half, :], r.wfull.at[mp, half, :], ss.wf.at[i - 1], rr.wf.at[i - 1], to)
    r.wfull[mp] = r.wout[...]
    r.vt1[64:80, :] = jnp.ones((16, 1024), bf16)
    ends = doc_ends(r.lengths)
    feature = lax.broadcasted_iota(jnp.int32, (64, 256), 0)
    loads[2].wait()
    mine = pl.ds(pl.multiple_of(256 * mp, 256), 256)
    r.cotq_s[...] = dot(slot_matrix(r.chosen[...]), r.cot[:, mine]).astype(bf16).reshape(EX, 16, 256)
    r.cotq[mp, ex] = r.cotq_s[ex]
    arrive(r.kvt.at[0, lax.rem(z + 3, 4)], rr.az.at[0])
    own_piece(1)
    arrive(r.kvt.at[0, lax.rem(z + 1, 4)], rr.az.at[2])
    own_piece(3)
    from_sides(0)
    arrive(r.kvt.at[0, lax.rem(z + 2, 4)], rr.az.at[1])
    own_piece(2)
    zp, to = zpeer(2)
    push(r.normed, r.nall.at[z], ss.na.at[1], rr.na.at[1], to)
    r.nall[z] = r.normed[...]
    for i in range(1, 4):
        arrive(r.q.at[lax.rem(z + 4 - i, 4)], rr.az.at[i + 2])
    for b in range(4):
        docs = doc_row(ends, (b * 8 + j) * 256, 256)
        r.qaug[b, 0:64] = r.q[b]
        r.qaug[b, 64:128] = jnp.where(feature == docs, 0.0, negative_fill).astype(bf16)
        r.peak[b] = jnp.full((1, 256), negative_fill, f32)
        r.acc[b] = jnp.zeros((80, 256), f32)

    def load_keys(slot, jp):
        for b in range(4):
            docs = doc_row(ends, (b * 8 + jp) * 256, 256)
            hot = (feature == docs).astype(f32).astype(bf16)
            r.kaug[256 * b:256 * b + 256, :] = transposed(
                jnp.concatenate([r.kvt[slot, b, 0:64], hot], axis=0))

    def scores(b, n, causal):
        s = dot(r.kaug[0:n, :], r.qaug[b])
        if causal:
            rows = lax.broadcasted_iota(jnp.int32, (n, 256), 0)
            cols = lax.broadcasted_iota(jnp.int32, (n, 256), 1)
            s = jnp.where(rows - 256 * b <= cols, s, negative_fill)
        return s

    def load_chunk(slot, jp):
        load_keys(slot, jp)
        for b in range(4):
            r.vt1[0:64, 256 * b:256 * b + 256] = r.kvt[slot, b, 64:128]

    def forward(tiles, causal):
        def gather(b, n, p, factor):
            r.acc[b] = r.acc[b] * factor + dot(r.vt1[:, 0:n], p)

        held = None
        for b, n in tiles:
            s = scores(b, n, causal)
            if held is not None:
                gather(*held)
            old = r.peak[b]
            new = jnp.maximum(old, jnp.max(s, axis=0, keepdims=True))
            held = (b, n, jnp.exp(s - new).astype(bf16), jnp.exp(old - new))
            r.peak[b] = new
        gather(*held)

    load_chunk(0, j)
    forward([(b, 256 * b + 256) for b in (3, 2, 1, 0)], True)

    def chunk(i, carry):
        u = i // 2
        side = ((u + 1) // 2) % 2
        xp = (x + d * (2 * (i % 2) - 1) * side + 2 * (u // 3) + 8) % 4
        jp = xp * 2 + (c + (1 - side) * (i % 2) + side * (u // 2)) % 2

        @pl.when(i == 1)
        def _():
            from_sides(1)
            from_far(0)
            for k in range(4):
                came(1, k)

        @pl.when(i == 2)
        def _():
            from_sides(3)
            from_far(1)
            from_sides(2)

        @pl.when(i == 3)
        def _():
            from_far(3)

        @pl.when(i == 4)
        def _():
            from_far(2)
            for k in range(4):
                came(4, k)
            to_all(lambda to: r.cotq_s.at[to], r.cotq.at[mp, ex], "co")

        @pl.when(i == 5)
        def _():
            for k in range(4):
                came(5, k)
            for i in range(1, 4):
                ym, to = ypeer(4 - i)
                arrive(r.wfull.at[ym, half, :], rr.wf.at[i - 1])
                remote(
                    r.wfull.at[ym, half, :], r.wfull.at[ym, half, :], ss.wd.at[i - 1], rr.wd.at[i - 1], sib).start()

        @pl.when(i == 7)
        def _():
            for k in range(4):
                came(7, k)

        load_chunk(i, jp)

        @pl.when(jp < j)
        def _():
            forward([(b, 256 * b + 256) for b in (3, 2, 1, 0)], False)

        @pl.when(jp > j)
        def _():
            forward([(b, 256 * b) for b in (3, 2, 1)], False)

        return carry

    lax.fori_loop(1, 8, chunk, 0)
    for b in range(4):
        total = r.acc[b, 64:65]
        ot = r.acc[b, 0:64] / total
        r.ot[b] = ot
        r.lse[b] = r.peak[b] + jnp.log(total)
        r.o_s[b] = ot.astype(bf16)
    for i in (1, 3, 2):
        zp, to = zpeer(i)
        push(r.o_s.at[zp], r.att.at[mp, z], ss.oz.at[i - 1], rr.oz.at[i - 1], to)
    r.att[mp, z] = r.o_s[z]
    for i in range(1, 4):
        zp, _ = zpeer(4 - i)
        arrive(r.att.at[mp, zp], rr.oz.at[i - 1])
    for i in (1, 3, 2):
        ym, to = ypeer(i)
        push(r.att.at[mp], r.att.at[mp], ss.oy.at[i - 1], rr.oy.at[i - 1], to)
    from_all(r.cotq_s.at[ex], lambda source: r.cotq.at[mp, source], "co")
    other = pl.ds(pl.multiple_of(128 - 128 * c, 128), 128)
    for i in range(1, 4):
        ym, _ = ypeer(4 - i)
        arrive(r.wfull.at[ym, other, :], rr.wd.at[i - 1])
    for i in range(1, 4):
        ym, _ = ypeer(4 - i)
        arrive(r.att.at[ym], rr.oy.at[i - 1])
    for i in (1, 3, 2):
        ym, to = ypeer(i)
        push(r.cotq.at[mp], r.cotq.at[mp], ss.cy.at[i - 1], rr.cy.at[i - 1], to)
    value = r.tokens[...].astype(f32) + dot(r.att[...].reshape(1024, 256), r.wfull[...].reshape(1024, 1024), 0, 0)
    r.resid[...] = value
    for k in range(4):
        @pl.when(mp == k)
        def _():
            r.rescol[...] = value[:, 256 * k:256 * k + 256]
    unit, _ = norm_parts(value)
    r.outgoing[...] = dot(slot_matrix(r.chosen[...]), (unit * r.gain2[...]).astype(bf16)).astype(bf16).reshape(
        EX, 16, 1024)
    to_all(lambda to: r.outgoing.at[to], r.arrived.at[ex], "di")
    r.arrived[ex] = r.outgoing[ex]
    loads[3].wait()
    for i in range(1, 4):
        ym, _ = ypeer(4 - i)
        arrive(r.cotq.at[ym], rr.cy.at[i - 1])
    for le in range(2):
        rows = jnp.concatenate([one_expert(r.cotq[k], le) for k in range(4)], axis=1)
        r.crows[le] = rows
        r.gh[le] = dot(rows, r.wex[le], 1, 1)
    loads[4].wait()
    from_all(r.outgoing.at[ex], lambda source: r.arrived.at[source], "di")
    for le in range(2):
        rows = one_expert(r.arrived[...], le)
        r.xrows[le] = rows
        hidden, slope = gelu_parts(dot(rows, r.win[le]))
        r.hid[le] = hidden.astype(bf16)
        gpre = (r.gh[le] * slope).astype(bf16)
        r.gpre[le] = gpre
        for k in range(4):
            r.part[le, k] = dot(gpre, r.win[le, 256 * k:256 * k + 256, :], 1, 1).astype(bf16)
        for i in (1, 3, 2):
            ym, to = ypeer(i)
            push(r.part.at[le, ym], r.rs.at[le, i - 1], ss.rs.at[3 * le + i - 1], rr.rs.at[3 * le + i - 1], to)
    stores = [
        pltpu.make_async_copy(src, dst, ls.store.at[i])
        for i, (src, dst) in enumerate([
            (r.xrows, r.x_hbm), (r.crows, r.c_hbm), (r.hid, r.hid_hbm), (r.gpre, r.gpre_hbm)])
    ]
    for copy in stores:
        copy.start()
    first = dot(r.hid[0], r.wex[0])
    r.branch[...] = both_experts(first, dot(r.hid[1], r.wex[1]))
    sums = []
    for le in range(2):
        total = r.part[le, mp].astype(f32)
        for i in range(3):
            arrive(r.rs.at[le, i], rr.rs.at[3 * le + i])
            total = total + r.rs[le, i].astype(f32)
        sums.append(total)
    r.back_s[...] = both_experts(sums[0], sums[1])
    to_all(lambda to: r.back_s.at[to], r.back.at[ex], "ba")
    r.back[ex] = r.back_s[ex]
    from_all(r.back_s.at[ex], lambda source: r.back.at[source], "ba")
    r.gn[mp] = dot(slot_matrix(r.chosen[...]), r.back[...].reshape(512, 256), 0, 0).astype(bf16)
    for i in (1, 3, 2):
        ym, to = ypeer(i)
        push(r.gn.at[mp], r.gn.at[mp], ss.gy.at[i - 1], rr.gy.at[i - 1], to)
    unit, inverse = norm_parts(r.resid[...])
    for i in range(1, 4):
        ym, _ = ypeer(4 - i)
        arrive(r.gn.at[ym], rr.gy.at[i - 1])
    grad = jnp.concatenate([r.gn[k] for k in range(4)], axis=1).astype(f32)
    grad_in, ggrad = norm_back(grad, r.gain2[...], unit, inverse)
    r.ggrad[...] = ggrad
    gres = r.cot[...].astype(f32) + grad_in
    r.gres[...] = gres
    low = gres.astype(bf16)
    r.dheads[...] = dot(r.wfull[mp], low, 1, 1).astype(bf16).reshape(4, 64, 256)
    for i in (1, 3, 2):
        zp, to = zpeer(i)
        push(r.dheads.at[zp], r.dob.at[z], ss.dz.at[i - 1], rr.dz.at[i - 1], to)
    r.dob[z] = r.dheads[z]
    wgrad = dot(r.att[mp].reshape(256, 256), low).astype(bf16)
    r.wgp[0] = wgrad[:, 0:512].reshape(4, 4, 16, 512)
    r.wgp[1] = wgrad[:, 512:1024].reshape(4, 4, 16, 512)
    push(r.wgp.at[1 - c], r.wgs, ss.wg.at[0], rr.wg.at[0], sib)
    for i in range(1, 4):
        ym, to = ypeer(i)
        push(
            r.branch.at[:, :, pl.ds(pl.multiple_of(256 * ym, 256), 256)], r.brs.at[i - 1],
            ss.br.at[i - 1], rr.br.at[i - 1], to)
    zero = jnp.zeros((64, 256), bf16)
    for i in range(1, 4):
        zp, _ = zpeer(4 - i)
        arrive(r.dob.at[zp], rr.dz.at[i - 1])
    arrive(r.wgs, rr.wg.at[0])
    r.wgq[...] = (r.wgp[c].astype(f32) + r.wgs[...].astype(f32)).astype(bf16)
    for i in (1, 3, 2):
        zp, to = zpeer(i)
        push(r.wgq.at[zp], r.wgz.at[i - 1], ss.wz.at[i - 1], rr.wz.at[i - 1], to)
    for i in (1, 3):
        zp, to = zpeer(i)
        push(r.normed, r.nall.at[z], ss.na.at[i - 1], rr.na.at[i - 1], to)
    for b in range(4):
        r.dopad[b, 0:64] = zero
        r.dopad[b, 64:128] = r.dob[b]
        r.qd[b, 0:256] = transposed(jnp.concatenate([r.q[b], zero], axis=0))
        r.qd[b, 256:512] = transposed(jnp.concatenate([zero, r.dob[b]], axis=0))
        r.delta[b] = jnp.sum(r.dob[b].astype(f32) * r.ot[b], axis=0, keepdims=True)
        r.dq[b] = jnp.zeros((64, 256), f32)

    def load_back(slot, jp):
        load_keys(slot, jp)
        for b in range(4):
            r.kvn[256 * b:256 * b + 256, :] = transposed(r.kvt[slot, b])
            r.kt[:, 256 * b:256 * b + 256] = r.kvt[slot, b, 0:64]

    def backward(tiles, causal):
        def gather(b, n, ds, p):
            added = dot(ds, r.qd[b, 0:256]) + dot(p, r.qd[b, 256:512])
            if b == 3:
                r.dkv[0:n] = added
            else:
                r.dkv[0:n] = r.dkv[0:n] + added
            r.dq[b] = r.dq[b] + dot(r.kt[:, 0:n], ds)

        held = None
        for b, n in tiles:
            s = scores(b, n, causal)
            dp = dot(r.kvn[0:n, :], r.dopad[b])
            if held is not None:
                gather(*held)
            p = jnp.exp(s - r.lse[b])
            held = (b, n, (p * (dp - r.delta[b])).astype(bf16), p.astype(bf16))
        gather(*held)

    def back_chunk(i, carry):
        p = i // 2
        w = p + (p // 2) * (1 - 2 * (p % 2))
        g = (2 + d * w + 4) % 4
        flip = 1 - i % 2
        odd = g % 2
        slot = odd * (2 + g // 2 + 2 * flip) + (1 - odd) * (3 * g + flip)
        xp = (x - d * g + 8) % 4
        jp = xp * 2 + (c + flip) % 2
        load_back(slot, jp)

        @pl.when(jp < j)
        def _():
            backward([(b, 256 * b + 256) for b in (3, 2, 1, 0)], False)

        @pl.when(jp > j)
        def _():
            r.dkv[768:1024] = jnp.zeros((256, 128), f32)
            backward([(b, 256 * b) for b in (3, 2, 1)], False)

        @pl.when(i % 2 == 0)
        def _():
            r.sb[p] = r.dkv[...].astype(bf16)
            remote(r.sb.at[p], r.sr.at[p], ss.sb.at[p], rr.sb.at[p], sib).start()

        @pl.when(i % 2 == 1)
        def _():
            arrive(r.sr.at[p], rr.sb.at[p])
            r.xs[p] = (r.dkv[...] + r.sr[p].astype(f32)).astype(bf16)

            @pl.when(p == 0)
            def _():
                remote(r.xs.at[0], r.xr.at[0], ss.xs.at[0], rr.xs.at[0], ahead).start()

            @pl.when(p == 2 - c)
            def _():
                remote(r.xs.at[p], r.xr.at[1], ss.xs.at[1], rr.xs.at[1], behind).start()

            @pl.when(p == 2)
            def _():
                arrive(r.xr.at[0], rr.xs.at[0])
                r.xs[3] = (r.xs[1 + c].astype(f32) + r.xr[0].astype(f32)).astype(bf16)
                remote(r.xs.at[3], r.xr.at[2], ss.xs.at[2], rr.xs.at[2], ahead).start()

        @pl.when(i == 1)
        def _():
            for k in range(3):
                arrive(r.wgz.at[k], rr.wz.at[k])
            total = r.wgq[z].astype(f32)
            for k in range(3):
                total = total + r.wgz[k].astype(f32)
            r.wgx[...] = total.astype(bf16)
            for k in (1, 3, 2):
                xq, to = xpeer(k)
                remote(r.wgx.at[xq], r.wgr.at[k - 1], ss.wx.at[k - 1], rr.wx.at[k - 1], to).start()

        @pl.when(i == 4)
        def _():
            total = r.branch[:, :, mine].astype(f32)
            for k in range(3):
                arrive(r.brs.at[k], rr.br.at[k])
                total = total + r.brs[k].astype(f32)
            r.bs[...] = total.astype(bf16)
            to_all(lambda to: r.bs.at[to], r.bret.at[ex], "bb")
            r.bret[ex] = r.bs[ex]

        @pl.when(i == 6)
        def _():
            total = r.wgx[x].astype(f32)
            for k in range(3):
                arrive(r.wgr.at[k], rr.wx.at[k])
                total = total + r.wgr[k].astype(f32)
            r.wgf[c, z, x] = total.astype(bf16)
            for k in (1, 3, 2):
                _, to = xpeer(k)
                remote(r.wgf.at[c, z, x], r.wgf.at[c, z, x], ss.wa.at[k - 1], rr.wa.at[k - 1], to).start()

        return carry

    lax.fori_loop(0, 7, back_chunk, 0)
    load_back(0, j)
    backward([(b, 256 * b + 256) for b in (3, 2, 1, 0)], True)
    for b in range(4):
        r.zs[b, 0:64] = (r.dq[b] * HEAD_DIM ** (-0.5)).astype(bf16)
    for i in (1, 3, 2):
        zp, to = zpeer(i)
        push(r.zs.at[zp, 0:64], r.zr.at[z, 0:64], ss.zq.at[i + 2], rr.zq.at[i + 2], to)
    r.resid[...] = norm_parts(r.tokens[...].astype(f32))[0]
    arrive(r.sr.at[3], rr.sb.at[3])
    total = r.dkv[...] + r.sr[3].astype(f32)
    for k in (1, 2):
        arrive(r.xr.at[k], rr.xs.at[k])
        total = total + r.xr[k].astype(f32)
    low = total.astype(bf16)
    for b in range(4):
        r.zs[b, 64:192] = transposed(low[256 * b:256 * b + 256])
    for i in (1, 3, 2):
        zp, to = zpeer(i)
        push(r.zs.at[zp, 64:192], r.zr.at[z, 64:192], ss.zq.at[i - 1], rr.zq.at[i - 1], to)
    r.zr[z] = r.zs[z]
    for i in range(1, 4):
        zp, _ = zpeer(4 - i)
        arrive(r.nall.at[zp], rr.na.at[i - 1])
    wt = dot(r.zs[0], r.nall[0])
    for b in range(1, 4):
        wt = wt + dot(r.zs[b], r.nall[b])
    wt = wt.astype(bf16)
    for k in range(8):
        r.wp[k] = wt[:, 128 * k:128 * k + 128]
    for i in range(1, 8):
        jt = lax.rem(j + i, 8)
        push(r.wp.at[jt], r.wr.at[i - 1], ss.wp.at[i - 1], rr.wp.at[i - 1], (z * 8 + jt, mp))
    for i in range(1, 4):
        xq, _ = xpeer(4 - i)
        arrive(r.wgf.at[c, z, xq], rr.wa.at[i - 1])
    for i in (1, 3, 2):
        _, to = zpeer(i)
        push(r.wgf.at[c, z], r.wgf.at[c, z], ss.wb.at[i - 1], rr.wb.at[i - 1], to)
    for i in range(1, 4):
        zp, _ = zpeer(4 - i)
        arrive(r.zr.at[zp, 0:64], rr.zq.at[i + 2])
        arrive(r.zr.at[zp, 64:192], rr.zq.at[i - 1])
    part = None
    for k in range(3):
        heads = transposed(jnp.concatenate([r.zr[h, 64 * k:64 * k + 64] for h in range(4)], axis=0))
        term = dot(heads, r.wqkv[k], 1, 1)
        part = term if part is None else part + term
    r.gnp[...] = part.astype(bf16).reshape(4, 64, 1024)
    one_gain = jnp.sum(part * r.resid[...], axis=0, keepdims=True)
    r.small[...] = one_gain
    for i in (1, 3, 2):
        ym, to = ypeer(i)
        push(r.small, r.smally.at[i - 1], ss.sy.at[i - 1], rr.sy.at[i - 1], to)
    for i in (1, 3, 2):
        ym, to = ypeer(i)
        push(r.gnp.at[ym], r.ry.at[i - 1], ss.ry.at[i - 1], rr.ry.at[i - 1], to)
    summed = r.wp[j].astype(f32)
    for i in range(7):
        arrive(r.wr.at[i], rr.wp.at[i])
        summed = summed + r.wr[i].astype(f32)
    r.pieces[ex] = summed.astype(bf16)
    spread(r.pieces, "pa", "pb")
    grad = r.gnp[mp].astype(f32)
    for i in range(3):
        arrive(r.ry.at[i], rr.ry.at[i])
        grad = grad + r.ry[i].astype(f32)
    here = pl.ds(pl.multiple_of(64 * mp, 64), 64)
    unit, inverse = norm_parts(r.tokens[here, :].astype(f32))
    grad_in, _ = norm_back(grad, r.gain1[...], unit, inverse)
    r.igrad[here, :] = (r.gres[here, :] + grad_in).astype(bf16)
    for i in (1, 3, 2):
        ym, to = ypeer(i)
        push(r.igrad.at[here, :], r.igrad.at[here, :], ss.ay.at[i - 1], rr.ay.at[i - 1], to)
    for i in range(3):
        arrive(r.smally.at[i], rr.sy.at[i])
        one_gain = one_gain + r.smally[i]
    r.smalle[ex, 0:1] = one_gain
    r.smalle[ex, 1:2] = r.ggrad[...]
    to_all(lambda to: r.smalle.at[ex], r.smalle.at[ex], "se")
    from_all(r.bs.at[ex], lambda source: r.bret.at[source], "bb")
    rows = dot(slot_matrix(r.chosen[...]), r.bret[...].reshape(512, 256), 0, 0)
    r.out[...] = (r.rescol[...] + rows).astype(bf16)
    for i in range(1, 4):
        zp, _ = zpeer(4 - i)
        arrive(r.wgf.at[c, zp], rr.wb.at[i - 1])
    push(r.wgf.at[c], r.wgf.at[c], ss.wc.at[0], rr.wc.at[0], sib)
    arrive(r.wgf.at[1 - c], rr.wc.at[0])
    for k in range(16):
        for core in range(2):
            r.wout_out[16 * k:16 * k + 16, 512 * core:512 * core + 512] = r.wgf[core, k // 4, k % 4]
    pass_on(r.pieces, "pa", "pb")
    passed(r.pieces, "pb")
    for k in range(3):
        for row in range(8):
            block = jnp.concatenate([r.pieces[8 * h + row, 64 * k:64 * k + 64] for h in range(4)], axis=0)
            r.qkv_out[k, 128 * row:128 * row + 128] = transposed(block)
    from_all(r.smalle.at[ex], lambda source: r.smalle.at[source], "se")
    both = jnp.sum(r.smalle[...], axis=0)
    r.gain1_out[...] = both[0:1]
    r.gain2_out[...] = both[1:2]
    for i in range(1, 4):
        ym, _ = ypeer(4 - i)
        there = pl.ds(pl.multiple_of(64 * ym, 64), 64)
        arrive(r.igrad.at[there, :], rr.ay.at[i - 1])
    for src, ssem in pending:
        left(src, ssem)
    for k in range(28):
        left(r.kvt.at[0, 0], ss.ag.at[k])
    for k in range(3):
        left(r.wfull.at[0, half, :], ss.wd.at[k])
    for p in range(4):
        left(r.sb.at[p], ss.sb.at[p])
    for p in range(3):
        left(r.xs.at[p], ss.xs.at[p])
        left(r.wgx.at[0], ss.wx.at[p])
        left(r.wgf.at[c, z, x], ss.wa.at[p])
    for copy in stores:
        copy.wait()


def layer(*args):
    spaces = {"x_hbm": ANY, "c_hbm": ANY, "hid_hbm": ANY, "gpre_hbm": ANY}
    return pl.pallas_call(
        layer_kernel,
        out_shape=[jax.ShapeDtypeStruct(s, t) for s, t in OUTS.values()],
        in_specs=[SM, VM, VM, VM, VM, ANY, ANY, ANY, ANY, ANY],
        out_specs=[spaces.get(name, VM) for name in OUTS],
        scratch_shapes=[pltpu.VMEM(s, t) for s, t in BUFFERS.values()]
        + [DMA(s) for group in (LOCAL, SENT, TAKEN) for s in group.values()],
        name="layer",
        compiler_params=pltpu.CompilerParams(
            collective_id=0, has_side_effects=True, vmem_limit_bytes=VMEM_BYTES),
    )(*args)


def finish_kernel(*refs):
    held = 10
    sources, results = refs[:held], refs[held:held + 8]
    x, gpre, hid, cots, qkv, wout, out, igrad, gain1, gain2 = refs[held + 8:2 * held + 8]
    in_buf, out_buf, qkv_buf, wout_buf, load, store, rest = refs[2 * held + 8:]
    in_grad, out_grad, qkv_o, wout_o, out_o, igrad_o, gain1_o, gain2_o = results
    buffers = (x, gpre, hid, cots, qkv, wout, out, igrad, gain1, gain2)
    loads = [pltpu.make_async_copy(a, b, load.at[i]) for i, (a, b) in enumerate(zip(sources, buffers, strict=True))]
    for copy in loads:
        copy.start()
    stores = []

    def put(src, dst, sem):
        copy = pltpu.make_async_copy(src, dst, sem)
        copy.start()
        stores.append(copy)

    for k, (left, right, buf, result) in enumerate(((x, gpre, in_buf, in_grad), (hid, cots, out_buf, out_grad))):
        loads[2 * k].wait()
        loads[2 * k + 1].wait()
        for e in range(2):
            for t in range(4):
                rows = pl.ds(256 * t, 256)
                buf[e, rows, :] = dot(left[e, :, 256 * t:256 * t + 256], right[e], 0, 0)
                put(buf.at[e, rows, :], result.at[e, rows, :], store.at[8 * k + 4 * e + t])
    for copy in loads[4:]:
        copy.wait()
    qkv_buf[...] = qkv[...].astype(f32)
    wout_buf[...] = wout[...].astype(f32)
    plain = ((qkv_buf, qkv_o), (wout_buf, wout_o), (out, out_o), (igrad, igrad_o), (gain1, gain1_o), (gain2, gain2_o))
    for k, (src, dst) in enumerate(plain):
        put(src, dst, rest.at[k])
    for copy in stores:
        copy.wait()


def finish(*args):
    big = ((2, 1024, 1024), f32)
    outs = [big, big, ((3, 1024, 256), f32), ((256, 1024), f32), ((256, 256), bf16), ((256, 1024), bf16)]
    outs += [((1, 1024), f32)] * 2
    return pl.pallas_call(
        finish_kernel,
        out_shape=[jax.ShapeDtypeStruct(s, t) for s, t in outs],
        in_specs=[ANY] * 10,
        out_specs=[ANY] * 8,
        scratch_shapes=[pltpu.VMEM(v.shape, v.dtype) for v in args]
        + [pltpu.VMEM(s, t) for s, t in outs[:4]] + [DMA((10,)), DMA((16,)), DMA((6,))],
        name="finish",
        compiler_params=pltpu.CompilerParams(vmem_limit_bytes=62 << 20),
        cost_estimate=pl.CostEstimate(flops=2 * 2 * 2 * 256 * 1024 * 1024, bytes_accessed=28 << 20, transcendentals=0),
    )(*args)


def on_device(
    tokens, hash_ids, lengths, norm1_gain, qkv_weight, out_weight, norm2_gain, expert_in, expert_out, cotangent,
):
    x, cots, hid, gpre, out, igrad, gain1, gain2, qkv, wout = layer(
        lengths, tokens, norm1_gain.reshape(1, 1024), norm2_gain.reshape(1, 1024), hash_ids.reshape(1, 256),
        jnp.transpose(qkv_weight, (1, 0, 2)), out_weight, cotangent, expert_in, expert_out)
    in_grad, out_grad, qkv, wout, out, igrad, gain1, gain2 = finish(
        x, gpre, hid, cots, qkv, wout, out, igrad, gain1, gain2)
    return out, igrad, gain1.reshape(1024), jnp.transpose(qkv, (1, 0, 2)), wout, gain2.reshape(1024), in_grad, out_grad


def solution(mesh):
    placed = (
        P("ex", None), P("ex", None), P(), P(), P(None, None, "mp"), P("mp", None), P(),
        P("ex", None, "mp"), P("ex", "mp", None), P("ex", None),
    )
    return jax.shard_map(
        on_device,
        mesh=mesh,
        in_specs=placed,
        out_specs=(
            P("ex", "mp"), P("ex", None), P(), P(None, None, "mp"), P("mp", None), P(),
            P("ex", None, "mp"), P("ex", "mp", None),
        ),
        check_vma=False,
    )
```

```python
import functools

import jax
import jax.numpy as jnp
from jax import lax
from jax.experimental import pallas as pl
from jax.experimental.pallas import tpu as pltpu
from jax.sharding import PartitionSpec as P

HEAD_DIM = 64
epsilon = 1e-05
negative_fill = -1e30
MESH = pl.DeviceIdType.MESH
bf16, f32 = jnp.bfloat16, jnp.float32
EX, MP = 32, 4
VMEM_BYTES = 54 << 20


def dot(a, b, ca=1, cb=0):
    return lax.dot_general(a, b, (((ca,), (cb,)), ((), ())), preferred_element_type=f32)


def place():
    ex, mp = lax.axis_index("ex"), lax.axis_index("mp")
    z, x, c = ex // 8, (ex // 2) % 4, ex % 2
    return ex, mp, z, x, c


def send(src, dst, ssem, rsem, device):
    copy = pltpu.make_async_remote_copy(
        src_ref=src, dst_ref=dst, send_sem=ssem, recv_sem=rsem, device_id=device, device_id_type=MESH
    )
    copy.start()
    return copy


def greet(ex, mp):
    bar = pltpu.get_barrier_semaphore()

    def one(d, carry):
        pl.semaphore_signal(bar, inc=1, device_id=(lax.rem(ex + d, EX), mp), device_id_type=MESH)
        return carry

    lax.fori_loop(1, EX, one, 0)
    for d in range(1, MP):
        pl.semaphore_signal(bar, inc=1, device_id=(ex, lax.rem(mp + d, MP)), device_id_type=MESH)
    return bar


def greeted(bar):
    pl.semaphore_wait(bar, EX - 1 + MP - 1)


def slot_matrix(chosen_row):
    tok = chosen_row.shape[1]
    experts = lax.broadcasted_iota(jnp.int32, (64, tok), 0)
    hot = (experts == chosen_row).astype(f32)
    rows = lax.broadcasted_iota(jnp.int32, (tok, tok), 0)
    cols = lax.broadcasted_iota(jnp.int32, (tok, tok), 1)
    before = (rows < cols).astype(bf16)
    earlier = dot(hot.astype(bf16), before)
    rank = jnp.sum(earlier * hot, axis=0, keepdims=True)
    target = chosen_row * 8 + rank.astype(jnp.int32)
    slots = lax.broadcasted_iota(jnp.int32, (512, tok), 0)
    return (slots == target).astype(f32).astype(bf16)


def doc_row(ends, first, count):
    pos = first + lax.broadcasted_iota(jnp.int32, (1, count), 1)
    row = jnp.zeros((1, count), jnp.int32)
    for end in ends:
        row = row + (pos >= end).astype(jnp.int32)
    return row


def doc_ends(lengths_ref):
    ends, total = [], 0
    for i in range(9):
        total = total + lengths_ref[i]
        ends.append(total)
    return ends


def norm_parts(v):
    mean = jnp.mean(v, axis=-1, keepdims=True)
    centred = v - mean
    inverse = lax.rsqrt(jnp.mean(centred * centred, axis=-1, keepdims=True) + epsilon)
    return centred * inverse, inverse


def transposed(v):
    return v.T


def norm_back(grad_out, gain_row, unit, inverse):
    scaled = grad_out * gain_row
    centred = scaled - jnp.mean(scaled, axis=-1, keepdims=True)
    grad_in = inverse * (centred - unit * jnp.mean(scaled * unit, axis=-1, keepdims=True))
    return grad_in, jnp.sum(grad_out * unit, axis=0, keepdims=True)


def gelu_parts(pre):
    k = 0.7978845608028654
    square = pre * pre
    t = jnp.tanh(k * pre * (1.0 + 0.044715 * square))
    half = 0.5 * (1.0 + t)
    slope = half + 0.5 * pre * (1.0 - t * t) * (k * (1.0 + 3 * 0.044715 * square))
    return pre * half, slope


def one_expert(rows, le):
    wide = rows.astype(f32)
    return wide[:, 8 * le:8 * le + 8].reshape(256, rows.shape[2]).astype(bf16)


def both_experts(first, second):
    width = first.shape[1]
    return jnp.concatenate([first.reshape(32, 8, width), second.reshape(32, 8, width)], axis=1).astype(bf16)


VM = pl.BlockSpec(memory_space=pltpu.VMEM)
SM = pl.BlockSpec(memory_space=pltpu.SMEM)
ANY = pl.BlockSpec(memory_space=pl.ANY)
DMA = pltpu.SemaphoreType.DMA
ROWS = (2, 256, 1024)

ARGS = ["lengths", "tokens", "gain1", "gain2", "chosen", "wqkv_hbm", "wout_hbm", "cot_hbm", "win_hbm", "wex_hbm"]
OUTS = {
    "xrows": (ROWS, bf16), "crows": (ROWS, bf16), "hid": (ROWS, bf16), "gpre": (ROWS, bf16),
    "out": ((256, 256), bf16), "igrad": ((256, 1024), bf16), "gain1_out": ((1, 1024), f32), "gain2_out": ((1, 1024), f32),
    "qkv_out": ((3, 1024, 256), bf16), "wout_out": ((256, 1024), bf16),
}
BUFFERS = {
    "wqkv": ((3, 1024, 256), bf16), "wout": ((256, 1024), bf16), "cot": ((256, 1024), bf16),
    "win": ((2, 1024, 1024), bf16), "wex": ((2, 1024, 1024), bf16), "normed": ((256, 1024), bf16),
    "nall": ((4, 256, 1024), bf16), "wfull": ((4, 256, 1024), bf16),
    "q_s": ((4, 64, 256), bf16), "kv_s": ((4, 128, 256), bf16), "q": ((4, 64, 256), bf16),
    "kvt": ((8, 4, 128, 256), bf16), "qaug": ((4, 128, 256), bf16), "kaug": ((1024, 128), bf16),
    "vt1": ((80, 1024), bf16), "acc": ((4, 80, 256), f32), "peak": ((4, 1, 256), f32),
    "ot": ((4, 64, 256), f32), "lse": ((4, 1, 256), f32), "o_s": ((4, 64, 256), bf16),
    "att": ((4, 4, 64, 256), bf16), "cotq_s": ((32, 16, 256), bf16), "cotq": ((4, 32, 16, 256), bf16),
    "outgoing": ((32, 16, 1024), bf16), "arrived": ((32, 16, 1024), bf16),
    "gh": (ROWS, f32),
    "part": ((2, 4, 256, 128), bf16), "rs": ((2, 3, 256, 128), bf16), "back_s": ((32, 16, 128), bf16),
    "back": ((32, 16, 128), bf16), "wide_s": ((32, 16, 512), bf16), "wide": ((32, 16, 512), bf16),
    "gb": ((4, 256, 128), bf16), "gbr": ((3, 256, 128), bf16), "gn": ((2, 4, 256, 128), bf16), "resid": ((256, 1024), f32),
    "rescol": ((256, 256), f32), "gres": ((256, 1024), f32), "branch": ((32, 16, 1024), bf16),
    "wgp": ((2, 4, 4, 16, 512), bf16), "wgs": ((4, 4, 16, 512), bf16), "wgq": ((4, 4, 16, 512), bf16),
    "wgz": ((3, 4, 16, 512), bf16), "wgx": ((4, 16, 512), bf16), "wgr": ((3, 16, 512), bf16),
    "wgf": ((2, 4, 4, 16, 512), bf16),
    "dheads": ((4, 64, 256), bf16), "dob": ((4, 64, 256), bf16), "brs": ((3, 32, 16, 256), bf16),
    "bs": ((32, 16, 256), bf16), "bret": ((32, 16, 256), bf16), "dopad": ((4, 128, 256), bf16),
    "qd": ((4, 512, 128), bf16), "delta": ((4, 1, 256), f32), "kvn": ((1024, 128), bf16),
    "kt": ((64, 1024), bf16), "dkv": ((1024, 128), f32), "dq": ((4, 64, 256), f32),
    "sb": ((4, 1024, 128), bf16), "sr": ((4, 1024, 128), bf16), "xs": ((4, 1024, 128), bf16),
    "xr": ((3, 1024, 128), bf16), "zs": ((4, 192, 256), bf16), "zr": ((4, 192, 256), bf16),
    "wpq": ((8, 64, 128), bf16), "wrq": ((7, 64, 128), bf16), "pieceq": ((32, 64, 128), bf16),
    "wpk": ((8, 128, 128), bf16), "wrk": ((7, 128, 128), bf16), "piecek": ((32, 128, 128), bf16),
    "gnp": ((4, 64, 1024), bf16), "ry": ((3, 64, 1024), bf16), "small": ((1, 1024), f32),
    "smally": ((3, 1, 1024), f32), "smalle": ((32, 2, 1024), f32), "ggrad": ((1, 1024), f32),
}
LOCAL = {"load": (5,)}
SENT = {
    "az": (6,), "ag": (28,), "wf": (3,), "wd": (3,), "co": (31,), "cy": (3,), "na": (3,), "oz": (3,), "oy": (3,),
    "di": (31,), "rs": (6,), "ba": (31,), "bc": (31,), "gb": (3,), "gy": (6,), "dz": (3,), "br": (3,), "bb": (31,), "sb": (4,), "xs": (3,),
    "wg": (1,), "wz": (3,), "wx": (3,), "wa": (3,), "wb": (3,), "wc": (1,), "zq": (6,), "wp": (7,), "wk": (7,), "pa": (15,), "pb": (16,), "pc": (15,), "pd": (16,),
    "ry": (3,), "ay": (3,), "sy": (3,), "se": (31,),
}
TAKEN = dict(SENT, ag=(32,))


class Refs:
    pass


def layer_kernel(*refs):
    r, ls, ss, rr = Refs(), Refs(), Refs(), Refs()
    names = [(r, k) for k in ARGS + list(OUTS) + list(BUFFERS)] + [(ls, k) for k in LOCAL]
    names += [(ss, k) for k in SENT] + [(rr, k) for k in TAKEN]
    for (group, name), ref in zip(names, refs, strict=True):
        setattr(group, name, ref)
    ex, mp, z, x, c = place()
    d = 1 - 2 * c
    j = x * 2 + c
    chip = ex // 2
    sib = (ex + d, mp)
    ahead = (z * 8 + lax.rem(x + d + 4, 4) * 2 + c, mp)
    behind = (z * 8 + lax.rem(x - d + 4, 4) * 2 + c, mp)
    pending = []

    def zpeer(i):
        zp = lax.rem(z + i, 4)
        return zp, (zp * 8 + j, mp)

    def ypeer(i):
        ym = lax.rem(mp + i, MP)
        return ym, (ex, ym)

    def xpeer(i):
        xq = lax.rem(x + i, 4)
        return xq, (z * 8 + xq * 2 + c, mp)

    def remote(src, dst, ssem, rsem, device):
        return pltpu.make_async_remote_copy(
            src_ref=src, dst_ref=dst, send_sem=ssem, recv_sem=rsem, device_id=device, device_id_type=MESH)

    def push(src, dst, ssem, rsem, device):
        remote(src, dst, ssem, rsem, device).start()
        pending.append((src, ssem))

    def arrive(dst, rsem):
        remote(dst, dst, rsem, rsem, sib).wait_recv()

    def left(src, ssem):
        remote(src, src, ssem, ssem, sib).wait_send()

    def to_all(src_of, dst, name):
        def one(k, carry):
            to = lax.rem(ex + k, EX)
            remote(src_of(to), dst, getattr(ss, name).at[k - 1], getattr(rr, name).at[k - 1], (to, mp)).start()
            return carry

        lax.fori_loop(1, EX, one, 0)

    def from_all(src, dst_of, name):
        def one(k, carry):
            left(src, getattr(ss, name).at[k - 1])
            arrive(dst_of(lax.rem(ex + EX - k, EX)), getattr(rr, name).at[k - 1])
            return carry

        lax.fori_loop(1, EX, one, 0)

    def spread(buf, far, near):
        def one(k, carry):
            to = lax.rem(chip + k, 16) * 2 + c
            remote(buf.at[ex], buf.at[ex], getattr(ss, far).at[k - 1], getattr(rr, far).at[k - 1], (to, mp)).start()
            return carry

        lax.fori_loop(1, 16, one, 0)
        remote(buf.at[ex], buf.at[ex], getattr(ss, near).at[0], getattr(rr, near).at[0], sib).start()

    def pass_on(buf, far, near):
        def one(k, carry):
            source = lax.rem(chip + 16 - k, 16) * 2 + c
            left(buf.at[ex], getattr(ss, far).at[k - 1])
            arrive(buf.at[source], getattr(rr, far).at[k - 1])
            remote(buf.at[source], buf.at[source], getattr(ss, near).at[k], getattr(rr, near).at[k], sib).start()
            return carry

        lax.fori_loop(1, 16, one, 0)

    def passed(buf, near):
        def one(k, carry):
            source = lax.rem(chip + 16 - k, 16) * 2 + 1 - c
            left(buf.at[ex], getattr(ss, near).at[k])
            arrive(buf.at[source], getattr(rr, near).at[k])
            return carry

        lax.fori_loop(0, 16, one, 0)

    bar = greet(ex, mp)
    loads = [
        pltpu.make_async_copy(src, dst, ls.load.at[i])
        for i, (src, dst) in enumerate([
            (r.wqkv_hbm, r.wqkv), (r.wout_hbm, r.wout), (r.cot_hbm, r.cot), (r.wex_hbm, r.wex), (r.win_hbm, r.win)])
    ]
    for copy in loads:
        copy.start()
    unit, _ = norm_parts(r.tokens[...].astype(f32))
    normed = (unit * r.gain1[...]).astype(bf16)
    r.normed[...] = normed
    loads[0].wait()
    kt = transposed(dot(normed, r.wqkv[1]).astype(bf16))
    vt = transposed(dot(normed, r.wqkv[2]).astype(bf16))
    qt = transposed((dot(normed, r.wqkv[0]).astype(bf16) * HEAD_DIM ** (-0.5)).astype(bf16))
    for h in range(4):
        r.q_s[h] = qt[64 * h:64 * h + 64]
        r.kv_s[h, 0:64] = kt[64 * h:64 * h + 64]
        r.kv_s[h, 64:128] = vt[64 * h:64 * h + 64]
    greeted(bar)
    for i in (1, 3, 2):
        zp, to = zpeer(i)
        push(r.kv_s.at[zp], r.kvt.at[0, z], ss.az.at[i - 1], rr.az.at[i - 1], to)
    r.kvt[0, z] = r.kv_s[z]

    def own_piece(k):
        zq = lax.rem(z + 4 - k, 4)
        remote(r.kvt.at[0, zq], r.kvt.at[2, zq], ss.ag.at[4 * 1 + k], rr.ag.at[4 * 2 + k], ahead).start()
        remote(r.kvt.at[0, zq], r.kvt.at[3, zq], ss.ag.at[4 * 2 + k], rr.ag.at[4 * 3 + k], behind).start()
        remote(r.kvt.at[0, zq], r.kvt.at[1, zq], ss.ag.at[k], rr.ag.at[4 * 1 + k], sib).start()

    def came(slot, k):
        arrive(r.kvt.at[slot, lax.rem(z + 4 - k, 4)], rr.ag.at[4 * slot + k])

    def from_sides(k):
        zq = lax.rem(z + 4 - k, 4)
        came(2, k)
        remote(r.kvt.at[2, zq], r.kvt.at[6, zq], ss.ag.at[4 * 3 + k], rr.ag.at[4 * 6 + k], ahead).start()
        remote(r.kvt.at[2, zq], r.kvt.at[5, zq], ss.ag.at[4 * 4 + k], rr.ag.at[4 * 5 + k], sib).start()
        came(3, k)
        remote(r.kvt.at[3, zq], r.kvt.at[4, zq], ss.ag.at[4 * 5 + k], rr.ag.at[4 * 4 + k], sib).start()

    def from_far(k):
        zq = lax.rem(z + 4 - k, 4)
        came(6, k)
        remote(r.kvt.at[6, zq], r.kvt.at[7, zq], ss.ag.at[4 * 6 + k], rr.ag.at[4 * 7 + k], sib).start()

    own_piece(0)
    for i in (1, 3, 2):
        zp, to = zpeer(i)
        push(r.q_s.at[zp], r.q.at[z], ss.az.at[i + 2], rr.az.at[i + 2], to)
    r.q[z] = r.q_s[z]
    loads[1].wait()
    half = pl.ds(pl.multiple_of(128 * c, 128), 128)
    for i in range(1, 4):
        ym, to = ypeer(i)
        push(r.wout.at[half, :], r.wfull.at[mp, half, :], ss.wf.at[i - 1], rr.wf.at[i - 1], to)
    r.wfull[mp] = r.wout[...]
    r.vt1[64:80, :] = jnp.ones((16, 1024), bf16)
    ends = doc_ends(r.lengths)
    feature = lax.broadcasted_iota(jnp.int32, (64, 256), 0)
    loads[2].wait()
    mine = pl.ds(pl.multiple_of(256 * mp, 256), 256)
    r.cotq_s[...] = dot(slot_matrix(r.chosen[...]), r.cot[:, mine]).astype(bf16).reshape(EX, 16, 256)
    r.cotq[mp, ex] = r.cotq_s[ex]
    arrive(r.kvt.at[0, lax.rem(z + 3, 4)], rr.az.at[0])
    own_piece(1)
    arrive(r.kvt.at[0, lax.rem(z + 1, 4)], rr.az.at[2])
    own_piece(3)
    from_sides(0)
    arrive(r.kvt.at[0, lax.rem(z + 2, 4)], rr.az.at[1])
    own_piece(2)
    zp, to = zpeer(2)
    push(r.normed, r.nall.at[z], ss.na.at[1], rr.na.at[1], to)
    r.nall[z] = r.normed[...]
    for i in range(1, 4):
        arrive(r.q.at[lax.rem(z + 4 - i, 4)], rr.az.at[i + 2])
    for b in range(4):
        docs = doc_row(ends, (b * 8 + j) * 256, 256)
        r.qaug[b, 0:64] = r.q[b]
        r.qaug[b, 64:128] = jnp.where(feature == docs, 0.0, negative_fill).astype(bf16)
        r.peak[b] = jnp.full((1, 256), negative_fill, f32)
        r.acc[b] = jnp.zeros((80, 256), f32)

    def load_keys(slot, jp):
        for b in range(4):
            docs = doc_row(ends, (b * 8 + jp) * 256, 256)
            hot = (feature == docs).astype(f32).astype(bf16)
            r.kaug[256 * b:256 * b + 256, :] = transposed(
                jnp.concatenate([r.kvt[slot, b, 0:64], hot], axis=0))

    def scores(b, n, causal):
        s = dot(r.kaug[0:n, :], r.qaug[b])
        if causal:
            rows = lax.broadcasted_iota(jnp.int32, (n, 256), 0)
            cols = lax.broadcasted_iota(jnp.int32, (n, 256), 1)
            s = jnp.where(rows - 256 * b <= cols, s, negative_fill)
        return s

    def load_chunk(slot, jp):
        load_keys(slot, jp)
        for b in range(4):
            r.vt1[0:64, 256 * b:256 * b + 256] = r.kvt[slot, b, 64:128]

    def forward(tiles, causal):
        def gather(b, n, p, factor):
            r.acc[b] = r.acc[b] * factor + dot(r.vt1[:, 0:n], p)

        held = None
        for b, n in tiles:
            s = scores(b, n, causal)
            if held is not None:
                gather(*held)
            old = r.peak[b]
            new = jnp.maximum(old, jnp.max(s, axis=0, keepdims=True))
            held = (b, n, jnp.exp(s - new).astype(bf16), jnp.exp(old - new))
            r.peak[b] = new
        gather(*held)

    load_chunk(0, j)
    forward([(b, 256 * b + 256) for b in (3, 2, 1, 0)], True)

    def chunk(i, carry):
        u = i // 2
        side = ((u + 1) // 2) % 2
        xp = (x + d * (2 * (i % 2) - 1) * side + 2 * (u // 3) + 8) % 4
        jp = xp * 2 + (c + (1 - side) * (i % 2) + side * (u // 2)) % 2

        @pl.when(i == 1)
        def _():
            from_sides(1)
            from_far(0)
            for k in range(4):
                came(1, k)

        @pl.when(i == 2)
        def _():
            from_sides(3)
            from_far(1)
            from_sides(2)

        @pl.when(i == 3)
        def _():
            from_far(3)

        @pl.when(i == 4)
        def _():
            from_far(2)
            for k in range(4):
                came(4, k)
            to_all(lambda to: r.cotq_s.at[to], r.cotq.at[mp, ex], "co")

        @pl.when(i == 5)
        def _():
            for k in range(4):
                came(5, k)
            for i in range(1, 4):
                ym, to = ypeer(4 - i)
                arrive(r.wfull.at[ym, half, :], rr.wf.at[i - 1])
                remote(
                    r.wfull.at[ym, half, :], r.wfull.at[ym, half, :], ss.wd.at[i - 1], rr.wd.at[i - 1], sib).start()

        @pl.when(i == 7)
        def _():
            for k in range(4):
                came(7, k)

        load_chunk(i, jp)

        @pl.when(jp < j)
        def _():
            forward([(b, 256 * b + 256) for b in (3, 2, 1, 0)], False)

        @pl.when(jp > j)
        def _():
            forward([(b, 256 * b) for b in (3, 2, 1)], False)

        return carry

    lax.fori_loop(1, 8, chunk, 0)
    for b in range(4):
        total = r.acc[b, 64:65]
        ot = r.acc[b, 0:64] / total
        r.ot[b] = ot
        r.lse[b] = r.peak[b] + jnp.log(total)
        r.o_s[b] = ot.astype(bf16)
    for i in (1, 3, 2):
        zp, to = zpeer(i)
        push(r.o_s.at[zp], r.att.at[mp, z], ss.oz.at[i - 1], rr.oz.at[i - 1], to)
    r.att[mp, z] = r.o_s[z]
    for i in range(1, 4):
        zp, _ = zpeer(4 - i)
        arrive(r.att.at[mp, zp], rr.oz.at[i - 1])
    for i in (1, 3, 2):
        ym, to = ypeer(i)
        push(r.att.at[mp], r.att.at[mp], ss.oy.at[i - 1], rr.oy.at[i - 1], to)
    from_all(r.cotq_s.at[ex], lambda source: r.cotq.at[mp, source], "co")
    other = pl.ds(pl.multiple_of(128 - 128 * c, 128), 128)
    for i in range(1, 4):
        ym, _ = ypeer(4 - i)
        arrive(r.wfull.at[ym, other, :], rr.wd.at[i - 1])
    for i in range(1, 4):
        ym, _ = ypeer(4 - i)
        arrive(r.att.at[ym], rr.oy.at[i - 1])
    for i in (1, 3, 2):
        ym, to = ypeer(i)
        push(r.cotq.at[mp], r.cotq.at[mp], ss.cy.at[i - 1], rr.cy.at[i - 1], to)
    value = r.tokens[...].astype(f32) + dot(r.att[...].reshape(1024, 256), r.wfull[...].reshape(1024, 1024), 0, 0)
    r.resid[...] = value
    for k in range(4):
        @pl.when(mp == k)
        def _():
            r.rescol[...] = value[:, 256 * k:256 * k + 256]
    unit, _ = norm_parts(value)
    r.outgoing[...] = dot(slot_matrix(r.chosen[...]), (unit * r.gain2[...]).astype(bf16)).astype(bf16).reshape(
        EX, 16, 1024)
    to_all(lambda to: r.outgoing.at[to], r.arrived.at[ex], "di")
    r.arrived[ex] = r.outgoing[ex]
    loads[3].wait()
    for i in range(1, 4):
        ym, _ = ypeer(4 - i)
        arrive(r.cotq.at[ym], rr.cy.at[i - 1])
    for le in range(2):
        rows = jnp.concatenate([one_expert(r.cotq[k], le) for k in range(4)], axis=1)
        r.crows[le] = rows
        r.gh[le] = dot(rows, r.wex[le], 1, 1)
    loads[4].wait()
    from_all(r.outgoing.at[ex], lambda source: r.arrived.at[source], "di")
    def expert_rows(le):
        rows = one_expert(r.arrived[...], le)
        r.xrows[le] = rows
        return dot(rows, r.win[le])

    def activate(le, pre):
        hidden, slope = gelu_parts(pre)
        r.hid[le] = hidden.astype(bf16)
        gpre = (r.gh[le] * slope).astype(bf16)
        r.gpre[le] = gpre
        return gpre

    def give_back(le, gpre):
        for k in range(4):
            product = dot(gpre, r.win[le, 256 * k:256 * k + 256, :], 1, 1)
            r.part[le, k] = product[:, 0:128].astype(bf16)
            r.gh[le, :, 128 * k:128 * k + 128] = product[:, 128:256]
        for i in (1, 3, 2):
            ym, to = ypeer(i)
            push(r.part.at[le, ym], r.rs.at[le, i - 1], ss.rs.at[3 * le + i - 1], rr.rs.at[3 * le + i - 1], to)

    first, second = expert_rows(0), expert_rows(1)
    gpre = activate(0, first)
    give_back(0, gpre)
    give_back(1, activate(1, second))
    r.wide_s[...] = both_experts(r.gh[0, :, 0:512], r.gh[1, :, 0:512])
    to_all(lambda to: r.wide_s.at[to], r.wide.at[ex], "bc")
    r.wide[ex] = r.wide_s[ex]
    first = dot(r.hid[0], r.wex[0])
    r.branch[...] = both_experts(first, dot(r.hid[1], r.wex[1]))
    sums = []
    for le in range(2):
        total = r.part[le, mp].astype(f32)
        for i in range(3):
            arrive(r.rs.at[le, i], rr.rs.at[3 * le + i])
            total = total + r.rs[le, i].astype(f32)
        sums.append(total)
    r.back_s[...] = both_experts(sums[0], sums[1])
    to_all(lambda to: r.back_s.at[to], r.back.at[ex], "ba")
    r.back[ex] = r.back_s[ex]
    placer = slot_matrix(r.chosen[...])
    from_all(r.wide_s.at[ex], lambda source: r.wide.at[source], "bc")
    rows = dot(placer, r.wide[...].reshape(512, 512), 0, 0).astype(bf16)
    for k in range(4):
        r.gb[k] = rows[:, 128 * k:128 * k + 128]
    for i in (1, 3, 2):
        ym, to = ypeer(i)
        push(r.gb.at[ym], r.gbr.at[i - 1], ss.gb.at[i - 1], rr.gb.at[i - 1], to)
    from_all(r.back_s.at[ex], lambda source: r.back.at[source], "ba")
    r.gn[0, mp] = dot(placer, r.back[...].reshape(512, 128), 0, 0).astype(bf16)
    for i in (1, 3, 2):
        ym, to = ypeer(i)
        push(r.gn.at[0, mp], r.gn.at[0, mp], ss.gy.at[i - 1], rr.gy.at[i - 1], to)
    total = r.gb[mp].astype(f32)
    for i in range(3):
        arrive(r.gbr.at[i], rr.gb.at[i])
        total = total + r.gbr[i].astype(f32)
    r.gn[1, mp] = total.astype(bf16)
    for i in (1, 3, 2):
        ym, to = ypeer(i)
        push(r.gn.at[1, mp], r.gn.at[1, mp], ss.gy.at[i + 2], rr.gy.at[i + 2], to)
    unit, inverse = norm_parts(r.resid[...])
    for i in range(1, 4):
        ym, _ = ypeer(4 - i)
        arrive(r.gn.at[0, ym], rr.gy.at[i - 1])
        arrive(r.gn.at[1, ym], rr.gy.at[i + 2])
    grad = jnp.concatenate([r.gn[k % 2, k // 2] for k in range(8)], axis=1).astype(f32)
    grad_in, ggrad = norm_back(grad, r.gain2[...], unit, inverse)
    r.ggrad[...] = ggrad
    gres = r.cot[...].astype(f32) + grad_in
    r.gres[...] = gres
    low = gres.astype(bf16)
    r.dheads[...] = dot(r.wfull[mp], low, 1, 1).astype(bf16).reshape(4, 64, 256)
    for i in (1, 3, 2):
        zp, to = zpeer(i)
        push(r.dheads.at[zp], r.dob.at[z], ss.dz.at[i - 1], rr.dz.at[i - 1], to)
    r.dob[z] = r.dheads[z]
    wgrad = dot(r.att[mp].reshape(256, 256), low).astype(bf16)
    r.wgp[0] = wgrad[:, 0:512].reshape(4, 4, 16, 512)
    r.wgp[1] = wgrad[:, 512:1024].reshape(4, 4, 16, 512)
    push(r.wgp.at[1 - c], r.wgs, ss.wg.at[0], rr.wg.at[0], sib)
    for i in range(1, 4):
        ym, to = ypeer(i)
        push(
            r.branch.at[:, :, pl.ds(pl.multiple_of(256 * ym, 256), 256)], r.brs.at[i - 1],
            ss.br.at[i - 1], rr.br.at[i - 1], to)
    zero = jnp.zeros((64, 256), bf16)
    for i in range(1, 4):
        zp, _ = zpeer(4 - i)
        arrive(r.dob.at[zp], rr.dz.at[i - 1])
    arrive(r.wgs, rr.wg.at[0])
    r.wgq[...] = (r.wgp[c].astype(f32) + r.wgs[...].astype(f32)).astype(bf16)
    for i in (1, 3, 2):
        zp, to = zpeer(i)
        push(r.wgq.at[zp], r.wgz.at[i - 1], ss.wz.at[i - 1], rr.wz.at[i - 1], to)
    for i in (1, 3):
        zp, to = zpeer(i)
        push(r.normed, r.nall.at[z], ss.na.at[i - 1], rr.na.at[i - 1], to)
    for b in range(4):
        r.dopad[b, 0:64] = zero
        r.dopad[b, 64:128] = r.dob[b]
        r.qd[b, 0:256] = transposed(jnp.concatenate([r.q[b], zero], axis=0))
        r.qd[b, 256:512] = transposed(jnp.concatenate([zero, r.dob[b]], axis=0))
        r.delta[b] = jnp.sum(r.dob[b].astype(f32) * r.ot[b], axis=0, keepdims=True)
        r.dq[b] = jnp.zeros((64, 256), f32)

    def load_back(slot, jp):
        load_keys(slot, jp)
        for b in range(4):
            r.kvn[256 * b:256 * b + 256, :] = transposed(r.kvt[slot, b])
            r.kt[:, 256 * b:256 * b + 256] = r.kvt[slot, b, 0:64]

    def backward(tiles, causal):
        def gather(b, n, ds, p):
            added = dot(ds, r.qd[b, 0:256]) + dot(p, r.qd[b, 256:512])
            if b == 3:
                r.dkv[0:n] = added
            else:
                r.dkv[0:n] = r.dkv[0:n] + added
            r.dq[b] = r.dq[b] + dot(r.kt[:, 0:n], ds)

        held = None
        for b, n in tiles:
            s = scores(b, n, causal)
            dp = dot(r.kvn[0:n, :], r.dopad[b])
            if held is not None:
                gather(*held)
            p = jnp.exp(s - r.lse[b])
            held = (b, n, (p * (dp - r.delta[b])).astype(bf16), p.astype(bf16))
        gather(*held)

    def back_chunk(i, carry):
        p = i // 2
        w = p + (p // 2) * (1 - 2 * (p % 2))
        g = (2 + d * w + 4) % 4
        flip = 1 - i % 2
        odd = g % 2
        slot = odd * (2 + g // 2 + 2 * flip) + (1 - odd) * (3 * g + flip)
        xp = (x - d * g + 8) % 4
        jp = xp * 2 + (c + flip) % 2
        load_back(slot, jp)

        @pl.when(jp < j)
        def _():
            backward([(b, 256 * b + 256) for b in (3, 2, 1, 0)], False)

        @pl.when(jp > j)
        def _():
            r.dkv[768:1024] = jnp.zeros((256, 128), f32)
            backward([(b, 256 * b) for b in (3, 2, 1)], False)

        @pl.when(i % 2 == 0)
        def _():
            r.sb[p] = r.dkv[...].astype(bf16)
            remote(r.sb.at[p], r.sr.at[p], ss.sb.at[p], rr.sb.at[p], sib).start()

        @pl.when(i % 2 == 1)
        def _():
            arrive(r.sr.at[p], rr.sb.at[p])
            r.xs[p] = (r.dkv[...] + r.sr[p].astype(f32)).astype(bf16)

            @pl.when(p == 0)
            def _():
                remote(r.xs.at[0], r.xr.at[0], ss.xs.at[0], rr.xs.at[0], ahead).start()

            @pl.when(p == 2 - c)
            def _():
                remote(r.xs.at[p], r.xr.at[1], ss.xs.at[1], rr.xs.at[1], behind).start()

            @pl.when(p == 2)
            def _():
                arrive(r.xr.at[0], rr.xs.at[0])
                r.xs[3] = (r.xs[1 + c].astype(f32) + r.xr[0].astype(f32)).astype(bf16)
                remote(r.xs.at[3], r.xr.at[2], ss.xs.at[2], rr.xs.at[2], ahead).start()

        @pl.when(i == 3)
        def _():
            for k in range(3):
                arrive(r.wgz.at[k], rr.wz.at[k])
            total = r.wgq[z].astype(f32)
            for k in range(3):
                total = total + r.wgz[k].astype(f32)
            r.wgx[...] = total.astype(bf16)
            for k in (1, 3, 2):
                xq, to = xpeer(k)
                remote(r.wgx.at[xq], r.wgr.at[k - 1], ss.wx.at[k - 1], rr.wx.at[k - 1], to).start()

        @pl.when(i == 4)
        def _():
            total = r.branch[:, :, mine].astype(f32)
            for k in range(3):
                arrive(r.brs.at[k], rr.br.at[k])
                total = total + r.brs[k].astype(f32)
            r.bs[...] = total.astype(bf16)

        @pl.when(i == 6)
        def _():
            total = r.wgx[x].astype(f32)
            for k in range(3):
                arrive(r.wgr.at[k], rr.wx.at[k])
                total = total + r.wgr[k].astype(f32)
            r.wgf[c, z, x] = total.astype(bf16)
            for k in (1, 3, 2):
                _, to = xpeer(k)
                remote(r.wgf.at[c, z, x], r.wgf.at[c, z, x], ss.wa.at[k - 1], rr.wa.at[k - 1], to).start()

        return carry

    lax.fori_loop(0, 7, back_chunk, 0)
    load_back(0, j)
    backward([(b, 256 * b + 256) for b in (3, 2, 1, 0)], True)
    for b in range(4):
        r.zs[b, 0:64] = (r.dq[b] * HEAD_DIM ** (-0.5)).astype(bf16)
    for i in (1, 3, 2):
        zp, to = zpeer(i)
        push(r.zs.at[zp, 0:64], r.zr.at[z, 0:64], ss.zq.at[i + 2], rr.zq.at[i + 2], to)
    to_all(lambda to: r.bs.at[to], r.bret.at[ex], "bb")
    r.bret[ex] = r.bs[ex]
    for i in range(1, 4):
        zp, _ = zpeer(4 - i)
        arrive(r.nall.at[zp], rr.na.at[i - 1])

    def weight_part(first, last, pieces, name):
        wt = dot(r.zs[0, first:last], r.nall[0])
        for b in range(1, 4):
            wt = wt + dot(r.zs[b, first:last], r.nall[b])
        wt = wt.astype(bf16)
        for k in range(8):
            pieces[0][k] = wt[:, 128 * k:128 * k + 128]
        for i in range(1, 8):
            jt = lax.rem(j + i, 8)
            push(
                pieces[0].at[jt], pieces[1].at[i - 1], getattr(ss, name).at[i - 1], getattr(rr, name).at[i - 1],
                (z * 8 + jt, mp))

    def weight_sum(pieces, name):
        summed = pieces[0][j].astype(f32)
        for i in range(7):
            arrive(pieces[1].at[i], getattr(rr, name).at[i])
            summed = summed + pieces[1][i].astype(f32)
        pieces[2][ex] = summed.astype(bf16)

    weight_part(0, 64, (r.wpq, r.wrq), "wp")
    r.resid[...] = norm_parts(r.tokens[...].astype(f32))[0]
    arrive(r.sr.at[3], rr.sb.at[3])
    total = r.dkv[...] + r.sr[3].astype(f32)
    for k in (1, 2):
        arrive(r.xr.at[k], rr.xs.at[k])
        total = total + r.xr[k].astype(f32)
    low = total.astype(bf16)
    for b in range(4):
        r.zs[b, 64:192] = transposed(low[256 * b:256 * b + 256])
    for i in (1, 3, 2):
        zp, to = zpeer(i)
        push(r.zs.at[zp, 64:192], r.zr.at[z, 64:192], ss.zq.at[i - 1], rr.zq.at[i - 1], to)
    r.zr[z] = r.zs[z]
    weight_part(64, 192, (r.wpk, r.wrk), "wk")
    for i in range(1, 4):
        xq, _ = xpeer(4 - i)
        arrive(r.wgf.at[c, z, xq], rr.wa.at[i - 1])
    for i in (1, 3, 2):
        _, to = zpeer(i)
        push(r.wgf.at[c, z], r.wgf.at[c, z], ss.wb.at[i - 1], rr.wb.at[i - 1], to)

    def heads(first):
        return transposed(jnp.concatenate([r.zr[h, first:first + 64] for h in range(4)], axis=0))

    for i in range(1, 4):
        zp, _ = zpeer(4 - i)
        arrive(r.zr.at[zp, 0:64], rr.zq.at[i + 2])
    part = dot(heads(0), r.wqkv[0], 1, 1)
    for i in range(1, 4):
        zp, _ = zpeer(4 - i)
        arrive(r.zr.at[zp, 64:192], rr.zq.at[i - 1])
    part = part + dot(heads(64), r.wqkv[1], 1, 1) + dot(heads(128), r.wqkv[2], 1, 1)
    r.gnp[...] = part.astype(bf16).reshape(4, 64, 1024)
    one_gain = jnp.sum(part * r.resid[...], axis=0, keepdims=True)
    r.small[...] = one_gain
    for i in (1, 3, 2):
        ym, to = ypeer(i)
        push(r.small, r.smally.at[i - 1], ss.sy.at[i - 1], rr.sy.at[i - 1], to)
    for i in (1, 3, 2):
        ym, to = ypeer(i)
        push(r.gnp.at[ym], r.ry.at[i - 1], ss.ry.at[i - 1], rr.ry.at[i - 1], to)
    weight_sum((r.wpq, r.wrq, r.pieceq), "wp")
    spread(r.pieceq, "pa", "pb")
    weight_sum((r.wpk, r.wrk, r.piecek), "wk")
    spread(r.piecek, "pc", "pd")
    grad = r.gnp[mp].astype(f32)
    for i in range(3):
        arrive(r.ry.at[i], rr.ry.at[i])
        grad = grad + r.ry[i].astype(f32)
    here = pl.ds(pl.multiple_of(64 * mp, 64), 64)
    unit, inverse = norm_parts(r.tokens[here, :].astype(f32))
    grad_in, _ = norm_back(grad, r.gain1[...], unit, inverse)
    r.igrad[here, :] = (r.gres[here, :] + grad_in).astype(bf16)
    for i in (1, 3, 2):
        ym, to = ypeer(i)
        push(r.igrad.at[here, :], r.igrad.at[here, :], ss.ay.at[i - 1], rr.ay.at[i - 1], to)
    for i in range(3):
        arrive(r.smally.at[i], rr.sy.at[i])
        one_gain = one_gain + r.smally[i]
    r.smalle[ex, 0:1] = one_gain
    r.smalle[ex, 1:2] = r.ggrad[...]
    to_all(lambda to: r.smalle.at[ex], r.smalle.at[ex], "se")
    from_all(r.bs.at[ex], lambda source: r.bret.at[source], "bb")
    rows = dot(slot_matrix(r.chosen[...]), r.bret[...].reshape(512, 256), 0, 0)
    r.out[...] = (r.rescol[...] + rows).astype(bf16)
    for i in range(1, 4):
        zp, _ = zpeer(4 - i)
        arrive(r.wgf.at[c, zp], rr.wb.at[i - 1])
    push(r.wgf.at[c], r.wgf.at[c], ss.wc.at[0], rr.wc.at[0], sib)
    arrive(r.wgf.at[1 - c], rr.wc.at[0])
    for k in range(16):
        for core in range(2):
            r.wout_out[16 * k:16 * k + 16, 512 * core:512 * core + 512] = r.wgf[core, k // 4, k % 4]
    pass_on(r.pieceq, "pa", "pb")
    pass_on(r.piecek, "pc", "pd")
    passed(r.pieceq, "pb")
    passed(r.piecek, "pd")
    for k in range(3):
        source, first = (r.pieceq, 0) if k == 0 else (r.piecek, 64 * k - 64)
        for row in range(8):
            block = jnp.concatenate([source[8 * h + row, first:first + 64] for h in range(4)], axis=0)
            r.qkv_out[k, 128 * row:128 * row + 128] = transposed(block)
    from_all(r.smalle.at[ex], lambda source: r.smalle.at[source], "se")
    both = jnp.sum(r.smalle[...], axis=0)
    r.gain1_out[...] = both[0:1]
    r.gain2_out[...] = both[1:2]
    for i in range(1, 4):
        ym, _ = ypeer(4 - i)
        there = pl.ds(pl.multiple_of(64 * ym, 64), 64)
        arrive(r.igrad.at[there, :], rr.ay.at[i - 1])
    for src, ssem in pending:
        left(src, ssem)
    for k in range(28):
        left(r.kvt.at[0, 0], ss.ag.at[k])
    for k in range(3):
        left(r.wfull.at[0, half, :], ss.wd.at[k])
    for p in range(4):
        left(r.sb.at[p], ss.sb.at[p])
    for p in range(3):
        left(r.xs.at[p], ss.xs.at[p])
        left(r.wgx.at[0], ss.wx.at[p])
        left(r.wgf.at[c, z, x], ss.wa.at[p])


def layer(*args):
    return pl.pallas_call(
        layer_kernel,
        out_shape=[pltpu.VMEM(s, t) for s, t in OUTS.values()],
        in_specs=[SM, VM, VM, VM, VM, ANY, ANY, ANY, ANY, ANY],
        out_specs=[VM] * len(OUTS),
        scratch_shapes=[pltpu.VMEM(s, t) for s, t in BUFFERS.values()]
        + [DMA(s) for group in (LOCAL, SENT, TAKEN) for s in group.values()],
        name="layer",
        compiler_params=pltpu.CompilerParams(
            collective_id=0, has_side_effects=True, vmem_limit_bytes=VMEM_BYTES),
    )(*args)


def finish_kernel(x, gpre, hid, cots, qkv, wout, out, igrad, gain1, gain2, *refs):
    in_grad, out_grad, qkv_o, wout_o, out_o, igrad_o, gain1_o, gain2_o = refs[:8]
    in_buf, out_buf, qkv_buf, wout_buf, store, rest = refs[8:]
    stores = []

    def put(src, dst, sem):
        copy = pltpu.make_async_copy(src, dst, sem)
        copy.start()
        stores.append(copy)

    for k, (left, right, buf, result) in enumerate(((x, gpre, in_buf, in_grad), (hid, cots, out_buf, out_grad))):
        for e in range(2):
            for t in range(4):
                rows = pl.ds(256 * t, 256)
                buf[e, rows, :] = dot(left[e, :, 256 * t:256 * t + 256], right[e], 0, 0)
                put(buf.at[e, rows, :], result.at[e, rows, :], store.at[8 * k + 4 * e + t])
    qkv_buf[...] = qkv[...].astype(f32)
    wout_buf[...] = wout[...].astype(f32)
    plain = ((qkv_buf, qkv_o), (wout_buf, wout_o), (out, out_o), (igrad, igrad_o), (gain1, gain1_o), (gain2, gain2_o))
    for k, (src, dst) in enumerate(plain):
        put(src, dst, rest.at[k])
    for copy in stores:
        copy.wait()


def finish(*args):
    big = ((2, 1024, 1024), f32)
    outs = [big, big, ((3, 1024, 256), f32), ((256, 1024), f32), ((256, 256), bf16), ((256, 1024), bf16)]
    outs += [((1, 1024), f32)] * 2
    return pl.pallas_call(
        finish_kernel,
        out_shape=[jax.ShapeDtypeStruct(s, t) for s, t in outs],
        in_specs=[VM] * 10,
        out_specs=[ANY] * 8,
        scratch_shapes=[pltpu.VMEM(s, t) for s, t in outs[:4]] + [DMA((16,)), DMA((6,))],
        name="finish",
        compiler_params=pltpu.CompilerParams(vmem_limit_bytes=36 << 20),
        cost_estimate=pl.CostEstimate(flops=2 * 2 * 2 * 256 * 1024 * 1024, bytes_accessed=28 << 20, transcendentals=0),
    )(*args)


def on_device(
    tokens, hash_ids, lengths, norm1_gain, qkv_weight, out_weight, norm2_gain, expert_in, expert_out, cotangent,
):
    x, cots, hid, gpre, out, igrad, gain1, gain2, qkv, wout = layer(
        lengths, tokens, norm1_gain.reshape(1, 1024), norm2_gain.reshape(1, 1024), hash_ids.reshape(1, 256),
        jnp.transpose(qkv_weight, (1, 0, 2)), out_weight, cotangent, expert_in, expert_out)
    in_grad, out_grad, qkv, wout, out, igrad, gain1, gain2 = finish(
        x, gpre, hid, cots, qkv, wout, out, igrad, gain1, gain2)
    return out, igrad, gain1.reshape(1024), jnp.transpose(qkv, (1, 0, 2)), wout, gain2.reshape(1024), in_grad, out_grad


def solution(mesh):
    placed = (
        P("ex", None), P("ex", None), P(), P(), P(None, None, "mp"), P("mp", None), P(),
        P("ex", None, "mp"), P("ex", "mp", None), P("ex", None),
    )
    return jax.shard_map(
        on_device,
        mesh=mesh,
        in_specs=placed,
        out_specs=(
            P("ex", "mp"), P("ex", None), P(), P(None, None, "mp"), P("mp", None), P(),
            P("ex", None, "mp"), P("ex", "mp", None),
        ),
        check_vma=False,
    )
```

```python
import functools

import jax
import jax.numpy as jnp
from jax import lax
from jax.experimental import pallas as pl
from jax.experimental.pallas import tpu as pltpu
from jax.sharding import PartitionSpec as P

HEAD_DIM = 64
epsilon = 1e-05
negative_fill = -1e30
MESH = pl.DeviceIdType.MESH
bf16, f32 = jnp.bfloat16, jnp.float32
EX, MP = 32, 4
VMEM_BYTES = 56 << 20


def dot(a, b, ca=1, cb=0):
    return lax.dot_general(a, b, (((ca,), (cb,)), ((), ())), preferred_element_type=f32)


def place():
    ex, mp = lax.axis_index("ex"), lax.axis_index("mp")
    z, x, c = ex // 8, (ex // 2) % 4, ex % 2
    return ex, mp, z, x, c


def send(src, dst, ssem, rsem, device):
    copy = pltpu.make_async_remote_copy(
        src_ref=src, dst_ref=dst, send_sem=ssem, recv_sem=rsem, device_id=device, device_id_type=MESH
    )
    copy.start()
    return copy


def greet(ex, mp):
    bar = pltpu.get_barrier_semaphore()

    def one(d, carry):
        pl.semaphore_signal(bar, inc=1, device_id=(lax.rem(ex + d, EX), mp), device_id_type=MESH)
        return carry

    lax.fori_loop(1, EX, one, 0)
    for d in range(1, MP):
        pl.semaphore_signal(bar, inc=1, device_id=(ex, lax.rem(mp + d, MP)), device_id_type=MESH)
    return bar


def greeted(bar):
    pl.semaphore_wait(bar, EX - 1 + MP - 1)


def slot_matrix(chosen_row):
    tok = chosen_row.shape[1]
    experts = lax.broadcasted_iota(jnp.int32, (64, tok), 0)
    hot = (experts == chosen_row).astype(f32)
    rows = lax.broadcasted_iota(jnp.int32, (tok, tok), 0)
    cols = lax.broadcasted_iota(jnp.int32, (tok, tok), 1)
    before = (rows < cols).astype(bf16)
    earlier = dot(hot.astype(bf16), before)
    rank = jnp.sum(earlier * hot, axis=0, keepdims=True)
    target = chosen_row * 8 + rank.astype(jnp.int32)
    slots = lax.broadcasted_iota(jnp.int32, (512, tok), 0)
    return (slots == target).astype(f32).astype(bf16)


def doc_row(ends, first, count):
    pos = first + lax.broadcasted_iota(jnp.int32, (1, count), 1)
    row = jnp.zeros((1, count), jnp.int32)
    for end in ends:
        row = row + (pos >= end).astype(jnp.int32)
    return row


def doc_ends(lengths_ref):
    ends, total = [], 0
    for i in range(9):
        total = total + lengths_ref[i]
        ends.append(total)
    return ends


def norm_parts(v):
    mean = jnp.mean(v, axis=-1, keepdims=True)
    centred = v - mean
    inverse = lax.rsqrt(jnp.mean(centred * centred, axis=-1, keepdims=True) + epsilon)
    return centred * inverse, inverse


def transposed(v):
    return v.T


def norm_back(grad_out, gain_row, unit, inverse):
    scaled = grad_out * gain_row
    centred = scaled - jnp.mean(scaled, axis=-1, keepdims=True)
    grad_in = inverse * (centred - unit * jnp.mean(scaled * unit, axis=-1, keepdims=True))
    return grad_in, jnp.sum(grad_out * unit, axis=0, keepdims=True)


def gelu_parts(pre):
    k = 0.7978845608028654
    square = pre * pre
    t = jnp.tanh(k * pre * (1.0 + 0.044715 * square))
    half = 0.5 * (1.0 + t)
    slope = half + 0.5 * pre * (1.0 - t * t) * (k * (1.0 + 3 * 0.044715 * square))
    return pre * half, slope


def one_expert(rows, le):
    wide = rows.astype(f32)
    return wide[:, 8 * le:8 * le + 8].reshape(256, rows.shape[2]).astype(bf16)


def both_experts(first, second):
    width = first.shape[1]
    return jnp.concatenate([first.reshape(32, 8, width), second.reshape(32, 8, width)], axis=1).astype(bf16)


VM = pl.BlockSpec(memory_space=pltpu.VMEM)
SM = pl.BlockSpec(memory_space=pltpu.SMEM)
ANY = pl.BlockSpec(memory_space=pl.ANY)
DMA = pltpu.SemaphoreType.DMA
ROWS = (2, 256, 1024)

ARGS = ["lengths", "tokens", "gain1", "gain2", "chosen", "wqkv_hbm", "wout_hbm", "cot_hbm", "win_hbm", "wex_hbm"]
OUTS = {
    "xrows": (ROWS, bf16), "crows": (ROWS, bf16), "hid": (ROWS, bf16), "gpre": (ROWS, bf16),
    "out": ((256, 256), bf16), "igrad": ((256, 1024), bf16), "gain1_out": ((1, 1024), f32), "gain2_out": ((1, 1024), f32),
    "qkv_out": ((3, 1024, 256), bf16), "wout_out": ((256, 1024), bf16),
}
BUFFERS = {
    "wqkv": ((3, 1024, 256), bf16), "cot": ((256, 1024), bf16),
    "weights": ((7, 1024, 1024), bf16), "placer": ((512, 256), bf16), "normed": ((256, 1024), bf16),
    "nall": ((4, 256, 1024), bf16), "wfull": ((4, 256, 1024), bf16),
    "q_s": ((4, 64, 256), bf16), "kv_s": ((4, 128, 256), bf16), "q": ((4, 64, 256), bf16),
    "kvt": ((8, 4, 128, 256), bf16), "qaug": ((4, 128, 256), bf16), "kaug": ((1024, 128), bf16),
    "vt1": ((80, 1024), bf16), "acc": ((4, 80, 256), f32), "peak": ((4, 1, 256), f32),
    "ot": ((4, 64, 256), f32), "lse": ((4, 1, 256), f32), "o_s": ((4, 64, 256), bf16),
    "att": ((4, 4, 64, 256), bf16), "cotq_s": ((32, 16, 256), bf16), "cotq": ((4, 32, 16, 256), bf16),
    "outgoing": ((32, 16, 1024), bf16), "arrived": ((32, 16, 1024), bf16),
    "gh": (ROWS, f32),
    "part": ((2, 4, 256, 128), bf16), "rs": ((2, 3, 256, 128), bf16), "back_s": ((32, 16, 128), bf16),
    "back": ((32, 16, 128), bf16), "wide_s": ((32, 16, 512), bf16), "wide": ((32, 16, 512), bf16),
    "gb": ((4, 256, 128), bf16), "gbr": ((3, 256, 128), bf16), "gn": ((2, 4, 256, 128), bf16), "resid": ((256, 1024), f32),
    "rescol": ((256, 256), f32), "gres": ((256, 1024), f32), "branch": ((32, 16, 1024), bf16),
    "wgp": ((2, 4, 4, 16, 512), bf16), "wgs": ((4, 4, 16, 512), bf16), "wgq": ((4, 4, 16, 512), bf16),
    "wgz": ((3, 4, 16, 512), bf16), "wgx": ((4, 16, 512), bf16), "wgr": ((3, 16, 512), bf16),
    "wgf": ((2, 4, 4, 16, 512), bf16),
    "dheads": ((4, 64, 256), bf16), "dob": ((4, 64, 256), bf16), "brs": ((3, 32, 16, 256), bf16),
    "bs": ((32, 16, 256), bf16), "bret": ((32, 16, 256), bf16), "dopad": ((4, 128, 256), bf16),
    "qd": ((4, 512, 128), bf16), "delta": ((4, 1, 256), f32), "kvn": ((1024, 128), bf16),
    "kt": ((64, 1024), bf16), "dkv": ((1024, 128), f32), "dq": ((4, 64, 256), f32),
    "sb": ((4, 1024, 128), bf16), "sr": ((4, 1024, 128), bf16), "xs": ((4, 1024, 128), bf16),
    "xr": ((3, 1024, 128), bf16), "zs": ((4, 192, 256), bf16), "zr": ((4, 192, 256), bf16),
    "wpq": ((8, 64, 128), bf16), "wrq": ((7, 64, 128), bf16),
    "wpk": ((8, 128, 128), bf16), "wrk": ((7, 128, 128), bf16),
    "pieces": ((3, 2, 4, 4, 64, 128), bf16),
    "gnp": ((4, 64, 1024), bf16), "ry": ((3, 64, 1024), bf16), "small": ((1, 1024), f32),
    "smally": ((3, 1, 1024), f32), "smalle": ((32, 1, 1024), f32), "smallf": ((32, 1, 1024), f32),
}
LOCAL = {"load": (5,)}
SENT = {
    "az": (6,), "ag": (28,), "wf": (3,), "wd": (3,), "co": (31,), "cy": (3,), "na": (6,), "oz": (3,), "oy": (12,),
    "di": (31,), "rs": (6,), "ba": (31,), "bc": (31,), "gb": (3,), "gy": (6,), "dz": (3,), "br": (3,), "bb": (31,), "sb": (4,), "xs": (3,),
    "wg": (1,), "wz": (3,), "wx": (3,), "wa": (3,), "wb": (3,), "wc": (1,), "zq": (6,), "wp": (7,), "wk": (7,), "pa": (9,), "pb": (9,), "pc": (3,),
    "ry": (3,), "ay": (3,), "sy": (3,), "se": (31,), "sf": (31,),
}
TAKEN = dict(SENT, ag=(32,))


class Refs:
    pass


def layer_kernel(*refs):
    r, ls, ss, rr = Refs(), Refs(), Refs(), Refs()
    names = [(r, k) for k in ARGS + list(OUTS) + list(BUFFERS)] + [(ls, k) for k in LOCAL]
    names += [(ss, k) for k in SENT] + [(rr, k) for k in TAKEN]
    for (group, name), ref in zip(names, refs, strict=True):
        setattr(group, name, ref)
    ex, mp, z, x, c = place()
    d = 1 - 2 * c
    j = x * 2 + c
    chip = ex // 2
    sib = (ex + d, mp)
    ahead = (z * 8 + lax.rem(x + d + 4, 4) * 2 + c, mp)
    behind = (z * 8 + lax.rem(x - d + 4, 4) * 2 + c, mp)
    pending = []

    def zpeer(i):
        zp = lax.rem(z + i, 4)
        return zp, (zp * 8 + j, mp)

    def ypeer(i):
        ym = lax.rem(mp + i, MP)
        return ym, (ex, ym)

    def xpeer(i):
        xq = lax.rem(x + i, 4)
        return xq, (z * 8 + xq * 2 + c, mp)

    def remote(src, dst, ssem, rsem, device):
        return pltpu.make_async_remote_copy(
            src_ref=src, dst_ref=dst, send_sem=ssem, recv_sem=rsem, device_id=device, device_id_type=MESH)

    def push(src, dst, ssem, rsem, device):
        remote(src, dst, ssem, rsem, device).start()
        pending.append((src, ssem))

    def arrive(dst, rsem):
        remote(dst, dst, rsem, rsem, sib).wait_recv()

    def left(src, ssem):
        remote(src, src, ssem, ssem, sib).wait_send()

    def to_all(src_of, dst, name):
        def one(k, carry):
            to = lax.rem(ex + k, EX)
            remote(src_of(to), dst, getattr(ss, name).at[k - 1], getattr(rr, name).at[k - 1], (to, mp)).start()
            return carry

        lax.fori_loop(1, EX, one, 0)

    def from_all(src, dst_of, name):
        def one(k, carry):
            left(src, getattr(ss, name).at[k - 1])
            arrive(dst_of(lax.rem(ex + EX - k, EX)), getattr(rr, name).at[k - 1])
            return carry

        lax.fori_loop(1, EX, one, 0)

    def gather_first(part):
        for i in (1, 3, 2):
            _, to = xpeer(i) if part == 1 else zpeer(i)
            own = r.pieces.at[part, c, z, x]
            push(own, own, ss.pa.at[3 * part + i - 1], rr.pa.at[3 * part + i - 1], to)

    def gather_second(part):
        for i in range(1, 4):
            if part == 1:
                xq, _ = xpeer(4 - i)
                arrive(r.pieces.at[part, c, z, xq], rr.pa.at[3 * part + i - 1])
            else:
                zp, _ = zpeer(4 - i)
                arrive(r.pieces.at[part, c, zp, x], rr.pa.at[3 * part + i - 1])
        row = r.pieces.at[part, c, z] if part == 1 else r.pieces.at[part, c, :, x]
        for i in (1, 3, 2):
            _, to = zpeer(i) if part == 1 else xpeer(i)
            push(row, row, ss.pb.at[3 * part + i - 1], rr.pb.at[3 * part + i - 1], to)

    def gather_third(part):
        for i in range(1, 4):
            if part == 1:
                zp, _ = zpeer(4 - i)
                arrive(r.pieces.at[part, c, zp], rr.pb.at[3 * part + i - 1])
            else:
                xq, _ = xpeer(4 - i)
                arrive(r.pieces.at[part, c, :, xq], rr.pb.at[3 * part + i - 1])
        push(r.pieces.at[part, c], r.pieces.at[part, c], ss.pc.at[part], rr.pc.at[part], sib)

    bar = greet(ex, mp)
    loads = [
        pltpu.make_async_copy(src, dst, ls.load.at[i])
        for i, (src, dst) in enumerate([
            (r.wqkv_hbm, r.wqkv), (r.wout_hbm, r.wfull.at[mp]), (r.cot_hbm, r.cot), (r.wex_hbm, r.weights.at[2:4]),
            (r.win_hbm, r.weights.at[0:2])])
    ]
    for copy in loads:
        copy.start()
    unit, _ = norm_parts(r.tokens[...].astype(f32))
    normed = (unit * r.gain1[...]).astype(bf16)
    r.normed[...] = normed
    loads[0].wait()
    kt = transposed(dot(normed, r.wqkv[1]).astype(bf16))
    vt = transposed(dot(normed, r.wqkv[2]).astype(bf16))
    qt = transposed((dot(normed, r.wqkv[0]).astype(bf16) * HEAD_DIM ** (-0.5)).astype(bf16))
    for h in range(4):
        r.q_s[h] = qt[64 * h:64 * h + 64]
        r.kv_s[h, 0:64] = kt[64 * h:64 * h + 64]
        r.kv_s[h, 64:128] = vt[64 * h:64 * h + 64]
    greeted(bar)
    for i in (1, 3, 2):
        zp, to = zpeer(i)
        push(r.kv_s.at[zp], r.kvt.at[0, z], ss.az.at[i - 1], rr.az.at[i - 1], to)
    r.kvt[0, z] = r.kv_s[z]

    def own_piece(k):
        zq = lax.rem(z + 4 - k, 4)
        remote(r.kvt.at[0, zq], r.kvt.at[2, zq], ss.ag.at[4 * 1 + k], rr.ag.at[4 * 2 + k], ahead).start()
        remote(r.kvt.at[0, zq], r.kvt.at[3, zq], ss.ag.at[4 * 2 + k], rr.ag.at[4 * 3 + k], behind).start()
        remote(r.kvt.at[0, zq], r.kvt.at[1, zq], ss.ag.at[k], rr.ag.at[4 * 1 + k], sib).start()

    def came(slot, k):
        arrive(r.kvt.at[slot, lax.rem(z + 4 - k, 4)], rr.ag.at[4 * slot + k])

    def from_sides(k):
        zq = lax.rem(z + 4 - k, 4)
        came(2, k)
        remote(r.kvt.at[2, zq], r.kvt.at[6, zq], ss.ag.at[4 * 3 + k], rr.ag.at[4 * 6 + k], ahead).start()
        remote(r.kvt.at[2, zq], r.kvt.at[5, zq], ss.ag.at[4 * 4 + k], rr.ag.at[4 * 5 + k], sib).start()
        came(3, k)
        remote(r.kvt.at[3, zq], r.kvt.at[4, zq], ss.ag.at[4 * 5 + k], rr.ag.at[4 * 4 + k], sib).start()

    def from_far(k):
        zq = lax.rem(z + 4 - k, 4)
        came(6, k)
        remote(r.kvt.at[6, zq], r.kvt.at[7, zq], ss.ag.at[4 * 6 + k], rr.ag.at[4 * 7 + k], sib).start()

    own_piece(0)
    for i in (1, 3, 2):
        zp, to = zpeer(i)
        push(r.q_s.at[zp], r.q.at[z], ss.az.at[i + 2], rr.az.at[i + 2], to)
    r.q[z] = r.q_s[z]
    loads[1].wait()
    half = pl.ds(pl.multiple_of(128 * c, 128), 128)
    for i in range(1, 4):
        ym, to = ypeer(i)
        push(r.wfull.at[mp, half, :], r.wfull.at[mp, half, :], ss.wf.at[i - 1], rr.wf.at[i - 1], to)
    r.vt1[64:80, :] = jnp.ones((16, 1024), bf16)
    ends = doc_ends(r.lengths)
    feature = lax.broadcasted_iota(jnp.int32, (64, 256), 0)
    loads[2].wait()
    mine = pl.ds(pl.multiple_of(256 * mp, 256), 256)
    r.placer[...] = slot_matrix(r.chosen[...])
    r.cotq_s[...] = dot(r.placer[...], r.cot[:, mine]).astype(bf16).reshape(EX, 16, 256)
    r.cotq[mp, ex] = r.cotq_s[ex]
    arrive(r.kvt.at[0, lax.rem(z + 3, 4)], rr.az.at[0])
    own_piece(1)
    arrive(r.kvt.at[0, lax.rem(z + 1, 4)], rr.az.at[2])
    own_piece(3)
    from_sides(0)
    arrive(r.kvt.at[0, lax.rem(z + 2, 4)], rr.az.at[1])
    own_piece(2)
    zp, to = zpeer(2)
    push(r.normed, r.nall.at[z], ss.na.at[1], rr.na.at[1], to)
    r.nall[z] = r.normed[...]
    for i in range(1, 4):
        arrive(r.q.at[lax.rem(z + 4 - i, 4)], rr.az.at[i + 2])
    for b in range(4):
        docs = doc_row(ends, (b * 8 + j) * 256, 256)
        r.qaug[b, 0:64] = r.q[b]
        r.qaug[b, 64:128] = jnp.where(feature == docs, 0.0, negative_fill).astype(bf16)
        r.peak[b] = jnp.full((1, 256), negative_fill, f32)
        r.acc[b] = jnp.zeros((80, 256), f32)

    def load_keys(slot, jp):
        for b in range(4):
            docs = doc_row(ends, (b * 8 + jp) * 256, 256)
            hot = (feature == docs).astype(f32).astype(bf16)
            r.kaug[256 * b:256 * b + 256, :] = transposed(
                jnp.concatenate([r.kvt[slot, b, 0:64], hot], axis=0))

    def scores(b, n, causal):
        s = dot(r.kaug[0:n, :], r.qaug[b])
        if causal:
            rows = lax.broadcasted_iota(jnp.int32, (n, 256), 0)
            cols = lax.broadcasted_iota(jnp.int32, (n, 256), 1)
            s = jnp.where(rows - 256 * b <= cols, s, negative_fill)
        return s

    def load_chunk(slot, jp):
        load_keys(slot, jp)
        for b in range(4):
            r.vt1[0:64, 256 * b:256 * b + 256] = r.kvt[slot, b, 64:128]

    def forward(tiles, causal):
        def gather(b, n, p, factor):
            r.acc[b] = r.acc[b] * factor + dot(r.vt1[:, 0:n], p)

        held = None
        for b, n in tiles:
            s = scores(b, n, causal)
            if held is not None:
                gather(*held)
            old = r.peak[b]
            new = jnp.maximum(old, jnp.max(s, axis=0, keepdims=True))
            held = (b, n, jnp.exp(s - new).astype(bf16), jnp.exp(old - new))
            r.peak[b] = new
        gather(*held)

    load_chunk(0, j)
    forward([(b, 256 * b + 256) for b in (3, 2, 1, 0)], True)

    def chunk(i, carry):
        u = i // 2
        side = ((u + 1) // 2) % 2
        xp = (x + d * (2 * (i % 2) - 1) * side + 2 * (u // 3) + 8) % 4
        jp = xp * 2 + (c + (1 - side) * (i % 2) + side * (u // 2)) % 2

        @pl.when(i == 1)
        def _():
            from_sides(1)
            from_far(0)
            for k in range(4):
                came(1, k)

        @pl.when(i == 2)
        def _():
            from_sides(3)
            from_far(1)
            from_sides(2)

        @pl.when(i == 3)
        def _():
            from_far(3)

        @pl.when(i == 4)
        def _():
            from_far(2)
            for k in range(4):
                came(4, k)
            to_all(lambda to: r.cotq_s.at[to], r.cotq.at[mp, ex], "co")

        @pl.when(i == 5)
        def _():
            for k in range(4):
                came(5, k)
            for i in range(1, 4):
                ym, to = ypeer(4 - i)
                arrive(r.wfull.at[ym, half, :], rr.wf.at[i - 1])
                remote(
                    r.wfull.at[ym, half, :], r.wfull.at[ym, half, :], ss.wd.at[i - 1], rr.wd.at[i - 1], sib).start()

        @pl.when(i == 7)
        def _():
            for k in range(4):
                came(7, k)

        load_chunk(i, jp)

        @pl.when(jp < j)
        def _():
            forward([(b, 256 * b + 256) for b in (3, 2, 1, 0)], False)

        @pl.when(jp > j)
        def _():
            forward([(b, 256 * b) for b in (3, 2, 1)], False)

        return carry

    lax.fori_loop(1, 8, chunk, 0)
    for b in range(4):
        total = r.acc[b, 64:65]
        ot = r.acc[b, 0:64] / total
        r.ot[b] = ot
        r.lse[b] = r.peak[b] + jnp.log(total)
        r.o_s[b] = ot.astype(bf16)
    for i in (1, 3, 2):
        zp, to = zpeer(i)
        push(r.o_s.at[zp], r.att.at[mp, z], ss.oz.at[i - 1], rr.oz.at[i - 1], to)
    r.att[mp, z] = r.o_s[z]
    def normed_half(part):
        rows = pl.ds(128 * part, 128)
        for i in (1, 3):
            zp, to = zpeer(i)
            push(
                r.normed.at[rows, :], r.nall.at[z, rows, :], ss.na.at[i - 1 + 3 * part],
                rr.na.at[i - 1 + 3 * part], to)

    def attended_piece(k):
        zq = lax.rem(z + 4 - k, 4)
        for i in (1, 3, 2):
            ym, to = ypeer(i)
            push(
                r.att.at[mp, zq], r.att.at[mp, zq], ss.oy.at[3 * k + i - 1], rr.oy.at[3 * k + i - 1], to)

    attended_piece(0)
    for k in (1, 3, 2):
        arrive(r.att.at[mp, lax.rem(z + 4 - k, 4)], rr.oz.at[k - 1])
        attended_piece(k)
    normed_half(0)
    from_all(r.cotq_s.at[ex], lambda source: r.cotq.at[mp, source], "co")
    other = pl.ds(pl.multiple_of(128 - 128 * c, 128), 128)
    for i in range(1, 4):
        ym, _ = ypeer(4 - i)
        arrive(r.wfull.at[ym, other, :], rr.wd.at[i - 1])
    for k in (0, 1, 3, 2):
        for i in range(1, 4):
            ym, _ = ypeer(4 - i)
            arrive(r.att.at[ym, lax.rem(z + 4 - k, 4)], rr.oy.at[3 * k + i - 1])
    for i in (1, 3, 2):
        ym, to = ypeer(i)
        push(r.cotq.at[mp], r.cotq.at[mp], ss.cy.at[i - 1], rr.cy.at[i - 1], to)
    def geometry(i):
        p = i // 2
        w = p + (p // 2) * (1 - 2 * (p % 2))
        g = (2 + d * w + 4) % 4
        flip = 1 - i % 2
        odd = g % 2
        slot = odd * (2 + g // 2 + 2 * flip) + (1 - odd) * (3 * g + flip)
        xp = (x - d * g + 8) % 4
        return slot, xp, xp * 2 + (c + flip) % 2

    def softmax(i, carry):
        slot, _, jp = geometry(i)
        load_keys(slot, jp)

        def keep(tiles):
            for b, n in tiles:
                r.weights[i, 0:n, 256 * b:256 * b + 256] = jnp.exp(scores(b, n, False) - r.lse[b]).astype(bf16)

        @pl.when(jp < j)
        def _():
            keep([(b, 256 * b + 256) for b in (3, 2, 1, 0)])

        @pl.when(jp > j)
        def _():
            keep([(b, 256 * b) for b in (3, 2, 1)])

        return carry

    value = r.tokens[...].astype(f32) + dot(r.att[...].reshape(1024, 256), r.wfull[...].reshape(1024, 1024), 0, 0)
    r.resid[...] = value
    for k in range(4):
        @pl.when(mp == k)
        def _():
            r.rescol[...] = value[:, 256 * k:256 * k + 256]
    unit, _ = norm_parts(value)
    normed = (unit * r.gain2[...]).astype(bf16)
    for step in (1, 3, 2, 0):
        plane = lax.rem(z + step, 4)
        r.outgoing[pl.ds(8 * plane, 8)] = dot(
            r.placer[pl.ds(pl.multiple_of(128 * plane, 128), 128), :], normed).astype(bf16).reshape(8, 16, 1024)

        def dispatch(k, carry):
            to = plane * 8 + lax.rem(j + k, 8)
            remote(
                r.outgoing.at[to], r.arrived.at[ex], ss.di.at[8 * step + k - 1], rr.di.at[8 * step + k - 1],
                (to, mp)).start()
            return carry

        lax.fori_loop(0 if step else 1, 8, dispatch, 0)
    r.arrived[ex] = r.outgoing[ex]
    lax.fori_loop(4, 7, softmax, 0)
    loads[3].wait()
    for i in range(1, 4):
        ym, _ = ypeer(4 - i)
        arrive(r.cotq.at[ym], rr.cy.at[i - 1])
    for le in range(2):
        rows = jnp.concatenate([one_expert(r.cotq[k], le) for k in range(4)], axis=1)
        r.crows[le] = rows
        r.gh[le] = dot(rows, r.weights[2 + le], 1, 1)
    loads[4].wait()

    def dispatched(k, carry):
        left(r.outgoing.at[ex], ss.di.at[k - 1])
        source = lax.rem(z + 4 - k // 8, 4) * 8 + lax.rem(j + 8 - k % 8, 8)
        arrive(r.arrived.at[source], rr.di.at[k - 1])
        return carry

    lax.fori_loop(1, EX, dispatched, 0)
    def expert_rows(le):
        rows = one_expert(r.arrived[...], le)
        r.xrows[le] = rows
        return dot(rows, r.weights[le])

    def activate(le, pre):
        hidden, slope = gelu_parts(pre)
        r.hid[le] = hidden.astype(bf16)
        gpre = (r.gh[le] * slope).astype(bf16)
        r.gpre[le] = gpre
        return gpre

    def give_back(le, gpre):
        for k in range(4):
            product = dot(gpre, r.weights[le, 256 * k:256 * k + 256, :], 1, 1)
            r.part[le, k] = product[:, 0:128].astype(bf16)
            r.gh[le, :, 128 * k:128 * k + 128] = product[:, 128:256]
        for i in (1, 3, 2):
            ym, to = ypeer(i)
            push(r.part.at[le, ym], r.rs.at[le, i - 1], ss.rs.at[3 * le + i - 1], rr.rs.at[3 * le + i - 1], to)

    first, second = expert_rows(0), expert_rows(1)
    gpre = activate(0, first)
    give_back(0, gpre)
    give_back(1, activate(1, second))
    r.wide_s[...] = both_experts(r.gh[0, :, 0:512], r.gh[1, :, 0:512])
    to_all(lambda to: r.wide_s.at[to], r.wide.at[ex], "bc")
    r.wide[ex] = r.wide_s[ex]
    first = dot(r.hid[0], r.weights[2])
    r.branch[...] = both_experts(first, dot(r.hid[1], r.weights[3]))
    lax.fori_loop(0, 4, softmax, 0)
    sums = []
    for le in range(2):
        total = r.part[le, mp].astype(f32)
        for i in range(3):
            arrive(r.rs.at[le, i], rr.rs.at[3 * le + i])
            total = total + r.rs[le, i].astype(f32)
        sums.append(total)
    r.back_s[...] = both_experts(sums[0], sums[1])
    to_all(lambda to: r.back_s.at[to], r.back.at[ex], "ba")
    r.back[ex] = r.back_s[ex]
    from_all(r.wide_s.at[ex], lambda source: r.wide.at[source], "bc")
    rows = dot(r.placer[...], r.wide[...].reshape(512, 512), 0, 0).astype(bf16)
    for k in range(4):
        r.gb[k] = rows[:, 128 * k:128 * k + 128]
    for i in (1, 3, 2):
        ym, to = ypeer(i)
        push(r.gb.at[ym], r.gbr.at[i - 1], ss.gb.at[i - 1], rr.gb.at[i - 1], to)
    from_all(r.back_s.at[ex], lambda source: r.back.at[source], "ba")
    r.gn[0, mp] = dot(r.placer[...], r.back[...].reshape(512, 128), 0, 0).astype(bf16)
    for i in (1, 3, 2):
        ym, to = ypeer(i)
        push(r.gn.at[0, mp], r.gn.at[0, mp], ss.gy.at[i - 1], rr.gy.at[i - 1], to)
    normed_half(1)
    total = r.gb[mp].astype(f32)
    for i in range(3):
        arrive(r.gbr.at[i], rr.gb.at[i])
        total = total + r.gbr[i].astype(f32)
    r.gn[1, mp] = total.astype(bf16)
    for i in (1, 3, 2):
        ym, to = ypeer(i)
        push(r.gn.at[1, mp], r.gn.at[1, mp], ss.gy.at[i + 2], rr.gy.at[i + 2], to)
    unit, inverse = norm_parts(r.resid[...])
    for i in range(1, 4):
        ym, _ = ypeer(4 - i)
        arrive(r.gn.at[0, ym], rr.gy.at[i - 1])
        arrive(r.gn.at[1, ym], rr.gy.at[i + 2])
    grad = jnp.concatenate([r.gn[k % 2, k // 2] for k in range(8)], axis=1).astype(f32)
    grad_in, ggrad = norm_back(grad, r.gain2[...], unit, inverse)
    r.smallf[ex] = ggrad
    gres = r.cot[...].astype(f32) + grad_in
    r.gres[...] = gres
    low = gres.astype(bf16)
    r.dheads[...] = dot(r.wfull[mp], low, 1, 1).astype(bf16).reshape(4, 64, 256)
    for i in (1, 3, 2):
        zp, to = zpeer(i)
        push(r.dheads.at[zp], r.dob.at[z], ss.dz.at[i - 1], rr.dz.at[i - 1], to)
    r.dob[z] = r.dheads[z]
    wgrad = dot(r.att[mp].reshape(256, 256), low).astype(bf16)
    r.wgp[0] = wgrad[:, 0:512].reshape(4, 4, 16, 512)
    r.wgp[1] = wgrad[:, 512:1024].reshape(4, 4, 16, 512)
    push(r.wgp.at[1 - c], r.wgs, ss.wg.at[0], rr.wg.at[0], sib)
    for i in range(1, 4):
        ym, to = ypeer(i)
        push(
            r.branch.at[:, :, pl.ds(pl.multiple_of(256 * ym, 256), 256)], r.brs.at[i - 1],
            ss.br.at[i - 1], rr.br.at[i - 1], to)
    zero = jnp.zeros((64, 256), bf16)
    to_all(lambda to: r.smallf.at[ex], r.smallf.at[ex], "sf")
    for i in range(1, 4):
        zp, _ = zpeer(4 - i)
        arrive(r.dob.at[zp], rr.dz.at[i - 1])
    arrive(r.wgs, rr.wg.at[0])
    r.wgq[...] = (r.wgp[c].astype(f32) + r.wgs[...].astype(f32)).astype(bf16)
    for i in (1, 3, 2):
        zp, to = zpeer(i)
        push(r.wgq.at[zp], r.wgz.at[i - 1], ss.wz.at[i - 1], rr.wz.at[i - 1], to)
    for b in range(4):
        r.dopad[b, 0:64] = zero
        r.dopad[b, 64:128] = r.dob[b]
        r.qd[b, 0:256] = transposed(jnp.concatenate([r.q[b], zero], axis=0))
        r.qd[b, 256:512] = transposed(jnp.concatenate([zero, r.dob[b]], axis=0))
        r.delta[b] = jnp.sum(r.dob[b].astype(f32) * r.ot[b], axis=0, keepdims=True)
        r.dq[b] = jnp.zeros((64, 256), f32)

    def load_back(slot):
        for b in range(4):
            r.kvn[256 * b:256 * b + 256, :] = transposed(r.kvt[slot, b])
            r.kt[:, 256 * b:256 * b + 256] = r.kvt[slot, b, 0:64]

    def backward(tiles, weights):
        def gather(b, n, ds, p):
            added = dot(ds, r.qd[b, 0:256]) + dot(p, r.qd[b, 256:512])
            if b == 3:
                r.dkv[0:n] = added
            else:
                r.dkv[0:n] = r.dkv[0:n] + added
            r.dq[b] = r.dq[b] + dot(r.kt[:, 0:n], ds)

        held = None
        for b, n in tiles:
            dp = dot(r.kvn[0:n, :], r.dopad[b])
            p = weights(b, n)
            if held is not None:
                gather(*held)
            held = (b, n, (p * (dp - r.delta[b])).astype(bf16), p.astype(bf16))
        gather(*held)

    def back_chunk(i, carry):
        slot, xp, jp = geometry(i)
        p = i // 2
        load_back(slot)

        def kept(b, n):
            return r.weights[i, 0:n, 256 * b:256 * b + 256]

        @pl.when(jp < j)
        def _():
            backward([(b, 256 * b + 256) for b in (3, 2, 1, 0)], kept)

        @pl.when(jp > j)
        def _():
            r.dkv[768:1024] = jnp.zeros((256, 128), f32)
            backward([(b, 256 * b) for b in (3, 2, 1)], kept)

        @pl.when(i % 2 == 0)
        def _():
            r.sb[p] = r.dkv[...].astype(bf16)
            remote(r.sb.at[p], r.sr.at[p], ss.sb.at[p], rr.sb.at[p], sib).start()

        @pl.when(i % 2 == 1)
        def _():
            arrive(r.sr.at[p], rr.sb.at[p])
            r.xs[p] = (r.dkv[...] + r.sr[p].astype(f32)).astype(bf16)

            @pl.when(p == 0)
            def _():
                remote(r.xs.at[0], r.xr.at[0], ss.xs.at[0], rr.xs.at[0], ahead).start()

            @pl.when(p == 2 - c)
            def _():
                remote(r.xs.at[p], r.xr.at[1], ss.xs.at[1], rr.xs.at[1], behind).start()

            @pl.when(p == 2)
            def _():
                arrive(r.xr.at[0], rr.xs.at[0])
                r.xs[3] = (r.xs[1 + c].astype(f32) + r.xr[0].astype(f32)).astype(bf16)
                remote(r.xs.at[3], r.xr.at[2], ss.xs.at[2], rr.xs.at[2], ahead).start()

        @pl.when(i == 2)
        def _():
            for k in range(3):
                arrive(r.wgz.at[k], rr.wz.at[k])
            total = r.wgq[z].astype(f32)
            for k in range(3):
                total = total + r.wgz[k].astype(f32)
            r.wgx[...] = total.astype(bf16)
            for k in (1, 3, 2):
                xq, to = xpeer(k)
                remote(r.wgx.at[xq], r.wgr.at[k - 1], ss.wx.at[k - 1], rr.wx.at[k - 1], to).start()

        @pl.when(i == 6)
        def _():
            total = r.branch[:, :, mine].astype(f32)
            for k in range(3):
                arrive(r.brs.at[k], rr.br.at[k])
                total = total + r.brs[k].astype(f32)
            r.bs[...] = total.astype(bf16)

        @pl.when(i == 5)
        def _():
            total = r.wgx[x].astype(f32)
            for k in range(3):
                arrive(r.wgr.at[k], rr.wx.at[k])
                total = total + r.wgr[k].astype(f32)
            r.wgf[c, z, x] = total.astype(bf16)
            for k in (1, 3, 2):
                _, to = xpeer(k)
                remote(r.wgf.at[c, z, x], r.wgf.at[c, z, x], ss.wa.at[k - 1], rr.wa.at[k - 1], to).start()

        return carry

    lax.fori_loop(0, 7, back_chunk, 0)
    load_back(0)
    load_keys(0, j)
    backward(
        [(b, 256 * b + 256) for b in (3, 2, 1, 0)], lambda b, n: jnp.exp(scores(b, n, True) - r.lse[b]))
    for b in range(4):
        r.zs[b, 0:64] = (r.dq[b] * HEAD_DIM ** (-0.5)).astype(bf16)
    for i in (1, 3, 2):
        zp, to = zpeer(i)
        push(r.zs.at[zp, 0:64], r.zr.at[z, 0:64], ss.zq.at[i + 2], rr.zq.at[i + 2], to)
    arrive(r.nall.at[lax.rem(z + 2, 4)], rr.na.at[1])
    for i in (1, 3):
        zp, _ = zpeer(4 - i)
        arrive(r.nall.at[zp, 0:128], rr.na.at[i - 1])
        arrive(r.nall.at[zp, 128:256], rr.na.at[i + 2])

    def weight_part(first, last, pieces, name):
        wt = dot(r.zs[0, first:last], r.nall[0])
        for b in range(1, 4):
            wt = wt + dot(r.zs[b, first:last], r.nall[b])
        wt = wt.astype(bf16)
        for k in range(8):
            pieces[0][k] = wt[:, 128 * k:128 * k + 128]
        for i in range(1, 8):
            jt = lax.rem(j + i, 8)
            push(
                pieces[0].at[jt], pieces[1].at[i - 1], getattr(ss, name).at[i - 1], getattr(rr, name).at[i - 1],
                (z * 8 + jt, mp))

    def weight_sum(pieces, name):
        total = pieces[0][j].astype(f32)
        for i in range(7):
            arrive(pieces[1].at[i], getattr(rr, name).at[i])
            total = total + pieces[1][i].astype(f32)
        return total.astype(bf16)

    weight_part(0, 64, (r.wpq, r.wrq), "wp")
    r.resid[...] = norm_parts(r.tokens[...].astype(f32))[0]
    arrive(r.sr.at[3], rr.sb.at[3])
    total = r.dkv[...] + r.sr[3].astype(f32)
    for k in (1, 2):
        arrive(r.xr.at[k], rr.xs.at[k])
        total = total + r.xr[k].astype(f32)
    low = total.astype(bf16)
    for b in range(4):
        r.zs[b, 64:192] = transposed(low[256 * b:256 * b + 256])
    for i in (1, 3, 2):
        zp, to = zpeer(i)
        push(r.zs.at[zp, 64:192], r.zr.at[z, 64:192], ss.zq.at[i - 1], rr.zq.at[i - 1], to)
    r.zr[z] = r.zs[z]
    weight_part(64, 192, (r.wpk, r.wrk), "wk")
    r.pieces[0, c, z, x] = weight_sum((r.wpq, r.wrq), "wp")
    gather_first(0)
    for k in range(1, 4):
        xq, _ = xpeer(4 - k)
        arrive(r.wgf.at[c, z, xq], rr.wa.at[k - 1])
    for k in (1, 3, 2):
        _, to = zpeer(k)
        push(r.wgf.at[c, z], r.wgf.at[c, z], ss.wb.at[k - 1], rr.wb.at[k - 1], to)

    def heads(first):
        return transposed(jnp.concatenate([r.zr[h, first:first + 64] for h in range(4)], axis=0))

    for i in range(1, 4):
        zp, _ = zpeer(4 - i)
        arrive(r.zr.at[zp, 0:64], rr.zq.at[i + 2])
    part = dot(heads(0), r.wqkv[0], 1, 1)
    for i in range(1, 4):
        zp, _ = zpeer(4 - i)
        arrive(r.zr.at[zp, 64:192], rr.zq.at[i - 1])
    part = part + dot(heads(64), r.wqkv[1], 1, 1) + dot(heads(128), r.wqkv[2], 1, 1)
    r.gnp[...] = part.astype(bf16).reshape(4, 64, 1024)
    one_gain = jnp.sum(part * r.resid[...], axis=0, keepdims=True)
    r.small[...] = one_gain
    for i in (1, 3, 2):
        ym, to = ypeer(i)
        push(r.small, r.smally.at[i - 1], ss.sy.at[i - 1], rr.sy.at[i - 1], to)
    for i in (1, 3, 2):
        ym, to = ypeer(i)
        push(r.gnp.at[ym], r.ry.at[i - 1], ss.ry.at[i - 1], rr.ry.at[i - 1], to)
    gather_second(0)
    both = weight_sum((r.wpk, r.wrk), "wk")
    r.pieces[1, c, z, x] = both[0:64]
    r.pieces[2, c, z, x] = both[64:128]
    gather_first(1)
    gather_first(2)
    for i in range(3):
        arrive(r.smally.at[i], rr.sy.at[i])
        one_gain = one_gain + r.smally[i]
    r.smalle[ex] = one_gain
    to_all(lambda to: r.smalle.at[ex], r.smalle.at[ex], "se")
    gather_second(1)
    gather_second(2)
    to_all(lambda to: r.bs.at[to], r.bret.at[ex], "bb")
    r.bret[ex] = r.bs[ex]
    gather_third(0)
    grad = r.gnp[mp].astype(f32)
    for i in range(3):
        arrive(r.ry.at[i], rr.ry.at[i])
        grad = grad + r.ry[i].astype(f32)
    here = pl.ds(pl.multiple_of(64 * mp, 64), 64)
    unit, inverse = norm_parts(r.tokens[here, :].astype(f32))
    grad_in, _ = norm_back(grad, r.gain1[...], unit, inverse)
    r.igrad[here, :] = (r.gres[here, :] + grad_in).astype(bf16)
    for i in (1, 3, 2):
        ym, to = ypeer(i)
        push(r.igrad.at[here, :], r.igrad.at[here, :], ss.ay.at[i - 1], rr.ay.at[i - 1], to)
    gather_third(1)
    gather_third(2)
    for i in range(1, 4):
        zp, _ = zpeer(4 - i)
        arrive(r.wgf.at[c, zp], rr.wb.at[i - 1])
    push(r.wgf.at[c], r.wgf.at[c], ss.wc.at[0], rr.wc.at[0], sib)
    arrive(r.wgf.at[1 - c], rr.wc.at[0])
    for k in range(16):
        for core in range(2):
            r.wout_out[16 * k:16 * k + 16, 512 * core:512 * core + 512] = r.wgf[core, k // 4, k % 4]
    for k in range(3):
        arrive(r.pieces.at[k, 1 - c], rr.pc.at[k])
        for row in range(8):
            block = jnp.concatenate([r.pieces[k, row % 2, h, row // 2] for h in range(4)], axis=0)
            r.qkv_out[k, 128 * row:128 * row + 128] = transposed(block)
    from_all(r.smalle.at[ex], lambda source: r.smalle.at[source], "se")
    from_all(r.smallf.at[ex], lambda source: r.smallf.at[source], "sf")
    r.gain1_out[...] = jnp.sum(r.smalle[...], axis=0)
    r.gain2_out[...] = jnp.sum(r.smallf[...], axis=0)
    from_all(r.bs.at[ex], lambda source: r.bret.at[source], "bb")
    rows = dot(r.placer[...], r.bret[...].reshape(512, 256), 0, 0)
    r.out[...] = (r.rescol[...] + rows).astype(bf16)
    for i in range(1, 4):
        ym, _ = ypeer(4 - i)
        there = pl.ds(pl.multiple_of(64 * ym, 64), 64)
        arrive(r.igrad.at[there, :], rr.ay.at[i - 1])
    for src, ssem in pending:
        left(src, ssem)
    for k in range(28):
        left(r.kvt.at[0, 0], ss.ag.at[k])
    for k in range(3):
        left(r.wfull.at[0, half, :], ss.wd.at[k])
    for p in range(4):
        left(r.sb.at[p], ss.sb.at[p])
    for p in range(3):
        left(r.xs.at[p], ss.xs.at[p])
        left(r.wgx.at[0], ss.wx.at[p])
        left(r.wgf.at[c, z, x], ss.wa.at[p])


def layer(*args):
    return pl.pallas_call(
        layer_kernel,
        out_shape=[pltpu.VMEM(s, t) for s, t in OUTS.values()],
        in_specs=[SM, VM, VM, VM, VM, ANY, ANY, ANY, ANY, ANY],
        out_specs=[VM] * len(OUTS),
        scratch_shapes=[pltpu.VMEM(s, t) for s, t in BUFFERS.values()]
        + [DMA(s) for group in (LOCAL, SENT, TAKEN) for s in group.values()],
        name="layer",
        compiler_params=pltpu.CompilerParams(
            collective_id=0, has_side_effects=True, vmem_limit_bytes=VMEM_BYTES),
    )(*args)


def finish_kernel(x, gpre, hid, cots, qkv, wout, out, igrad, gain1, gain2, *refs):
    in_grad, out_grad, qkv_o, wout_o, out_o, igrad_o, gain1_o, gain2_o = refs[:8]
    in_buf, out_buf, qkv_buf, wout_buf, store, rest = refs[8:]
    stores = []

    def put(src, dst, sem):
        copy = pltpu.make_async_copy(src, dst, sem)
        copy.start()
        stores.append(copy)

    for k, (left, right, buf, result) in enumerate(((x, gpre, in_buf, in_grad), (hid, cots, out_buf, out_grad))):
        for e in range(2):
            for t in range(4):
                rows = pl.ds(256 * t, 256)
                buf[e, rows, :] = dot(left[e, :, 256 * t:256 * t + 256], right[e], 0, 0)
                put(buf.at[e, rows, :], result.at[e, rows, :], store.at[8 * k + 4 * e + t])
    qkv_buf[...] = qkv[...].astype(f32)
    wout_buf[...] = wout[...].astype(f32)
    plain = ((qkv_buf, qkv_o), (wout_buf, wout_o), (out, out_o), (igrad, igrad_o), (gain1, gain1_o), (gain2, gain2_o))
    for k, (src, dst) in enumerate(plain):
        put(src, dst, rest.at[k])
    for copy in stores:
        copy.wait()


def finish(*args):
    big = ((2, 1024, 1024), f32)
    outs = [big, big, ((3, 1024, 256), f32), ((256, 1024), f32), ((256, 256), bf16), ((256, 1024), bf16)]
    outs += [((1, 1024), f32)] * 2
    return pl.pallas_call(
        finish_kernel,
        out_shape=[jax.ShapeDtypeStruct(s, t) for s, t in outs],
        in_specs=[VM] * 10,
        out_specs=[ANY] * 8,
        scratch_shapes=[pltpu.VMEM(s, t) for s, t in outs[:4]] + [DMA((16,)), DMA((6,))],
        name="finish",
        compiler_params=pltpu.CompilerParams(vmem_limit_bytes=36 << 20),
        cost_estimate=pl.CostEstimate(flops=2 * 2 * 2 * 256 * 1024 * 1024, bytes_accessed=28 << 20, transcendentals=0),
    )(*args)


def on_device(
    tokens, hash_ids, lengths, norm1_gain, qkv_weight, out_weight, norm2_gain, expert_in, expert_out, cotangent,
):
    x, cots, hid, gpre, out, igrad, gain1, gain2, qkv, wout = layer(
        lengths, tokens, norm1_gain.reshape(1, 1024), norm2_gain.reshape(1, 1024), hash_ids.reshape(1, 256),
        jnp.transpose(qkv_weight, (1, 0, 2)), out_weight, cotangent, expert_in, expert_out)
    in_grad, out_grad, qkv, wout, out, igrad, gain1, gain2 = finish(
        x, gpre, hid, cots, qkv, wout, out, igrad, gain1, gain2)
    return out, igrad, gain1.reshape(1024), jnp.transpose(qkv, (1, 0, 2)), wout, gain2.reshape(1024), in_grad, out_grad


def solution(mesh):
    placed = (
        P("ex", None), P("ex", None), P(), P(), P(None, None, "mp"), P("mp", None), P(),
        P("ex", None, "mp"), P("ex", "mp", None), P("ex", None),
    )
    return jax.shard_map(
        on_device,
        mesh=mesh,
        in_specs=placed,
        out_specs=(
            P("ex", "mp"), P("ex", None), P(), P(None, None, "mp"), P("mp", None), P(),
            P("ex", None, "mp"), P("ex", "mp", None),
        ),
        check_vma=False,
    )
```

```python
import functools

import jax
import jax.numpy as jnp
from jax import lax
from jax.experimental import pallas as pl
from jax.experimental.pallas import tpu as pltpu
from jax.sharding import PartitionSpec as P

HEAD_DIM = 64
epsilon = 1e-05
negative_fill = -1e30
MESH = pl.DeviceIdType.MESH
bf16, f32 = jnp.bfloat16, jnp.float32
EX, MP = 32, 4
VMEM_BYTES = 56 << 20


def dot(a, b, ca=1, cb=0):
    return lax.dot_general(a, b, (((ca,), (cb,)), ((), ())), preferred_element_type=f32)


def place():
    ex, mp = lax.axis_index("ex"), lax.axis_index("mp")
    z, x, c = ex // 8, (ex // 2) % 4, ex % 2
    return ex, mp, z, x, c


def send(src, dst, ssem, rsem, device):
    copy = pltpu.make_async_remote_copy(
        src_ref=src, dst_ref=dst, send_sem=ssem, recv_sem=rsem, device_id=device, device_id_type=MESH
    )
    copy.start()
    return copy


def greet(ex, mp):
    bar = pltpu.get_barrier_semaphore()

    def one(d, carry):
        pl.semaphore_signal(bar, inc=1, device_id=(lax.rem(ex + d, EX), mp), device_id_type=MESH)
        return carry

    lax.fori_loop(1, EX, one, 0)
    for d in range(1, MP):
        pl.semaphore_signal(bar, inc=1, device_id=(ex, lax.rem(mp + d, MP)), device_id_type=MESH)
    return bar


def greeted(bar):
    pl.semaphore_wait(bar, EX - 1 + MP - 1)


def slot_matrix(chosen_row):
    tok = chosen_row.shape[1]
    experts = lax.broadcasted_iota(jnp.int32, (64, tok), 0)
    hot = (experts == chosen_row).astype(f32)
    rows = lax.broadcasted_iota(jnp.int32, (tok, tok), 0)
    cols = lax.broadcasted_iota(jnp.int32, (tok, tok), 1)
    before = (rows < cols).astype(bf16)
    earlier = dot(hot.astype(bf16), before)
    rank = jnp.sum(earlier * hot, axis=0, keepdims=True)
    target = chosen_row * 8 + rank.astype(jnp.int32)
    slots = lax.broadcasted_iota(jnp.int32, (512, tok), 0)
    return (slots == target).astype(f32).astype(bf16)


def doc_row(ends, first, count):
    pos = first + lax.broadcasted_iota(jnp.int32, (1, count), 1)
    row = jnp.zeros((1, count), jnp.int32)
    for end in ends:
        row = row + (pos >= end).astype(jnp.int32)
    return row


def doc_ends(lengths_ref):
    ends, total = [], 0
    for i in range(9):
        total = total + lengths_ref[i]
        ends.append(total)
    return ends


def norm_parts(v):
    mean = jnp.mean(v, axis=-1, keepdims=True)
    centred = v - mean
    inverse = lax.rsqrt(jnp.mean(centred * centred, axis=-1, keepdims=True) + epsilon)
    return centred * inverse, inverse


def transposed(v):
    return v.T


def norm_back(grad_out, gain_row, unit, inverse):
    scaled = grad_out * gain_row
    centred = scaled - jnp.mean(scaled, axis=-1, keepdims=True)
    grad_in = inverse * (centred - unit * jnp.mean(scaled * unit, axis=-1, keepdims=True))
    return grad_in, jnp.sum(grad_out * unit, axis=0, keepdims=True)


def gelu_parts(pre):
    k = 0.7978845608028654
    square = pre * pre
    t = jnp.tanh(k * pre * (1.0 + 0.044715 * square))
    half = 0.5 * (1.0 + t)
    slope = half + 0.5 * pre * (1.0 - t * t) * (k * (1.0 + 3 * 0.044715 * square))
    return pre * half, slope


def one_expert(rows, le):
    wide = rows.astype(f32)
    return wide[:, 8 * le:8 * le + 8].reshape(256, rows.shape[2]).astype(bf16)


def both_experts(first, second):
    width = first.shape[1]
    return jnp.concatenate([first.reshape(32, 8, width), second.reshape(32, 8, width)], axis=1).astype(bf16)


VM = pl.BlockSpec(memory_space=pltpu.VMEM)
SM = pl.BlockSpec(memory_space=pltpu.SMEM)
ANY = pl.BlockSpec(memory_space=pl.ANY)
DMA = pltpu.SemaphoreType.DMA
ROWS = (2, 256, 1024)

ARGS = ["lengths", "tokens", "gain1", "gain2", "chosen", "wqkv_hbm", "wout_hbm", "cot_hbm", "win_hbm", "wex_hbm"]
OUTS = {
    "xrows": (ROWS, bf16), "crows": (ROWS, bf16), "hid": (ROWS, bf16), "gpre": (ROWS, bf16),
    "out": ((256, 256), bf16), "igrad": ((256, 1024), bf16), "gain1_out": ((1, 1024), f32), "gain2_out": ((1, 1024), f32),
    "qkv_out": ((3, 1024, 256), bf16), "wout_out": ((256, 1024), bf16),
}
BUFFERS = {
    "wqkv": ((3, 1024, 256), bf16), "cot": ((256, 1024), bf16),
    "weights": ((7, 1024, 1024), bf16), "placer": ((512, 256), bf16), "normed": ((256, 1024), bf16),
    "nall": ((4, 256, 1024), bf16), "wfull": ((4, 256, 1024), bf16),
    "q_s": ((4, 64, 256), bf16), "kv_s": ((4, 128, 256), bf16), "q": ((4, 64, 256), bf16),
    "kvt": ((8, 4, 128, 256), bf16), "qaug": ((4, 128, 256), bf16), "kaug": ((1024, 128), bf16),
    "vt1": ((80, 1024), bf16), "acc": ((4, 80, 256), f32), "peak": ((4, 1, 256), f32),
    "ot": ((4, 64, 256), f32), "lse": ((4, 1, 256), f32), "o_s": ((4, 64, 256), bf16),
    "att": ((4, 4, 64, 256), bf16), "cotq_s": ((32, 16, 256), bf16), "cotq": ((4, 32, 16, 256), bf16),
    "outgoing": ((32, 16, 1024), bf16), "arrived": ((32, 16, 1024), bf16),
    "gh": (ROWS, f32),
    "part": ((2, 4, 256, 128), bf16), "rs": ((2, 3, 256, 128), bf16), "back_s": ((32, 16, 128), bf16),
    "back": ((32, 16, 128), bf16), "wide_s": ((32, 16, 512), bf16), "wide": ((32, 16, 512), bf16),
    "gb": ((4, 256, 128), bf16), "gbr": ((3, 256, 128), bf16), "gn": ((2, 4, 256, 128), bf16), "resid": ((256, 1024), f32),
    "rescol": ((256, 256), f32), "gres": ((256, 1024), f32), "branch": ((32, 16, 1024), bf16),
    "wgp": ((2, 4, 4, 16, 512), bf16), "wgs": ((4, 4, 16, 512), bf16), "wgq": ((4, 4, 16, 512), bf16),
    "wgz": ((3, 4, 16, 512), bf16), "wgx": ((4, 16, 512), bf16), "wgr": ((3, 16, 512), bf16),
    "wgf": ((2, 4, 4, 16, 512), bf16),
    "dheads": ((4, 64, 256), bf16), "dob": ((4, 64, 256), bf16), "brs": ((3, 32, 16, 256), bf16),
    "bs": ((32, 16, 256), bf16), "bret": ((32, 16, 256), bf16), "dopad": ((4, 128, 256), bf16),
    "qd": ((4, 512, 128), bf16), "delta": ((4, 1, 256), f32), "kvn": ((1024, 128), bf16),
    "kt": ((64, 1024), bf16), "dkv": ((1024, 128), f32), "dq": ((4, 64, 256), f32),
    "sb": ((4, 1024, 128), bf16), "sr": ((4, 1024, 128), bf16), "xs": ((4, 1024, 128), bf16),
    "xr": ((3, 1024, 128), bf16), "zs": ((4, 192, 256), bf16), "zr": ((4, 192, 256), bf16),
    "wpq": ((8, 64, 128), bf16), "wrq": ((7, 64, 128), bf16),
    "wpk": ((8, 128, 128), bf16), "wrk": ((7, 128, 128), bf16),
    "pieces": ((3, 2, 4, 4, 64, 128), bf16),
    "gnp": ((4, 64, 1024), bf16), "ry": ((3, 64, 1024), bf16), "small": ((1, 1024), f32),
    "smally": ((3, 1, 1024), f32), "smalle": ((32, 1, 1024), f32), "smallf": ((32, 1, 1024), f32),
}
LOCAL = {"load": (5,)}
SENT = dict.fromkeys(
    ("az", "aq", "ag", "wf", "wd", "co", "cy", "na", "oz", "oy", "di", "rs", "ba", "bc", "gb", "gy", "dz", "br", "bb", "sb",
     "xs", "wg", "wz", "wx", "wa", "wb", "wc", "zd", "zq", "wp", "wk", "ry", "ay", "sy", "se", "sf"),
    (1,))
SENT.update(pa=(3,), pb=(3,), pc=(3,))
TAKEN = dict(SENT, az=(3,), ag=(16,), oz=(3,), sb=(4,), xs=(3,))


class Refs:
    pass


def layer_kernel(*refs):
    r, ls, ss, rr = Refs(), Refs(), Refs(), Refs()
    names = [(r, k) for k in ARGS + list(OUTS) + list(BUFFERS)] + [(ls, k) for k in LOCAL]
    names += [(ss, k) for k in SENT] + [(rr, k) for k in TAKEN]
    for (group, name), ref in zip(names, refs, strict=True):
        setattr(group, name, ref)
    ex, mp, z, x, c = place()
    d = 1 - 2 * c
    j = x * 2 + c
    chip = ex // 2
    sib = (ex + d, mp)
    ahead = (z * 8 + lax.rem(x + d + 4, 4) * 2 + c, mp)
    behind = (z * 8 + lax.rem(x - d + 4, 4) * 2 + c, mp)

    def zpeer(i):
        zp = lax.rem(z + i, 4)
        return zp, (zp * 8 + j, mp)

    def ypeer(i):
        ym = lax.rem(mp + i, MP)
        return ym, (ex, ym)

    def xpeer(i):
        xq = lax.rem(x + i, 4)
        return xq, (z * 8 + xq * 2 + c, mp)

    def remote(src, dst, ssem, rsem, device):
        return pltpu.make_async_remote_copy(
            src_ref=src, dst_ref=dst, send_sem=ssem, recv_sem=rsem, device_id=device, device_id_type=MESH)

    def push(src, dst, ssem, rsem, device):
        remote(src, dst, ssem, rsem, device).start()

    def arrive(dst, rsem):
        remote(dst, dst, rsem, rsem, sib).wait_recv()

    def left(src, ssem):
        remote(src, src, ssem, ssem, sib).wait_send()

    def to_all(src_of, dst, name):
        def one(k, carry):
            to = lax.rem(ex + k, EX)
            remote(src_of(to), dst, getattr(ss, name).at[0], getattr(rr, name).at[0], (to, mp)).start()
            return carry

        lax.fori_loop(1, EX, one, 0)

    def gather_first(part):
        for i in (1, 3, 2):
            _, to = xpeer(i) if part == 1 else zpeer(i)
            own = r.pieces.at[part, c, z, x]
            push(own, own, ss.pa.at[part], rr.pa.at[part], to)

    def gather_second(part):
        arrive(r.pieces.at[part, 0, 0, 0:3], rr.pa.at[part])
        row = r.pieces.at[part, c, z] if part == 1 else r.pieces.at[part, c, :, x]
        for i in (1, 3, 2):
            _, to = zpeer(i) if part == 1 else xpeer(i)
            push(row, row, ss.pb.at[part], rr.pb.at[part], to)

    def gather_third(part):
        arrive(r.pieces.at[part, 0, 0:3], rr.pb.at[part])
        push(r.pieces.at[part, c], r.pieces.at[part, c], ss.pc.at[part], rr.pc.at[part], sib)

    bar = greet(ex, mp)
    loads = [
        pltpu.make_async_copy(src, dst, ls.load.at[i])
        for i, (src, dst) in enumerate([
            (r.wqkv_hbm, r.wqkv), (r.wout_hbm, r.wfull.at[mp]), (r.cot_hbm, r.cot), (r.wex_hbm, r.weights.at[2:4]),
            (r.win_hbm, r.weights.at[0:2])])
    ]
    for copy in loads:
        copy.start()
    unit, _ = norm_parts(r.tokens[...].astype(f32))
    normed = (unit * r.gain1[...]).astype(bf16)
    r.normed[...] = normed
    loads[0].wait()
    kt = transposed(dot(normed, r.wqkv[1]).astype(bf16))
    vt = transposed(dot(normed, r.wqkv[2]).astype(bf16))
    qt = transposed((dot(normed, r.wqkv[0]).astype(bf16) * HEAD_DIM ** (-0.5)).astype(bf16))
    for h in range(4):
        r.q_s[h] = qt[64 * h:64 * h + 64]
        r.kv_s[h, 0:64] = kt[64 * h:64 * h + 64]
        r.kv_s[h, 64:128] = vt[64 * h:64 * h + 64]
    greeted(bar)
    for i in (1, 3, 2):
        zp, to = zpeer(i)
        push(r.kv_s.at[zp], r.kvt.at[0, z], ss.az.at[0], rr.az.at[i - 1], to)
    r.kvt[0, z] = r.kv_s[z]

    def own_piece(k):
        zq = lax.rem(z + 4 - k, 4)
        remote(r.kvt.at[0, zq], r.kvt.at[2, zq], ss.ag.at[0], rr.ag.at[4 + k], ahead).start()
        remote(r.kvt.at[0, zq], r.kvt.at[3, zq], ss.ag.at[0], rr.ag.at[8 + k], behind).start()
        remote(r.kvt.at[0, zq], r.kvt.at[1, zq], ss.ag.at[0], rr.ag.at[0], sib).start()

    def came(slot, k):
        arrive(r.kvt.at[slot, lax.rem(z + 4 - k, 4)], rr.ag.at[{2: 4, 3: 8, 6: 12}[slot] + k])

    def came_whole(slot):
        arrive(r.kvt.at[slot], rr.ag.at[{1: 0, 4: 1, 5: 2, 7: 3}[slot]])

    def from_sides(k):
        zq = lax.rem(z + 4 - k, 4)
        came(2, k)
        remote(r.kvt.at[2, zq], r.kvt.at[6, zq], ss.ag.at[0], rr.ag.at[12 + k], ahead).start()
        remote(r.kvt.at[2, zq], r.kvt.at[5, zq], ss.ag.at[0], rr.ag.at[2], sib).start()
        came(3, k)
        remote(r.kvt.at[3, zq], r.kvt.at[4, zq], ss.ag.at[0], rr.ag.at[1], sib).start()

    def from_far(k):
        zq = lax.rem(z + 4 - k, 4)
        came(6, k)
        remote(r.kvt.at[6, zq], r.kvt.at[7, zq], ss.ag.at[0], rr.ag.at[3], sib).start()

    own_piece(0)
    for i in (1, 3, 2):
        zp, to = zpeer(i)
        push(r.q_s.at[zp], r.q.at[z], ss.aq.at[0], rr.aq.at[0], to)
    r.q[z] = r.q_s[z]
    loads[1].wait()
    half = pl.ds(pl.multiple_of(128 * c, 128), 128)
    for i in range(1, 4):
        ym, to = ypeer(i)
        push(r.wfull.at[mp, half, :], r.wfull.at[mp, half, :], ss.wf.at[0], rr.wf.at[0], to)
    r.vt1[64:80, :] = jnp.ones((16, 1024), bf16)
    ends = doc_ends(r.lengths)
    feature = lax.broadcasted_iota(jnp.int32, (64, 256), 0)
    loads[2].wait()
    mine = pl.ds(pl.multiple_of(256 * mp, 256), 256)
    r.placer[...] = slot_matrix(r.chosen[...])
    r.cotq_s[...] = dot(r.placer[...], r.cot[:, mine]).astype(bf16).reshape(EX, 16, 256)
    r.cotq[mp, ex] = r.cotq_s[ex]
    arrive(r.kvt.at[0, lax.rem(z + 3, 4)], rr.az.at[0])
    own_piece(1)
    arrive(r.kvt.at[0, lax.rem(z + 1, 4)], rr.az.at[2])
    own_piece(3)
    from_sides(0)
    arrive(r.kvt.at[0, lax.rem(z + 2, 4)], rr.az.at[1])
    own_piece(2)
    zp, to = zpeer(2)
    push(r.normed, r.nall.at[z], ss.na.at[0], rr.na.at[0], to)
    r.nall[z] = r.normed[...]
    arrive(r.q.at[0:3], rr.aq.at[0])
    for b in range(4):
        docs = doc_row(ends, (b * 8 + j) * 256, 256)
        r.qaug[b, 0:64] = r.q[b]
        r.qaug[b, 64:128] = jnp.where(feature == docs, 0.0, negative_fill).astype(bf16)
        r.peak[b] = jnp.full((1, 256), negative_fill, f32)
        r.acc[b] = jnp.zeros((80, 256), f32)

    def load_keys(slot, jp):
        for b in range(4):
            docs = doc_row(ends, (b * 8 + jp) * 256, 256)
            hot = (feature == docs).astype(f32).astype(bf16)
            r.kaug[256 * b:256 * b + 256, :] = transposed(
                jnp.concatenate([r.kvt[slot, b, 0:64], hot], axis=0))

    def scores(b, n, causal):
        s = dot(r.kaug[0:n, :], r.qaug[b])
        if causal:
            rows = lax.broadcasted_iota(jnp.int32, (n, 256), 0)
            cols = lax.broadcasted_iota(jnp.int32, (n, 256), 1)
            s = jnp.where(rows - 256 * b <= cols, s, negative_fill)
        return s

    def load_chunk(slot, jp):
        load_keys(slot, jp)
        for b in range(4):
            r.vt1[0:64, 256 * b:256 * b + 256] = r.kvt[slot, b, 64:128]

    def forward(tiles, causal):
        def gather(b, n, p, factor):
            r.acc[b] = r.acc[b] * factor + dot(r.vt1[:, 0:n], p)

        held = None
        for b, n in tiles:
            s = scores(b, n, causal)
            if held is not None:
                gather(*held)
            old = r.peak[b]
            new = jnp.maximum(old, jnp.max(s, axis=0, keepdims=True))
            held = (b, n, jnp.exp(s - new).astype(bf16), jnp.exp(old - new))
            r.peak[b] = new
        gather(*held)

    load_chunk(0, j)
    forward([(b, 256 * b + 256) for b in (3, 2, 1, 0)], True)

    def chunk(i, carry):
        u = i // 2
        side = ((u + 1) // 2) % 2
        xp = (x + d * (2 * (i % 2) - 1) * side + 2 * (u // 3) + 8) % 4
        jp = xp * 2 + (c + (1 - side) * (i % 2) + side * (u // 2)) % 2

        @pl.when(i == 1)
        def _():
            from_sides(1)
            from_far(0)
            came_whole(1)

        @pl.when(i == 2)
        def _():
            from_sides(3)
            from_far(1)
            from_sides(2)

        @pl.when(i == 3)
        def _():
            from_far(3)

        @pl.when(i == 4)
        def _():
            from_far(2)
            came_whole(4)
            to_all(lambda to: r.cotq_s.at[to], r.cotq.at[mp, ex], "co")

        @pl.when(i == 5)
        def _():
            came_whole(5)
            arrive(r.wfull.at[0:3, 0:128, :], rr.wf.at[0])
            for i in range(1, 4):
                ym, to = ypeer(4 - i)
                remote(
                    r.wfull.at[ym, half, :], r.wfull.at[ym, half, :], ss.wd.at[0], rr.wd.at[0], sib).start()

        @pl.when(i == 7)
        def _():
            came_whole(7)

        load_chunk(i, jp)

        @pl.when(jp < j)
        def _():
            forward([(b, 256 * b + 256) for b in (3, 2, 1, 0)], False)

        @pl.when(jp > j)
        def _():
            forward([(b, 256 * b) for b in (3, 2, 1)], False)

        return carry

    lax.fori_loop(1, 8, chunk, 0)
    for b in range(4):
        total = r.acc[b, 64:65]
        ot = r.acc[b, 0:64] / total
        r.ot[b] = ot
        r.lse[b] = r.peak[b] + jnp.log(total)
        r.o_s[b] = ot.astype(bf16)
    for i in (1, 3, 2):
        zp, to = zpeer(i)
        push(r.o_s.at[zp], r.att.at[mp, z], ss.oz.at[0], rr.oz.at[i - 1], to)
    r.att[mp, z] = r.o_s[z]
    def normed_half(part):
        rows = pl.ds(128 * part, 128)
        for i in (1, 3):
            zp, to = zpeer(i)
            push(
                r.normed.at[rows, :], r.nall.at[z, rows, :], ss.na.at[0],
                rr.na.at[0], to)

    def attended_piece(k):
        zq = lax.rem(z + 4 - k, 4)
        for i in (1, 3, 2):
            ym, to = ypeer(i)
            push(
                r.att.at[mp, zq], r.att.at[mp, zq], ss.oy.at[0], rr.oy.at[0], to)

    attended_piece(0)
    for k in (1, 3, 2):
        arrive(r.att.at[mp, lax.rem(z + 4 - k, 4)], rr.oz.at[k - 1])
        attended_piece(k)
    normed_half(0)
    arrive(r.cotq.at[0, 0:31], rr.co.at[0])
    arrive(r.wfull.at[0:3, 0:128, :], rr.wd.at[0])
    arrive(r.att.at[0:3], rr.oy.at[0])
    for i in (1, 3, 2):
        ym, to = ypeer(i)
        push(r.cotq.at[mp], r.cotq.at[mp], ss.cy.at[0], rr.cy.at[0], to)
    def geometry(i):
        p = i // 2
        w = p + (p // 2) * (1 - 2 * (p % 2))
        g = (2 + d * w + 4) % 4
        flip = 1 - i % 2
        odd = g % 2
        slot = odd * (2 + g // 2 + 2 * flip) + (1 - odd) * (3 * g + flip)
        xp = (x - d * g + 8) % 4
        return slot, xp, xp * 2 + (c + flip) % 2

    def softmax(i, carry):
        slot, _, jp = geometry(i)
        load_keys(slot, jp)

        def keep(tiles):
            for b, n in tiles:
                r.weights[i, 0:n, 256 * b:256 * b + 256] = jnp.exp(scores(b, n, False) - r.lse[b]).astype(bf16)

        @pl.when(jp < j)
        def _():
            keep([(b, 256 * b + 256) for b in (3, 2, 1, 0)])

        @pl.when(jp > j)
        def _():
            keep([(b, 256 * b) for b in (3, 2, 1)])

        return carry

    value = r.tokens[...].astype(f32) + dot(r.att[...].reshape(1024, 256), r.wfull[...].reshape(1024, 1024), 0, 0)
    r.resid[...] = value
    for k in range(4):
        @pl.when(mp == k)
        def _():
            r.rescol[...] = value[:, 256 * k:256 * k + 256]
    unit, _ = norm_parts(value)
    normed = (unit * r.gain2[...]).astype(bf16)
    for step in (1, 3, 2, 0):
        plane = lax.rem(z + step, 4)
        r.outgoing[pl.ds(8 * plane, 8)] = dot(
            r.placer[pl.ds(pl.multiple_of(128 * plane, 128), 128), :], normed).astype(bf16).reshape(8, 16, 1024)

        def dispatch(k, carry):
            to = plane * 8 + lax.rem(j + k, 8)
            remote(
                r.outgoing.at[to], r.arrived.at[ex], ss.di.at[0], rr.di.at[0],
                (to, mp)).start()
            return carry

        lax.fori_loop(0 if step else 1, 8, dispatch, 0)
    r.arrived[ex] = r.outgoing[ex]
    lax.fori_loop(4, 7, softmax, 0)
    loads[3].wait()
    arrive(r.cotq.at[0:3], rr.cy.at[0])
    for le in range(2):
        rows = jnp.concatenate([one_expert(r.cotq[k], le) for k in range(4)], axis=1)
        r.crows[le] = rows
        r.gh[le] = dot(rows, r.weights[2 + le], 1, 1)
    loads[4].wait()
    arrive(r.arrived.at[0:31], rr.di.at[0])
    def expert_rows(le):
        rows = one_expert(r.arrived[...], le)
        r.xrows[le] = rows
        return dot(rows, r.weights[le])

    def activate(le, pre):
        hidden, slope = gelu_parts(pre)
        r.hid[le] = hidden.astype(bf16)
        gpre = (r.gh[le] * slope).astype(bf16)
        r.gpre[le] = gpre
        return gpre

    def give_back(le, gpre):
        for k in range(4):
            product = dot(gpre, r.weights[le, 256 * k:256 * k + 256, :], 1, 1)
            r.part[le, k] = product[:, 0:128].astype(bf16)
            r.gh[le, :, 128 * k:128 * k + 128] = product[:, 128:256]
        for i in (1, 3, 2):
            ym, to = ypeer(i)
            push(r.part.at[le, ym], r.rs.at[le, i - 1], ss.rs.at[0], rr.rs.at[0], to)

    first, second = expert_rows(0), expert_rows(1)
    gpre = activate(0, first)
    give_back(0, gpre)
    give_back(1, activate(1, second))
    r.wide_s[...] = both_experts(r.gh[0, :, 0:512], r.gh[1, :, 0:512])
    to_all(lambda to: r.wide_s.at[to], r.wide.at[ex], "bc")
    r.wide[ex] = r.wide_s[ex]
    first = dot(r.hid[0], r.weights[2])
    r.branch[...] = both_experts(first, dot(r.hid[1], r.weights[3]))
    lax.fori_loop(0, 4, softmax, 0)
    arrive(r.rs, rr.rs.at[0])
    sums = []
    for le in range(2):
        total = r.part[le, mp].astype(f32)
        for i in range(3):
            total = total + r.rs[le, i].astype(f32)
        sums.append(total)
    r.back_s[...] = both_experts(sums[0], sums[1])
    to_all(lambda to: r.back_s.at[to], r.back.at[ex], "ba")
    r.back[ex] = r.back_s[ex]
    arrive(r.wide.at[0:31], rr.bc.at[0])
    rows = dot(r.placer[...], r.wide[...].reshape(512, 512), 0, 0).astype(bf16)
    for k in range(4):
        r.gb[k] = rows[:, 128 * k:128 * k + 128]
    for i in (1, 3, 2):
        ym, to = ypeer(i)
        push(r.gb.at[ym], r.gbr.at[i - 1], ss.gb.at[0], rr.gb.at[0], to)
    arrive(r.back.at[0:31], rr.ba.at[0])
    r.gn[0, mp] = dot(r.placer[...], r.back[...].reshape(512, 128), 0, 0).astype(bf16)
    for i in (1, 3, 2):
        ym, to = ypeer(i)
        push(r.gn.at[0, mp], r.gn.at[0, mp], ss.gy.at[0], rr.gy.at[0], to)
    normed_half(1)
    total = r.gb[mp].astype(f32)
    arrive(r.gbr, rr.gb.at[0])
    for i in range(3):
        total = total + r.gbr[i].astype(f32)
    r.gn[1, mp] = total.astype(bf16)
    for i in (1, 3, 2):
        ym, to = ypeer(i)
        push(r.gn.at[1, mp], r.gn.at[1, mp], ss.gy.at[0], rr.gy.at[0], to)
    unit, inverse = norm_parts(r.resid[...])
    arrive(r.gn.at[:, 0:3], rr.gy.at[0])
    grad = jnp.concatenate([r.gn[k % 2, k // 2] for k in range(8)], axis=1).astype(f32)
    grad_in, ggrad = norm_back(grad, r.gain2[...], unit, inverse)
    r.smallf[ex] = ggrad
    gres = r.cot[...].astype(f32) + grad_in
    r.gres[...] = gres
    low = gres.astype(bf16)
    r.dheads[...] = dot(r.wfull[mp], low, 1, 1).astype(bf16).reshape(4, 64, 256)
    for i in (1, 3, 2):
        zp, to = zpeer(i)
        push(r.dheads.at[zp], r.dob.at[z], ss.dz.at[0], rr.dz.at[0], to)
    r.dob[z] = r.dheads[z]
    wgrad = dot(r.att[mp].reshape(256, 256), low).astype(bf16)
    r.wgp[0] = wgrad[:, 0:512].reshape(4, 4, 16, 512)
    r.wgp[1] = wgrad[:, 512:1024].reshape(4, 4, 16, 512)
    push(r.wgp.at[1 - c], r.wgs, ss.wg.at[0], rr.wg.at[0], sib)
    for i in range(1, 4):
        ym, to = ypeer(i)
        push(
            r.branch.at[:, :, pl.ds(pl.multiple_of(256 * ym, 256), 256)], r.brs.at[i - 1],
            ss.br.at[0], rr.br.at[0], to)
    zero = jnp.zeros((64, 256), bf16)
    to_all(lambda to: r.smallf.at[ex], r.smallf.at[ex], "sf")
    arrive(r.dob.at[0:3], rr.dz.at[0])
    arrive(r.wgs, rr.wg.at[0])
    r.wgq[...] = (r.wgp[c].astype(f32) + r.wgs[...].astype(f32)).astype(bf16)
    for i in (1, 3, 2):
        zp, to = zpeer(i)
        push(r.wgq.at[zp], r.wgz.at[i - 1], ss.wz.at[0], rr.wz.at[0], to)
    for b in range(4):
        r.dopad[b, 0:64] = zero
        r.dopad[b, 64:128] = r.dob[b]
        r.qd[b, 0:256] = transposed(jnp.concatenate([r.q[b], zero], axis=0))
        r.qd[b, 256:512] = transposed(jnp.concatenate([zero, r.dob[b]], axis=0))
        r.delta[b] = jnp.sum(r.dob[b].astype(f32) * r.ot[b], axis=0, keepdims=True)
        r.dq[b] = jnp.zeros((64, 256), f32)

    def load_back(slot):
        for b in range(4):
            r.kvn[256 * b:256 * b + 256, :] = transposed(r.kvt[slot, b])
            r.kt[:, 256 * b:256 * b + 256] = r.kvt[slot, b, 0:64]

    def backward(tiles, weights):
        def gather(b, n, ds, p):
            added = dot(ds, r.qd[b, 0:256]) + dot(p, r.qd[b, 256:512])
            if b == 3:
                r.dkv[0:n] = added
            else:
                r.dkv[0:n] = r.dkv[0:n] + added
            r.dq[b] = r.dq[b] + dot(r.kt[:, 0:n], ds)

        held = None
        for b, n in tiles:
            dp = dot(r.kvn[0:n, :], r.dopad[b])
            p = weights(b, n)
            if held is not None:
                gather(*held)
            held = (b, n, (p * (dp - r.delta[b])).astype(bf16), p.astype(bf16))
        gather(*held)

    def back_chunk(i, carry):
        slot, xp, jp = geometry(i)
        p = i // 2
        load_back(slot)

        def kept(b, n):
            return r.weights[i, 0:n, 256 * b:256 * b + 256]

        @pl.when(jp < j)
        def _():
            backward([(b, 256 * b + 256) for b in (3, 2, 1, 0)], kept)

        @pl.when(jp > j)
        def _():
            r.dkv[768:1024] = jnp.zeros((256, 128), f32)
            backward([(b, 256 * b) for b in (3, 2, 1)], kept)

        @pl.when(i % 2 == 0)
        def _():
            r.sb[p] = r.dkv[...].astype(bf16)
            remote(r.sb.at[p], r.sr.at[p], ss.sb.at[0], rr.sb.at[p], sib).start()

        @pl.when(i % 2 == 1)
        def _():
            arrive(r.sr.at[p], rr.sb.at[p])
            r.xs[p] = (r.dkv[...] + r.sr[p].astype(f32)).astype(bf16)

            @pl.when(p == 0)
            def _():
                remote(r.xs.at[0], r.xr.at[0], ss.xs.at[0], rr.xs.at[0], ahead).start()

            @pl.when(p == 2 - c)
            def _():
                remote(r.xs.at[p], r.xr.at[1], ss.xs.at[0], rr.xs.at[1], behind).start()

            @pl.when(p == 2)
            def _():
                arrive(r.xr.at[0], rr.xs.at[0])
                r.xs[3] = (r.xs[1 + c].astype(f32) + r.xr[0].astype(f32)).astype(bf16)
                remote(r.xs.at[3], r.xr.at[2], ss.xs.at[0], rr.xs.at[2], ahead).start()

        @pl.when(i == 2)
        def _():
            arrive(r.wgz, rr.wz.at[0])
            total = r.wgq[z].astype(f32)
            for k in range(3):
                total = total + r.wgz[k].astype(f32)
            r.wgx[...] = total.astype(bf16)
            for k in (1, 3, 2):
                xq, to = xpeer(k)
                remote(r.wgx.at[xq], r.wgr.at[k - 1], ss.wx.at[0], rr.wx.at[0], to).start()

        @pl.when(i == 6)
        def _():
            total = r.branch[:, :, mine].astype(f32)
            arrive(r.brs, rr.br.at[0])
            for k in range(3):
                total = total + r.brs[k].astype(f32)
            r.bs[...] = total.astype(bf16)

        @pl.when(i == 5)
        def _():
            total = r.wgx[x].astype(f32)
            arrive(r.wgr, rr.wx.at[0])
            for k in range(3):
                total = total + r.wgr[k].astype(f32)
            r.wgf[c, z, x] = total.astype(bf16)
            for k in (1, 3, 2):
                _, to = xpeer(k)
                remote(r.wgf.at[c, z, x], r.wgf.at[c, z, x], ss.wa.at[0], rr.wa.at[0], to).start()

        return carry

    lax.fori_loop(0, 7, back_chunk, 0)
    load_back(0)
    load_keys(0, j)
    backward(
        [(b, 256 * b + 256) for b in (3, 2, 1, 0)], lambda b, n: jnp.exp(scores(b, n, True) - r.lse[b]))
    for b in range(4):
        r.zs[b, 0:64] = (r.dq[b] * HEAD_DIM ** (-0.5)).astype(bf16)
    for i in (1, 3, 2):
        zp, to = zpeer(i)
        push(r.zs.at[zp, 0:64], r.zr.at[z, 0:64], ss.zd.at[0], rr.zd.at[0], to)
    arrive(r.nall.at[0:3], rr.na.at[0])

    def weight_part(first, last, pieces, name):
        wt = dot(r.zs[0, first:last], r.nall[0])
        for b in range(1, 4):
            wt = wt + dot(r.zs[b, first:last], r.nall[b])
        wt = wt.astype(bf16)
        for k in range(8):
            pieces[0][k] = wt[:, 128 * k:128 * k + 128]
        for i in range(1, 8):
            jt = lax.rem(j + i, 8)
            push(
                pieces[0].at[jt], pieces[1].at[i - 1], getattr(ss, name).at[0], getattr(rr, name).at[0],
                (z * 8 + jt, mp))

    def weight_sum(pieces, name):
        total = pieces[0][j].astype(f32)
        arrive(pieces[1], getattr(rr, name).at[0])
        for i in range(7):
            total = total + pieces[1][i].astype(f32)
        return total.astype(bf16)

    weight_part(0, 64, (r.wpq, r.wrq), "wp")
    r.resid[...] = norm_parts(r.tokens[...].astype(f32))[0]
    arrive(r.sr.at[3], rr.sb.at[3])
    total = r.dkv[...] + r.sr[3].astype(f32)
    for k in (1, 2):
        arrive(r.xr.at[k], rr.xs.at[k])
        total = total + r.xr[k].astype(f32)
    low = total.astype(bf16)
    for b in range(4):
        r.zs[b, 64:192] = transposed(low[256 * b:256 * b + 256])
    for i in (1, 3, 2):
        zp, to = zpeer(i)
        push(r.zs.at[zp, 64:192], r.zr.at[z, 64:192], ss.zq.at[0], rr.zq.at[0], to)
    r.zr[z] = r.zs[z]
    weight_part(64, 192, (r.wpk, r.wrk), "wk")
    r.pieces[0, c, z, x] = weight_sum((r.wpq, r.wrq), "wp")
    gather_first(0)
    arrive(r.wgf.at[0, 0, 0:3], rr.wa.at[0])
    for k in (1, 3, 2):
        _, to = zpeer(k)
        push(r.wgf.at[c, z], r.wgf.at[c, z], ss.wb.at[0], rr.wb.at[0], to)

    def heads(first):
        return transposed(jnp.concatenate([r.zr[h, first:first + 64] for h in range(4)], axis=0))

    arrive(r.zr.at[0:3, 0:64], rr.zd.at[0])
    part = dot(heads(0), r.wqkv[0], 1, 1)
    arrive(r.zr.at[0:3, 64:192], rr.zq.at[0])
    part = part + dot(heads(64), r.wqkv[1], 1, 1) + dot(heads(128), r.wqkv[2], 1, 1)
    r.gnp[...] = part.astype(bf16).reshape(4, 64, 1024)
    one_gain = jnp.sum(part * r.resid[...], axis=0, keepdims=True)
    r.small[...] = one_gain
    for i in (1, 3, 2):
        ym, to = ypeer(i)
        push(r.small, r.smally.at[i - 1], ss.sy.at[0], rr.sy.at[0], to)
    for i in (1, 3, 2):
        ym, to = ypeer(i)
        push(r.gnp.at[ym], r.ry.at[i - 1], ss.ry.at[0], rr.ry.at[0], to)
    gather_second(0)
    both = weight_sum((r.wpk, r.wrk), "wk")
    r.pieces[1, c, z, x] = both[0:64]
    r.pieces[2, c, z, x] = both[64:128]
    gather_first(1)
    gather_first(2)
    arrive(r.smally, rr.sy.at[0])
    for i in range(3):
        one_gain = one_gain + r.smally[i]
    r.smalle[ex] = one_gain
    to_all(lambda to: r.smalle.at[ex], r.smalle.at[ex], "se")
    gather_second(1)
    gather_second(2)
    to_all(lambda to: r.bs.at[to], r.bret.at[ex], "bb")
    r.bret[ex] = r.bs[ex]
    gather_third(0)
    grad = r.gnp[mp].astype(f32)
    arrive(r.ry, rr.ry.at[0])
    for i in range(3):
        grad = grad + r.ry[i].astype(f32)
    here = pl.ds(pl.multiple_of(64 * mp, 64), 64)
    unit, inverse = norm_parts(r.tokens[here, :].astype(f32))
    grad_in, _ = norm_back(grad, r.gain1[...], unit, inverse)
    r.igrad[here, :] = (r.gres[here, :] + grad_in).astype(bf16)
    for i in (1, 3, 2):
        ym, to = ypeer(i)
        push(r.igrad.at[here, :], r.igrad.at[here, :], ss.ay.at[0], rr.ay.at[0], to)
    gather_third(1)
    gather_third(2)
    arrive(r.wgf.at[0, 0:3], rr.wb.at[0])
    push(r.wgf.at[c], r.wgf.at[c], ss.wc.at[0], rr.wc.at[0], sib)
    arrive(r.wgf.at[1 - c], rr.wc.at[0])
    for k in range(16):
        for core in range(2):
            r.wout_out[16 * k:16 * k + 16, 512 * core:512 * core + 512] = r.wgf[core, k // 4, k % 4]
    for k in range(3):
        arrive(r.pieces.at[k, 1 - c], rr.pc.at[k])
        for row in range(8):
            block = jnp.concatenate([r.pieces[k, row % 2, h, row // 2] for h in range(4)], axis=0)
            r.qkv_out[k, 128 * row:128 * row + 128] = transposed(block)
    arrive(r.smalle.at[0:31], rr.se.at[0])
    arrive(r.smallf.at[0:31], rr.sf.at[0])
    r.gain1_out[...] = jnp.sum(r.smalle[...], axis=0)
    r.gain2_out[...] = jnp.sum(r.smallf[...], axis=0)
    arrive(r.bret.at[0:31], rr.bb.at[0])
    rows = dot(r.placer[...], r.bret[...].reshape(512, 256), 0, 0)
    r.out[...] = (r.rescol[...] + rows).astype(bf16)
    arrive(r.igrad.at[0:192, :], rr.ay.at[0])
    sent = {
        "az": r.kv_s.at[0:3], "aq": r.q_s.at[0:3], "ag": r.kvt.at[0:7], "wf": r.wfull.at[0:3, 0:128, :],
        "wd": r.wfull.at[0:3, 0:128, :], "co": r.cotq_s.at[0:31], "cy": r.cotq.at[0:3], "na": r.nall.at[0:3],
        "oz": r.o_s.at[0:3], "oy": r.att.at[0:3], "di": r.outgoing.at[0:31], "rs": r.rs, "ba": r.back_s.at[0:31],
        "bc": r.wide_s.at[0:31], "gb": r.gb.at[0:3], "gy": r.gn.at[:, 0:3], "dz": r.dheads.at[0:3], "br": r.brs,
        "bb": r.bs.at[0:31], "sb": r.sb, "xs": r.xs.at[0:3], "wg": r.wgs, "wz": r.wgq.at[0:3], "wx": r.wgr,
        "wa": r.wgr, "wb": r.wgf.at[0, 0:3], "wc": r.wgf.at[0], "zd": r.zs.at[0:3, 0:64], "zq": r.zs.at[0:3, 64:192],
        "wp": r.wrq, "wk": r.wrk, "ry": r.ry, "ay": r.ry, "sy": r.smally, "se": r.smalle.at[0:31],
        "sf": r.smallf.at[0:31],
    }
    for name, ref in sent.items():
        left(ref, getattr(ss, name).at[0])
    for part in range(3):
        left(r.pieces.at[0, 0, 0, 0:3], ss.pa.at[part])
        left(r.pieces.at[0, 0, 0:3], ss.pb.at[part])
        left(r.pieces.at[0, 0], ss.pc.at[part])


def layer(*args):
    return pl.pallas_call(
        layer_kernel,
        out_shape=[pltpu.VMEM(s, t) for s, t in OUTS.values()],
        in_specs=[SM, VM, VM, VM, VM, ANY, ANY, ANY, ANY, ANY],
        out_specs=[VM] * len(OUTS),
        scratch_shapes=[pltpu.VMEM(s, t) for s, t in BUFFERS.values()]
        + [DMA(s) for group in (LOCAL, SENT, TAKEN) for s in group.values()],
        name="layer",
        compiler_params=pltpu.CompilerParams(
            collective_id=0, has_side_effects=True, vmem_limit_bytes=VMEM_BYTES),
    )(*args)


def finish_kernel(x, gpre, hid, cots, qkv, wout, out, igrad, gain1, gain2, *refs):
    in_grad, out_grad, qkv_o, wout_o, out_o, igrad_o, gain1_o, gain2_o = refs[:8]
    in_buf, out_buf, qkv_buf, wout_buf, store, rest = refs[8:]
    stores = []

    def put(src, dst, sem):
        copy = pltpu.make_async_copy(src, dst, sem)
        copy.start()
        stores.append(copy)

    for k, (left, right, buf, result) in enumerate(((x, gpre, in_buf, in_grad), (hid, cots, out_buf, out_grad))):
        for e in range(2):
            for t in range(4):
                rows = pl.ds(256 * t, 256)
                buf[e, rows, :] = dot(left[e, :, 256 * t:256 * t + 256], right[e], 0, 0)
                put(buf.at[e, rows, :], result.at[e, rows, :], store.at[8 * k + 4 * e + t])
    qkv_buf[...] = qkv[...].astype(f32)
    wout_buf[...] = wout[...].astype(f32)
    plain = ((qkv_buf, qkv_o), (wout_buf, wout_o), (out, out_o), (igrad, igrad_o), (gain1, gain1_o), (gain2, gain2_o))
    for k, (src, dst) in enumerate(plain):
        put(src, dst, rest.at[k])
    for copy in stores:
        copy.wait()


def finish(*args):
    big = ((2, 1024, 1024), f32)
    outs = [big, big, ((3, 1024, 256), f32), ((256, 1024), f32), ((256, 256), bf16), ((256, 1024), bf16)]
    outs += [((1, 1024), f32)] * 2
    return pl.pallas_call(
        finish_kernel,
        out_shape=[jax.ShapeDtypeStruct(s, t) for s, t in outs],
        in_specs=[VM] * 10,
        out_specs=[ANY] * 8,
        scratch_shapes=[pltpu.VMEM(s, t) for s, t in outs[:4]] + [DMA((16,)), DMA((6,))],
        name="finish",
        compiler_params=pltpu.CompilerParams(vmem_limit_bytes=36 << 20),
        cost_estimate=pl.CostEstimate(flops=2 * 2 * 2 * 256 * 1024 * 1024, bytes_accessed=28 << 20, transcendentals=0),
    )(*args)


def on_device(
    tokens, hash_ids, lengths, norm1_gain, qkv_weight, out_weight, norm2_gain, expert_in, expert_out, cotangent,
):
    x, cots, hid, gpre, out, igrad, gain1, gain2, qkv, wout = layer(
        lengths, tokens, norm1_gain.reshape(1, 1024), norm2_gain.reshape(1, 1024), hash_ids.reshape(1, 256),
        jnp.transpose(qkv_weight, (1, 0, 2)), out_weight, cotangent, expert_in, expert_out)
    in_grad, out_grad, qkv, wout, out, igrad, gain1, gain2 = finish(
        x, gpre, hid, cots, qkv, wout, out, igrad, gain1, gain2)
    return out, igrad, gain1.reshape(1024), jnp.transpose(qkv, (1, 0, 2)), wout, gain2.reshape(1024), in_grad, out_grad


def solution(mesh):
    placed = (
        P("ex", None), P("ex", None), P(), P(), P(None, None, "mp"), P("mp", None), P(),
        P("ex", None, "mp"), P("ex", "mp", None), P("ex", None),
    )
    return jax.shard_map(
        on_device,
        mesh=mesh,
        in_specs=placed,
        out_specs=(
            P("ex", "mp"), P("ex", None), P(), P(None, None, "mp"), P("mp", None), P(),
            P("ex", None, "mp"), P("ex", "mp", None),
        ),
        check_vma=False,
    )
```

```python
import functools

import jax
import jax.numpy as jnp
from jax import lax
from jax.experimental import pallas as pl
from jax.experimental.pallas import tpu as pltpu
from jax.sharding import PartitionSpec as P

HEAD_DIM = 64
epsilon = 1e-05
negative_fill = -1e30
MESH = pl.DeviceIdType.MESH
bf16, f32 = jnp.bfloat16, jnp.float32
EX, MP = 32, 4
VMEM_BYTES = 56 << 20


def dot(a, b, ca=1, cb=0):
    return lax.dot_general(a, b, (((ca,), (cb,)), ((), ())), preferred_element_type=f32)


def place():
    ex, mp = lax.axis_index("ex"), lax.axis_index("mp")
    z, x, c = ex // 8, (ex // 2) % 4, ex % 2
    return ex, mp, z, x, c


def send(src, dst, ssem, rsem, device):
    copy = pltpu.make_async_remote_copy(
        src_ref=src, dst_ref=dst, send_sem=ssem, recv_sem=rsem, device_id=device, device_id_type=MESH
    )
    copy.start()
    return copy


def greet(ex, mp):
    bar = pltpu.get_barrier_semaphore()

    def one(d, carry):
        pl.semaphore_signal(bar, inc=1, device_id=(lax.rem(ex + d, EX), mp), device_id_type=MESH)
        return carry

    lax.fori_loop(1, EX, one, 0)
    for d in range(1, MP):
        pl.semaphore_signal(bar, inc=1, device_id=(ex, lax.rem(mp + d, MP)), device_id_type=MESH)
    return bar


def greeted(bar):
    pl.semaphore_wait(bar, EX - 1 + MP - 1)


def slot_matrix(chosen_row):
    tok = chosen_row.shape[1]
    experts = lax.broadcasted_iota(jnp.int32, (64, tok), 0)
    hot = (experts == chosen_row).astype(f32)
    rows = lax.broadcasted_iota(jnp.int32, (tok, tok), 0)
    cols = lax.broadcasted_iota(jnp.int32, (tok, tok), 1)
    before = (rows < cols).astype(bf16)
    earlier = dot(hot.astype(bf16), before)
    rank = jnp.sum(earlier * hot, axis=0, keepdims=True)
    target = chosen_row * 8 + rank.astype(jnp.int32)
    slots = lax.broadcasted_iota(jnp.int32, (512, tok), 0)
    return (slots == target).astype(f32).astype(bf16)


def doc_row(ends, first, count):
    pos = first + lax.broadcasted_iota(jnp.int32, (1, count), 1)
    row = jnp.zeros((1, count), jnp.int32)
    for end in ends:
        row = row + (pos >= end).astype(jnp.int32)
    return row


def doc_ends(lengths_ref):
    ends, total = [], 0
    for i in range(9):
        total = total + lengths_ref[i]
        ends.append(total)
    return ends


def norm_parts(v):
    mean = jnp.mean(v, axis=-1, keepdims=True)
    centred = v - mean
    inverse = lax.rsqrt(jnp.mean(centred * centred, axis=-1, keepdims=True) + epsilon)
    return centred * inverse, inverse


def transposed(v):
    return v.T


def norm_back(grad_out, gain_row, unit, inverse):
    scaled = grad_out * gain_row
    centred = scaled - jnp.mean(scaled, axis=-1, keepdims=True)
    grad_in = inverse * (centred - unit * jnp.mean(scaled * unit, axis=-1, keepdims=True))
    return grad_in, jnp.sum(grad_out * unit, axis=0, keepdims=True)


def gelu_parts(pre):
    k = 0.7978845608028654
    square = pre * pre
    t = jnp.tanh(k * pre * (1.0 + 0.044715 * square))
    half = 0.5 * (1.0 + t)
    slope = half + 0.5 * pre * (1.0 - t * t) * (k * (1.0 + 3 * 0.044715 * square))
    return pre * half, slope


def one_expert(rows, le):
    wide = rows.astype(f32)
    return wide[:, 8 * le:8 * le + 8].reshape(256, rows.shape[2]).astype(bf16)


def both_experts(first, second):
    width = first.shape[1]
    return jnp.concatenate([first.reshape(32, 8, width), second.reshape(32, 8, width)], axis=1).astype(bf16)


VM = pl.BlockSpec(memory_space=pltpu.VMEM)
SM = pl.BlockSpec(memory_space=pltpu.SMEM)
ANY = pl.BlockSpec(memory_space=pl.ANY)
DMA = pltpu.SemaphoreType.DMA
ROWS = (2, 256, 1024)

ARGS = ["lengths", "tokens", "gain1", "gain2", "chosen", "wqkv_hbm", "wout_hbm", "cot_hbm", "win_hbm", "wex_hbm"]
OUTS = {
    "xrows": (ROWS, bf16), "crows": (ROWS, bf16), "hid": (ROWS, bf16), "gpre": (ROWS, bf16),
    "out": ((256, 256), bf16), "igrad": ((256, 1024), bf16), "gain1_out": ((1, 1024), f32), "gain2_out": ((1, 1024), f32),
    "qkv_out": ((3, 1024, 256), bf16), "wout_out": ((256, 1024), bf16),
}
BUFFERS = {
    "wqkv": ((3, 1024, 256), bf16), "cot": ((256, 1024), bf16),
    "weights": ((7, 1024, 1024), bf16), "placer": ((512, 256), bf16), "normed": ((256, 1024), bf16),
    "nall": ((4, 256, 1024), bf16), "wfull": ((4, 256, 1024), bf16),
    "q_s": ((4, 64, 256), bf16), "kv_s": ((4, 128, 256), bf16), "q": ((4, 64, 256), bf16),
    "kvt": ((8, 4, 128, 256), bf16), "qaug": ((4, 128, 256), bf16), "kaug": ((1024, 128), bf16),
    "vt1": ((80, 1024), bf16), "acc": ((4, 80, 256), f32), "peak": ((4, 1, 256), f32),
    "ot": ((4, 64, 256), f32), "lse": ((4, 1, 256), f32), "o_s": ((4, 64, 256), bf16),
    "att": ((4, 4, 64, 256), bf16), "cotq_s": ((32, 16, 256), bf16), "cotq": ((4, 32, 16, 256), bf16),
    "slots": ((64, 16, 1024), bf16),
    "gh": (ROWS, f32),
    "part": ((2, 4, 256, 128), bf16), "rs": ((2, 3, 256, 128), bf16), "back_s": ((32, 16, 128), bf16),
    "back": ((32, 16, 128), bf16), "wide_s": ((32, 16, 512), bf16), "wide": ((32, 16, 512), bf16),
    "gb": ((4, 256, 128), bf16), "gbr": ((3, 256, 128), bf16), "gn": ((2, 4, 256, 128), bf16), "resid": ((256, 1024), f32),
    "rescol": ((256, 256), f32), "gres": ((256, 1024), f32), "branch": ((32, 16, 1024), bf16),
    "wgp": ((2, 4, 4, 16, 512), bf16), "wgs": ((4, 4, 16, 512), bf16), "wgq": ((4, 4, 16, 512), bf16),
    "wgz": ((3, 4, 16, 512), bf16), "wgx": ((4, 16, 512), bf16), "wgr": ((3, 16, 512), bf16),
    "wgf": ((2, 4, 4, 16, 512), bf16),
    "dheads": ((4, 64, 256), bf16), "dob": ((4, 64, 256), bf16), "brs": ((3, 32, 16, 256), bf16),
    "bs": ((32, 16, 256), bf16), "bret": ((32, 16, 256), bf16), "dopad": ((4, 128, 256), bf16),
    "qd": ((4, 512, 128), bf16), "delta": ((4, 1, 256), f32), "kvn": ((1024, 128), bf16),
    "kt": ((64, 1024), bf16), "dkv": ((1024, 128), f32), "dq": ((4, 64, 256), f32),
    "sb": ((4, 1024, 128), bf16), "sr": ((4, 1024, 128), bf16), "xs": ((4, 1024, 128), bf16),
    "xr": ((3, 1024, 128), bf16), "zs": ((4, 192, 256), bf16), "zr": ((4, 192, 256), bf16),
    "wpq": ((8, 64, 128), bf16), "wrq": ((7, 64, 128), bf16),
    "wpk": ((8, 128, 128), bf16), "wrk": ((7, 128, 128), bf16),
    "pieces": ((3, 2, 4, 4, 64, 128), bf16),
    "gnp": ((4, 64, 1024), bf16), "ry": ((3, 64, 1024), bf16), "small": ((1, 1024), f32),
    "smally": ((3, 1, 1024), f32), "smalle": ((32, 1, 1024), f32), "smallf": ((32, 1, 1024), f32),
}
LOCAL = {"load": (5,)}
SENT = dict.fromkeys(
    ("az", "aq", "ag", "wf", "wd", "co", "cy", "na", "oz", "oy", "di", "rs", "ba", "bc", "gb", "gy", "dz", "br", "bb", "sb",
     "xs", "wg", "wz", "wx", "wa", "wb", "wc", "zd", "zq", "wp", "wk", "ry", "ay", "sy", "se", "sf"),
    (1,))
SENT.update(pa=(3,), pb=(3,), pc=(3,))
TAKEN = dict(SENT, ry=(2,), az=(3,), ag=(16,), oz=(3,), sb=(4,), xs=(3,))


class Refs:
    pass


def layer_kernel(*refs):
    r, ls, ss, rr = Refs(), Refs(), Refs(), Refs()
    names = [(r, k) for k in ARGS + list(OUTS) + list(BUFFERS)] + [(ls, k) for k in LOCAL]
    names += [(ss, k) for k in SENT] + [(rr, k) for k in TAKEN]
    for (group, name), ref in zip(names, refs, strict=True):
        setattr(group, name, ref)
    ex, mp, z, x, c = place()
    d = 1 - 2 * c
    j = x * 2 + c
    chip = ex // 2
    sib = (ex + d, mp)
    ahead = (z * 8 + lax.rem(x + d + 4, 4) * 2 + c, mp)
    behind = (z * 8 + lax.rem(x - d + 4, 4) * 2 + c, mp)

    def zpeer(i):
        zp = lax.rem(z + i, 4)
        return zp, (zp * 8 + j, mp)

    def ypeer(i):
        ym = lax.rem(mp + i, MP)
        return ym, (ex, ym)

    def xpeer(i):
        xq = lax.rem(x + i, 4)
        return xq, (z * 8 + xq * 2 + c, mp)

    def remote(src, dst, ssem, rsem, device):
        return pltpu.make_async_remote_copy(
            src_ref=src, dst_ref=dst, send_sem=ssem, recv_sem=rsem, device_id=device, device_id_type=MESH)

    def push(src, dst, ssem, rsem, device):
        remote(src, dst, ssem, rsem, device).start()

    def arrive(dst, rsem):
        remote(dst, dst, rsem, rsem, sib).wait_recv()

    def left(src, ssem):
        remote(src, src, ssem, ssem, sib).wait_send()

    def to_all(src_of, dst, name):
        def one(k, carry):
            to = lax.rem(ex + k, EX)
            remote(src_of(to), dst, getattr(ss, name).at[0], getattr(rr, name).at[0], (to, mp)).start()
            return carry

        lax.fori_loop(1, EX, one, 0)

    def gather_first(part):
        for i in (1, 3, 2):
            _, to = xpeer(i) if part == 1 else zpeer(i)
            own = r.pieces.at[part, c, z, x]
            push(own, own, ss.pa.at[part], rr.pa.at[part], to)

    def gather_second(part):
        arrive(r.pieces.at[part, 0, 0, 0:3], rr.pa.at[part])
        row = r.pieces.at[part, c, z] if part == 1 else r.pieces.at[part, c, :, x]
        for i in (1, 3, 2):
            _, to = zpeer(i) if part == 1 else xpeer(i)
            push(row, row, ss.pb.at[part], rr.pb.at[part], to)

    def gather_third(part):
        arrive(r.pieces.at[part, 0, 0:3], rr.pb.at[part])
        push(r.pieces.at[part, c], r.pieces.at[part, c], ss.pc.at[part], rr.pc.at[part], sib)

    bar = greet(ex, mp)
    loads = [
        pltpu.make_async_copy(src, dst, ls.load.at[i])
        for i, (src, dst) in enumerate([
            (r.wqkv_hbm, r.wqkv), (r.wout_hbm, r.wfull.at[mp]), (r.cot_hbm, r.cot), (r.wex_hbm, r.weights.at[2:4]),
            (r.win_hbm, r.weights.at[0:2])])
    ]
    for copy in loads:
        copy.start()
    unit, _ = norm_parts(r.tokens[...].astype(f32))
    normed = (unit * r.gain1[...]).astype(bf16)
    r.normed[...] = normed
    loads[0].wait()
    kt = transposed(dot(normed, r.wqkv[1]).astype(bf16))
    vt = transposed(dot(normed, r.wqkv[2]).astype(bf16))
    for h in range(4):
        r.kv_s[h, 0:64] = kt[64 * h:64 * h + 64]
        r.kv_s[h, 64:128] = vt[64 * h:64 * h + 64]
    greeted(bar)
    for i in (1, 3, 2):
        zp, to = zpeer(i)
        push(r.kv_s.at[zp], r.kvt.at[0, z], ss.az.at[0], rr.az.at[i - 1], to)
    r.kvt[0, z] = r.kv_s[z]

    def own_piece(k):
        zq = lax.rem(z + 4 - k, 4)
        remote(r.kvt.at[0, zq], r.kvt.at[2, zq], ss.ag.at[0], rr.ag.at[4 + k], ahead).start()
        remote(r.kvt.at[0, zq], r.kvt.at[3, zq], ss.ag.at[0], rr.ag.at[8 + k], behind).start()
        remote(r.kvt.at[0, zq], r.kvt.at[1, zq], ss.ag.at[0], rr.ag.at[0], sib).start()

    def came(slot, k):
        arrive(r.kvt.at[slot, lax.rem(z + 4 - k, 4)], rr.ag.at[{2: 4, 3: 8, 6: 12}[slot] + k])

    def came_whole(slot):
        arrive(r.kvt.at[slot], rr.ag.at[{1: 0, 4: 1, 5: 2, 7: 3}[slot]])

    def from_sides(k):
        zq = lax.rem(z + 4 - k, 4)
        came(2, k)
        remote(r.kvt.at[2, zq], r.kvt.at[6, zq], ss.ag.at[0], rr.ag.at[12 + k], ahead).start()
        remote(r.kvt.at[2, zq], r.kvt.at[5, zq], ss.ag.at[0], rr.ag.at[2], sib).start()
        came(3, k)
        remote(r.kvt.at[3, zq], r.kvt.at[4, zq], ss.ag.at[0], rr.ag.at[1], sib).start()

    def from_far(k):
        zq = lax.rem(z + 4 - k, 4)
        came(6, k)
        remote(r.kvt.at[6, zq], r.kvt.at[7, zq], ss.ag.at[0], rr.ag.at[3], sib).start()

    own_piece(0)
    qt = transposed((dot(normed, r.wqkv[0]).astype(bf16) * HEAD_DIM ** (-0.5)).astype(bf16))
    for h in range(4):
        r.q_s[h] = qt[64 * h:64 * h + 64]
    for i in (1, 3, 2):
        zp, to = zpeer(i)
        push(r.q_s.at[zp], r.q.at[z], ss.aq.at[0], rr.aq.at[0], to)
    r.q[z] = r.q_s[z]
    loads[1].wait()
    half = pl.ds(pl.multiple_of(128 * c, 128), 128)
    for i in range(1, 4):
        ym, to = ypeer(i)
        push(r.wfull.at[mp, half, :], r.wfull.at[mp, half, :], ss.wf.at[0], rr.wf.at[0], to)
    r.vt1[64:80, :] = jnp.ones((16, 1024), bf16)
    ends = doc_ends(r.lengths)
    feature = lax.broadcasted_iota(jnp.int32, (64, 256), 0)
    loads[2].wait()
    mine = pl.ds(pl.multiple_of(256 * mp, 256), 256)
    r.placer[...] = slot_matrix(r.chosen[...])
    r.cotq_s[...] = dot(r.placer[...], r.cot[:, mine]).astype(bf16).reshape(EX, 16, 256)
    r.cotq[mp, ex] = r.cotq_s[ex]
    arrive(r.kvt.at[0, lax.rem(z + 3, 4)], rr.az.at[0])
    own_piece(1)
    arrive(r.kvt.at[0, lax.rem(z + 1, 4)], rr.az.at[2])
    own_piece(3)
    from_sides(0)
    arrive(r.kvt.at[0, lax.rem(z + 2, 4)], rr.az.at[1])
    own_piece(2)
    zp, to = zpeer(2)
    push(r.normed, r.nall.at[z], ss.na.at[0], rr.na.at[0], to)
    r.nall[z] = r.normed[...]
    arrive(r.q.at[0:3], rr.aq.at[0])
    for b in range(4):
        docs = doc_row(ends, (b * 8 + j) * 256, 256)
        r.qaug[b, 0:64] = r.q[b]
        r.qaug[b, 64:128] = jnp.where(feature == docs, 0.0, negative_fill).astype(bf16)
        r.peak[b] = jnp.full((1, 256), negative_fill, f32)
        r.acc[b] = jnp.zeros((80, 256), f32)

    def load_keys(slot, jp):
        for b in range(4):
            docs = doc_row(ends, (b * 8 + jp) * 256, 256)
            hot = (feature == docs).astype(f32).astype(bf16)
            r.kaug[256 * b:256 * b + 256, :] = transposed(
                jnp.concatenate([r.kvt[slot, b, 0:64], hot], axis=0))

    def scores(b, n, causal):
        s = dot(r.kaug[0:n, :], r.qaug[b])
        if causal:
            rows = lax.broadcasted_iota(jnp.int32, (n, 256), 0)
            cols = lax.broadcasted_iota(jnp.int32, (n, 256), 1)
            s = jnp.where(rows - 256 * b <= cols, s, negative_fill)
        return s

    def load_chunk(slot, jp):
        load_keys(slot, jp)
        for b in range(4):
            r.vt1[0:64, 256 * b:256 * b + 256] = r.kvt[slot, b, 64:128]

    def forward(tiles, causal):
        def gather(b, n, p, factor):
            r.acc[b] = r.acc[b] * factor + dot(r.vt1[:, 0:n], p)

        held = None
        for b, n in tiles:
            s = scores(b, n, causal)
            if held is not None:
                gather(*held)
            old = r.peak[b]
            new = jnp.maximum(old, jnp.max(s, axis=0, keepdims=True))
            held = (b, n, jnp.exp(s - new).astype(bf16), jnp.exp(old - new))
            r.peak[b] = new
        gather(*held)

    load_chunk(0, j)
    forward([(b, 256 * b + 256) for b in (3, 2, 1, 0)], True)

    def chunk(i, carry):
        u = i // 2
        side = ((u + 1) // 2) % 2
        xp = (x + d * (2 * (i % 2) - 1) * side + 2 * (u // 3) + 8) % 4
        jp = xp * 2 + (c + (1 - side) * (i % 2) + side * (u // 2)) % 2

        @pl.when(i == 1)
        def _():
            from_sides(1)
            from_far(0)
            came_whole(1)

        @pl.when(i == 2)
        def _():
            from_sides(3)
            from_far(1)
            from_sides(2)

        @pl.when(i == 3)
        def _():
            from_far(3)

        @pl.when(i == 4)
        def _():
            from_far(2)
            came_whole(4)
            to_all(lambda to: r.cotq_s.at[to], r.cotq.at[mp, ex], "co")

        @pl.when(i == 5)
        def _():
            came_whole(5)
            arrive(r.wfull.at[0:3, 0:128, :], rr.wf.at[0])
            for i in range(1, 4):
                ym, to = ypeer(4 - i)
                remote(
                    r.wfull.at[ym, half, :], r.wfull.at[ym, half, :], ss.wd.at[0], rr.wd.at[0], sib).start()

        @pl.when(i == 7)
        def _():
            came_whole(7)

        load_chunk(i, jp)

        @pl.when(jp < j)
        def _():
            forward([(b, 256 * b + 256) for b in (3, 2, 1, 0)], False)

        @pl.when(jp > j)
        def _():
            forward([(b, 256 * b) for b in (3, 2, 1)], False)

        return carry

    lax.fori_loop(1, 8, chunk, 0)
    for b in range(4):
        total = r.acc[b, 64:65]
        ot = r.acc[b, 0:64] / total
        r.ot[b] = ot
        r.lse[b] = r.peak[b] + jnp.log(total)
        r.o_s[b] = ot.astype(bf16)
    for i in (1, 3, 2):
        zp, to = zpeer(i)
        push(r.o_s.at[zp], r.att.at[mp, z], ss.oz.at[0], rr.oz.at[i - 1], to)
    r.att[mp, z] = r.o_s[z]
    def normed_half(part):
        rows = pl.ds(128 * part, 128)
        for i in (1, 3):
            zp, to = zpeer(i)
            push(
                r.normed.at[rows, :], r.nall.at[z, rows, :], ss.na.at[0],
                rr.na.at[0], to)

    def attended_piece(k):
        zq = lax.rem(z + 4 - k, 4)
        for i in (1, 3, 2):
            ym, to = ypeer(i)
            push(
                r.att.at[mp, zq], r.att.at[mp, zq], ss.oy.at[0], rr.oy.at[0], to)

    attended_piece(0)
    for k in (1, 3, 2):
        arrive(r.att.at[mp, lax.rem(z + 4 - k, 4)], rr.oz.at[k - 1])
        attended_piece(k)
    normed_half(0)
    arrive(r.cotq.at[0, 0:31], rr.co.at[0])
    arrive(r.wfull.at[0:3, 0:128, :], rr.wd.at[0])
    arrive(r.att.at[0:3], rr.oy.at[0])
    for i in (1, 3, 2):
        ym, to = ypeer(i)
        push(r.cotq.at[mp], r.cotq.at[mp], ss.cy.at[0], rr.cy.at[0], to)
    def geometry(i):
        p = i // 2
        w = p + (p // 2) * (1 - 2 * (p % 2))
        g = (2 + d * w + 4) % 4
        flip = 1 - i % 2
        odd = g % 2
        slot = odd * (2 + g // 2 + 2 * flip) + (1 - odd) * (3 * g + flip)
        xp = (x - d * g + 8) % 4
        return slot, xp, xp * 2 + (c + flip) % 2

    def softmax(i, carry):
        slot, _, jp = geometry(i)
        load_keys(slot, jp)

        def keep(tiles):
            for b, n in tiles:
                r.weights[i, 0:n, 256 * b:256 * b + 256] = jnp.exp(scores(b, n, False) - r.lse[b]).astype(bf16)

        @pl.when(jp < j)
        def _():
            keep([(b, 256 * b + 256) for b in (3, 2, 1, 0)])

        @pl.when(jp > j)
        def _():
            keep([(b, 256 * b) for b in (3, 2, 1)])

        return carry

    value = r.tokens[...].astype(f32) + dot(r.att[...].reshape(1024, 256), r.wfull[...].reshape(1024, 1024), 0, 0)
    r.resid[...] = value
    for k in range(4):
        @pl.when(mp == k)
        def _():
            r.rescol[...] = value[:, 256 * k:256 * k + 256]
    unit, _ = norm_parts(value)
    normed = (unit * r.gain2[...]).astype(bf16)
    for step in (1, 3, 2, 0):
        plane = lax.rem(z + step, 4)
        r.slots[pl.ds(8 * plane, 8)] = dot(
            r.placer[pl.ds(pl.multiple_of(128 * plane, 128), 128), :], normed).astype(bf16).reshape(8, 16, 1024)

        def dispatch(k, carry):
            to = plane * 8 + lax.rem(j + k, 8)
            remote(
                r.slots.at[to], r.slots.at[32 + ex], ss.di.at[0], rr.di.at[0],
                (to, mp)).start()
            return carry

        lax.fori_loop(0 if step else 1, 8, dispatch, 0)
    r.slots[32 + ex] = r.slots[ex]
    lax.fori_loop(4, 7, softmax, 0)
    loads[3].wait()
    arrive(r.cotq.at[0:3], rr.cy.at[0])
    for le in range(2):
        rows = jnp.concatenate([one_expert(r.cotq[k], le) for k in range(4)], axis=1)
        r.crows[le] = rows
        r.gh[le] = dot(rows, r.weights[2 + le], 1, 1)
    loads[4].wait()
    arrive(r.slots.at[32:63], rr.di.at[0])
    def expert_rows(le):
        rows = one_expert(r.slots[32:64], le)
        r.xrows[le] = rows
        return dot(rows, r.weights[le])

    def activate(le, pre):
        hidden, slope = gelu_parts(pre)
        r.hid[le] = hidden.astype(bf16)
        gpre = (r.gh[le] * slope).astype(bf16)
        r.gpre[le] = gpre
        return gpre

    def give_back(le, gpre):
        for k in range(4):
            product = dot(gpre, r.weights[le, 256 * k:256 * k + 256, :], 1, 1)
            r.part[le, k] = product[:, 0:128].astype(bf16)
            r.gh[le, :, 128 * k:128 * k + 128] = product[:, 128:256]
        for i in (1, 3, 2):
            ym, to = ypeer(i)
            push(r.part.at[le, ym], r.rs.at[le, i - 1], ss.rs.at[0], rr.rs.at[0], to)

    first, second = expert_rows(0), expert_rows(1)
    gpre = activate(0, first)
    give_back(0, gpre)
    give_back(1, activate(1, second))
    r.wide_s[...] = both_experts(r.gh[0, :, 0:512], r.gh[1, :, 0:512])
    to_all(lambda to: r.wide_s.at[to], r.wide.at[ex], "bc")
    r.wide[ex] = r.wide_s[ex]
    first = dot(r.hid[0], r.weights[2])
    r.branch[...] = both_experts(first, dot(r.hid[1], r.weights[3]))
    lax.fori_loop(0, 4, softmax, 0)
    arrive(r.rs, rr.rs.at[0])
    sums = []
    for le in range(2):
        total = r.part[le, mp].astype(f32)
        for i in range(3):
            total = total + r.rs[le, i].astype(f32)
        sums.append(total)
    r.back_s[...] = both_experts(sums[0], sums[1])
    to_all(lambda to: r.back_s.at[to], r.back.at[ex], "ba")
    r.back[ex] = r.back_s[ex]
    arrive(r.wide.at[0:31], rr.bc.at[0])
    rows = dot(r.placer[...], r.wide[...].reshape(512, 512), 0, 0).astype(bf16)
    for k in range(4):
        r.gb[k] = rows[:, 128 * k:128 * k + 128]
    for i in (1, 3, 2):
        ym, to = ypeer(i)
        push(r.gb.at[ym], r.gbr.at[i - 1], ss.gb.at[0], rr.gb.at[0], to)
    arrive(r.back.at[0:31], rr.ba.at[0])
    r.gn[0, mp] = dot(r.placer[...], r.back[...].reshape(512, 128), 0, 0).astype(bf16)
    for i in (1, 3, 2):
        ym, to = ypeer(i)
        push(r.gn.at[0, mp], r.gn.at[0, mp], ss.gy.at[0], rr.gy.at[0], to)
    normed_half(1)
    total = r.gb[mp].astype(f32)
    arrive(r.gbr, rr.gb.at[0])
    for i in range(3):
        total = total + r.gbr[i].astype(f32)
    r.gn[1, mp] = total.astype(bf16)
    for i in (1, 3, 2):
        ym, to = ypeer(i)
        push(r.gn.at[1, mp], r.gn.at[1, mp], ss.gy.at[0], rr.gy.at[0], to)
    unit, inverse = norm_parts(r.resid[...])
    left(r.slots.at[0:31], ss.di.at[0])
    load_keys(0, j)
    for b in (3, 2, 1, 0):
        n = 256 * b + 256
        own = jnp.exp(scores(b, n, True) - r.lse[b]).astype(bf16)
        r.slots[0:n // 16, :, 256 * b:256 * b + 256] = own.reshape(n // 16, 16, 256)
    arrive(r.gn.at[:, 0:3], rr.gy.at[0])
    grad = jnp.concatenate([r.gn[k % 2, k // 2] for k in range(8)], axis=1).astype(f32)
    grad_in, ggrad = norm_back(grad, r.gain2[...], unit, inverse)
    r.smallf[ex] = ggrad
    gres = r.cot[...].astype(f32) + grad_in
    r.gres[...] = gres
    low = gres.astype(bf16)
    r.dheads[...] = dot(r.wfull[mp], low, 1, 1).astype(bf16).reshape(4, 64, 256)
    for i in (1, 3, 2):
        zp, to = zpeer(i)
        push(r.dheads.at[zp], r.dob.at[z], ss.dz.at[0], rr.dz.at[0], to)
    r.dob[z] = r.dheads[z]
    wgrad = dot(r.att[mp].reshape(256, 256), low).astype(bf16)
    r.wgp[0] = wgrad[:, 0:512].reshape(4, 4, 16, 512)
    r.wgp[1] = wgrad[:, 512:1024].reshape(4, 4, 16, 512)
    push(r.wgp.at[1 - c], r.wgs, ss.wg.at[0], rr.wg.at[0], sib)
    for i in range(1, 4):
        ym, to = ypeer(i)
        push(
            r.branch.at[:, :, pl.ds(pl.multiple_of(256 * ym, 256), 256)], r.brs.at[i - 1],
            ss.br.at[0], rr.br.at[0], to)
    zero = jnp.zeros((64, 256), bf16)
    to_all(lambda to: r.smallf.at[ex], r.smallf.at[ex], "sf")
    arrive(r.dob.at[0:3], rr.dz.at[0])
    arrive(r.wgs, rr.wg.at[0])
    r.wgq[...] = (r.wgp[c].astype(f32) + r.wgs[...].astype(f32)).astype(bf16)
    for i in (1, 3, 2):
        zp, to = zpeer(i)
        push(r.wgq.at[zp], r.wgz.at[i - 1], ss.wz.at[0], rr.wz.at[0], to)
    for b in range(4):
        r.dopad[b, 0:64] = zero
        r.dopad[b, 64:128] = r.dob[b]
        r.qd[b, 0:256] = transposed(jnp.concatenate([r.q[b], zero], axis=0))
        r.qd[b, 256:512] = transposed(jnp.concatenate([zero, r.dob[b]], axis=0))
        r.delta[b] = jnp.sum(r.dob[b].astype(f32) * r.ot[b], axis=0, keepdims=True)
        r.dq[b] = jnp.zeros((64, 256), f32)

    def load_back(slot):
        for b in range(4):
            r.kvn[256 * b:256 * b + 256, :] = transposed(r.kvt[slot, b])
            r.kt[:, 256 * b:256 * b + 256] = r.kvt[slot, b, 0:64]

    def backward(tiles, weights):
        def gather(b, n, ds, p):
            added = dot(ds, r.qd[b, 0:256]) + dot(p, r.qd[b, 256:512])
            if b == 3:
                r.dkv[0:n] = added
            else:
                r.dkv[0:n] = r.dkv[0:n] + added
            r.dq[b] = r.dq[b] + dot(r.kt[:, 0:n], ds)

        held = None
        for b, n in tiles:
            dp = dot(r.kvn[0:n, :], r.dopad[b])
            p = weights(b, n)
            if held is not None:
                gather(*held)
            held = (b, n, (p * (dp - r.delta[b])).astype(bf16), p.astype(bf16))
        gather(*held)

    def back_chunk(i, carry):
        slot, xp, jp = geometry(i)
        p = i // 2
        load_back(slot)

        def kept(b, n):
            return r.weights[i, 0:n, 256 * b:256 * b + 256]

        @pl.when(jp < j)
        def _():
            backward([(b, 256 * b + 256) for b in (3, 2, 1, 0)], kept)

        @pl.when(jp > j)
        def _():
            r.dkv[768:1024] = jnp.zeros((256, 128), f32)
            backward([(b, 256 * b) for b in (3, 2, 1)], kept)

        @pl.when(i % 2 == 0)
        def _():
            r.sb[p] = r.dkv[...].astype(bf16)
            remote(r.sb.at[p], r.sr.at[p], ss.sb.at[0], rr.sb.at[p], sib).start()

        @pl.when(i % 2 == 1)
        def _():
            arrive(r.sr.at[p], rr.sb.at[p])
            r.xs[p] = (r.dkv[...] + r.sr[p].astype(f32)).astype(bf16)

            @pl.when(p == 0)
            def _():
                remote(r.xs.at[0], r.xr.at[0], ss.xs.at[0], rr.xs.at[0], ahead).start()

            @pl.when(p == 2 - c)
            def _():
                remote(r.xs.at[p], r.xr.at[1], ss.xs.at[0], rr.xs.at[1], behind).start()

            @pl.when(p == 2)
            def _():
                arrive(r.xr.at[0], rr.xs.at[0])
                r.xs[3] = (r.xs[1 + c].astype(f32) + r.xr[0].astype(f32)).astype(bf16)
                remote(r.xs.at[3], r.xr.at[2], ss.xs.at[0], rr.xs.at[2], ahead).start()

        @pl.when(i == 2)
        def _():
            arrive(r.wgz, rr.wz.at[0])
            total = r.wgq[z].astype(f32)
            for k in range(3):
                total = total + r.wgz[k].astype(f32)
            r.wgx[...] = total.astype(bf16)
            for k in (1, 3, 2):
                xq, to = xpeer(k)
                remote(r.wgx.at[xq], r.wgr.at[k - 1], ss.wx.at[0], rr.wx.at[0], to).start()

        @pl.when(i == 6)
        def _():
            total = r.branch[:, :, mine].astype(f32)
            arrive(r.brs, rr.br.at[0])
            for k in range(3):
                total = total + r.brs[k].astype(f32)
            r.bs[...] = total.astype(bf16)

        @pl.when(i == 5)
        def _():
            total = r.wgx[x].astype(f32)
            arrive(r.wgr, rr.wx.at[0])
            for k in range(3):
                total = total + r.wgr[k].astype(f32)
            r.wgf[c, z, x] = total.astype(bf16)
            for k in (1, 3, 2):
                _, to = xpeer(k)
                remote(r.wgf.at[c, z, x], r.wgf.at[c, z, x], ss.wa.at[0], rr.wa.at[0], to).start()

        return carry

    lax.fori_loop(0, 7, back_chunk, 0)
    load_back(0)
    backward(
        [(b, 256 * b + 256) for b in (3, 2, 1, 0)],
        lambda b, n: r.slots[0:n // 16, :, 256 * b:256 * b + 256].reshape(n, 256))
    for b in range(4):
        r.zs[b, 0:64] = (r.dq[b] * HEAD_DIM ** (-0.5)).astype(bf16)
    for i in (1, 3, 2):
        zp, to = zpeer(i)
        push(r.zs.at[zp, 0:64], r.zr.at[z, 0:64], ss.zd.at[0], rr.zd.at[0], to)
    arrive(r.nall.at[0:3], rr.na.at[0])

    def weight_part(first, last, pieces, name):
        wt = dot(r.zs[0, first:last], r.nall[0])
        for b in range(1, 4):
            wt = wt + dot(r.zs[b, first:last], r.nall[b])
        wt = wt.astype(bf16)
        for k in range(8):
            pieces[0][k] = wt[:, 128 * k:128 * k + 128]
        for i in range(1, 8):
            jt = lax.rem(j + i, 8)
            push(
                pieces[0].at[jt], pieces[1].at[i - 1], getattr(ss, name).at[0], getattr(rr, name).at[0],
                (z * 8 + jt, mp))

    def weight_sum(pieces, name):
        total = pieces[0][j].astype(f32)
        arrive(pieces[1], getattr(rr, name).at[0])
        for i in range(7):
            total = total + pieces[1][i].astype(f32)
        return total.astype(bf16)

    weight_part(0, 64, (r.wpq, r.wrq), "wp")
    r.resid[...] = norm_parts(r.tokens[...].astype(f32))[0]
    arrive(r.sr.at[3], rr.sb.at[3])
    total = r.dkv[...] + r.sr[3].astype(f32)
    for k in (1, 2):
        arrive(r.xr.at[k], rr.xs.at[k])
        total = total + r.xr[k].astype(f32)
    low = total.astype(bf16)
    for b in range(4):
        r.zs[b, 64:192] = transposed(low[256 * b:256 * b + 256])
    for i in (1, 3, 2):
        zp, to = zpeer(i)
        push(r.zs.at[zp, 64:192], r.zr.at[z, 64:192], ss.zq.at[0], rr.zq.at[0], to)
    r.zr[z] = r.zs[z]
    weight_part(64, 192, (r.wpk, r.wrk), "wk")
    r.pieces[0, c, z, x] = weight_sum((r.wpq, r.wrq), "wp")
    gather_first(0)
    arrive(r.wgf.at[0, 0, 0:3], rr.wa.at[0])
    for k in (1, 3, 2):
        _, to = zpeer(k)
        push(r.wgf.at[c, z], r.wgf.at[c, z], ss.wb.at[0], rr.wb.at[0], to)

    def heads(first):
        return transposed(jnp.concatenate([r.zr[h, first:first + 64] for h in range(4)], axis=0))

    arrive(r.zr.at[0:3, 0:64], rr.zd.at[0])
    part = dot(heads(0), r.wqkv[0], 1, 1)
    arrive(r.zr.at[0:3, 64:192], rr.zq.at[0])
    part = part + dot(heads(64), r.wqkv[1], 1, 1) + dot(heads(128), r.wqkv[2], 1, 1)
    r.gnp[...] = part.astype(bf16).reshape(4, 64, 1024)
    one_gain = jnp.sum(part * r.resid[...], axis=0, keepdims=True)
    r.small[...] = one_gain
    for i in (1, 3, 2):
        ym, to = ypeer(i)
        push(r.small, r.smally.at[i - 1], ss.sy.at[0], rr.sy.at[0], to)
    for first in (0, 32):
        rows = pl.ds(first, 32)
        for i in (1, 3, 2):
            ym, to = ypeer(i)
            push(r.gnp.at[ym, rows, :], r.ry.at[i - 1, rows, :], ss.ry.at[0], rr.ry.at[first // 32], to)
    both = weight_sum((r.wpk, r.wrk), "wk")
    r.pieces[1, c, z, x] = both[0:64]
    r.pieces[2, c, z, x] = both[64:128]
    gather_first(1)
    gather_first(2)
    gather_second(0)
    arrive(r.wgf.at[0, 0:3], rr.wb.at[0])
    push(r.wgf.at[c], r.wgf.at[c], ss.wc.at[0], rr.wc.at[0], sib)
    def norm_rows(first):
        grad = r.gnp[mp, first:first + 32].astype(f32)
        arrive(r.ry.at[:, first:first + 32], rr.ry.at[first // 32])
        for i in range(3):
            grad = grad + r.ry[i, first:first + 32].astype(f32)
        here = pl.ds(pl.multiple_of(64 * mp + first, 32), 32)
        unit, inverse = norm_parts(r.tokens[here, :].astype(f32))
        grad_in, _ = norm_back(grad, r.gain1[...], unit, inverse)
        r.igrad[here, :] = (r.gres[here, :] + grad_in).astype(bf16)
        for i in (1, 3, 2):
            ym, to = ypeer(i)
            push(r.igrad.at[here, :], r.igrad.at[here, :], ss.ay.at[0], rr.ay.at[0], to)

    gather_second(1)
    gather_second(2)
    arrive(r.smally, rr.sy.at[0])
    for i in range(3):
        one_gain = one_gain + r.smally[i]
    r.smalle[ex] = one_gain
    to_all(lambda to: r.smalle.at[ex], r.smalle.at[ex], "se")
    norm_rows(0)
    gather_third(0)
    norm_rows(32)
    to_all(lambda to: r.bs.at[to], r.bret.at[ex], "bb")
    r.bret[ex] = r.bs[ex]
    arrive(r.wgf.at[1 - c], rr.wc.at[0])
    for k in range(16):
        for core in range(2):
            r.wout_out[16 * k:16 * k + 16, 512 * core:512 * core + 512] = r.wgf[core, k // 4, k % 4]
    gather_third(1)
    gather_third(2)
    arrive(r.smalle.at[0:31], rr.se.at[0])
    arrive(r.smallf.at[0:31], rr.sf.at[0])
    r.gain1_out[...] = jnp.sum(r.smalle[...], axis=0)
    r.gain2_out[...] = jnp.sum(r.smallf[...], axis=0)
    for k in range(3):
        arrive(r.pieces.at[k, 1 - c], rr.pc.at[k])
        for row in range(8):
            block = jnp.concatenate([r.pieces[k, row % 2, h, row // 2] for h in range(4)], axis=0)
            r.qkv_out[k, 128 * row:128 * row + 128] = transposed(block)
    arrive(r.bret.at[0:31], rr.bb.at[0])
    rows = dot(r.placer[...], r.bret[...].reshape(512, 256), 0, 0)
    r.out[...] = (r.rescol[...] + rows).astype(bf16)
    arrive(r.igrad.at[0:192, :], rr.ay.at[0])
    sent = {
        "az": r.kv_s.at[0:3], "aq": r.q_s.at[0:3], "ag": r.kvt.at[0:7], "wf": r.wfull.at[0:3, 0:128, :],
        "wd": r.wfull.at[0:3, 0:128, :], "co": r.cotq_s.at[0:31], "cy": r.cotq.at[0:3], "na": r.nall.at[0:3],
        "oz": r.o_s.at[0:3], "oy": r.att.at[0:3], "rs": r.rs, "ba": r.back_s.at[0:31],
        "bc": r.wide_s.at[0:31], "gb": r.gb.at[0:3], "gy": r.gn.at[:, 0:3], "dz": r.dheads.at[0:3], "br": r.brs,
        "bb": r.bs.at[0:31], "sb": r.sb, "xs": r.xs.at[0:3], "wg": r.wgs, "wz": r.wgq.at[0:3], "wx": r.wgr,
        "wa": r.wgr, "wb": r.wgf.at[0, 0:3], "wc": r.wgf.at[0], "zd": r.zs.at[0:3, 0:64], "zq": r.zs.at[0:3, 64:192],
        "wp": r.wrq, "wk": r.wrk, "ry": r.ry, "ay": r.ry, "sy": r.smally, "se": r.smalle.at[0:31],
        "sf": r.smallf.at[0:31],
    }
    for name, ref in sent.items():
        left(ref, getattr(ss, name).at[0])
    for part in range(3):
        left(r.pieces.at[0, 0, 0, 0:3], ss.pa.at[part])
        left(r.pieces.at[0, 0, 0:3], ss.pb.at[part])
        left(r.pieces.at[0, 0], ss.pc.at[part])


def layer(*args):
    return pl.pallas_call(
        layer_kernel,
        out_shape=[pltpu.VMEM(s, t) for s, t in OUTS.values()],
        in_specs=[SM, VM, VM, VM, VM, ANY, ANY, ANY, ANY, ANY],
        out_specs=[VM] * len(OUTS),
        scratch_shapes=[pltpu.VMEM(s, t) for s, t in BUFFERS.values()]
        + [DMA(s) for group in (LOCAL, SENT, TAKEN) for s in group.values()],
        name="layer",
        compiler_params=pltpu.CompilerParams(
            collective_id=0, has_side_effects=True, vmem_limit_bytes=VMEM_BYTES),
    )(*args)


def finish_kernel(x, gpre, hid, cots, qkv, wout, out, igrad, gain1, gain2, *refs):
    in_grad, out_grad, qkv_o, wout_o, out_o, igrad_o, gain1_o, gain2_o = refs[:8]
    in_buf, out_buf, qkv_buf, wout_buf, store, rest = refs[8:]
    stores = []

    def put(src, dst, sem):
        copy = pltpu.make_async_copy(src, dst, sem)
        copy.start()
        stores.append(copy)

    for k, (left, right, buf, result) in enumerate(((x, gpre, in_buf, in_grad), (hid, cots, out_buf, out_grad))):
        for e in range(2):
            for t in range(4):
                rows = pl.ds(256 * t, 256)
                buf[e, rows, :] = dot(left[e, :, 256 * t:256 * t + 256], right[e], 0, 0)
                put(buf.at[e, rows, :], result.at[e, rows, :], store.at[8 * k + 4 * e + t])
    qkv_buf[...] = qkv[...].astype(f32)
    wout_buf[...] = wout[...].astype(f32)
    plain = ((qkv_buf, qkv_o), (wout_buf, wout_o), (out, out_o), (igrad, igrad_o), (gain1, gain1_o), (gain2, gain2_o))
    for k, (src, dst) in enumerate(plain):
        put(src, dst, rest.at[k])
    for copy in stores:
        copy.wait()


def finish(*args):
    big = ((2, 1024, 1024), f32)
    outs = [big, big, ((3, 1024, 256), f32), ((256, 1024), f32), ((256, 256), bf16), ((256, 1024), bf16)]
    outs += [((1, 1024), f32)] * 2
    return pl.pallas_call(
        finish_kernel,
        out_shape=[jax.ShapeDtypeStruct(s, t) for s, t in outs],
        in_specs=[VM] * 10,
        out_specs=[ANY] * 8,
        scratch_shapes=[pltpu.VMEM(s, t) for s, t in outs[:4]] + [DMA((16,)), DMA((6,))],
        name="finish",
        compiler_params=pltpu.CompilerParams(vmem_limit_bytes=36 << 20),
        cost_estimate=pl.CostEstimate(flops=2 * 2 * 2 * 256 * 1024 * 1024, bytes_accessed=28 << 20, transcendentals=0),
    )(*args)


def on_device(
    tokens, hash_ids, lengths, norm1_gain, qkv_weight, out_weight, norm2_gain, expert_in, expert_out, cotangent,
):
    x, cots, hid, gpre, out, igrad, gain1, gain2, qkv, wout = layer(
        lengths, tokens, norm1_gain.reshape(1, 1024), norm2_gain.reshape(1, 1024), hash_ids.reshape(1, 256),
        jnp.transpose(qkv_weight, (1, 0, 2)), out_weight, cotangent, expert_in, expert_out)
    in_grad, out_grad, qkv, wout, out, igrad, gain1, gain2 = finish(
        x, gpre, hid, cots, qkv, wout, out, igrad, gain1, gain2)
    return out, igrad, gain1.reshape(1024), jnp.transpose(qkv, (1, 0, 2)), wout, gain2.reshape(1024), in_grad, out_grad


def solution(mesh):
    placed = (
        P("ex", None), P("ex", None), P(), P(), P(None, None, "mp"), P("mp", None), P(),
        P("ex", None, "mp"), P("ex", "mp", None), P("ex", None),
    )
    return jax.shard_map(
        on_device,
        mesh=mesh,
        in_specs=placed,
        out_specs=(
            P("ex", "mp"), P("ex", None), P(), P(None, None, "mp"), P("mp", None), P(),
            P("ex", None, "mp"), P("ex", "mp", None),
        ),
        check_vma=False,
    )
```

```python
import functools

import jax
import jax.numpy as jnp
from jax import lax
from jax.experimental import pallas as pl
from jax.experimental.pallas import tpu as pltpu
from jax.sharding import PartitionSpec as P

HEAD_DIM = 64
epsilon = 1e-05
negative_fill = -1e30
MESH = pl.DeviceIdType.MESH
bf16, f32 = jnp.bfloat16, jnp.float32
EX, MP = 32, 4
VMEM_BYTES = 56 << 20


def dot(a, b, ca=1, cb=0):
    return lax.dot_general(a, b, (((ca,), (cb,)), ((), ())), preferred_element_type=f32)


def place():
    ex, mp = lax.axis_index("ex"), lax.axis_index("mp")
    z, x, c = ex // 8, (ex // 2) % 4, ex % 2
    return ex, mp, z, x, c


def send(src, dst, ssem, rsem, device):
    copy = pltpu.make_async_remote_copy(
        src_ref=src, dst_ref=dst, send_sem=ssem, recv_sem=rsem, device_id=device, device_id_type=MESH
    )
    copy.start()
    return copy


def greet(ex, mp):
    bar = pltpu.get_barrier_semaphore()

    def one(d, carry):
        pl.semaphore_signal(bar, inc=1, device_id=(lax.rem(ex + d, EX), mp), device_id_type=MESH)
        return carry

    lax.fori_loop(1, EX, one, 0)
    for d in range(1, MP):
        pl.semaphore_signal(bar, inc=1, device_id=(ex, lax.rem(mp + d, MP)), device_id_type=MESH)
    return bar


def greeted(bar):
    pl.semaphore_wait(bar, EX - 1 + MP - 1)


def slot_matrix(chosen_row):
    tok = chosen_row.shape[1]
    experts = lax.broadcasted_iota(jnp.int32, (64, tok), 0)
    hot = (experts == chosen_row).astype(f32)
    rows = lax.broadcasted_iota(jnp.int32, (tok, tok), 0)
    cols = lax.broadcasted_iota(jnp.int32, (tok, tok), 1)
    before = (rows < cols).astype(bf16)
    earlier = dot(hot.astype(bf16), before)
    rank = jnp.sum(earlier * hot, axis=0, keepdims=True)
    target = chosen_row * 8 + rank.astype(jnp.int32)
    slots = lax.broadcasted_iota(jnp.int32, (512, tok), 0)
    return (slots == target).astype(f32).astype(bf16)


def doc_row(ends, first, count):
    pos = first + lax.broadcasted_iota(jnp.int32, (1, count), 1)
    row = jnp.zeros((1, count), jnp.int32)
    for end in ends:
        row = row + (pos >= end).astype(jnp.int32)
    return row


def doc_ends(lengths_ref):
    ends, total = [], 0
    for i in range(9):
        total = total + lengths_ref[i]
        ends.append(total)
    return ends


def norm_parts(v):
    mean = jnp.mean(v, axis=-1, keepdims=True)
    centred = v - mean
    inverse = lax.rsqrt(jnp.mean(centred * centred, axis=-1, keepdims=True) + epsilon)
    return centred * inverse, inverse


def transposed(v):
    return v.T


def norm_back(grad_out, gain_row, unit, inverse):
    scaled = grad_out * gain_row
    centred = scaled - jnp.mean(scaled, axis=-1, keepdims=True)
    grad_in = inverse * (centred - unit * jnp.mean(scaled * unit, axis=-1, keepdims=True))
    return grad_in, jnp.sum(grad_out * unit, axis=0, keepdims=True)


def gelu_parts(pre):
    k = 0.7978845608028654
    square = pre * pre
    t = jnp.tanh(k * pre * (1.0 + 0.044715 * square))
    half = 0.5 * (1.0 + t)
    slope = half + 0.5 * pre * (1.0 - t * t) * (k * (1.0 + 3 * 0.044715 * square))
    return pre * half, slope


def one_expert(rows, le):
    wide = rows.astype(f32)
    return wide[:, 8 * le:8 * le + 8].reshape(256, rows.shape[2]).astype(bf16)


def both_experts(first, second):
    width = first.shape[1]
    return jnp.concatenate([first.reshape(32, 8, width), second.reshape(32, 8, width)], axis=1).astype(bf16)


VM = pl.BlockSpec(memory_space=pltpu.VMEM)
SM = pl.BlockSpec(memory_space=pltpu.SMEM)
ANY = pl.BlockSpec(memory_space=pl.ANY)
DMA = pltpu.SemaphoreType.DMA
ROWS = (2, 256, 1024)

ARGS = ["lengths", "tokens", "gain1", "gain2", "chosen", "wqkv_hbm", "wout_hbm", "cot_hbm", "win_hbm", "wex_hbm"]
OUTS = {
    "xrows": (ROWS, bf16), "crows": (ROWS, bf16), "hid": (ROWS, bf16), "gpre": (ROWS, bf16),
    "out": ((256, 256), bf16), "igrad": ((256, 1024), bf16), "gain1_out": ((1, 1024), f32), "gain2_out": ((1, 1024), f32),
    "qkv_out": ((3, 1024, 256), bf16), "wout_out": ((256, 1024), bf16),
}
BUFFERS = {
    "wqkv": ((3, 1024, 256), bf16), "cot": ((256, 1024), bf16),
    "weights": ((7, 1024, 1024), bf16), "placer": ((512, 256), bf16), "normed": ((256, 1024), bf16),
    "nall": ((4, 256, 1024), bf16), "wfull": ((4, 256, 1024), bf16),
    "q_s": ((4, 64, 256), bf16), "kv_s": ((4, 128, 256), bf16), "q": ((4, 64, 256), bf16),
    "kvt": ((8, 4, 128, 256), bf16), "qaug": ((4, 128, 256), bf16), "kaug": ((1024, 128), bf16),
    "vt1": ((80, 1024), bf16), "acc": ((4, 80, 256), f32), "peak": ((4, 1, 256), f32),
    "ot": ((4, 64, 256), f32), "lse": ((4, 1, 256), f32), "o_s": ((4, 64, 256), bf16),
    "att": ((4, 4, 64, 256), bf16), "cotq_s": ((32, 16, 256), bf16), "cotq": ((4, 32, 16, 256), bf16),
    "slots": ((64, 16, 1024), bf16),
    "gh": (ROWS, f32),
    "part": ((2, 4, 256, 128), bf16), "rs": ((2, 3, 256, 128), bf16), "back_s": ((32, 16, 128), bf16),
    "back": ((32, 16, 128), bf16), "wide_s": ((32, 16, 512), bf16), "wide": ((32, 16, 512), bf16),
    "gb": ((4, 256, 128), bf16), "gbr": ((3, 256, 128), bf16), "gn": ((2, 4, 256, 128), bf16), "resid": ((256, 1024), f32),
    "rescol": ((256, 256), f32), "gres": ((256, 1024), f32), "branch": ((32, 16, 1024), bf16),
    "wgp": ((2, 4, 4, 16, 512), bf16), "wgs": ((4, 4, 16, 512), bf16), "wgq": ((4, 4, 16, 512), bf16),
    "wgz": ((3, 4, 16, 512), bf16), "wgx": ((4, 16, 512), bf16), "wgr": ((3, 16, 512), bf16),
    "wgf": ((2, 4, 4, 16, 512), bf16),
    "dheads": ((4, 64, 256), bf16), "dob": ((4, 64, 256), bf16), "brs": ((3, 32, 16, 256), bf16),
    "bs": ((32, 16, 256), bf16), "bz": ((4, 8, 16, 256), bf16), "bret": ((4, 8, 16, 256), bf16), "dopad": ((4, 128, 256), bf16),
    "qd": ((4, 512, 128), bf16), "delta": ((4, 1, 256), f32), "kvn": ((1024, 128), bf16),
    "kt": ((64, 1024), bf16), "dkv": ((1024, 128), f32), "dq": ((4, 64, 256), f32),
    "sb": ((4, 1024, 128), bf16), "sr": ((4, 1024, 128), bf16), "xs": ((4, 1024, 128), bf16),
    "xr": ((3, 1024, 128), bf16), "zs": ((4, 192, 256), bf16), "zr": ((4, 192, 256), bf16),
    "wpq": ((8, 64, 128), bf16), "wrq": ((7, 64, 128), bf16),
    "wpk": ((8, 128, 128), bf16), "wrk": ((7, 128, 128), bf16),
    "pieces": ((3, 2, 4, 4, 64, 128), bf16),
    "gnp": ((4, 64, 1024), bf16), "ry": ((3, 64, 1024), bf16), "small": ((1, 1024), f32),
    "smally": ((3, 1, 1024), f32), "gsum": ((2, 1024), f32), "gz": ((3, 2, 1024), f32), "gps": ((2, 1024), f32), "gp": ((7, 2, 1024), f32),
}
LOCAL = {"load": (5,)}
SENT = dict.fromkeys(
    ("az", "aq", "ag", "wf", "wd", "co", "cy", "na", "oz", "oy", "di", "rs", "ba", "bc", "gb", "gy", "dz", "br", "bb", "sb",
     "xs", "wg", "wz", "wx", "wa", "wb", "wc", "zd", "zq", "wp", "wk", "ry", "ay", "sy", "se", "sf", "bp"),
    (1,))
SENT.update(pa=(3,), pb=(3,), pc=(3,))
TAKEN = dict(SENT, ry=(2,), az=(3,), ag=(16,), oz=(3,), sb=(4,), xs=(3,))


class Refs:
    pass


def layer_kernel(*refs):
    r, ls, ss, rr = Refs(), Refs(), Refs(), Refs()
    names = [(r, k) for k in ARGS + list(OUTS) + list(BUFFERS)] + [(ls, k) for k in LOCAL]
    names += [(ss, k) for k in SENT] + [(rr, k) for k in TAKEN]
    for (group, name), ref in zip(names, refs, strict=True):
        setattr(group, name, ref)
    ex, mp, z, x, c = place()
    d = 1 - 2 * c
    j = x * 2 + c
    chip = ex // 2
    sib = (ex + d, mp)
    ahead = (z * 8 + lax.rem(x + d + 4, 4) * 2 + c, mp)
    behind = (z * 8 + lax.rem(x - d + 4, 4) * 2 + c, mp)

    def zpeer(i):
        zp = lax.rem(z + i, 4)
        return zp, (zp * 8 + j, mp)

    def ypeer(i):
        ym = lax.rem(mp + i, MP)
        return ym, (ex, ym)

    def xpeer(i):
        xq = lax.rem(x + i, 4)
        return xq, (z * 8 + xq * 2 + c, mp)

    def remote(src, dst, ssem, rsem, device):
        return pltpu.make_async_remote_copy(
            src_ref=src, dst_ref=dst, send_sem=ssem, recv_sem=rsem, device_id=device, device_id_type=MESH)

    def push(src, dst, ssem, rsem, device):
        remote(src, dst, ssem, rsem, device).start()

    def arrive(dst, rsem):
        remote(dst, dst, rsem, rsem, sib).wait_recv()

    def left(src, ssem):
        remote(src, src, ssem, ssem, sib).wait_send()

    def to_all(src_of, dst, name):
        def one(k, carry):
            to = lax.rem(ex + k, EX)
            remote(src_of(to), dst, getattr(ss, name).at[0], getattr(rr, name).at[0], (to, mp)).start()
            return carry

        lax.fori_loop(1, EX, one, 0)

    def gather_first(part):
        for i in (1, 3, 2):
            _, to = xpeer(i) if part == 1 else zpeer(i)
            own = r.pieces.at[part, c, z, x]
            push(own, own, ss.pa.at[part], rr.pa.at[part], to)

    def gather_second(part):
        arrive(r.pieces.at[part, 0, 0, 0:3], rr.pa.at[part])
        row = r.pieces.at[part, c, z] if part == 1 else r.pieces.at[part, c, :, x]
        for i in (1, 3, 2):
            _, to = zpeer(i) if part == 1 else xpeer(i)
            push(row, row, ss.pb.at[part], rr.pb.at[part], to)

    def gather_third(part):
        arrive(r.pieces.at[part, 0, 0:3], rr.pb.at[part])
        push(r.pieces.at[part, c], r.pieces.at[part, c], ss.pc.at[part], rr.pc.at[part], sib)

    bar = greet(ex, mp)
    loads = [
        pltpu.make_async_copy(src, dst, ls.load.at[i])
        for i, (src, dst) in enumerate([
            (r.wqkv_hbm, r.wqkv), (r.wout_hbm, r.wfull.at[mp]), (r.cot_hbm, r.cot), (r.wex_hbm, r.weights.at[2:4]),
            (r.win_hbm, r.weights.at[0:2])])
    ]
    for copy in loads:
        copy.start()
    unit, _ = norm_parts(r.tokens[...].astype(f32))
    normed = (unit * r.gain1[...]).astype(bf16)
    r.normed[...] = normed
    loads[0].wait()
    kt = transposed(dot(normed, r.wqkv[1]).astype(bf16))
    vt = transposed(dot(normed, r.wqkv[2]).astype(bf16))
    for h in range(4):
        r.kv_s[h, 0:64] = kt[64 * h:64 * h + 64]
        r.kv_s[h, 64:128] = vt[64 * h:64 * h + 64]
    greeted(bar)
    for i in (1, 3, 2):
        zp, to = zpeer(i)
        push(r.kv_s.at[zp], r.kvt.at[0, z], ss.az.at[0], rr.az.at[i - 1], to)
    r.kvt[0, z] = r.kv_s[z]

    def own_piece(k):
        zq = lax.rem(z + 4 - k, 4)
        remote(r.kvt.at[0, zq], r.kvt.at[2, zq], ss.ag.at[0], rr.ag.at[4 + k], ahead).start()
        remote(r.kvt.at[0, zq], r.kvt.at[3, zq], ss.ag.at[0], rr.ag.at[8 + k], behind).start()
        remote(r.kvt.at[0, zq], r.kvt.at[1, zq], ss.ag.at[0], rr.ag.at[0], sib).start()

    def came(slot, k):
        arrive(r.kvt.at[slot, lax.rem(z + 4 - k, 4)], rr.ag.at[{2: 4, 3: 8, 6: 12}[slot] + k])

    def came_whole(slot):
        arrive(r.kvt.at[slot], rr.ag.at[{1: 0, 4: 1, 5: 2, 7: 3}[slot]])

    def from_sides(k):
        zq = lax.rem(z + 4 - k, 4)
        came(2, k)
        remote(r.kvt.at[2, zq], r.kvt.at[6, zq], ss.ag.at[0], rr.ag.at[12 + k], ahead).start()
        remote(r.kvt.at[2, zq], r.kvt.at[5, zq], ss.ag.at[0], rr.ag.at[2], sib).start()
        came(3, k)
        remote(r.kvt.at[3, zq], r.kvt.at[4, zq], ss.ag.at[0], rr.ag.at[1], sib).start()

    def from_far(k):
        zq = lax.rem(z + 4 - k, 4)
        came(6, k)
        remote(r.kvt.at[6, zq], r.kvt.at[7, zq], ss.ag.at[0], rr.ag.at[3], sib).start()

    own_piece(0)
    qt = transposed((dot(normed, r.wqkv[0]).astype(bf16) * HEAD_DIM ** (-0.5)).astype(bf16))
    for h in range(4):
        r.q_s[h] = qt[64 * h:64 * h + 64]
    for i in (1, 3, 2):
        zp, to = zpeer(i)
        push(r.q_s.at[zp], r.q.at[z], ss.aq.at[0], rr.aq.at[0], to)
    r.q[z] = r.q_s[z]
    loads[1].wait()
    half = pl.ds(pl.multiple_of(128 * c, 128), 128)
    for i in range(1, 4):
        ym, to = ypeer(i)
        push(r.wfull.at[mp, half, :], r.wfull.at[mp, half, :], ss.wf.at[0], rr.wf.at[0], to)
    r.vt1[64:80, :] = jnp.ones((16, 1024), bf16)
    ends = doc_ends(r.lengths)
    feature = lax.broadcasted_iota(jnp.int32, (64, 256), 0)
    loads[2].wait()
    mine = pl.ds(pl.multiple_of(256 * mp, 256), 256)
    r.placer[...] = slot_matrix(r.chosen[...])
    r.cotq_s[...] = dot(r.placer[...], r.cot[:, mine]).astype(bf16).reshape(EX, 16, 256)
    r.cotq[mp, ex] = r.cotq_s[ex]
    arrive(r.kvt.at[0, lax.rem(z + 3, 4)], rr.az.at[0])
    own_piece(1)
    arrive(r.kvt.at[0, lax.rem(z + 1, 4)], rr.az.at[2])
    own_piece(3)
    from_sides(0)
    arrive(r.kvt.at[0, lax.rem(z + 2, 4)], rr.az.at[1])
    own_piece(2)
    zp, to = zpeer(2)
    push(r.normed, r.nall.at[z], ss.na.at[0], rr.na.at[0], to)
    r.nall[z] = r.normed[...]
    arrive(r.q.at[0:3], rr.aq.at[0])
    for b in range(4):
        docs = doc_row(ends, (b * 8 + j) * 256, 256)
        r.qaug[b, 0:64] = r.q[b]
        r.qaug[b, 64:128] = jnp.where(feature == docs, 0.0, negative_fill).astype(bf16)
        r.peak[b] = jnp.full((1, 256), negative_fill, f32)
        r.acc[b] = jnp.zeros((80, 256), f32)

    def load_keys(slot, jp):
        for b in range(4):
            docs = doc_row(ends, (b * 8 + jp) * 256, 256)
            hot = (feature == docs).astype(f32).astype(bf16)
            r.kaug[256 * b:256 * b + 256, :] = transposed(
                jnp.concatenate([r.kvt[slot, b, 0:64], hot], axis=0))

    def scores(b, n, causal):
        s = dot(r.kaug[0:n, :], r.qaug[b])
        if causal:
            rows = lax.broadcasted_iota(jnp.int32, (n, 256), 0)
            cols = lax.broadcasted_iota(jnp.int32, (n, 256), 1)
            s = jnp.where(rows - 256 * b <= cols, s, negative_fill)
        return s

    def load_chunk(slot, jp):
        load_keys(slot, jp)
        for b in range(4):
            r.vt1[0:64, 256 * b:256 * b + 256] = r.kvt[slot, b, 64:128]

    def forward(tiles, causal):
        def gather(b, n, p, factor):
            r.acc[b] = r.acc[b] * factor + dot(r.vt1[:, 0:n], p)

        held = None
        for b, n in tiles:
            s = scores(b, n, causal)
            if held is not None:
                gather(*held)
            old = r.peak[b]
            new = jnp.maximum(old, jnp.max(s, axis=0, keepdims=True))
            held = (b, n, jnp.exp(s - new).astype(bf16), jnp.exp(old - new))
            r.peak[b] = new
        gather(*held)

    load_chunk(0, j)
    forward([(b, 256 * b + 256) for b in (3, 2, 1, 0)], True)

    def chunk(i, carry):
        u = i // 2
        side = ((u + 1) // 2) % 2
        xp = (x + d * (2 * (i % 2) - 1) * side + 2 * (u // 3) + 8) % 4
        jp = xp * 2 + (c + (1 - side) * (i % 2) + side * (u // 2)) % 2

        @pl.when(i == 1)
        def _():
            from_sides(1)
            from_far(0)
            came_whole(1)

        @pl.when(i == 2)
        def _():
            from_sides(3)
            from_far(1)
            from_sides(2)

        @pl.when(i == 3)
        def _():
            from_far(3)

        @pl.when(i == 4)
        def _():
            from_far(2)
            came_whole(4)
            to_all(lambda to: r.cotq_s.at[to], r.cotq.at[mp, ex], "co")

        @pl.when(i == 5)
        def _():
            came_whole(5)
            arrive(r.wfull.at[0:3, 0:128, :], rr.wf.at[0])
            for i in range(1, 4):
                ym, to = ypeer(4 - i)
                remote(
                    r.wfull.at[ym, half, :], r.wfull.at[ym, half, :], ss.wd.at[0], rr.wd.at[0], sib).start()

        @pl.when(i == 7)
        def _():
            came_whole(7)

        load_chunk(i, jp)

        @pl.when(jp < j)
        def _():
            forward([(b, 256 * b + 256) for b in (3, 2, 1, 0)], False)

        @pl.when(jp > j)
        def _():
            forward([(b, 256 * b) for b in (3, 2, 1)], False)

        return carry

    lax.fori_loop(1, 8, chunk, 0)
    for b in range(4):
        total = r.acc[b, 64:65]
        ot = r.acc[b, 0:64] / total
        r.ot[b] = ot
        r.lse[b] = r.peak[b] + jnp.log(total)
        r.o_s[b] = ot.astype(bf16)
    for i in (1, 3, 2):
        zp, to = zpeer(i)
        push(r.o_s.at[zp], r.att.at[mp, z], ss.oz.at[0], rr.oz.at[i - 1], to)
    r.att[mp, z] = r.o_s[z]
    def normed_half(part):
        rows = pl.ds(128 * part, 128)
        for i in (1, 3):
            zp, to = zpeer(i)
            push(
                r.normed.at[rows, :], r.nall.at[z, rows, :], ss.na.at[0],
                rr.na.at[0], to)

    def attended_piece(k):
        zq = lax.rem(z + 4 - k, 4)
        for i in (1, 3, 2):
            ym, to = ypeer(i)
            push(
                r.att.at[mp, zq], r.att.at[mp, zq], ss.oy.at[0], rr.oy.at[0], to)

    attended_piece(0)
    for k in (1, 3, 2):
        arrive(r.att.at[mp, lax.rem(z + 4 - k, 4)], rr.oz.at[k - 1])
        attended_piece(k)
    normed_half(0)
    arrive(r.cotq.at[0, 0:31], rr.co.at[0])
    arrive(r.wfull.at[0:3, 0:128, :], rr.wd.at[0])
    arrive(r.att.at[0:3], rr.oy.at[0])
    for i in (1, 3, 2):
        ym, to = ypeer(i)
        push(r.cotq.at[mp], r.cotq.at[mp], ss.cy.at[0], rr.cy.at[0], to)
    def geometry(i):
        p = i // 2
        w = p + (p // 2) * (1 - 2 * (p % 2))
        g = (2 + d * w + 4) % 4
        flip = 1 - i % 2
        odd = g % 2
        slot = odd * (2 + g // 2 + 2 * flip) + (1 - odd) * (3 * g + flip)
        xp = (x - d * g + 8) % 4
        return slot, xp, xp * 2 + (c + flip) % 2

    def softmax(i, carry):
        slot, _, jp = geometry(i)
        load_keys(slot, jp)

        def keep(tiles):
            for b, n in tiles:
                r.weights[i, 0:n, 256 * b:256 * b + 256] = jnp.exp(scores(b, n, False) - r.lse[b]).astype(bf16)

        @pl.when(jp < j)
        def _():
            keep([(b, 256 * b + 256) for b in (3, 2, 1, 0)])

        @pl.when(jp > j)
        def _():
            keep([(b, 256 * b) for b in (3, 2, 1)])

        return carry

    value = r.tokens[...].astype(f32) + dot(r.att[...].reshape(1024, 256), r.wfull[...].reshape(1024, 1024), 0, 0)
    r.resid[...] = value
    for k in range(4):
        @pl.when(mp == k)
        def _():
            r.rescol[...] = value[:, 256 * k:256 * k + 256]
    unit, _ = norm_parts(value)
    normed = (unit * r.gain2[...]).astype(bf16)
    for step in (1, 3, 2, 0):
        plane = lax.rem(z + step, 4)
        r.slots[pl.ds(8 * plane, 8)] = dot(
            r.placer[pl.ds(pl.multiple_of(128 * plane, 128), 128), :], normed).astype(bf16).reshape(8, 16, 1024)

        def dispatch(k, carry):
            to = plane * 8 + lax.rem(j + k, 8)
            remote(
                r.slots.at[to], r.slots.at[32 + ex], ss.di.at[0], rr.di.at[0],
                (to, mp)).start()
            return carry

        lax.fori_loop(0 if step else 1, 8, dispatch, 0)
    r.slots[32 + ex] = r.slots[ex]
    lax.fori_loop(4, 7, softmax, 0)
    loads[3].wait()
    arrive(r.cotq.at[0:3], rr.cy.at[0])
    for le in range(2):
        rows = jnp.concatenate([one_expert(r.cotq[k], le) for k in range(4)], axis=1)
        r.crows[le] = rows
        r.gh[le] = dot(rows, r.weights[2 + le], 1, 1)
    loads[4].wait()
    arrive(r.slots.at[32:63], rr.di.at[0])
    def expert_rows(le):
        rows = one_expert(r.slots[32:64], le)
        r.xrows[le] = rows
        return dot(rows, r.weights[le])

    def activate(le, pre):
        hidden, slope = gelu_parts(pre)
        r.hid[le] = hidden.astype(bf16)
        gpre = (r.gh[le] * slope).astype(bf16)
        r.gpre[le] = gpre
        return gpre

    def give_back(le, gpre):
        for k in range(4):
            product = dot(gpre, r.weights[le, 256 * k:256 * k + 256, :], 1, 1)
            r.part[le, k] = product[:, 0:128].astype(bf16)
            r.gh[le, :, 128 * k:128 * k + 128] = product[:, 128:256]
        for i in (1, 3, 2):
            ym, to = ypeer(i)
            push(r.part.at[le, ym], r.rs.at[le, i - 1], ss.rs.at[0], rr.rs.at[0], to)

    first, second = expert_rows(0), expert_rows(1)
    gpre = activate(0, first)
    give_back(0, gpre)
    give_back(1, activate(1, second))
    r.wide_s[...] = both_experts(r.gh[0, :, 0:512], r.gh[1, :, 0:512])
    to_all(lambda to: r.wide_s.at[to], r.wide.at[ex], "bc")
    r.wide[ex] = r.wide_s[ex]
    first = dot(r.hid[0], r.weights[2])
    r.branch[...] = both_experts(first, dot(r.hid[1], r.weights[3]))
    lax.fori_loop(0, 4, softmax, 0)
    arrive(r.rs, rr.rs.at[0])
    sums = []
    for le in range(2):
        total = r.part[le, mp].astype(f32)
        for i in range(3):
            total = total + r.rs[le, i].astype(f32)
        sums.append(total)
    r.back_s[...] = both_experts(sums[0], sums[1])
    to_all(lambda to: r.back_s.at[to], r.back.at[ex], "ba")
    r.back[ex] = r.back_s[ex]
    arrive(r.wide.at[0:31], rr.bc.at[0])
    rows = dot(r.placer[...], r.wide[...].reshape(512, 512), 0, 0).astype(bf16)
    for k in range(4):
        r.gb[k] = rows[:, 128 * k:128 * k + 128]
    for i in (1, 3, 2):
        ym, to = ypeer(i)
        push(r.gb.at[ym], r.gbr.at[i - 1], ss.gb.at[0], rr.gb.at[0], to)
    arrive(r.back.at[0:31], rr.ba.at[0])
    r.gn[0, mp] = dot(r.placer[...], r.back[...].reshape(512, 128), 0, 0).astype(bf16)
    for i in (1, 3, 2):
        ym, to = ypeer(i)
        push(r.gn.at[0, mp], r.gn.at[0, mp], ss.gy.at[0], rr.gy.at[0], to)
    normed_half(1)
    total = r.gb[mp].astype(f32)
    arrive(r.gbr, rr.gb.at[0])
    for i in range(3):
        total = total + r.gbr[i].astype(f32)
    r.gn[1, mp] = total.astype(bf16)
    for i in (1, 3, 2):
        ym, to = ypeer(i)
        push(r.gn.at[1, mp], r.gn.at[1, mp], ss.gy.at[0], rr.gy.at[0], to)
    unit, inverse = norm_parts(r.resid[...])
    left(r.slots.at[0:31], ss.di.at[0])
    load_keys(0, j)
    for b in (3, 2, 1, 0):
        n = 256 * b + 256
        own = jnp.exp(scores(b, n, True) - r.lse[b]).astype(bf16)
        r.slots[0:n // 16, :, 256 * b:256 * b + 256] = own.reshape(n // 16, 16, 256)
    arrive(r.gn.at[:, 0:3], rr.gy.at[0])
    grad = jnp.concatenate([r.gn[k % 2, k // 2] for k in range(8)], axis=1).astype(f32)
    grad_in, ggrad = norm_back(grad, r.gain2[...], unit, inverse)
    r.gsum[1:2] = ggrad
    gres = r.cot[...].astype(f32) + grad_in
    r.gres[...] = gres
    low = gres.astype(bf16)
    r.dheads[...] = dot(r.wfull[mp], low, 1, 1).astype(bf16).reshape(4, 64, 256)
    for i in (1, 3, 2):
        zp, to = zpeer(i)
        push(r.dheads.at[zp], r.dob.at[z], ss.dz.at[0], rr.dz.at[0], to)
    r.dob[z] = r.dheads[z]
    wgrad = dot(r.att[mp].reshape(256, 256), low).astype(bf16)
    r.wgp[0] = wgrad[:, 0:512].reshape(4, 4, 16, 512)
    r.wgp[1] = wgrad[:, 512:1024].reshape(4, 4, 16, 512)
    push(r.wgp.at[1 - c], r.wgs, ss.wg.at[0], rr.wg.at[0], sib)
    for i in range(1, 4):
        ym, to = ypeer(i)
        push(
            r.branch.at[:, :, pl.ds(pl.multiple_of(256 * ym, 256), 256)], r.brs.at[i - 1],
            ss.br.at[0], rr.br.at[0], to)
    zero = jnp.zeros((64, 256), bf16)
    arrive(r.dob.at[0:3], rr.dz.at[0])
    arrive(r.wgs, rr.wg.at[0])
    r.wgq[...] = (r.wgp[c].astype(f32) + r.wgs[...].astype(f32)).astype(bf16)
    for i in (1, 3, 2):
        zp, to = zpeer(i)
        push(r.wgq.at[zp], r.wgz.at[i - 1], ss.wz.at[0], rr.wz.at[0], to)
    for b in range(4):
        r.dopad[b, 0:64] = zero
        r.dopad[b, 64:128] = r.dob[b]
        r.qd[b, 0:256] = transposed(jnp.concatenate([r.q[b], zero], axis=0))
        r.qd[b, 256:512] = transposed(jnp.concatenate([zero, r.dob[b]], axis=0))
        r.delta[b] = jnp.sum(r.dob[b].astype(f32) * r.ot[b], axis=0, keepdims=True)
        r.dq[b] = jnp.zeros((64, 256), f32)

    def load_back(slot):
        for b in range(4):
            r.kvn[256 * b:256 * b + 256, :] = transposed(r.kvt[slot, b])
            r.kt[:, 256 * b:256 * b + 256] = r.kvt[slot, b, 0:64]

    def backward(tiles, weights):
        def gather(b, n, ds, p):
            added = dot(ds, r.qd[b, 0:256]) + dot(p, r.qd[b, 256:512])
            if b == 3:
                r.dkv[0:n] = added
            else:
                r.dkv[0:n] = r.dkv[0:n] + added
            r.dq[b] = r.dq[b] + dot(r.kt[:, 0:n], ds)

        held = None
        for b, n in tiles:
            dp = dot(r.kvn[0:n, :], r.dopad[b])
            p = weights(b, n)
            if held is not None:
                gather(*held)
            held = (b, n, (p * (dp - r.delta[b])).astype(bf16), p.astype(bf16))
        gather(*held)

    def back_chunk(i, carry):
        slot, xp, jp = geometry(i)
        p = i // 2
        load_back(slot)

        def kept(b, n):
            return r.weights[i, 0:n, 256 * b:256 * b + 256]

        @pl.when(jp < j)
        def _():
            backward([(b, 256 * b + 256) for b in (3, 2, 1, 0)], kept)

        @pl.when(jp > j)
        def _():
            r.dkv[768:1024] = jnp.zeros((256, 128), f32)
            backward([(b, 256 * b) for b in (3, 2, 1)], kept)

        @pl.when(i % 2 == 0)
        def _():
            r.sb[p] = r.dkv[...].astype(bf16)
            remote(r.sb.at[p], r.sr.at[p], ss.sb.at[0], rr.sb.at[p], sib).start()

        @pl.when(i % 2 == 1)
        def _():
            arrive(r.sr.at[p], rr.sb.at[p])
            r.xs[p] = (r.dkv[...] + r.sr[p].astype(f32)).astype(bf16)

            @pl.when(p == 0)
            def _():
                remote(r.xs.at[0], r.xr.at[0], ss.xs.at[0], rr.xs.at[0], ahead).start()

            @pl.when(p == 2 - c)
            def _():
                remote(r.xs.at[p], r.xr.at[1], ss.xs.at[0], rr.xs.at[1], behind).start()

            @pl.when(p == 2)
            def _():
                arrive(r.xr.at[0], rr.xs.at[0])
                r.xs[3] = (r.xs[1 + c].astype(f32) + r.xr[0].astype(f32)).astype(bf16)
                remote(r.xs.at[3], r.xr.at[2], ss.xs.at[0], rr.xs.at[2], ahead).start()

        @pl.when(i == 2)
        def _():
            arrive(r.wgz, rr.wz.at[0])
            total = r.wgq[z].astype(f32)
            for k in range(3):
                total = total + r.wgz[k].astype(f32)
            r.wgx[...] = total.astype(bf16)
            for k in (1, 3, 2):
                xq, to = xpeer(k)
                remote(r.wgx.at[xq], r.wgr.at[k - 1], ss.wx.at[0], rr.wx.at[0], to).start()

        @pl.when(i == 6)
        def _():
            total = r.branch[:, :, mine].astype(f32)
            arrive(r.brs, rr.br.at[0])
            for k in range(3):
                total = total + r.brs[k].astype(f32)
            r.bs[...] = total.astype(bf16)
            for k in (1, 3, 2):
                zp, to = zpeer(k)
                remote(
                    r.bs.at[pl.ds(8 * zp, 8)], r.bz.at[z], ss.bb.at[0], rr.bb.at[0], to).start()
            r.bz[z] = r.bs[pl.ds(8 * z, 8)]

        @pl.when(i == 5)
        def _():
            total = r.wgx[x].astype(f32)
            arrive(r.wgr, rr.wx.at[0])
            for k in range(3):
                total = total + r.wgr[k].astype(f32)
            r.wgf[c, z, x] = total.astype(bf16)
            for k in (1, 3, 2):
                _, to = xpeer(k)
                remote(r.wgf.at[c, z, x], r.wgf.at[c, z, x], ss.wa.at[0], rr.wa.at[0], to).start()

        return carry

    lax.fori_loop(0, 7, back_chunk, 0)
    load_back(0)
    backward(
        [(b, 256 * b + 256) for b in (3, 2, 1, 0)],
        lambda b, n: r.slots[0:n // 16, :, 256 * b:256 * b + 256].reshape(n, 256))
    for b in range(4):
        r.zs[b, 0:64] = (r.dq[b] * HEAD_DIM ** (-0.5)).astype(bf16)
    for i in (1, 3, 2):
        zp, to = zpeer(i)
        push(r.zs.at[zp, 0:64], r.zr.at[z, 0:64], ss.zd.at[0], rr.zd.at[0], to)
    arrive(r.nall.at[0:3], rr.na.at[0])

    def weight_part(first, last, pieces, name):
        wt = dot(r.zs[0, first:last], r.nall[0])
        for b in range(1, 4):
            wt = wt + dot(r.zs[b, first:last], r.nall[b])
        wt = wt.astype(bf16)
        for k in range(8):
            pieces[0][k] = wt[:, 128 * k:128 * k + 128]
        for i in range(1, 8):
            jt = lax.rem(j + i, 8)
            push(
                pieces[0].at[jt], pieces[1].at[i - 1], getattr(ss, name).at[0], getattr(rr, name).at[0],
                (z * 8 + jt, mp))

    def weight_sum(pieces, name):
        total = pieces[0][j].astype(f32)
        arrive(pieces[1], getattr(rr, name).at[0])
        for i in range(7):
            total = total + pieces[1][i].astype(f32)
        return total.astype(bf16)

    weight_part(0, 64, (r.wpq, r.wrq), "wp")
    r.resid[...] = norm_parts(r.tokens[...].astype(f32))[0]
    arrive(r.sr.at[3], rr.sb.at[3])
    total = r.dkv[...] + r.sr[3].astype(f32)
    for k in (1, 2):
        arrive(r.xr.at[k], rr.xs.at[k])
        total = total + r.xr[k].astype(f32)
    low = total.astype(bf16)
    for b in range(4):
        r.zs[b, 64:192] = transposed(low[256 * b:256 * b + 256])
    for i in (1, 3, 2):
        zp, to = zpeer(i)
        push(r.zs.at[zp, 64:192], r.zr.at[z, 64:192], ss.zq.at[0], rr.zq.at[0], to)
    r.zr[z] = r.zs[z]
    weight_part(64, 192, (r.wpk, r.wrk), "wk")
    r.pieces[0, c, z, x] = weight_sum((r.wpq, r.wrq), "wp")
    gather_first(0)
    arrive(r.wgf.at[0, 0, 0:3], rr.wa.at[0])
    for k in (1, 3, 2):
        _, to = zpeer(k)
        push(r.wgf.at[c, z], r.wgf.at[c, z], ss.wb.at[0], rr.wb.at[0], to)

    def heads(first):
        return transposed(jnp.concatenate([r.zr[h, first:first + 64] for h in range(4)], axis=0))

    arrive(r.zr.at[0:3, 0:64], rr.zd.at[0])
    part = dot(heads(0), r.wqkv[0], 1, 1)
    arrive(r.zr.at[0:3, 64:192], rr.zq.at[0])
    part = part + dot(heads(64), r.wqkv[1], 1, 1) + dot(heads(128), r.wqkv[2], 1, 1)
    r.gnp[...] = part.astype(bf16).reshape(4, 64, 1024)
    one_gain = jnp.sum(part * r.resid[...], axis=0, keepdims=True)
    r.small[...] = one_gain
    for i in (1, 3, 2):
        ym, to = ypeer(i)
        push(r.small, r.smally.at[i - 1], ss.sy.at[0], rr.sy.at[0], to)
    for first in (0, 32):
        rows = pl.ds(first, 32)
        for i in (1, 3, 2):
            ym, to = ypeer(i)
            push(r.gnp.at[ym, rows, :], r.ry.at[i - 1, rows, :], ss.ry.at[0], rr.ry.at[first // 32], to)
    both = weight_sum((r.wpk, r.wrk), "wk")
    r.pieces[1, c, z, x] = both[0:64]
    r.pieces[2, c, z, x] = both[64:128]
    gather_first(1)
    gather_first(2)
    gather_second(0)
    arrive(r.wgf.at[0, 0:3], rr.wb.at[0])
    push(r.wgf.at[c], r.wgf.at[c], ss.wc.at[0], rr.wc.at[0], sib)
    def norm_rows(first):
        grad = r.gnp[mp, first:first + 32].astype(f32)
        arrive(r.ry.at[:, first:first + 32], rr.ry.at[first // 32])
        for i in range(3):
            grad = grad + r.ry[i, first:first + 32].astype(f32)
        here = pl.ds(pl.multiple_of(64 * mp + first, 32), 32)
        unit, inverse = norm_parts(r.tokens[here, :].astype(f32))
        grad_in, _ = norm_back(grad, r.gain1[...], unit, inverse)
        r.igrad[here, :] = (r.gres[here, :] + grad_in).astype(bf16)
        for i in (1, 3, 2):
            ym, to = ypeer(i)
            push(r.igrad.at[here, :], r.igrad.at[here, :], ss.ay.at[0], rr.ay.at[0], to)

    gather_second(1)
    gather_second(2)
    arrive(r.bz.at[0:3], rr.bb.at[0])
    for i in range(1, 8):
        jt = lax.rem(j + i, 8)
        push(r.bz.at[:, jt], r.bret.at[:, j], ss.bp.at[0], rr.bp.at[0], (z * 8 + jt, mp))
    for b in range(4):
        r.bret[b, j] = r.bz[b, j]
    arrive(r.smally, rr.sy.at[0])
    for i in range(3):
        one_gain = one_gain + r.smally[i]
    r.gsum[0:1] = one_gain
    for i in (1, 3, 2):
        _, to = zpeer(i)
        push(r.gsum, r.gz.at[i - 1], ss.se.at[0], rr.se.at[0], to)
    norm_rows(0)
    gather_third(0)
    norm_rows(32)
    arrive(r.gz, rr.se.at[0])
    r.gps[...] = r.gsum[...] + r.gz[0] + r.gz[1] + r.gz[2]
    for i in range(1, 8):
        jt = lax.rem(j + i, 8)
        push(r.gps, r.gp.at[i - 1], ss.sf.at[0], rr.sf.at[0], (z * 8 + jt, mp))
    arrive(r.wgf.at[1 - c], rr.wc.at[0])
    for k in range(16):
        for core in range(2):
            r.wout_out[16 * k:16 * k + 16, 512 * core:512 * core + 512] = r.wgf[core, k // 4, k % 4]
    gather_third(1)
    gather_third(2)
    for k in range(3):
        arrive(r.pieces.at[k, 1 - c], rr.pc.at[k])
        for row in range(8):
            block = jnp.concatenate([r.pieces[k, row % 2, h, row // 2] for h in range(4)], axis=0)
            r.qkv_out[k, 128 * row:128 * row + 128] = transposed(block)
    arrive(r.bret.at[:, 0:7], rr.bp.at[0])
    rows = dot(r.placer[...], r.bret[...].reshape(512, 256), 0, 0)
    r.out[...] = (r.rescol[...] + rows).astype(bf16)
    arrive(r.gp, rr.sf.at[0])
    both = r.gps[...] + jnp.sum(r.gp[...], axis=0)
    r.gain1_out[...] = both[0:1]
    r.gain2_out[...] = both[1:2]
    arrive(r.igrad.at[0:192, :], rr.ay.at[0])
    sent = {
        "az": r.kv_s.at[0:3], "aq": r.q_s.at[0:3], "ag": r.kvt.at[0:7], "wf": r.wfull.at[0:3, 0:128, :],
        "wd": r.wfull.at[0:3, 0:128, :], "co": r.cotq_s.at[0:31], "cy": r.cotq.at[0:3], "na": r.nall.at[0:3],
        "oz": r.o_s.at[0:3], "oy": r.att.at[0:3], "rs": r.rs, "ba": r.back_s.at[0:31],
        "bc": r.wide_s.at[0:31], "gb": r.gb.at[0:3], "gy": r.gn.at[:, 0:3], "dz": r.dheads.at[0:3], "br": r.brs,
        "bb": r.bz.at[0:3], "bp": r.bret.at[:, 0:7], "sb": r.sb, "xs": r.xs.at[0:3], "wg": r.wgs, "wz": r.wgq.at[0:3], "wx": r.wgr,
        "wa": r.wgr, "wb": r.wgf.at[0, 0:3], "wc": r.wgf.at[0], "zd": r.zs.at[0:3, 0:64], "zq": r.zs.at[0:3, 64:192],
        "wp": r.wrq, "wk": r.wrk, "ry": r.ry, "ay": r.ry, "sy": r.smally, "se": r.gz, "sf": r.gp,
    }
    for name, ref in sent.items():
        left(ref, getattr(ss, name).at[0])
    for part in range(3):
        left(r.pieces.at[0, 0, 0, 0:3], ss.pa.at[part])
        left(r.pieces.at[0, 0, 0:3], ss.pb.at[part])
        left(r.pieces.at[0, 0], ss.pc.at[part])


def layer(*args):
    return pl.pallas_call(
        layer_kernel,
        out_shape=[pltpu.VMEM(s, t) for s, t in OUTS.values()],
        in_specs=[SM, VM, VM, VM, VM, ANY, ANY, ANY, ANY, ANY],
        out_specs=[VM] * len(OUTS),
        scratch_shapes=[pltpu.VMEM(s, t) for s, t in BUFFERS.values()]
        + [DMA(s) for group in (LOCAL, SENT, TAKEN) for s in group.values()],
        name="layer",
        compiler_params=pltpu.CompilerParams(
            collective_id=0, has_side_effects=True, vmem_limit_bytes=VMEM_BYTES),
    )(*args)


def finish_kernel(x, gpre, hid, cots, qkv, wout, out, igrad, gain1, gain2, *refs):
    in_grad, out_grad, qkv_o, wout_o, out_o, igrad_o, gain1_o, gain2_o = refs[:8]
    in_buf, out_buf, qkv_buf, wout_buf, store, rest = refs[8:]
    stores = []

    def put(src, dst, sem):
        copy = pltpu.make_async_copy(src, dst, sem)
        copy.start()
        stores.append(copy)

    for k, (left, right, buf, result) in enumerate(((x, gpre, in_buf, in_grad), (hid, cots, out_buf, out_grad))):
        for e in range(2):
            for t in range(4):
                rows = pl.ds(256 * t, 256)
                buf[e, rows, :] = dot(left[e, :, 256 * t:256 * t + 256], right[e], 0, 0)
                put(buf.at[e, rows, :], result.at[e, rows, :], store.at[8 * k + 4 * e + t])
    qkv_buf[...] = qkv[...].astype(f32)
    wout_buf[...] = wout[...].astype(f32)
    plain = ((qkv_buf, qkv_o), (wout_buf, wout_o), (out, out_o), (igrad, igrad_o), (gain1, gain1_o), (gain2, gain2_o))
    for k, (src, dst) in enumerate(plain):
        put(src, dst, rest.at[k])
    for copy in stores:
        copy.wait()


def finish(*args):
    big = ((2, 1024, 1024), f32)
    outs = [big, big, ((3, 1024, 256), f32), ((256, 1024), f32), ((256, 256), bf16), ((256, 1024), bf16)]
    outs += [((1, 1024), f32)] * 2
    return pl.pallas_call(
        finish_kernel,
        out_shape=[jax.ShapeDtypeStruct(s, t) for s, t in outs],
        in_specs=[VM] * 10,
        out_specs=[ANY] * 8,
        scratch_shapes=[pltpu.VMEM(s, t) for s, t in outs[:4]] + [DMA((16,)), DMA((6,))],
        name="finish",
        compiler_params=pltpu.CompilerParams(vmem_limit_bytes=36 << 20),
        cost_estimate=pl.CostEstimate(flops=2 * 2 * 2 * 256 * 1024 * 1024, bytes_accessed=28 << 20, transcendentals=0),
    )(*args)


def on_device(
    tokens, hash_ids, lengths, norm1_gain, qkv_weight, out_weight, norm2_gain, expert_in, expert_out, cotangent,
):
    x, cots, hid, gpre, out, igrad, gain1, gain2, qkv, wout = layer(
        lengths, tokens, norm1_gain.reshape(1, 1024), norm2_gain.reshape(1, 1024), hash_ids.reshape(1, 256),
        jnp.transpose(qkv_weight, (1, 0, 2)), out_weight, cotangent, expert_in, expert_out)
    in_grad, out_grad, qkv, wout, out, igrad, gain1, gain2 = finish(
        x, gpre, hid, cots, qkv, wout, out, igrad, gain1, gain2)
    return out, igrad, gain1.reshape(1024), jnp.transpose(qkv, (1, 0, 2)), wout, gain2.reshape(1024), in_grad, out_grad


def solution(mesh):
    placed = (
        P("ex", None), P("ex", None), P(), P(), P(None, None, "mp"), P("mp", None), P(),
        P("ex", None, "mp"), P("ex", "mp", None), P("ex", None),
    )
    return jax.shard_map(
        on_device,
        mesh=mesh,
        in_specs=placed,
        out_specs=(
            P("ex", "mp"), P("ex", None), P(), P(None, None, "mp"), P("mp", None), P(),
            P("ex", None, "mp"), P("ex", "mp", None),
        ),
        check_vma=False,
    )
```

```python
import functools

import jax
import jax.numpy as jnp
from jax import lax
from jax.experimental import pallas as pl
from jax.experimental.pallas import tpu as pltpu
from jax.sharding import PartitionSpec as P

HEAD_DIM = 64
epsilon = 1e-05
negative_fill = -1e30
MESH = pl.DeviceIdType.MESH
bf16, f32 = jnp.bfloat16, jnp.float32
EX, MP = 32, 4
VMEM_BYTES = 56 << 20


def dot(a, b, ca=1, cb=0):
    return lax.dot_general(a, b, (((ca,), (cb,)), ((), ())), preferred_element_type=f32)


def place():
    ex, mp = lax.axis_index("ex"), lax.axis_index("mp")
    z, x, c = ex // 8, (ex // 2) % 4, ex % 2
    return ex, mp, z, x, c


def send(src, dst, ssem, rsem, device):
    copy = pltpu.make_async_remote_copy(
        src_ref=src, dst_ref=dst, send_sem=ssem, recv_sem=rsem, device_id=device, device_id_type=MESH
    )
    copy.start()
    return copy


def greet(ex, mp):
    bar = pltpu.get_barrier_semaphore()

    def one(d, carry):
        pl.semaphore_signal(bar, inc=1, device_id=(lax.rem(ex + d, EX), mp), device_id_type=MESH)
        return carry

    lax.fori_loop(1, EX, one, 0)
    for d in range(1, MP):
        pl.semaphore_signal(bar, inc=1, device_id=(ex, lax.rem(mp + d, MP)), device_id_type=MESH)
    return bar


def greeted(bar):
    pl.semaphore_wait(bar, EX - 1 + MP - 1)


def slot_matrix(chosen_row):
    tok = chosen_row.shape[1]
    experts = lax.broadcasted_iota(jnp.int32, (64, tok), 0)
    hot = (experts == chosen_row).astype(f32)
    rows = lax.broadcasted_iota(jnp.int32, (tok, tok), 0)
    cols = lax.broadcasted_iota(jnp.int32, (tok, tok), 1)
    before = (rows < cols).astype(bf16)
    earlier = dot(hot.astype(bf16), before)
    rank = jnp.sum(earlier * hot, axis=0, keepdims=True)
    target = chosen_row * 8 + rank.astype(jnp.int32)
    slots = lax.broadcasted_iota(jnp.int32, (512, tok), 0)
    return (slots == target).astype(f32).astype(bf16)


def doc_row(ends, first, count):
    pos = first + lax.broadcasted_iota(jnp.int32, (1, count), 1)
    row = jnp.zeros((1, count), jnp.int32)
    for end in ends:
        row = row + (pos >= end).astype(jnp.int32)
    return row


def doc_ends(lengths_ref):
    ends, total = [], 0
    for i in range(9):
        total = total + lengths_ref[i]
        ends.append(total)
    return ends


def norm_parts(v):
    mean = jnp.mean(v, axis=-1, keepdims=True)
    centred = v - mean
    inverse = lax.rsqrt(jnp.mean(centred * centred, axis=-1, keepdims=True) + epsilon)
    return centred * inverse, inverse


def transposed(v):
    return v.T


def norm_back(grad_out, gain_row, unit, inverse):
    scaled = grad_out * gain_row
    centred = scaled - jnp.mean(scaled, axis=-1, keepdims=True)
    grad_in = inverse * (centred - unit * jnp.mean(scaled * unit, axis=-1, keepdims=True))
    return grad_in, jnp.sum(grad_out * unit, axis=0, keepdims=True)


def gelu_parts(pre):
    k = 0.7978845608028654
    square = pre * pre
    t = jnp.tanh(k * pre * (1.0 + 0.044715 * square))
    half = 0.5 * (1.0 + t)
    slope = half + 0.5 * pre * (1.0 - t * t) * (k * (1.0 + 3 * 0.044715 * square))
    return pre * half, slope


def one_expert(rows, le):
    wide = rows.astype(f32)
    return wide[:, 8 * le:8 * le + 8].reshape(256, rows.shape[2]).astype(bf16)


def both_experts(first, second):
    width = first.shape[1]
    return jnp.concatenate([first.reshape(32, 8, width), second.reshape(32, 8, width)], axis=1).astype(bf16)


VM = pl.BlockSpec(memory_space=pltpu.VMEM)
SM = pl.BlockSpec(memory_space=pltpu.SMEM)
ANY = pl.BlockSpec(memory_space=pl.ANY)
DMA = pltpu.SemaphoreType.DMA
ROWS = (2, 256, 1024)

ARGS = ["lengths", "tokens_hbm", "gain1", "gain2", "chosen", "wqkv_hbm", "wout_hbm", "cot_hbm", "win_hbm", "wex_hbm"]
OUTS = {
    "xrows": (ROWS, bf16), "crows": (ROWS, bf16), "hid": (ROWS, bf16), "gpre": (ROWS, bf16),
    "out": ((256, 256), bf16), "igrad": ((256, 1024), bf16), "gain1_out": ((1, 1024), f32), "gain2_out": ((1, 1024), f32),
    "qkv_out": ((3, 1024, 256), bf16), "wout_out": ((256, 1024), bf16),
}
BUFFERS = {
    "tokens": ((256, 1024), bf16),
    "wqkv": ((3, 1024, 256), bf16), "cot": ((256, 1024), bf16),
    "weights": ((7, 1024, 1024), bf16), "placer": ((512, 256), bf16), "normed": ((256, 1024), bf16),
    "nall": ((4, 256, 1024), bf16), "wfull": ((4, 256, 1024), bf16),
    "q_s": ((4, 64, 256), bf16), "kv_s": ((4, 128, 256), bf16), "q": ((4, 64, 256), bf16),
    "kvt": ((8, 4, 128, 256), bf16), "qaug": ((4, 128, 256), bf16), "kaug": ((1024, 128), bf16),
    "vt1": ((80, 1024), bf16), "acc": ((4, 80, 256), f32), "peak": ((4, 1, 256), f32),
    "ot": ((4, 64, 256), f32), "lse": ((4, 1, 256), f32), "o_s": ((4, 64, 256), bf16),
    "att": ((4, 4, 64, 256), bf16), "cotq_s": ((32, 16, 256), bf16), "cotq": ((4, 32, 16, 256), bf16),
    "slots": ((64, 16, 1024), bf16),
    "gh": (ROWS, f32),
    "part": ((2, 4, 256, 128), bf16), "rs": ((2, 3, 256, 128), bf16), "back_s": ((32, 16, 128), bf16),
    "back": ((32, 16, 128), bf16), "wide_s": ((32, 16, 512), bf16), "wide": ((32, 16, 512), bf16),
    "gb": ((4, 256, 128), bf16), "gbr": ((3, 256, 128), bf16), "gn": ((2, 4, 256, 128), bf16), "resid": ((256, 1024), f32),
    "rescol": ((256, 256), f32), "gres": ((256, 1024), f32), "branch": ((32, 16, 1024), bf16),
    "wgp": ((2, 4, 4, 16, 512), bf16), "wgs": ((4, 4, 16, 512), bf16), "wgq": ((4, 4, 16, 512), bf16),
    "wgz": ((3, 4, 16, 512), bf16), "wgx": ((4, 16, 512), bf16), "wgr": ((3, 16, 512), bf16),
    "wgf": ((2, 4, 4, 16, 512), bf16),
    "dheads": ((4, 64, 256), bf16), "dob": ((4, 64, 256), bf16), "brs": ((3, 32, 16, 256), bf16),
    "bs": ((32, 16, 256), bf16), "bz": ((4, 8, 16, 256), bf16), "bret": ((4, 8, 16, 256), bf16), "dopad": ((4, 128, 256), bf16),
    "qd": ((4, 512, 128), bf16), "delta": ((4, 1, 256), f32), "kvn": ((1024, 128), bf16),
    "kt": ((64, 1024), bf16), "dkv": ((1024, 128), f32), "dq": ((4, 64, 256), f32),
    "sb": ((4, 1024, 128), bf16), "sr": ((4, 1024, 128), bf16), "xs": ((4, 1024, 128), bf16),
    "xr": ((3, 1024, 128), bf16), "zs": ((4, 192, 256), bf16), "zr": ((4, 192, 256), bf16),
    "wpq": ((8, 64, 128), bf16), "wrq": ((7, 64, 128), bf16),
    "wpk": ((8, 128, 128), bf16), "wrk": ((7, 128, 128), bf16),
    "pieces": ((3, 2, 4, 4, 64, 128), bf16),
    "gnp": ((4, 64, 1024), bf16), "ry": ((3, 64, 1024), bf16), "small": ((1, 1024), f32),
    "smally": ((3, 1, 1024), f32), "gsum": ((2, 1024), f32), "gz": ((3, 2, 1024), f32), "gps": ((2, 1024), f32), "gp": ((7, 2, 1024), f32),
}
LOCAL = {"load": (6,)}
SENT = dict.fromkeys(
    ("az", "aq", "ag", "wf", "wd", "co", "cy", "na", "oz", "oy", "di", "rs", "ba", "bc", "gb", "gy", "dz", "br", "bb", "sb",
     "xs", "wg", "wz", "wx", "wa", "wb", "wc", "zd", "zq", "wp", "wk", "ry", "ay", "sy", "se", "sf", "bp"),
    (1,))
SENT.update(pa=(3,), pb=(3,), pc=(3,))
TAKEN = dict(SENT, ry=(2,), az=(3,), ag=(16,), oz=(3,), sb=(4,), xs=(3,))


class Refs:
    pass


def layer_kernel(*refs):
    r, ls, ss, rr = Refs(), Refs(), Refs(), Refs()
    names = [(r, k) for k in ARGS + list(OUTS) + list(BUFFERS)] + [(ls, k) for k in LOCAL]
    names += [(ss, k) for k in SENT] + [(rr, k) for k in TAKEN]
    for (group, name), ref in zip(names, refs, strict=True):
        setattr(group, name, ref)
    ex, mp, z, x, c = place()
    d = 1 - 2 * c
    j = x * 2 + c
    chip = ex // 2
    sib = (ex + d, mp)
    ahead = (z * 8 + lax.rem(x + d + 4, 4) * 2 + c, mp)
    behind = (z * 8 + lax.rem(x - d + 4, 4) * 2 + c, mp)

    def zpeer(i):
        zp = lax.rem(z + i, 4)
        return zp, (zp * 8 + j, mp)

    def ypeer(i):
        ym = lax.rem(mp + i, MP)
        return ym, (ex, ym)

    def xpeer(i):
        xq = lax.rem(x + i, 4)
        return xq, (z * 8 + xq * 2 + c, mp)

    def remote(src, dst, ssem, rsem, device):
        return pltpu.make_async_remote_copy(
            src_ref=src, dst_ref=dst, send_sem=ssem, recv_sem=rsem, device_id=device, device_id_type=MESH)

    def push(src, dst, ssem, rsem, device):
        remote(src, dst, ssem, rsem, device).start()

    def arrive(dst, rsem):
        remote(dst, dst, rsem, rsem, sib).wait_recv()

    def left(src, ssem):
        remote(src, src, ssem, ssem, sib).wait_send()

    def to_all(src_of, dst, name):
        def one(k, carry):
            to = lax.rem(ex + k, EX)
            remote(src_of(to), dst, getattr(ss, name).at[0], getattr(rr, name).at[0], (to, mp)).start()
            return carry

        lax.fori_loop(1, EX, one, 0)

    def gather_first(part):
        for i in (1, 3, 2):
            _, to = xpeer(i) if part == 1 else zpeer(i)
            own = r.pieces.at[part, c, z, x]
            push(own, own, ss.pa.at[part], rr.pa.at[part], to)

    def gather_second(part):
        arrive(r.pieces.at[part, 0, 0, 0:3], rr.pa.at[part])
        row = r.pieces.at[part, c, z] if part == 1 else r.pieces.at[part, c, :, x]
        for i in (1, 3, 2):
            _, to = zpeer(i) if part == 1 else xpeer(i)
            push(row, row, ss.pb.at[part], rr.pb.at[part], to)

    def gather_third(part):
        arrive(r.pieces.at[part, 0, 0:3], rr.pb.at[part])
        push(r.pieces.at[part, c], r.pieces.at[part, c], ss.pc.at[part], rr.pc.at[part], sib)

    loads = [
        pltpu.make_async_copy(src, dst, ls.load.at[i])
        for i, (src, dst) in enumerate([
            (r.tokens_hbm, r.tokens), (r.wqkv_hbm, r.wqkv), (r.wout_hbm, r.wfull.at[mp]), (r.cot_hbm, r.cot), (r.wex_hbm, r.weights.at[2:4]),
            (r.win_hbm, r.weights.at[0:2])])
    ]
    for copy in loads:
        copy.start()
    bar = greet(ex, mp)
    loads[0].wait()
    unit, _ = norm_parts(r.tokens[...].astype(f32))
    normed = (unit * r.gain1[...]).astype(bf16)
    r.normed[...] = normed
    loads[1].wait()
    kt = transposed(dot(normed, r.wqkv[1]).astype(bf16))
    vt = transposed(dot(normed, r.wqkv[2]).astype(bf16))
    for h in range(4):
        r.kv_s[h, 0:64] = kt[64 * h:64 * h + 64]
        r.kv_s[h, 64:128] = vt[64 * h:64 * h + 64]
    greeted(bar)
    for i in (1, 3, 2):
        zp, to = zpeer(i)
        push(r.kv_s.at[zp], r.kvt.at[0, z], ss.az.at[0], rr.az.at[i - 1], to)
    r.kvt[0, z] = r.kv_s[z]

    def own_piece(k):
        zq = lax.rem(z + 4 - k, 4)
        remote(r.kvt.at[0, zq], r.kvt.at[2, zq], ss.ag.at[0], rr.ag.at[4 + k], ahead).start()
        remote(r.kvt.at[0, zq], r.kvt.at[3, zq], ss.ag.at[0], rr.ag.at[8 + k], behind).start()
        remote(r.kvt.at[0, zq], r.kvt.at[1, zq], ss.ag.at[0], rr.ag.at[0], sib).start()

    def came(slot, k):
        arrive(r.kvt.at[slot, lax.rem(z + 4 - k, 4)], rr.ag.at[{2: 4, 3: 8, 6: 12}[slot] + k])

    def came_whole(slot):
        arrive(r.kvt.at[slot], rr.ag.at[{1: 0, 4: 1, 5: 2, 7: 3}[slot]])

    def from_sides(k):
        zq = lax.rem(z + 4 - k, 4)
        came(2, k)
        remote(r.kvt.at[2, zq], r.kvt.at[6, zq], ss.ag.at[0], rr.ag.at[12 + k], ahead).start()
        remote(r.kvt.at[2, zq], r.kvt.at[5, zq], ss.ag.at[0], rr.ag.at[2], sib).start()
        came(3, k)
        remote(r.kvt.at[3, zq], r.kvt.at[4, zq], ss.ag.at[0], rr.ag.at[1], sib).start()

    def from_far(k):
        zq = lax.rem(z + 4 - k, 4)
        came(6, k)
        remote(r.kvt.at[6, zq], r.kvt.at[7, zq], ss.ag.at[0], rr.ag.at[3], sib).start()

    own_piece(0)
    qt = transposed((dot(normed, r.wqkv[0]).astype(bf16) * HEAD_DIM ** (-0.5)).astype(bf16))
    for h in range(4):
        r.q_s[h] = qt[64 * h:64 * h + 64]
    for i in (1, 3, 2):
        zp, to = zpeer(i)
        push(r.q_s.at[zp], r.q.at[z], ss.aq.at[0], rr.aq.at[0], to)
    r.q[z] = r.q_s[z]
    loads[2].wait()
    half = pl.ds(pl.multiple_of(128 * c, 128), 128)
    for i in range(1, 4):
        ym, to = ypeer(i)
        push(r.wfull.at[mp, half, :], r.wfull.at[mp, half, :], ss.wf.at[0], rr.wf.at[0], to)
    r.vt1[64:80, :] = jnp.ones((16, 1024), bf16)
    ends = doc_ends(r.lengths)
    feature = lax.broadcasted_iota(jnp.int32, (64, 256), 0)
    loads[3].wait()
    mine = pl.ds(pl.multiple_of(256 * mp, 256), 256)
    r.placer[...] = slot_matrix(r.chosen[...])
    r.cotq_s[...] = dot(r.placer[...], r.cot[:, mine]).astype(bf16).reshape(EX, 16, 256)
    r.cotq[mp, ex] = r.cotq_s[ex]
    arrive(r.kvt.at[0, lax.rem(z + 3, 4)], rr.az.at[0])
    own_piece(1)
    arrive(r.kvt.at[0, lax.rem(z + 1, 4)], rr.az.at[2])
    own_piece(3)
    from_sides(0)
    arrive(r.kvt.at[0, lax.rem(z + 2, 4)], rr.az.at[1])
    own_piece(2)
    zp, to = zpeer(2)
    push(r.normed, r.nall.at[z], ss.na.at[0], rr.na.at[0], to)
    r.nall[z] = r.normed[...]
    arrive(r.q.at[0:3], rr.aq.at[0])
    for b in range(4):
        docs = doc_row(ends, (b * 8 + j) * 256, 256)
        r.qaug[b, 0:64] = r.q[b]
        r.qaug[b, 64:128] = jnp.where(feature == docs, 0.0, negative_fill).astype(bf16)
        r.peak[b] = jnp.full((1, 256), negative_fill, f32)
        r.acc[b] = jnp.zeros((80, 256), f32)

    def load_keys(slot, jp):
        for b in range(4):
            docs = doc_row(ends, (b * 8 + jp) * 256, 256)
            hot = (feature == docs).astype(f32).astype(bf16)
            r.kaug[256 * b:256 * b + 256, :] = transposed(
                jnp.concatenate([r.kvt[slot, b, 0:64], hot], axis=0))

    def scores(b, n, causal):
        s = dot(r.kaug[0:n, :], r.qaug[b])
        if causal:
            rows = lax.broadcasted_iota(jnp.int32, (n, 256), 0)
            cols = lax.broadcasted_iota(jnp.int32, (n, 256), 1)
            s = jnp.where(rows - 256 * b <= cols, s, negative_fill)
        return s

    def load_chunk(slot, jp):
        load_keys(slot, jp)
        for b in range(4):
            r.vt1[0:64, 256 * b:256 * b + 256] = r.kvt[slot, b, 64:128]

    def forward(tiles, causal):
        def gather(b, n, p, factor):
            r.acc[b] = r.acc[b] * factor + dot(r.vt1[:, 0:n], p)

        held = None
        for b, n in tiles:
            s = scores(b, n, causal)
            if held is not None:
                gather(*held)
            old = r.peak[b]
            new = jnp.maximum(old, jnp.max(s, axis=0, keepdims=True))
            held = (b, n, jnp.exp(s - new).astype(bf16), jnp.exp(old - new))
            r.peak[b] = new
        gather(*held)

    load_chunk(0, j)
    forward([(b, 256 * b + 256) for b in (3, 2, 1, 0)], True)

    def chunk(i, carry):
        u = i // 2
        side = ((u + 1) // 2) % 2
        xp = (x + d * (2 * (i % 2) - 1) * side + 2 * (u // 3) + 8) % 4
        jp = xp * 2 + (c + (1 - side) * (i % 2) + side * (u // 2)) % 2

        @pl.when(i == 1)
        def _():
            from_sides(1)
            from_far(0)
            came_whole(1)

        @pl.when(i == 2)
        def _():
            from_sides(3)
            from_far(1)
            from_sides(2)

        @pl.when(i == 3)
        def _():
            from_far(3)

        @pl.when(i == 4)
        def _():
            from_far(2)
            came_whole(4)
            to_all(lambda to: r.cotq_s.at[to], r.cotq.at[mp, ex], "co")

        @pl.when(i == 5)
        def _():
            came_whole(5)
            arrive(r.wfull.at[0:3, 0:128, :], rr.wf.at[0])
            for i in range(1, 4):
                ym, to = ypeer(4 - i)
                remote(
                    r.wfull.at[ym, half, :], r.wfull.at[ym, half, :], ss.wd.at[0], rr.wd.at[0], sib).start()

        @pl.when(i == 7)
        def _():
            came_whole(7)

        load_chunk(i, jp)

        @pl.when(jp < j)
        def _():
            forward([(b, 256 * b + 256) for b in (3, 2, 1, 0)], False)

        @pl.when(jp > j)
        def _():
            forward([(b, 256 * b) for b in (3, 2, 1)], False)

        return carry

    lax.fori_loop(1, 8, chunk, 0)
    for b in range(4):
        total = r.acc[b, 64:65]
        ot = r.acc[b, 0:64] / total
        r.ot[b] = ot
        r.lse[b] = r.peak[b] + jnp.log(total)
        r.o_s[b] = ot.astype(bf16)
    for i in (1, 3, 2):
        zp, to = zpeer(i)
        push(r.o_s.at[zp], r.att.at[mp, z], ss.oz.at[0], rr.oz.at[i - 1], to)
    r.att[mp, z] = r.o_s[z]
    def normed_half(part):
        rows = pl.ds(128 * part, 128)
        for i in (1, 3):
            zp, to = zpeer(i)
            push(
                r.normed.at[rows, :], r.nall.at[z, rows, :], ss.na.at[0],
                rr.na.at[0], to)

    def attended_piece(k):
        zq = lax.rem(z + 4 - k, 4)
        for i in (1, 3, 2):
            ym, to = ypeer(i)
            push(
                r.att.at[mp, zq], r.att.at[mp, zq], ss.oy.at[0], rr.oy.at[0], to)

    attended_piece(0)
    for k in (1, 3, 2):
        arrive(r.att.at[mp, lax.rem(z + 4 - k, 4)], rr.oz.at[k - 1])
        attended_piece(k)
    normed_half(0)
    arrive(r.cotq.at[0, 0:31], rr.co.at[0])
    arrive(r.wfull.at[0:3, 0:128, :], rr.wd.at[0])
    arrive(r.att.at[0:3], rr.oy.at[0])
    for i in (1, 3, 2):
        ym, to = ypeer(i)
        push(r.cotq.at[mp], r.cotq.at[mp], ss.cy.at[0], rr.cy.at[0], to)
    def geometry(i):
        p = i // 2
        w = p + (p // 2) * (1 - 2 * (p % 2))
        g = (2 + d * w + 4) % 4
        flip = 1 - i % 2
        odd = g % 2
        slot = odd * (2 + g // 2 + 2 * flip) + (1 - odd) * (3 * g + flip)
        xp = (x - d * g + 8) % 4
        return slot, xp, xp * 2 + (c + flip) % 2

    def softmax(i, carry):
        slot, _, jp = geometry(i)
        load_keys(slot, jp)

        def keep(tiles):
            for b, n in tiles:
                r.weights[i, 0:n, 256 * b:256 * b + 256] = jnp.exp(scores(b, n, False) - r.lse[b]).astype(bf16)

        @pl.when(jp < j)
        def _():
            keep([(b, 256 * b + 256) for b in (3, 2, 1, 0)])

        @pl.when(jp > j)
        def _():
            keep([(b, 256 * b) for b in (3, 2, 1)])

        return carry

    value = r.tokens[...].astype(f32) + dot(r.att[...].reshape(1024, 256), r.wfull[...].reshape(1024, 1024), 0, 0)
    r.resid[...] = value
    for k in range(4):
        @pl.when(mp == k)
        def _():
            r.rescol[...] = value[:, 256 * k:256 * k + 256]
    unit, _ = norm_parts(value)
    normed = (unit * r.gain2[...]).astype(bf16)
    for step in (1, 3, 2, 0):
        plane = lax.rem(z + step, 4)
        r.slots[pl.ds(8 * plane, 8)] = dot(
            r.placer[pl.ds(pl.multiple_of(128 * plane, 128), 128), :], normed).astype(bf16).reshape(8, 16, 1024)

        def dispatch(k, carry):
            to = plane * 8 + lax.rem(j + k, 8)
            remote(
                r.slots.at[to], r.slots.at[32 + ex], ss.di.at[0], rr.di.at[0],
                (to, mp)).start()
            return carry

        lax.fori_loop(0 if step else 1, 8, dispatch, 0)
    r.slots[32 + ex] = r.slots[ex]
    lax.fori_loop(4, 7, softmax, 0)
    loads[4].wait()
    arrive(r.cotq.at[0:3], rr.cy.at[0])
    for le in range(2):
        rows = jnp.concatenate([one_expert(r.cotq[k], le) for k in range(4)], axis=1)
        r.crows[le] = rows
        r.gh[le] = dot(rows, r.weights[2 + le], 1, 1)
    loads[5].wait()
    arrive(r.slots.at[32:63], rr.di.at[0])
    def expert_rows(le):
        rows = one_expert(r.slots[32:64], le)
        r.xrows[le] = rows
        return dot(rows, r.weights[le])

    def activate(le, pre):
        hidden, slope = gelu_parts(pre)
        r.hid[le] = hidden.astype(bf16)
        gpre = (r.gh[le] * slope).astype(bf16)
        r.gpre[le] = gpre
        return gpre

    def give_back(le, gpre):
        for k in range(4):
            product = dot(gpre, r.weights[le, 256 * k:256 * k + 256, :], 1, 1)
            r.part[le, k] = product[:, 0:128].astype(bf16)
            r.gh[le, :, 128 * k:128 * k + 128] = product[:, 128:256]
        for i in (1, 3, 2):
            ym, to = ypeer(i)
            push(r.part.at[le, ym], r.rs.at[le, i - 1], ss.rs.at[0], rr.rs.at[0], to)

    first, second = expert_rows(0), expert_rows(1)
    gpre = activate(0, first)
    give_back(0, gpre)
    give_back(1, activate(1, second))
    r.wide_s[...] = both_experts(r.gh[0, :, 0:512], r.gh[1, :, 0:512])
    to_all(lambda to: r.wide_s.at[to], r.wide.at[ex], "bc")
    r.wide[ex] = r.wide_s[ex]
    first = dot(r.hid[0], r.weights[2])
    r.branch[...] = both_experts(first, dot(r.hid[1], r.weights[3]))
    lax.fori_loop(0, 4, softmax, 0)
    arrive(r.rs, rr.rs.at[0])
    sums = []
    for le in range(2):
        total = r.part[le, mp].astype(f32)
        for i in range(3):
            total = total + r.rs[le, i].astype(f32)
        sums.append(total)
    r.back_s[...] = both_experts(sums[0], sums[1])
    to_all(lambda to: r.back_s.at[to], r.back.at[ex], "ba")
    r.back[ex] = r.back_s[ex]
    arrive(r.wide.at[0:31], rr.bc.at[0])
    rows = dot(r.placer[...], r.wide[...].reshape(512, 512), 0, 0).astype(bf16)
    for k in range(4):
        r.gb[k] = rows[:, 128 * k:128 * k + 128]
    for i in (1, 3, 2):
        ym, to = ypeer(i)
        push(r.gb.at[ym], r.gbr.at[i - 1], ss.gb.at[0], rr.gb.at[0], to)
    arrive(r.back.at[0:31], rr.ba.at[0])
    r.gn[0, mp] = dot(r.placer[...], r.back[...].reshape(512, 128), 0, 0).astype(bf16)
    for i in (1, 3, 2):
        ym, to = ypeer(i)
        push(r.gn.at[0, mp], r.gn.at[0, mp], ss.gy.at[0], rr.gy.at[0], to)
    normed_half(1)
    total = r.gb[mp].astype(f32)
    arrive(r.gbr, rr.gb.at[0])
    for i in range(3):
        total = total + r.gbr[i].astype(f32)
    r.gn[1, mp] = total.astype(bf16)
    for i in (1, 3, 2):
        ym, to = ypeer(i)
        push(r.gn.at[1, mp], r.gn.at[1, mp], ss.gy.at[0], rr.gy.at[0], to)
    unit, inverse = norm_parts(r.resid[...])
    left(r.slots.at[0:31], ss.di.at[0])
    load_keys(0, j)
    for b in (3, 2, 1, 0):
        n = 256 * b + 256
        own = jnp.exp(scores(b, n, True) - r.lse[b]).astype(bf16)
        r.slots[0:n // 16, :, 256 * b:256 * b + 256] = own.reshape(n // 16, 16, 256)
    arrive(r.gn.at[:, 0:3], rr.gy.at[0])
    grad = jnp.concatenate([r.gn[k % 2, k // 2] for k in range(8)], axis=1).astype(f32)
    grad_in, ggrad = norm_back(grad, r.gain2[...], unit, inverse)
    r.gsum[1:2] = ggrad
    gres = r.cot[...].astype(f32) + grad_in
    r.gres[...] = gres
    low = gres.astype(bf16)
    r.dheads[...] = dot(r.wfull[mp], low, 1, 1).astype(bf16).reshape(4, 64, 256)
    for i in (1, 3, 2):
        zp, to = zpeer(i)
        push(r.dheads.at[zp], r.dob.at[z], ss.dz.at[0], rr.dz.at[0], to)
    r.dob[z] = r.dheads[z]
    wgrad = dot(r.att[mp].reshape(256, 256), low).astype(bf16)
    r.wgp[0] = wgrad[:, 0:512].reshape(4, 4, 16, 512)
    r.wgp[1] = wgrad[:, 512:1024].reshape(4, 4, 16, 512)
    push(r.wgp.at[1 - c], r.wgs, ss.wg.at[0], rr.wg.at[0], sib)
    for i in range(1, 4):
        ym, to = ypeer(i)
        push(
            r.branch.at[:, :, pl.ds(pl.multiple_of(256 * ym, 256), 256)], r.brs.at[i - 1],
            ss.br.at[0], rr.br.at[0], to)
    zero = jnp.zeros((64, 256), bf16)
    arrive(r.dob.at[0:3], rr.dz.at[0])
    arrive(r.wgs, rr.wg.at[0])
    r.wgq[...] = (r.wgp[c].astype(f32) + r.wgs[...].astype(f32)).astype(bf16)
    for i in (1, 3, 2):
        zp, to = zpeer(i)
        push(r.wgq.at[zp], r.wgz.at[i - 1], ss.wz.at[0], rr.wz.at[0], to)
    for b in range(4):
        r.dopad[b, 0:64] = zero
        r.dopad[b, 64:128] = r.dob[b]
        r.qd[b, 0:256] = transposed(jnp.concatenate([r.q[b], zero], axis=0))
        r.qd[b, 256:512] = transposed(jnp.concatenate([zero, r.dob[b]], axis=0))
        r.delta[b] = jnp.sum(r.dob[b].astype(f32) * r.ot[b], axis=0, keepdims=True)
        r.dq[b] = jnp.zeros((64, 256), f32)

    def load_back(slot):
        for b in range(4):
            r.kvn[256 * b:256 * b + 256, :] = transposed(r.kvt[slot, b])
            r.kt[:, 256 * b:256 * b + 256] = r.kvt[slot, b, 0:64]

    def backward(tiles, weights):
        def gather(b, n, ds, p):
            added = dot(ds, r.qd[b, 0:256]) + dot(p, r.qd[b, 256:512])
            if b == 3:
                r.dkv[0:n] = added
            else:
                r.dkv[0:n] = r.dkv[0:n] + added
            r.dq[b] = r.dq[b] + dot(r.kt[:, 0:n], ds)

        held = None
        for b, n in tiles:
            dp = dot(r.kvn[0:n, :], r.dopad[b])
            p = weights(b, n)
            if held is not None:
                gather(*held)
            held = (b, n, (p * (dp - r.delta[b])).astype(bf16), p.astype(bf16))
        gather(*held)

    def back_chunk(i, carry):
        slot, xp, jp = geometry(i)
        p = i // 2
        load_back(slot)

        def kept(b, n):
            return r.weights[i, 0:n, 256 * b:256 * b + 256]

        @pl.when(jp < j)
        def _():
            backward([(b, 256 * b + 256) for b in (3, 2, 1, 0)], kept)

        @pl.when(jp > j)
        def _():
            r.dkv[768:1024] = jnp.zeros((256, 128), f32)
            backward([(b, 256 * b) for b in (3, 2, 1)], kept)

        @pl.when(i % 2 == 0)
        def _():
            r.sb[p] = r.dkv[...].astype(bf16)
            remote(r.sb.at[p], r.sr.at[p], ss.sb.at[0], rr.sb.at[p], sib).start()

        @pl.when(i % 2 == 1)
        def _():
            arrive(r.sr.at[p], rr.sb.at[p])
            r.xs[p] = (r.dkv[...] + r.sr[p].astype(f32)).astype(bf16)

            @pl.when(p == 0)
            def _():
                remote(r.xs.at[0], r.xr.at[0], ss.xs.at[0], rr.xs.at[0], ahead).start()

            @pl.when(p == 2 - c)
            def _():
                remote(r.xs.at[p], r.xr.at[1], ss.xs.at[0], rr.xs.at[1], behind).start()

            @pl.when(p == 2)
            def _():
                arrive(r.xr.at[0], rr.xs.at[0])
                r.xs[3] = (r.xs[1 + c].astype(f32) + r.xr[0].astype(f32)).astype(bf16)
                remote(r.xs.at[3], r.xr.at[2], ss.xs.at[0], rr.xs.at[2], ahead).start()

        @pl.when(i == 2)
        def _():
            arrive(r.wgz, rr.wz.at[0])
            total = r.wgq[z].astype(f32)
            for k in range(3):
                total = total + r.wgz[k].astype(f32)
            r.wgx[...] = total.astype(bf16)
            for k in (1, 3, 2):
                xq, to = xpeer(k)
                remote(r.wgx.at[xq], r.wgr.at[k - 1], ss.wx.at[0], rr.wx.at[0], to).start()

        @pl.when(i == 6)
        def _():
            total = r.branch[:, :, mine].astype(f32)
            arrive(r.brs, rr.br.at[0])
            for k in range(3):
                total = total + r.brs[k].astype(f32)
            r.bs[...] = total.astype(bf16)
            for k in (1, 3, 2):
                zp, to = zpeer(k)
                remote(
                    r.bs.at[pl.ds(8 * zp, 8)], r.bz.at[z], ss.bb.at[0], rr.bb.at[0], to).start()
            r.bz[z] = r.bs[pl.ds(8 * z, 8)]

        @pl.when(i == 5)
        def _():
            total = r.wgx[x].astype(f32)
            arrive(r.wgr, rr.wx.at[0])
            for k in range(3):
                total = total + r.wgr[k].astype(f32)
            r.wgf[c, z, x] = total.astype(bf16)
            for k in (1, 3, 2):
                _, to = xpeer(k)
                remote(r.wgf.at[c, z, x], r.wgf.at[c, z, x], ss.wa.at[0], rr.wa.at[0], to).start()

        return carry

    lax.fori_loop(0, 7, back_chunk, 0)
    load_back(0)
    backward(
        [(b, 256 * b + 256) for b in (3, 2, 1, 0)],
        lambda b, n: r.slots[0:n // 16, :, 256 * b:256 * b + 256].reshape(n, 256))
    for b in range(4):
        r.zs[b, 0:64] = (r.dq[b] * HEAD_DIM ** (-0.5)).astype(bf16)
    for i in (1, 3, 2):
        zp, to = zpeer(i)
        push(r.zs.at[zp, 0:64], r.zr.at[z, 0:64], ss.zd.at[0], rr.zd.at[0], to)
    arrive(r.nall.at[0:3], rr.na.at[0])

    def weight_part(first, last, pieces, name):
        wt = dot(r.zs[0, first:last], r.nall[0])
        for b in range(1, 4):
            wt = wt + dot(r.zs[b, first:last], r.nall[b])
        wt = wt.astype(bf16)
        for k in range(8):
            pieces[0][k] = wt[:, 128 * k:128 * k + 128]
        for i in range(1, 8):
            jt = lax.rem(j + i, 8)
            push(
                pieces[0].at[jt], pieces[1].at[i - 1], getattr(ss, name).at[0], getattr(rr, name).at[0],
                (z * 8 + jt, mp))

    def weight_sum(pieces, name):
        total = pieces[0][j].astype(f32)
        arrive(pieces[1], getattr(rr, name).at[0])
        for i in range(7):
            total = total + pieces[1][i].astype(f32)
        return total.astype(bf16)

    weight_part(0, 64, (r.wpq, r.wrq), "wp")
    r.resid[...] = norm_parts(r.tokens[...].astype(f32))[0]
    arrive(r.sr.at[3], rr.sb.at[3])
    total = r.dkv[...] + r.sr[3].astype(f32)
    for k in (1, 2):
        arrive(r.xr.at[k], rr.xs.at[k])
        total = total + r.xr[k].astype(f32)
    low = total.astype(bf16)
    for b in range(4):
        r.zs[b, 64:192] = transposed(low[256 * b:256 * b + 256])
    for i in (1, 3, 2):
        zp, to = zpeer(i)
        push(r.zs.at[zp, 64:192], r.zr.at[z, 64:192], ss.zq.at[0], rr.zq.at[0], to)
    r.zr[z] = r.zs[z]
    weight_part(64, 192, (r.wpk, r.wrk), "wk")
    r.pieces[0, c, z, x] = weight_sum((r.wpq, r.wrq), "wp")
    gather_first(0)
    arrive(r.wgf.at[0, 0, 0:3], rr.wa.at[0])
    for k in (1, 3, 2):
        _, to = zpeer(k)
        push(r.wgf.at[c, z], r.wgf.at[c, z], ss.wb.at[0], rr.wb.at[0], to)

    def heads(first):
        return transposed(jnp.concatenate([r.zr[h, first:first + 64] for h in range(4)], axis=0))

    arrive(r.zr.at[0:3, 0:64], rr.zd.at[0])
    part = dot(heads(0), r.wqkv[0], 1, 1)
    arrive(r.zr.at[0:3, 64:192], rr.zq.at[0])
    part = part + dot(heads(64), r.wqkv[1], 1, 1) + dot(heads(128), r.wqkv[2], 1, 1)
    r.gnp[...] = part.astype(bf16).reshape(4, 64, 1024)
    one_gain = jnp.sum(part * r.resid[...], axis=0, keepdims=True)
    r.small[...] = one_gain
    for i in (1, 3, 2):
        ym, to = ypeer(i)
        push(r.small, r.smally.at[i - 1], ss.sy.at[0], rr.sy.at[0], to)
    for first in (0, 32):
        rows = pl.ds(first, 32)
        for i in (1, 3, 2):
            ym, to = ypeer(i)
            push(r.gnp.at[ym, rows, :], r.ry.at[i - 1, rows, :], ss.ry.at[0], rr.ry.at[first // 32], to)
    both = weight_sum((r.wpk, r.wrk), "wk")
    r.pieces[1, c, z, x] = both[0:64]
    r.pieces[2, c, z, x] = both[64:128]
    gather_first(1)
    gather_first(2)
    gather_second(0)
    arrive(r.wgf.at[0, 0:3], rr.wb.at[0])
    push(r.wgf.at[c], r.wgf.at[c], ss.wc.at[0], rr.wc.at[0], sib)
    def norm_rows(first):
        grad = r.gnp[mp, first:first + 32].astype(f32)
        arrive(r.ry.at[:, first:first + 32], rr.ry.at[first // 32])
        for i in range(3):
            grad = grad + r.ry[i, first:first + 32].astype(f32)
        here = pl.ds(pl.multiple_of(64 * mp + first, 32), 32)
        unit, inverse = norm_parts(r.tokens[here, :].astype(f32))
        grad_in, _ = norm_back(grad, r.gain1[...], unit, inverse)
        r.igrad[here, :] = (r.gres[here, :] + grad_in).astype(bf16)
        for i in (1, 3, 2):
            ym, to = ypeer(i)
            push(r.igrad.at[here, :], r.igrad.at[here, :], ss.ay.at[0], rr.ay.at[0], to)

    gather_second(1)
    gather_second(2)
    arrive(r.bz.at[0:3], rr.bb.at[0])
    for i in range(1, 8):
        jt = lax.rem(j + i, 8)
        push(r.bz.at[:, jt], r.bret.at[:, j], ss.bp.at[0], rr.bp.at[0], (z * 8 + jt, mp))
    for b in range(4):
        r.bret[b, j] = r.bz[b, j]
    arrive(r.smally, rr.sy.at[0])
    for i in range(3):
        one_gain = one_gain + r.smally[i]
    r.gsum[0:1] = one_gain
    for i in (1, 3, 2):
        _, to = zpeer(i)
        push(r.gsum, r.gz.at[i - 1], ss.se.at[0], rr.se.at[0], to)
    norm_rows(0)
    gather_third(0)
    norm_rows(32)
    arrive(r.gz, rr.se.at[0])
    r.gps[...] = r.gsum[...] + r.gz[0] + r.gz[1] + r.gz[2]
    for i in range(1, 8):
        jt = lax.rem(j + i, 8)
        push(r.gps, r.gp.at[i - 1], ss.sf.at[0], rr.sf.at[0], (z * 8 + jt, mp))
    arrive(r.wgf.at[1 - c], rr.wc.at[0])
    for k in range(16):
        for core in range(2):
            r.wout_out[16 * k:16 * k + 16, 512 * core:512 * core + 512] = r.wgf[core, k // 4, k % 4]
    gather_third(1)
    gather_third(2)
    for k in range(3):
        arrive(r.pieces.at[k, 1 - c], rr.pc.at[k])
        for row in range(8):
            block = jnp.concatenate([r.pieces[k, row % 2, h, row // 2] for h in range(4)], axis=0)
            r.qkv_out[k, 128 * row:128 * row + 128] = transposed(block)
    arrive(r.bret.at[:, 0:7], rr.bp.at[0])
    rows = dot(r.placer[...], r.bret[...].reshape(512, 256), 0, 0)
    r.out[...] = (r.rescol[...] + rows).astype(bf16)
    arrive(r.gp, rr.sf.at[0])
    both = r.gps[...] + jnp.sum(r.gp[...], axis=0)
    r.gain1_out[...] = both[0:1]
    r.gain2_out[...] = both[1:2]
    arrive(r.igrad.at[0:192, :], rr.ay.at[0])
    sent = {
        "az": r.kv_s.at[0:3], "aq": r.q_s.at[0:3], "ag": r.kvt.at[0:7], "wf": r.wfull.at[0:3, 0:128, :],
        "wd": r.wfull.at[0:3, 0:128, :], "co": r.cotq_s.at[0:31], "cy": r.cotq.at[0:3], "na": r.nall.at[0:3],
        "oz": r.o_s.at[0:3], "oy": r.att.at[0:3], "rs": r.rs, "ba": r.back_s.at[0:31],
        "bc": r.wide_s.at[0:31], "gb": r.gb.at[0:3], "gy": r.gn.at[:, 0:3], "dz": r.dheads.at[0:3], "br": r.brs,
        "bb": r.bz.at[0:3], "bp": r.bret.at[:, 0:7], "sb": r.sb, "xs": r.xs.at[0:3], "wg": r.wgs, "wz": r.wgq.at[0:3], "wx": r.wgr,
        "wa": r.wgr, "wb": r.wgf.at[0, 0:3], "wc": r.wgf.at[0], "zd": r.zs.at[0:3, 0:64], "zq": r.zs.at[0:3, 64:192],
        "wp": r.wrq, "wk": r.wrk, "ry": r.ry, "ay": r.ry, "sy": r.smally, "se": r.gz, "sf": r.gp,
    }
    for name, ref in sent.items():
        left(ref, getattr(ss, name).at[0])
    for part in range(3):
        left(r.pieces.at[0, 0, 0, 0:3], ss.pa.at[part])
        left(r.pieces.at[0, 0, 0:3], ss.pb.at[part])
        left(r.pieces.at[0, 0], ss.pc.at[part])


def layer(*args):
    return pl.pallas_call(
        layer_kernel,
        out_shape=[pltpu.VMEM(s, t) for s, t in OUTS.values()],
        in_specs=[SM, ANY, VM, VM, VM, ANY, ANY, ANY, ANY, ANY],
        out_specs=[VM] * len(OUTS),
        scratch_shapes=[pltpu.VMEM(s, t) for s, t in BUFFERS.values()]
        + [DMA(s) for group in (LOCAL, SENT, TAKEN) for s in group.values()],
        name="layer",
        compiler_params=pltpu.CompilerParams(
            collective_id=0, has_side_effects=True, vmem_limit_bytes=VMEM_BYTES),
    )(*args)


def finish_kernel(x, gpre, hid, cots, qkv, wout, out, igrad, gain1, gain2, *refs):
    in_grad, out_grad, qkv_o, wout_o, out_o, igrad_o, gain1_o, gain2_o = refs[:8]
    in_buf, out_buf, qkv_buf, wout_buf, store, rest = refs[8:]
    stores = []

    def put(src, dst, sem):
        copy = pltpu.make_async_copy(src, dst, sem)
        copy.start()
        stores.append(copy)

    for k, (left, right, buf, result) in enumerate(((x, gpre, in_buf, in_grad), (hid, cots, out_buf, out_grad))):
        for e in range(2):
            for t in range(4):
                rows = pl.ds(256 * t, 256)
                buf[e, rows, :] = dot(left[e, :, 256 * t:256 * t + 256], right[e], 0, 0)
                put(buf.at[e, rows, :], result.at[e, rows, :], store.at[8 * k + 4 * e + t])
    qkv_buf[...] = qkv[...].astype(f32)
    wout_buf[...] = wout[...].astype(f32)
    plain = ((qkv_buf, qkv_o), (wout_buf, wout_o), (out, out_o), (igrad, igrad_o), (gain1, gain1_o), (gain2, gain2_o))
    for k, (src, dst) in enumerate(plain):
        put(src, dst, rest.at[k])
    for copy in stores:
        copy.wait()


def finish(*args):
    big = ((2, 1024, 1024), f32)
    outs = [big, big, ((3, 1024, 256), f32), ((256, 1024), f32), ((256, 256), bf16), ((256, 1024), bf16)]
    outs += [((1, 1024), f32)] * 2
    return pl.pallas_call(
        finish_kernel,
        out_shape=[jax.ShapeDtypeStruct(s, t) for s, t in outs],
        in_specs=[VM] * 10,
        out_specs=[ANY] * 8,
        scratch_shapes=[pltpu.VMEM(s, t) for s, t in outs[:4]] + [DMA((16,)), DMA((6,))],
        name="finish",
        compiler_params=pltpu.CompilerParams(vmem_limit_bytes=36 << 20),
        cost_estimate=pl.CostEstimate(flops=2 * 2 * 2 * 256 * 1024 * 1024, bytes_accessed=28 << 20, transcendentals=0),
    )(*args)


def on_device(
    tokens, hash_ids, lengths, norm1_gain, qkv_weight, out_weight, norm2_gain, expert_in, expert_out, cotangent,
):
    x, cots, hid, gpre, out, igrad, gain1, gain2, qkv, wout = layer(
        lengths, tokens, norm1_gain.reshape(1, 1024), norm2_gain.reshape(1, 1024), hash_ids.reshape(1, 256),
        jnp.transpose(qkv_weight, (1, 0, 2)), out_weight, cotangent, expert_in, expert_out)
    in_grad, out_grad, qkv, wout, out, igrad, gain1, gain2 = finish(
        x, gpre, hid, cots, qkv, wout, out, igrad, gain1, gain2)
    return out, igrad, gain1.reshape(1024), jnp.transpose(qkv, (1, 0, 2)), wout, gain2.reshape(1024), in_grad, out_grad


def solution(mesh):
    placed = (
        P("ex", None), P("ex", None), P(), P(), P(None, None, "mp"), P("mp", None), P(),
        P("ex", None, "mp"), P("ex", "mp", None), P("ex", None),
    )
    return jax.shard_map(
        on_device,
        mesh=mesh,
        in_specs=placed,
        out_specs=(
            P("ex", "mp"), P("ex", None), P(), P(None, None, "mp"), P("mp", None), P(),
            P("ex", None, "mp"), P("ex", "mp", None),
        ),
        check_vma=False,
    )
```
